32 devices in a mesh: groups: 2 (over x), clus: 16 (over z, y, core).
Axes of the slice: x: 2, y: 2, z: 4, core: 2. Of those that a mesh axis runs over, the one named last changes fastest.
Arguments:
- mesh_current: float32 [2, 131072], P(None, ('groups', 'clus')), parts along dimension 1, may hold values from -6 to 6
- branch_entry: int32 [2, 262144], P(None, ('groups', 'clus')), parts along dimension 1, may hold values from 0 to 6143, as said below
- branch_sign: int32 [2, 262144], P(None, ('groups', 'clus')), parts along dimension 1, may hold values from 0 to 1
- need_slots: int32 [512, 128], P(('groups', 'clus')), parts along dimension 0, may hold values from -1 to 4095, as said below
- resistance: float32 [262144], P(('groups', 'clus')), parts along dimension 0, may hold values from 0.3 to 3
- near_blocks: bfloat16 [2048, 4, 128, 128], P(('groups', 'clus')), parts along dimension 0, may hold values from -0.25 to 0.25
- near_source: int32 [2048, 4], P(('groups', 'clus')), parts along dimension 0, may hold values from 0 to 63
- basis_in: bfloat16 [2048, 32, 128], P(('groups', 'clus')), parts along dimension 0, may hold values from -0.5 to 0.5
- coupling: bfloat16 [2048, 16, 32, 32], P(('groups', 'clus')), parts along dimension 0, may hold values from -0.25 to 0.25
- basis_out: bfloat16 [2048, 32, 128], P(('groups', 'clus')), parts along dimension 0, may hold values from -1 to 1
- admissible: int32 [2048, 16], P(('groups', 'clus')), parts along dimension 0, may hold values from 0 to 1023, as said below
- port_mesh: int32 [128], P('groups'), parts along dimension 0, may hold values from 0 to 65535, as said below
- port_coupling: float32 [2, 64, 64], replicated, may hold values from -0.75 to 0.75
Outputs:
- mesh_voltage: float32 [2, 131072], P(None, ('groups', 'clus')), parts along dimension 1
The draws below stay inside these ranges and needn't reach their ends.
There are 2 independent parts, one for each index of `groups`. The reference program is written for one: setup_inputs(seed, part) draws one part's arguments, and reference() takes and returns one part's arrays. A program takes and returns all parts, laid end to end along the dimension named above; an argument that names none is the same for every part. Nothing has to cross between parts.
Inputs may be any that keep to these rules, and one draw needn't show every extreme that they name: `need_slots`: row d * 16 + p holds distinct meshes of device p, counted from 0 within it, in its first slots and -1 in the rest. Row d * 16 + d is all -1; row d * 16 + (d + 1) % 16 has no -1. `branch_entry`: A value below 4096 is a mesh of the branch's own device d. Any other value is 4096 + p * 128 + s with p != d and slot s of row d * 16 + p of need_slots not -1. `admissible`: entry k of row t is (t + k * 64 + o) % 1024 with 1 <= o < 64; the entries of a row are distinct and never t. `port_mesh`: distinct meshes.
All inputs are finite; a program needn't handle non-finite values.
Results may differ from the reference program's by a relative error of at most 0.0021.
Values may be sent and summed in bfloat16 or wider, within the bound.
No kernel may reach another device: no remote copies, remote signals or barrier semaphores. Data moves between devices by JAX's collectives and lax.ppermute only.
A program may use at most 320 MiB of HBM per device.

```python
import math
import jax
import jax.numpy as jnp
from jax import lax

TILE_SIZE = 128
FAR_RANK = 32
NEAR_COUNT = 4
FAR_COUNT = 16
ENTRIES = 2
SLOT_COUNT = 128
PORT_COUNT = 64
TILE_DEV = 64
BRANCH_DEV = 8192
MESH_DEV = 4096
TILES = 1024
BRANCHES = 131072
MESHES = 65536
N_CLUS = 16


def slot_counts(key):
    drawn_counts = jax.random.randint(jax.random.fold_in(key, 11), (N_CLUS, N_CLUS), 1, SLOT_COUNT + 1)
    device_rows = jnp.arange(N_CLUS, dtype=jnp.int32)
    filled = device_rows[None, :] == (device_rows[:, None] + 1) % N_CLUS
    counts = jnp.where(filled, SLOT_COUNT, drawn_counts)
    return jnp.where(device_rows[:, None] == device_rows[None, :], 0, counts).astype(jnp.int32)


def first_meshes(one_key):
    return jax.random.permutation(one_key, MESH_DEV)[:SLOT_COUNT].astype(jnp.int32)


def draw_need_slots(key, part):
    counts = slot_counts(key).reshape(-1)
    mesh_keys = jax.random.split(jax.random.fold_in(key, 12), N_CLUS * N_CLUS)
    chosen = jax.vmap(first_meshes)(mesh_keys)
    places = jnp.arange(SLOT_COUNT, dtype=jnp.int32)
    return jnp.where(places[None, :] < counts[:, None], chosen, -1).astype(jnp.int32)


def draw_branch_entry(key, part):
    counts = slot_counts(key)
    entry_shape = (ENTRIES, BRANCHES)
    owner_device = jnp.broadcast_to(jnp.arange(BRANCHES, dtype=jnp.int32) // BRANCH_DEV, entry_shape)
    remote = jax.random.randint(jax.random.fold_in(key, 21), entry_shape, 0, 4) == 0
    peer_step = jax.random.randint(jax.random.fold_in(key, 22), entry_shape, 1, N_CLUS)
    peer = (owner_device + peer_step) % N_CLUS
    filled = counts[owner_device, peer]
    slot_place = jax.random.randint(jax.random.fold_in(key, 23), entry_shape, 0, filled)
    local_mesh = jax.random.randint(jax.random.fold_in(key, 24), entry_shape, 0, MESH_DEV)
    forced = (jnp.arange(BRANCHES, dtype=jnp.int32)[None, :] % BRANCH_DEV == 0) & (jnp.arange(ENTRIES, dtype=jnp.int32)[:, None] == ENTRIES - 1)
    peer = jnp.where(forced, (owner_device + 1) % N_CLUS, peer)
    slot_place = jnp.where(forced, SLOT_COUNT - 1, slot_place)
    remote = remote | forced
    return jnp.where(remote, MESH_DEV + peer * SLOT_COUNT + slot_place, local_mesh).astype(jnp.int32)


def draw_admissible(key, part):
    band_width = TILES // FAR_COUNT
    band_offset = jax.random.randint(jax.random.fold_in(key, 41), (TILES, FAR_COUNT), 1, band_width)
    tile_rows = jnp.arange(TILES, dtype=jnp.int32)[:, None]
    band_index = jnp.arange(FAR_COUNT, dtype=jnp.int32)[None, :]
    return ((tile_rows + band_index * band_width + band_offset) % TILES).astype(jnp.int32)


def draw_port_mesh(key, part):
    return jax.random.permutation(jax.random.fold_in(key, 51), MESHES)[:PORT_COUNT].astype(jnp.int32)


def plant(result, rng, smallest, largest):
    place = [jax.random.randint(jax.random.fold_in(rng, axis), (), 0, length) for axis, length in enumerate(result.shape)]
    longest = result.shape.index(max(result.shape))
    beside = place[:longest] + [(place[longest] + 1) % result.shape[longest]] + place[longest + 1:]
    return result.at[tuple(place)].set(smallest).at[tuple(beside)].set(largest)


def block_levels(key, extent, cuts, least, largest):
    factor_of, own = 1.0, jax.random.fold_in(key, 6)
    for dim, shards_of in cuts:
        steps = jnp.exp(jax.random.uniform(jax.random.fold_in(own, dim), (shards_of,), jnp.float32, least / len(cuts), largest / len(cuts)))
        factor_of = factor_of * jnp.repeat(steps, extent[dim] // shards_of).reshape([-1 if axis == dim else 1 for axis in range(len(extent))])
    return factor_of


def scatter_about(own_key, dims, spread, limit, pieces=(), kind=jnp.bfloat16):
    result = jax.random.normal(own_key, dims, jnp.float32) * spread
    if len(pieces) > 0:
        result = block_levels(own_key, dims, pieces, -0.22, 0.18) * result
    return jnp.clip(result, min=-limit, max=limit).astype(kind)


def setup_inputs(seed: int = 0, part: int = 0) -> dict:
    seeds = jax.random.split(jax.random.key(seed), 14)
    part_keys = jax.random.split(jax.random.fold_in(seeds[13], part), 14)
    return {
        "mesh_current": scatter_about(part_keys[0], (2, MESHES), 1.0, 6.0, ((1, 16),), jnp.float32),
        "branch_entry": draw_branch_entry(jax.random.fold_in(jax.random.fold_in(seeds[13], part), 71), part),
        "branch_sign": plant(jax.random.randint(part_keys[2], (ENTRIES, BRANCHES), 0, 2), jax.random.fold_in(part_keys[2], 1), 0, 1).astype(jnp.int32),
        "need_slots": draw_need_slots(jax.random.fold_in(jax.random.fold_in(seeds[13], part), 71), part),
        "resistance": jnp.clip(jnp.exp(math.log(3.0) - 2.3025851 * jax.random.uniform(part_keys[4], (BRANCHES,), jnp.float32) ** block_levels(part_keys[4], (BRANCHES,), ((0, 16),), -0.2, 0.2)), 0.3, 3.0),
        "near_blocks": scatter_about(part_keys[5], (TILES, NEAR_COUNT, TILE_SIZE, TILE_SIZE), (NEAR_COUNT * TILE_SIZE) ** -0.5, 0.25, ((0, 16),)),
        "near_source": plant(jax.random.randint(part_keys[6], (TILES, NEAR_COUNT), 0, TILE_DEV), jax.random.fold_in(part_keys[6], 1), 0, TILE_DEV - 1).astype(jnp.int32),
        "basis_in": scatter_about(part_keys[7], (TILES, FAR_RANK, TILE_SIZE), TILE_SIZE ** -0.5, 0.5, ((0, 16),)),
        "coupling": scatter_about(part_keys[8], (TILES, FAR_COUNT, FAR_RANK, FAR_RANK), (FAR_COUNT * FAR_RANK) ** -0.5, 0.25, ((0, 16),)),
        "basis_out": scatter_about(part_keys[9], (TILES, FAR_RANK, TILE_SIZE), FAR_RANK ** -0.5, 1.0, ((0, 16),)),
        "admissible": draw_admissible(jax.random.fold_in(jax.random.fold_in(seeds[13], part), 71), part),
        "port_mesh": draw_port_mesh(jax.random.fold_in(jax.random.fold_in(seeds[13], part), 71), part),
        "port_coupling": scatter_about(seeds[12], (2, PORT_COUNT, PORT_COUNT), PORT_COUNT ** -0.5, 0.75, (), jnp.float32),
    }


def near_part(block):
    blocks, source, inputs = block
    gathered = inputs[:, source]
    return jnp.einsum("tkij,ctkj->cti", blocks.astype(jnp.float32), gathered.astype(jnp.float32))


def segment_one(values, segment_ids):
    return jax.ops.segment_sum(values, segment_ids, num_segments=MESHES)


def reference(mesh_current, branch_entry, branch_sign, need_slots, resistance, near_blocks, near_source, basis_in, coupling, basis_out, admissible, port_mesh, port_coupling):
    devices = jnp.arange(N_CLUS, dtype=jnp.int32)
    table_width = MESH_DEV + N_CLUS * SLOT_COUNT
    needed = jnp.maximum(need_slots, 0).reshape(N_CLUS, N_CLUS * SLOT_COUNT)
    owner_base = jnp.repeat(devices * MESH_DEV, SLOT_COUNT)
    slot_mesh = needed + owner_base[None, :]
    own_mesh = devices[:, None] * MESH_DEV + jnp.arange(MESH_DEV, dtype=jnp.int32)[None, :]
    lookup_table = jnp.concatenate([own_mesh, slot_mesh], axis=1).reshape(-1)
    entries = branch_entry.reshape(ENTRIES, N_CLUS, BRANCH_DEV)
    flat_index = (devices[None, :, None] * table_width + entries).astype(jnp.int32)
    incident = lookup_table[flat_index].reshape(ENTRIES, BRANCHES)
    orient = (2 * branch_sign - 1).astype(jnp.float32)
    branch_current = jnp.sum(orient[None] * mesh_current[:, incident], axis=1)
    branch_input = branch_current.astype(jnp.bfloat16).reshape(2, TILES, TILE_SIZE)
    by_device = jnp.transpose(branch_input.reshape(2, N_CLUS, TILE_DEV, TILE_SIZE), (1, 0, 2, 3))
    near = lax.map(near_part, (near_blocks.reshape(N_CLUS, TILE_DEV, NEAR_COUNT, TILE_SIZE, TILE_SIZE), near_source.reshape(N_CLUS, TILE_DEV, NEAR_COUNT), by_device))
    near_field = jnp.transpose(near, (1, 0, 2, 3)).reshape(2, TILES, TILE_SIZE)
    far_coeff = jnp.einsum("tri,cti->ctr", basis_in.astype(jnp.float32), branch_input.astype(jnp.float32)).astype(jnp.bfloat16)
    picked = far_coeff[:, admissible]
    far_mixed = jnp.einsum("tkrq,ctkq->ctr", coupling.astype(jnp.float32), picked.astype(jnp.float32)).astype(jnp.bfloat16)
    far_field = jnp.einsum("tri,ctr->cti", basis_out.astype(jnp.float32), far_mixed.astype(jnp.float32))
    reactive = (near_field + far_field).reshape(2, BRANCHES)
    branch_voltage = resistance[None, :] * branch_current + jnp.stack([-reactive[1], reactive[0]])
    contributions = (orient[None] * branch_voltage[:, None, :]).reshape(2, -1)
    mesh_voltage = jax.vmap(segment_one, in_axes=(0, None))(contributions, incident.reshape(-1))
    port_current = mesh_current[:, port_mesh]
    high = lax.Precision.HIGHEST
    real_part = jnp.dot(port_coupling[0], port_current[0], precision=high) - jnp.dot(port_coupling[1], port_current[1], precision=high)
    imag_part = jnp.dot(port_coupling[0], port_current[1], precision=high) + jnp.dot(port_coupling[1], port_current[0], precision=high)
    mesh_voltage = mesh_voltage.at[:, port_mesh].add(jnp.stack([real_part, imag_part]))
    return mesh_voltage
```

```python
import functools

import jax
import jax.numpy as jnp
from jax import lax
from jax.experimental import pallas as pl
from jax.experimental.pallas import tpu as pltpu
from jax.sharding import PartitionSpec as P

F32 = jnp.float32
BF16 = jnp.bfloat16
VMEM_LIMIT = 48 * 1024 * 1024
NT = (((1,), (1,)), ((), ()))


def params():
    return pltpu.CompilerParams(vmem_limit_bytes=VMEM_LIMIT)


def lane_pick(row, lanes):
    spread = jnp.broadcast_to(row, lanes.shape)
    return jnp.take_along_axis(spread, lanes, axis=1, mode="promise_in_bounds")


def dot_nt(left, right, precision=None):
    return lax.dot_general(
        left, right, NT, preferred_element_type=F32, precision=precision
    )


def serve_kernel(mesh_ref, asked_ref, port_ref, out_ref):
    rows = mesh_ref.shape[1] // 128
    peers = asked_ref.shape[0]
    asked = jnp.maximum(asked_ref[...], 0)
    high, low = asked >> 7, asked & 127
    port = jnp.broadcast_to(port_ref[...], (8, 128))
    port_high, port_low = port >> 7, port & 127
    real = jnp.zeros(asked.shape, F32)
    imag = jnp.zeros(asked.shape, F32)
    port_value = jnp.zeros((8, 128), F32)
    lane = lax.broadcasted_iota(jnp.int32, (8, 128), 1)
    for r in range(rows):
        real_row = mesh_ref[0:1, r * 128 : (r + 1) * 128]
        imag_row = mesh_ref[1:2, r * 128 : (r + 1) * 128]
        here = high == r
        real = jnp.where(here, lane_pick(real_row, low), real)
        imag = jnp.where(here, lane_pick(imag_row, low), imag)
        both = jnp.where(
            lane < 64, lane_pick(real_row, port_low), lane_pick(imag_row, port_low)
        )
        port_value = jnp.where(port_high == r, both, port_value)
    out_ref[:, 0, :] = real
    out_ref[:, 1, :] = imag
    out_ref[:, 2, :] = jnp.broadcast_to(port_value[0:1], (peers, 128))
    out_ref[:, 3, :] = jnp.zeros((peers, 128), F32)


def current_kernel(mesh_ref, remote_ref, code_ref, basis_ref, current_ref, input_ref, coeff_ref):
    own_rows = mesh_ref.shape[1] // 128
    peers = remote_ref.shape[0]
    tiles = code_ref.shape[1]

    def lookup(g, carry):
        start = pl.multiple_of(g * 8, 8)
        total = [None, None]
        for k in range(2):
            code = code_ref[k, pl.ds(start, 8), :]
            entry = code >> 1
            high, low = entry >> 7, entry & 127
            value = [jnp.zeros((8, 128), F32), jnp.zeros((8, 128), F32)]
            for r in range(own_rows + peers):
                here = high == r
                for c in range(2):
                    if r < own_rows:
                        row = mesh_ref[c : c + 1, r * 128 : (r + 1) * 128]
                    else:
                        row = remote_ref[r - own_rows, c : c + 1, :]
                    value[c] = jnp.where(here, lane_pick(row, low), value[c])
            along = (code & 1) == 1
            for c in range(2):
                signed = jnp.where(along, value[c], -value[c])
                total[c] = signed if k == 0 else total[c] + signed
        current_ref[0, pl.ds(start, 8), :] = total[0]
        current_ref[1, pl.ds(start, 8), :] = total[1]
        return carry

    lax.fori_loop(0, tiles // 8, lookup, 0)
    block_row = lax.broadcasted_iota(jnp.int32, (16, 256), 0) % 8
    block_lane = lax.broadcasted_iota(jnp.int32, (16, 256), 1) // 32
    own_block = block_row == block_lane
    fold = (
        lax.broadcasted_iota(jnp.int32, (256, 128), 0) % 32
        == lax.broadcasted_iota(jnp.int32, (256, 128), 1) % 32
    ).astype(F32).astype(BF16)
    lane = lax.broadcasted_iota(jnp.int32, (8, 128), 1)
    for g in range(tiles // 8):
        real = current_ref[0, g * 8 : g * 8 + 8, :]
        imag = current_ref[1, g * 8 : g * 8 + 8, :]
        both = jnp.concatenate([real, imag], axis=0).astype(BF16)
        rounded = both.astype(F32)
        input_ref[g * 8 : g * 8 + 8, 0, :] = rounded[0:8]
        input_ref[g * 8 : g * 8 + 8, 1, :] = rounded[8:16]
        full = dot_nt(both, basis_ref[g * 256 : (g + 1) * 256, :])
        kept = jnp.where(own_block, full, 0.0).astype(BF16)
        coeff = jnp.dot(kept, fold, preferred_element_type=F32)
        coeff_ref[g * 8 : g * 8 + 8, :] = jnp.where(lane % 64 < 32, coeff[0:8], coeff[8:16])


def near_kernel(source_ref, input_ref, blocks_ref, out_ref):
    step = pl.program_id(0)
    count = blocks_ref.shape[1]
    for t in range(blocks_ref.shape[0]):
        total = None
        for k in range(count):
            picked = input_ref[source_ref[step * blocks_ref.shape[0] + t, k]]
            picked = jnp.concatenate([picked, jnp.zeros((6, 128), F32)], axis=0)
            term = dot_nt(picked.astype(BF16), blocks_ref[t, k])
            total = term if total is None else total + term
        out_ref[0, t : t + 1, :] = total[0:1]
        out_ref[1, t : t + 1, :] = total[1:2]


def split(value):
    top = value.astype(BF16)
    return top, (value - top.astype(F32)).astype(BF16)


def place(high, low, values, rows):
    sub_high = lax.broadcasted_iota(jnp.int32, (rows, 128), 0)
    sub_low = lax.broadcasted_iota(jnp.int32, (128, 128), 0)
    left, right = [], []
    for i in range(high.shape[0]):
        here = jnp.broadcast_to(high[i : i + 1], (rows, 128)) == sub_high
        parts = []
        for value in values:
            spread = jnp.where(here, jnp.broadcast_to(value[i : i + 1], (rows, 128)), 0.0)
            parts.extend(split(spread))
        left.append(jnp.concatenate(parts, axis=0))
        there = jnp.broadcast_to(low[i : i + 1], (128, 128)) == sub_low
        right.append(jnp.where(there, 1.0, 0.0).astype(BF16))
    return jnp.concatenate(left, axis=1), jnp.concatenate(right, axis=1)


def voltage_kernel(
    place_ref, coeff_ref, admissible_ref, coupling_ref, basis_ref, near_ref, current_ref,
    resistance_ref, code_ref, own_ref, slot_ref, voltage_ref, total_ref,
):
    peers, tile_dev, _ = coeff_ref.shape
    far_count = admissible_ref.shape[1]
    all_tiles = peers * tile_dev
    band = all_tiles // far_count
    spans = band // tile_dev + 1
    own_rows = own_ref.shape[1]
    rows = own_rows + peers
    device = place_ref[0]
    window = lax.broadcasted_iota(jnp.int32, (tile_dev, spans * tile_dev), 1)
    lane_block = lax.broadcasted_iota(jnp.int32, (tile_dev, 128), 1) // 32
    quads = [[], []]
    for quad in range(far_count // 4):
        pieces = []
        for k in range(quad * 4, quad * 4 + 4):
            first = device + k * (band // tile_dev)
            blocks = [coeff_ref[(first + i) % peers] for i in range(spans)]
            column = admissible_ref[:, k : k + 1] - (first % peers) * tile_dev
            column = jnp.where(column < 0, column + all_tiles, column)
            picks = jnp.where(column == window, 1.0, 0.0).astype(BF16)
            piece = jnp.dot(picks, jnp.concatenate(blocks, axis=0), preferred_element_type=F32)
            pieces.append((piece, pltpu.roll(piece, 32, 1)))
        for c in range(2):
            chosen = pieces[0][c]
            for b in range(1, 4):
                chosen = jnp.where(lane_block == b, pieces[b][(b + c) % 2], chosen)
            quads[c].append(chosen)
    picked = [jnp.concatenate(parts, axis=1) for parts in quads]
    own_block = (
        lax.broadcasted_iota(jnp.int32, (16, 256), 0) % 8
        == lax.broadcasted_iota(jnp.int32, (16, 256), 1) // 32
    )
    for g in range(tile_dev // 8):
        rows8 = slice(g * 8, g * 8 + 8)
        both = jnp.concatenate([picked[0][rows8], picked[1][rows8]], axis=0).astype(BF16)
        mixed = dot_nt(both, coupling_ref[g * 256 : (g + 1) * 256, :])
        mixed = jnp.where(own_block, mixed, 0.0).astype(BF16)
        far = jnp.dot(mixed, basis_ref[g * 256 : (g + 1) * 256, :], preferred_element_type=F32)
        resistance = resistance_ref[rows8, :]
        voltage_ref[0, rows8, :] = resistance * current_ref[0, rows8, :] - (
            near_ref[1, rows8, :] + far[8:16]
        )
        voltage_ref[1, rows8, :] = resistance * current_ref[1, rows8, :] + (
            near_ref[0, rows8, :] + far[0:8]
        )
    total_ref[...] = jnp.zeros_like(total_ref)

    def gather_up(g, carry):
        start = pl.multiple_of(g * 8, 8)
        for k in range(2):
            code = code_ref[k, pl.ds(start, 8), :]
            entry = code >> 1
            along = (code & 1) == 1
            values = []
            for c in range(2):
                voltage = voltage_ref[c, pl.ds(start, 8), :]
                values.append(jnp.where(along, voltage, -voltage))
            left, right = place(entry >> 7, entry & 127, values, rows)
            total_ref[...] += dot_nt(left, right)
        return carry

    lax.fori_loop(0, tile_dev // 8, gather_up, 0)
    for c in range(2):
        summed = total_ref[2 * c * rows : (2 * c + 1) * rows, :] + total_ref[
            (2 * c + 1) * rows : (2 * c + 2) * rows, :
        ]
        own_ref[c] = summed[:own_rows]
        slot_ref[:, c, :] = summed[own_rows:]


def finish_kernel(own_ref, arrived_ref, asked_ref, port_ref, remote_ref, impedance_ref, out_ref):
    rows = own_ref.shape[1]
    ports = impedance_ref.shape[1]
    peers = asked_ref.shape[0]
    asked = asked_ref[...]
    total = None
    for start in range(0, peers, 8):
        part = asked[start : start + 8]
        values = [arrived_ref[start : start + 8, c, :] for c in range(2)]
        left, right = place(part >> 7, part & 127, values, rows)
        term = dot_nt(left, right)
        total = term if total is None else total + term
    port_current = jnp.sum(remote_ref[:, 2, :], axis=0, keepdims=True)
    real = port_current[:, :ports]
    imag = port_current[:, ports:]
    both = jnp.concatenate([real, imag, jnp.zeros((6, ports), F32)], axis=0)
    by_real = dot_nt(both, impedance_ref[0], lax.Precision.HIGHEST)
    by_imag = dot_nt(both, impedance_ref[1], lax.Precision.HIGHEST)
    pad = jnp.zeros((1, 128 - ports), F32)
    terms = [
        jnp.concatenate([by_real[0:1] - by_imag[1:2], pad], axis=1),
        jnp.concatenate([by_real[1:2] + by_imag[0:1], pad], axis=1),
    ]
    port = port_ref[...]
    port = jnp.where(lax.broadcasted_iota(jnp.int32, port.shape, 1) < ports, port, -1)
    left, right = place(port >> 7, port & 127, terms, rows)
    total = total + dot_nt(left, right)
    for c in range(2):
        summed = own_ref[c] + (
            total[2 * c * rows : (2 * c + 1) * rows] + total[(2 * c + 1) * rows : (2 * c + 2) * rows]
        )
        for r in range(rows):
            out_ref[c : c + 1, r * 128 : (r + 1) * 128] = summed[r : r + 1]


def per_device(
    mesh_current,
    branch_entry,
    branch_sign,
    need_slots,
    resistance,
    near_blocks,
    near_source,
    basis_in,
    coupling,
    basis_out,
    admissible,
    port_mesh,
    port_coupling,
):
    peers = lax.axis_size("clus")
    device = lax.axis_index("clus")
    mesh_dev = mesh_current.shape[1]
    tiles, near_count, width, _ = near_blocks.shape
    rank = basis_in.shape[1]
    far_count = admissible.shape[1]
    own_rows = mesh_dev // 128
    vmem = pl.BlockSpec(memory_space=pltpu.VMEM)
    smem = pl.BlockSpec(memory_space=pltpu.SMEM)
    shape = jax.ShapeDtypeStruct

    port_here = port_mesh - device * mesh_dev
    owned = (port_here >= 0) & (port_here < mesh_dev)
    port_here = jnp.where(owned, port_here, -1)
    port_pair = jnp.concatenate([port_here, port_here]).reshape(1, 128)
    code = (branch_entry * 2 + branch_sign).reshape(2, tiles, width)
    coupling_rows = jnp.transpose(coupling, (0, 2, 1, 3)).reshape(tiles * rank, far_count * rank)
    basis_in_rows = basis_in.reshape(tiles * rank, width)
    basis_out_rows = basis_out.reshape(tiles * rank, width)

    asked = lax.all_to_all(need_slots, "clus", 0, 0, tiled=True)
    served = pl.pallas_call(
        serve_kernel,
        out_shape=shape((peers, 4, 128), F32),
        in_specs=[vmem] * 3,
        out_specs=vmem,
        compiler_params=params(),
        name="serve",
    )(mesh_current, asked, port_pair)
    remote = lax.all_to_all(served, "clus", 0, 0, tiled=True)
    current, tile_input, coeff = pl.pallas_call(
        current_kernel,
        out_shape=(
            shape((2, tiles, width), F32),
            shape((tiles, 2, width), F32),
            shape((tiles, 128), F32),
        ),
        in_specs=[vmem] * 4,
        out_specs=(vmem,) * 3,
        compiler_params=params(),
        name="currents",
    )(mesh_current, remote, code, basis_in_rows)
    all_coeff = lax.all_gather(coeff.astype(BF16), "clus", axis=0, tiled=False)
    step = 8
    near = pl.pallas_call(
        near_kernel,
        out_shape=shape((2, tiles, width), F32),
        grid_spec=pltpu.PrefetchScalarGridSpec(
            num_scalar_prefetch=1,
            grid=(tiles // step,),
            in_specs=[
                pl.BlockSpec((tiles, 2, width), lambda i, s: (0, 0, 0)),
                pl.BlockSpec((step, near_count, width, width), lambda i, s: (i, 0, 0, 0)),
            ],
            out_specs=pl.BlockSpec((2, step, width), lambda i, s: (0, i, 0)),
        ),
        compiler_params=params(),
        cost_estimate=pl.CostEstimate(
            flops=4 * near_blocks.size, bytes_accessed=2 * near_blocks.size, transcendentals=0
        ),
        name="near_field",
    )(near_source, tile_input, near_blocks)
    own, slots = pl.pallas_call(
        voltage_kernel,
        out_shape=(shape((2, own_rows, 128), F32), shape((peers, 2, 128), F32)),
        in_specs=[smem] + [vmem] * 8,
        out_specs=(vmem,) * 2,
        scratch_shapes=[
            pltpu.VMEM((2, tiles, width), F32),
            pltpu.VMEM((4 * (own_rows + peers), 128), F32),
        ],
        compiler_params=params(),
        name="voltages",
    )(
        device.reshape(1),
        all_coeff,
        admissible,
        coupling_rows,
        basis_out_rows,
        near,
        current,
        resistance.reshape(tiles, width),
        code,
    )
    arrived = lax.all_to_all(slots, "clus", 0, 0, tiled=True)
    return pl.pallas_call(
        finish_kernel,
        out_shape=shape((2, mesh_dev), F32),
        in_specs=[vmem] * 6,
        out_specs=vmem,
        compiler_params=params(),
        name="finish",
    )(own, arrived, asked, port_pair, remote, port_coupling)


def solution(mesh):
    in_specs = (
        P(None, ("groups", "clus")),
        P(None, ("groups", "clus")),
        P(None, ("groups", "clus")),
        P(("groups", "clus"), None),
        P(("groups", "clus")),
        P(("groups", "clus"), None, None, None),
        P(("groups", "clus"), None),
        P(("groups", "clus"), None, None),
        P(("groups", "clus"), None, None, None),
        P(("groups", "clus"), None, None),
        P(("groups", "clus"), None),
        P("groups"),
        P(),
    )
    out_specs = P(None, ("groups", "clus"))
    return jax.shard_map(
        per_device, mesh=mesh, in_specs=in_specs, out_specs=out_specs, check_vma=False
    )
```

```python
import functools

import jax
import jax.numpy as jnp
from jax import lax
from jax.experimental import pallas as pl
from jax.experimental.pallas import tpu as pltpu
from jax.sharding import PartitionSpec as P

F32 = jnp.float32
BF16 = jnp.bfloat16
VMEM_LIMIT = 48 * 1024 * 1024
NT = (((1,), (1,)), ((), ()))


def params():
    return pltpu.CompilerParams(vmem_limit_bytes=VMEM_LIMIT)


def small_cost():
    return pl.CostEstimate(flops=10**9, bytes_accessed=8 * 10**6, transcendentals=0)


def lane_pick(row, lanes):
    spread = jnp.broadcast_to(row, lanes.shape)
    return jnp.take_along_axis(spread, lanes, axis=1, mode="promise_in_bounds")


def dot_nt(left, right, precision=None):
    return lax.dot_general(
        left, right, NT, preferred_element_type=F32, precision=precision
    )


def serve_kernel(mesh_ref, asked_ref, port_ref, out_ref):
    rows = mesh_ref.shape[1] // 128
    peers = asked_ref.shape[0]
    asked = jnp.maximum(asked_ref[...], 0)
    high, low = asked >> 7, asked & 127
    port = jnp.broadcast_to(port_ref[...], (8, 128))
    port_high, port_low = port >> 7, port & 127
    real = jnp.zeros(asked.shape, F32)
    imag = jnp.zeros(asked.shape, F32)
    port_value = jnp.zeros((8, 128), F32)
    lane = lax.broadcasted_iota(jnp.int32, (8, 128), 1)
    for r in range(rows):
        real_row = mesh_ref[0:1, r * 128 : (r + 1) * 128]
        imag_row = mesh_ref[1:2, r * 128 : (r + 1) * 128]
        here = high == r
        real = jnp.where(here, lane_pick(real_row, low), real)
        imag = jnp.where(here, lane_pick(imag_row, low), imag)
        both = jnp.where(
            lane < 64, lane_pick(real_row, port_low), lane_pick(imag_row, port_low)
        )
        port_value = jnp.where(port_high == r, both, port_value)
    out_ref[:, 0, :] = real
    out_ref[:, 1, :] = imag
    out_ref[:, 2, :] = jnp.broadcast_to(port_value[0:1], (peers, 128))
    out_ref[:, 3, :] = jnp.zeros((peers, 128), F32)


def own_lookup_kernel(mesh_ref, code_ref, out_ref):
    rows = mesh_ref.shape[1] // 128

    def row_of(r, c):
        return mesh_ref[c : c + 1, r * 128 : (r + 1) * 128]

    def block(g, carry):
        start = pl.multiple_of(g * 8, 8)
        total = lookup(code_ref, start, 0, rows, row_of)
        out_ref[0, pl.ds(start, 8), :] = total[0]
        out_ref[1, pl.ds(start, 8), :] = total[1]
        return carry

    lax.fori_loop(0, code_ref.shape[1] // 8, block, 0)


def lookup(code_ref, start, first, count, row_of):
    total = [None, None]
    for k in range(2):
        code = code_ref[k, pl.ds(start, 8), :]
        high, low = (code >> 8) - first, (code >> 1) & 127
        value = [jnp.zeros((8, 128), F32), jnp.zeros((8, 128), F32)]
        for r in range(count):
            here = high == r
            for c in range(2):
                value[c] = jnp.where(here, lane_pick(row_of(r, c), low), value[c])
        along = (code & 1) == 1
        for c in range(2):
            signed = jnp.where(along, value[c], -value[c])
            total[c] = signed if k == 0 else total[c] + signed
    return total


def current_kernel(own_ref, remote_ref, code_ref, basis_ref, current_ref, coeff_ref, *, first):
    peers = remote_ref.shape[0]
    tiles = code_ref.shape[1]
    rank = basis_ref.shape[0] // tiles

    def row_of(r, c):
        return remote_ref[r, c : c + 1, :]

    def block(g, carry):
        start = pl.multiple_of(g * 8, 8)
        total = lookup(code_ref, start, first, peers, row_of)
        for c in range(2):
            current_ref[c, pl.ds(start, 8), :] = total[c] + own_ref[c, pl.ds(start, 8), :]
        return carry

    lax.fori_loop(0, tiles // 8, block, 0)
    inputs = jnp.concatenate([current_ref[0], current_ref[1]], axis=0)
    inputs = inputs.T.astype(BF16)
    lane_tile = lax.broadcasted_iota(jnp.int32, (rank, 2 * tiles), 1) % tiles
    chosen = jnp.zeros((rank, 2 * tiles), F32)
    for g in range(tiles // 8):
        full = jnp.dot(
            basis_ref[g * 8 * rank : (g + 1) * 8 * rank, :], inputs, preferred_element_type=F32
        )
        for i in range(8):
            chosen = jnp.where(
                lane_tile == g * 8 + i, full[i * rank : (i + 1) * rank], chosen
            )
    coeff_ref[...] = chosen.astype(BF16)


def near_kernel(source_ref, current_ref, blocks_ref, out_ref, inputs_ref, total_ref):
    step = pl.program_id(0)
    steps = pl.num_programs(0)
    tile_step, count, width, _ = blocks_ref.shape
    tiles = tile_step * steps
    lane_tile = lax.broadcasted_iota(jnp.int32, (width, 128), 1) % 64

    @pl.when(step == 0)
    def _():
        rows = jnp.concatenate([current_ref[0], current_ref[1]], axis=0)
        columns = rows.T.astype(BF16)
        row_index = lax.broadcasted_iota(jnp.int32, (128, 128), 0)
        for k in range(count):
            picks = jnp.where(row_index == source_ref[k : k + 1, :], 1.0, 0.0).astype(BF16)
            inputs_ref[k * width : (k + 1) * width, :] = jnp.dot(
                columns, picks, preferred_element_type=F32
            ).astype(BF16)
        total_ref[...] = jnp.zeros_like(total_ref)

    total = total_ref[...]
    for t in range(tile_step):
        block = jnp.concatenate([blocks_ref[t, k] for k in range(count)], axis=1)
        full = jnp.dot(block, inputs_ref[...], preferred_element_type=F32)
        total = jnp.where(lane_tile == step * tile_step + t, full, total)
    total_ref[...] = total

    @pl.when(step == steps - 1)
    def _():
        rows = total_ref[...].T
        out_ref[0] = rows[:64]
        out_ref[1] = rows[64:]


def split(value):
    top = value.astype(BF16)
    return top, (value - top.astype(F32)).astype(BF16)


def place(high, low, values, rows):
    sub_high = lax.broadcasted_iota(jnp.int32, (rows, 128), 0)
    sub_low = lax.broadcasted_iota(jnp.int32, (128, 128), 0)
    left, right = [], []
    for i in range(high.shape[0]):
        here = jnp.broadcast_to(high[i : i + 1], (rows, 128)) == sub_high
        parts = []
        for value in values:
            spread = jnp.where(here, jnp.broadcast_to(value[i : i + 1], (rows, 128)), 0.0)
            parts.extend(split(spread))
        left.append(jnp.concatenate(parts, axis=0))
        there = jnp.broadcast_to(low[i : i + 1], (128, 128)) == sub_low
        right.append(jnp.where(there, 1.0, 0.0).astype(BF16))
    return jnp.concatenate(left, axis=1), jnp.concatenate(right, axis=1)


def scatter(code_ref, voltage_ref, total_ref, first, rows):
    total_ref[...] = jnp.zeros_like(total_ref)

    def block(g, carry):
        start = pl.multiple_of(g * 8, 8)
        for k in range(2):
            code = code_ref[k, pl.ds(start, 8), :]
            along = (code & 1) == 1
            values = []
            for c in range(2):
                voltage = voltage_ref[c, pl.ds(start, 8), :]
                values.append(jnp.where(along, voltage, -voltage))
            left, right = place((code >> 8) - first, (code >> 1) & 127, values, rows)
            total_ref[...] += dot_nt(left, right)
        return carry

    lax.fori_loop(0, code_ref.shape[1] // 8, block, 0)
    return [
        total_ref[2 * c * rows : (2 * c + 1) * rows, :]
        + total_ref[(2 * c + 1) * rows : (2 * c + 2) * rows, :]
        for c in range(2)
    ]


def voltage_kernel(*refs, first):
    coeff_refs = refs[:-12]
    (
        target_ref, coupling_ref, basis_ref, near_ref, current_ref, resistance_ref,
        code_ref, voltage_ref, slot_ref, picked_ref, mixed_ref, total_ref,
    ) = refs[-12:]
    peers = len(coeff_refs)
    rank, lanes = coeff_refs[0].shape
    far_count, _, _, tiles = coupling_ref.shape
    spans = target_ref.shape[0] // far_count
    stride = peers // far_count
    row_index = lax.broadcasted_iota(jnp.int32, (lanes, lanes), 0)
    for k in range(far_count):
        piece = None
        for i in range(spans):
            row = k * spans + i
            picks = jnp.where(row_index == target_ref[row : row + 1, :], 1.0, 0.0).astype(BF16)
            term = jnp.dot(
                coeff_refs[(k * stride + i) % peers][...], picks, preferred_element_type=F32
            )
            piece = term if piece is None else piece + term
        picked_ref[0, k] = piece[:, :tiles]
        picked_ref[1, k] = piece[:, tiles:]

    def mix(g, carry):
        total = [[None, None] for _ in range(4)]
        for k in range(far_count):
            picked = [picked_ref[c, k] for c in range(2)]
            for i in range(4):
                block = coupling_ref[k, g * 4 + i].astype(F32)
                for c in range(2):
                    product = block * picked[c]
                    part = product[0:8]
                    for q in range(8, rank, 8):
                        part = part + product[q : q + 8]
                    total[i][c] = part if k == 0 else total[i][c] + part
        for i in range(4):
            for c in range(2):
                row = jnp.sum(total[i][c], axis=0, keepdims=True)
                mixed_ref[pl.ds(g * 4 + i, 1), c * tiles : (c + 1) * tiles] = row
        return carry

    lax.fori_loop(0, rank // 4, mix, 0)
    mixed = mixed_ref[...].T.astype(BF16)
    wide = 8 * rank
    spread = jnp.where(
        lax.broadcasted_iota(jnp.int32, (rank, wide), 0)
        == lax.broadcasted_iota(jnp.int32, (rank, wide), 1) % rank,
        1.0,
        0.0,
    ).astype(BF16)
    repeated = jnp.dot(mixed, spread, preferred_element_type=F32)
    own_block = (
        lax.broadcasted_iota(jnp.int32, (16, wide), 0) % 8
        == lax.broadcasted_iota(jnp.int32, (16, wide), 1) // rank
    )
    for g in range(tiles // 8):
        rows8 = slice(g * 8, g * 8 + 8)
        both = jnp.concatenate(
            [repeated[rows8], repeated[tiles + g * 8 : tiles + g * 8 + 8]], axis=0
        )
        both = jnp.where(own_block, both, 0.0).astype(BF16)
        far = jnp.dot(
            both, basis_ref[g * wide : (g + 1) * wide, :], preferred_element_type=F32
        )
        resistance = resistance_ref[rows8, :]
        voltage_ref[0, rows8, :] = resistance * current_ref[0, rows8, :] - (
            near_ref[1, rows8, :] + far[8:16]
        )
        voltage_ref[1, rows8, :] = resistance * current_ref[1, rows8, :] + (
            near_ref[0, rows8, :] + far[0:8]
        )
    sums = scatter(code_ref, voltage_ref, total_ref, first, slot_ref.shape[0])
    for c in range(2):
        slot_ref[:, c, :] = sums[c]


def own_sum_kernel(code_ref, voltage_ref, own_ref, total_ref):
    sums = scatter(code_ref, voltage_ref, total_ref, 0, own_ref.shape[1])
    for c in range(2):
        own_ref[c] = sums[c]


def finish_kernel(own_ref, arrived_ref, asked_ref, port_ref, remote_ref, impedance_ref, out_ref):
    rows = own_ref.shape[1]
    ports = impedance_ref.shape[1]
    peers = asked_ref.shape[0]
    asked = asked_ref[...]
    total = None
    for start in range(0, peers, 8):
        part = asked[start : start + 8]
        values = [arrived_ref[start : start + 8, c, :] for c in range(2)]
        left, right = place(part >> 7, part & 127, values, rows)
        term = dot_nt(left, right)
        total = term if total is None else total + term
    port_current = jnp.sum(remote_ref[:, 2, :], axis=0, keepdims=True)
    real = port_current[:, :ports]
    imag = port_current[:, ports:]
    both = jnp.concatenate([real, imag, jnp.zeros((6, ports), F32)], axis=0)
    by_real = dot_nt(both, impedance_ref[0], lax.Precision.HIGHEST)
    by_imag = dot_nt(both, impedance_ref[1], lax.Precision.HIGHEST)
    pad = jnp.zeros((1, 128 - ports), F32)
    terms = [
        jnp.concatenate([by_real[0:1] - by_imag[1:2], pad], axis=1),
        jnp.concatenate([by_real[1:2] + by_imag[0:1], pad], axis=1),
    ]
    port = port_ref[...]
    port = jnp.where(lax.broadcasted_iota(jnp.int32, port.shape, 1) < ports, port, -1)
    left, right = place(port >> 7, port & 127, terms, rows)
    total = total + dot_nt(left, right)
    for c in range(2):
        summed = own_ref[c] + (
            total[2 * c * rows : (2 * c + 1) * rows] + total[(2 * c + 1) * rows : (2 * c + 2) * rows]
        )
        for r in range(rows):
            out_ref[c : c + 1, r * 128 : (r + 1) * 128] = summed[r : r + 1]


def per_device(
    mesh_current,
    branch_entry,
    branch_sign,
    need_slots,
    resistance,
    near_blocks,
    near_source,
    basis_in,
    coupling,
    basis_out,
    admissible,
    port_mesh,
    port_coupling,
):
    peers = lax.axis_size("clus")
    device = lax.axis_index("clus")
    mesh_dev = mesh_current.shape[1]
    tiles, near_count, width, _ = near_blocks.shape
    rank = basis_in.shape[1]
    far_count = admissible.shape[1]
    own_rows = mesh_dev // 128
    vmem = pl.BlockSpec(memory_space=pltpu.VMEM)
    shape = jax.ShapeDtypeStruct

    port_here = port_mesh - device * mesh_dev
    owned = (port_here >= 0) & (port_here < mesh_dev)
    port_here = jnp.where(owned, port_here, -1)
    port_pair = jnp.concatenate([port_here, port_here]).reshape(1, 128)
    code = (branch_entry * 2 + branch_sign).reshape(2, tiles, width)
    coupling_lanes = jnp.transpose(coupling, (1, 2, 3, 0))
    basis_in_rows = basis_in.reshape(tiles * rank, width)
    basis_out_rows = basis_out.reshape(tiles * rank, width)
    half = jnp.arange(2 * tiles, dtype=jnp.int32) // tiles
    sources = jnp.transpose(near_source)
    sources = jnp.concatenate([sources, sources], axis=1) + half[None] * tiles
    band = peers * tiles // far_count
    spans = band // tiles + 1
    bases = device * tiles + jnp.arange(far_count, dtype=jnp.int32) * band
    shifted = (jnp.transpose(admissible) - bases[:, None]) % (peers * tiles)
    shifted = jnp.concatenate([shifted, shifted], axis=1)[:, None, :]
    shifted = shifted - jnp.arange(spans, dtype=jnp.int32)[None, :, None] * tiles
    inside = (shifted >= 0) & (shifted < tiles)
    targets = jnp.where(inside, shifted + half * tiles, -1).reshape(far_count * spans, 2 * tiles)

    asked = lax.all_to_all(need_slots, "clus", 0, 0, tiled=True)
    served = pl.pallas_call(
        serve_kernel,
        out_shape=shape((peers, 4, 128), F32),
        in_specs=[vmem] * 3,
        out_specs=vmem,
        compiler_params=params(),
        name="serve",
    )(mesh_current, asked, port_pair)
    remote = lax.all_to_all(served, "clus", 0, 0, tiled=True)
    own_part = pl.pallas_call(
        own_lookup_kernel,
        out_shape=shape((2, tiles, width), F32),
        in_specs=[vmem] * 2,
        out_specs=vmem,
        compiler_params=params(),
        cost_estimate=small_cost(),
        name="own_lookup",
    )(mesh_current, code)
    current, coeff = pl.pallas_call(
        functools.partial(current_kernel, first=own_rows),
        out_shape=(shape((2, tiles, width), F32), shape((rank, 2 * tiles), BF16)),
        in_specs=[vmem] * 4,
        out_specs=(vmem,) * 2,
        compiler_params=params(),
        name="currents",
    )(own_part, remote, code, basis_in_rows)
    shifts = [coeff]
    for j in range(1, peers):
        pairs = [((i + j) % peers, i) for i in range(peers)]
        shifts.append(lax.ppermute(coeff, "clus", pairs))
    step = 8
    near = pl.pallas_call(
        near_kernel,
        out_shape=shape((2, tiles, width), F32),
        grid=(tiles // step,),
        in_specs=[
            pl.BlockSpec((near_count, 2 * tiles), lambda i: (0, 0)),
            pl.BlockSpec((2, tiles, width), lambda i: (0, 0, 0)),
            pl.BlockSpec((step, near_count, width, width), lambda i: (i, 0, 0, 0)),
        ],
        out_specs=pl.BlockSpec((2, tiles, width), lambda i: (0, 0, 0)),
        scratch_shapes=[
            pltpu.VMEM((near_count * width, 2 * tiles), BF16),
            pltpu.VMEM((width, 2 * tiles), F32),
        ],
        compiler_params=params(),
        cost_estimate=pl.CostEstimate(
            flops=256 * near_blocks.size, bytes_accessed=2 * near_blocks.size, transcendentals=0
        ),
        name="near_field",
    )(sources, current, near_blocks)
    voltage, slots = pl.pallas_call(
        functools.partial(voltage_kernel, first=own_rows),
        out_shape=(shape((2, tiles, width), F32), shape((peers, 2, 128), F32)),
        in_specs=[vmem] * (peers + 7),
        out_specs=(vmem,) * 2,
        scratch_shapes=[
            pltpu.VMEM((2, far_count, rank, tiles), F32),
            pltpu.VMEM((rank, 2 * tiles), F32),
            pltpu.VMEM((4 * peers, 128), F32),
        ],
        compiler_params=params(),
        name="voltages",
    )(
        *shifts,
        targets,
        coupling_lanes,
        basis_out_rows,
        near,
        current,
        resistance.reshape(tiles, width),
        code,
    )
    arrived = lax.all_to_all(slots, "clus", 0, 0, tiled=True)
    own = pl.pallas_call(
        own_sum_kernel,
        out_shape=shape((2, own_rows, 128), F32),
        in_specs=[vmem] * 2,
        out_specs=vmem,
        scratch_shapes=[pltpu.VMEM((4 * own_rows, 128), F32)],
        compiler_params=params(),
        cost_estimate=small_cost(),
        name="own_sums",
    )(code, voltage)
    return pl.pallas_call(
        finish_kernel,
        out_shape=shape((2, mesh_dev), F32),
        in_specs=[vmem] * 6,
        out_specs=vmem,
        compiler_params=params(),
        name="finish",
    )(own, arrived, asked, port_pair, remote, port_coupling)


def solution(mesh):
    in_specs = (
        P(None, ("groups", "clus")),
        P(None, ("groups", "clus")),
        P(None, ("groups", "clus")),
        P(("groups", "clus"), None),
        P(("groups", "clus")),
        P(("groups", "clus"), None, None, None),
        P(("groups", "clus"), None),
        P(("groups", "clus"), None, None),
        P(("groups", "clus"), None, None, None),
        P(("groups", "clus"), None, None),
        P(("groups", "clus"), None),
        P("groups"),
        P(),
    )
    out_specs = P(None, ("groups", "clus"))
    return jax.shard_map(
        per_device, mesh=mesh, in_specs=in_specs, out_specs=out_specs, check_vma=False
    )
```

```python
import functools

import jax
import jax.numpy as jnp
from jax import lax
from jax.experimental import pallas as pl
from jax.experimental.pallas import tpu as pltpu
from jax.sharding import PartitionSpec as P

F32 = jnp.float32
BF16 = jnp.bfloat16
SPREAD = ("groups", "chips", "core")
VMEM_LIMIT = 28 * 1024 * 1024
NT = (((1,), (1,)), ((), ()))


def params():
    return pltpu.CompilerParams(vmem_limit_bytes=VMEM_LIMIT)


def small_cost():
    return pl.CostEstimate(flops=10**9, bytes_accessed=8 * 10**6, transcendentals=0)


def lane_pick(row, lanes):
    spread = jnp.broadcast_to(row, lanes.shape)
    return jnp.take_along_axis(spread, lanes, axis=1, mode="promise_in_bounds")


def dot_nt(left, right, precision=None):
    return lax.dot_general(
        left, right, NT, preferred_element_type=F32, precision=precision
    )


def pack_kernel(core_ref, mesh_ref, need_ref, port_ref, out_ref):
    rows = mesh_ref.shape[1] // 128
    chips = out_ref.shape[0]
    port = jnp.broadcast_to(port_ref[...], (8, 128))
    port_high, port_low = port >> 7, port & 127
    port_value = jnp.zeros((8, 128), F32)
    lane = lax.broadcasted_iota(jnp.int32, (8, 128), 1)
    for r in range(rows):
        real_row = mesh_ref[0:1, r * 128 : (r + 1) * 128]
        imag_row = mesh_ref[1:2, r * 128 : (r + 1) * 128]
        both = jnp.where(
            lane < 64, lane_pick(real_row, port_low), lane_pick(imag_row, port_low)
        )
        port_value = jnp.where(port_high == r, both, port_value)
        for chip in range(chips):
            out_ref[chip, r : r + 1, :] = real_row
            out_ref[chip, rows + r : rows + r + 1, :] = imag_row
    need = [need_ref[pl.ds(c, chips, 2), :].astype(F32) for c in range(2)]
    first = core_ref[0] == 0
    out_ref[:, 2 * rows, :] = jnp.where(first, need[0], need[1])
    out_ref[:, 2 * rows + 1, :] = jnp.where(first, need[1], need[0])
    out_ref[:, 2 * rows + 2, :] = jnp.broadcast_to(port_value[0:1], (chips, 128))
    for r in range(2 * rows + 3, out_ref.shape[1]):
        out_ref[:, r, :] = jnp.zeros((chips, 128), F32)


def own_lookup_kernel(mesh_ref, code_ref, out_ref):
    rows = mesh_ref.shape[1] // 128

    def row_of(r, c):
        return mesh_ref[c : c + 1, r * 128 : (r + 1) * 128]

    def block(g, carry):
        start = pl.multiple_of(g * 8, 8)
        total = lookup(code_ref, start, 0, rows, row_of)
        out_ref[0, pl.ds(start, 8), :] = total[0]
        out_ref[1, pl.ds(start, 8), :] = total[1]
        return carry

    lax.fori_loop(0, code_ref.shape[1] // 8, block, 0)


def lookup(code_ref, start, first, count, row_of):
    total = [None, None]
    for k in range(2):
        code = code_ref[k, pl.ds(start, 8), :]
        high, low = (code >> 8) - first, (code >> 1) & 127
        value = [jnp.zeros((8, 128), F32), jnp.zeros((8, 128), F32)]
        for r in range(count):
            here = high == r
            for c in range(2):
                value[c] = jnp.where(here, lane_pick(row_of(r, c), low), value[c])
        along = (code & 1) == 1
        for c in range(2):
            signed = jnp.where(along, value[c], -value[c])
            total[c] = signed if k == 0 else total[c] + signed
    return total


def current_kernel(
    core_ref, own_ref, same_ref, other_ref, need_ref, code_ref, basis_ref, current_ref, coeff_ref,
    table_ref, *, first,
):
    chips = same_ref.shape[0]
    peers = 2 * chips
    tiles = code_ref.shape[1]
    rank = basis_ref.shape[0] // tiles
    first_core = core_ref[0] == 0
    need = [jnp.maximum(need_ref[pl.ds(c, chips, 2), :], 0) for c in range(2)]
    need = [jnp.where(first_core, need[0], need[1]), jnp.where(first_core, need[1], need[0])]
    found = []
    for wanted, pack_ref in zip(need, (same_ref, other_ref)):
        high, low = wanted >> 7, wanted & 127
        value = [jnp.zeros((chips, 128), F32), jnp.zeros((chips, 128), F32)]
        for r in range(first):
            here = high == r
            for c in range(2):
                row = pack_ref[:, c * first + r, :]
                picked = jnp.take_along_axis(row, low, axis=1, mode="promise_in_bounds")
                value[c] = jnp.where(here, picked, value[c])
        found.append(value)
    for c in range(2):
        same, other = found[0][c], found[1][c]
        table_ref[c, pl.ds(0, chips, 2), :] = jnp.where(first_core, same, other)
        table_ref[c, pl.ds(1, chips, 2), :] = jnp.where(first_core, other, same)

    def row_of(r, c):
        return table_ref[c, r : r + 1, :]

    def block(g, carry):
        start = pl.multiple_of(g * 8, 8)
        total = lookup(code_ref, start, first, peers, row_of)
        for c in range(2):
            current_ref[c, pl.ds(start, 8), :] = total[c] + own_ref[c, pl.ds(start, 8), :]
        return carry

    lax.fori_loop(0, tiles // 8, block, 0)
    inputs = jnp.concatenate([current_ref[0], current_ref[1]], axis=0)
    inputs = inputs.T.astype(BF16)
    lane_tile = lax.broadcasted_iota(jnp.int32, (rank, 2 * tiles), 1) % tiles
    full = jnp.dot(basis_ref[...], inputs, preferred_element_type=F32)
    chosen = jnp.zeros((rank, 2 * tiles), F32)
    for t in range(tiles):
        chosen = jnp.where(lane_tile == t, full[t * rank : (t + 1) * rank], chosen)
    coeff = chosen.astype(BF16)
    for p in range(peers):
        coeff_ref[p] = coeff


def near_kernel(source_ref, current_ref, blocks_ref, out_ref, inputs_ref):
    tiles, count, width, _ = blocks_ref.shape
    lane_tile = lax.broadcasted_iota(jnp.int32, (width, 128), 1) % tiles
    rows = jnp.concatenate([current_ref[0], current_ref[1]], axis=0)
    columns = rows.T.astype(BF16)
    row_index = lax.broadcasted_iota(jnp.int32, (128, 128), 0)
    for k in range(count):
        picks = jnp.where(row_index == source_ref[k : k + 1, :], 1.0, 0.0).astype(BF16)
        inputs_ref[k * width : (k + 1) * width, :] = jnp.dot(
            columns, picks, preferred_element_type=F32
        ).astype(BF16)
    inputs = inputs_ref[...]
    total = jnp.zeros((width, 128), F32)
    for g in range(tiles // 8):
        block = jnp.concatenate(
            [
                blocks_ref[g * 8 : g * 8 + 8, k].reshape(8 * width, width)
                for k in range(count)
            ],
            axis=1,
        )
        full = jnp.dot(block, inputs, preferred_element_type=F32)
        for i in range(8):
            total = jnp.where(
                lane_tile == g * 8 + i, full[i * width : (i + 1) * width], total
            )
    rows = total.T
    out_ref[0] = rows[:tiles]
    out_ref[1] = rows[tiles:]


def split(value):
    top = value.astype(BF16)
    return top, (value - top.astype(F32)).astype(BF16)


def place(high, low, values, rows):
    sub_high = lax.broadcasted_iota(jnp.int32, (rows, 128), 0)
    sub_low = lax.broadcasted_iota(jnp.int32, (128, 128), 0)
    left, right = [], []
    for i in range(high.shape[0]):
        here = jnp.broadcast_to(high[i : i + 1], (rows, 128)) == sub_high
        parts = []
        for value in values:
            spread = jnp.where(here, jnp.broadcast_to(value[i : i + 1], (rows, 128)), 0.0)
            parts.extend(split(spread))
        left.append(jnp.concatenate(parts, axis=0))
        there = jnp.broadcast_to(low[i : i + 1], (128, 128)) == sub_low
        right.append(jnp.where(there, 1.0, 0.0).astype(BF16))
    return jnp.concatenate(left, axis=1), jnp.concatenate(right, axis=1)


def scatter(code_ref, voltage_ref, total_ref, first, rows):
    total_ref[...] = jnp.zeros_like(total_ref)

    def block(g, carry):
        start = pl.multiple_of(g * 8, 8)
        for k in range(2):
            code = code_ref[k, pl.ds(start, 8), :]
            along = (code & 1) == 1
            values = []
            for c in range(2):
                voltage = voltage_ref[c, pl.ds(start, 8), :]
                values.append(jnp.where(along, voltage, -voltage))
            left, right = place((code >> 8) - first, (code >> 1) & 127, values, rows)
            total_ref[...] += dot_nt(left, right)
        return carry

    lax.fori_loop(0, code_ref.shape[1] // 8, block, 0)
    return [
        total_ref[2 * c * rows : (2 * c + 1) * rows, :]
        + total_ref[(2 * c + 1) * rows : (2 * c + 2) * rows, :]
        for c in range(2)
    ]


def voltage_kernel(*refs, first):
    (
        place_ref, coeff_ref, target_ref, coupling_ref, basis_ref, near_ref, current_ref, resistance_ref,
        code_ref, voltage_ref, slot_ref, picked_ref, mixed_ref, total_ref,
    ) = refs
    peers, rank, lanes = coeff_ref.shape
    device = place_ref[0]
    far_count, _, _, tiles = coupling_ref.shape
    spans = target_ref.shape[0] // far_count
    stride = peers // far_count
    row_index = lax.broadcasted_iota(jnp.int32, (lanes, lanes), 0)
    for k in range(far_count):
        piece = None
        for i in range(spans):
            row = k * spans + i
            picks = jnp.where(row_index == target_ref[row : row + 1, :], 1.0, 0.0).astype(BF16)
            term = jnp.dot(
                coeff_ref[(device + k * stride + i) % peers], picks, preferred_element_type=F32
            )
            piece = term if piece is None else piece + term
        picked_ref[0, k] = piece[:, :tiles]
        picked_ref[1, k] = piece[:, tiles:]

    def mix(g, carry):
        total = [[None, None] for _ in range(4)]
        for k in range(far_count):
            picked = [picked_ref[c, k] for c in range(2)]
            for i in range(4):
                block = coupling_ref[k, g * 4 + i].astype(F32)
                for c in range(2):
                    product = block * picked[c]
                    part = product[0:8]
                    for q in range(8, rank, 8):
                        part = part + product[q : q + 8]
                    total[i][c] = part if k == 0 else total[i][c] + part
        for i in range(4):
            for c in range(2):
                row = jnp.sum(total[i][c], axis=0, keepdims=True)
                mixed_ref[pl.ds(g * 4 + i, 1), c * tiles : (c + 1) * tiles] = row
        return carry

    lax.fori_loop(0, rank // 4, mix, 0)
    mixed = mixed_ref[...].T.astype(BF16)
    wide = 8 * rank
    spread = jnp.where(
        lax.broadcasted_iota(jnp.int32, (rank, wide), 0)
        == lax.broadcasted_iota(jnp.int32, (rank, wide), 1) % rank,
        1.0,
        0.0,
    ).astype(BF16)
    repeated = jnp.dot(mixed, spread, preferred_element_type=F32)
    own_block = (
        lax.broadcasted_iota(jnp.int32, (16, wide), 0) % 8
        == lax.broadcasted_iota(jnp.int32, (16, wide), 1) // rank
    )
    for g in range(tiles // 8):
        rows8 = slice(g * 8, g * 8 + 8)
        both = jnp.concatenate(
            [repeated[rows8], repeated[tiles + g * 8 : tiles + g * 8 + 8]], axis=0
        )
        both = jnp.where(own_block, both, 0.0).astype(BF16)
        far = jnp.dot(
            both, basis_ref[g * wide : (g + 1) * wide, :], preferred_element_type=F32
        )
        resistance = resistance_ref[rows8, :]
        voltage_ref[0, rows8, :] = resistance * current_ref[0, rows8, :] - (
            near_ref[1, rows8, :] + far[8:16]
        )
        voltage_ref[1, rows8, :] = resistance * current_ref[1, rows8, :] + (
            near_ref[0, rows8, :] + far[0:8]
        )
    sums = scatter(code_ref, voltage_ref, total_ref, first, slot_ref.shape[0])
    for c in range(2):
        slot_ref[:, c, :] = sums[c]


def own_sum_kernel(code_ref, voltage_ref, own_ref, total_ref):
    sums = scatter(code_ref, voltage_ref, total_ref, 0, own_ref.shape[1])
    for c in range(2):
        own_ref[c] = sums[c]


def finish_kernel(
    core_ref, own_ref, arrived_ref, same_ref, other_ref, port_ref, impedance_ref, out_ref
):
    rows = own_ref.shape[1]
    ports = impedance_ref.shape[1]
    chips = same_ref.shape[0]
    same = same_ref[:, 2 * rows, :].astype(jnp.int32)
    other = other_ref[:, 2 * rows + 1, :].astype(jnp.int32)
    first_core = core_ref[0] == 0
    total = None
    for core in range(2):
        asked = jnp.where(first_core, same, other) if core == 0 else jnp.where(first_core, other, same)
        values = [arrived_ref[:, core, c, :] for c in range(2)]
        left, right = place(asked >> 7, asked & 127, values, rows)
        term = dot_nt(left, right)
        total = term if total is None else total + term
    port_current = jnp.sum(
        same_ref[:, 2 * rows + 2, :] + other_ref[:, 2 * rows + 2, :], axis=0, keepdims=True
    )
    real = port_current[:, :ports]
    imag = port_current[:, ports:]
    both = jnp.concatenate([real, imag, jnp.zeros((6, ports), F32)], axis=0)
    by_real = dot_nt(both, impedance_ref[0], lax.Precision.HIGHEST)
    by_imag = dot_nt(both, impedance_ref[1], lax.Precision.HIGHEST)
    pad = jnp.zeros((1, 128 - ports), F32)
    terms = [
        jnp.concatenate([by_real[0:1] - by_imag[1:2], pad], axis=1),
        jnp.concatenate([by_real[1:2] + by_imag[0:1], pad], axis=1),
    ]
    port = port_ref[...]
    port = jnp.where(lax.broadcasted_iota(jnp.int32, port.shape, 1) < ports, port, -1)
    left, right = place(port >> 7, port & 127, terms, rows)
    total = total + dot_nt(left, right)
    for c in range(2):
        summed = own_ref[c] + (
            total[2 * c * rows : (2 * c + 1) * rows] + total[(2 * c + 1) * rows : (2 * c + 2) * rows]
        )
        for r in range(rows):
            out_ref[c : c + 1, r * 128 : (r + 1) * 128] = summed[r : r + 1]


def per_device(
    mesh_current,
    branch_entry,
    branch_sign,
    need_slots,
    resistance,
    near_blocks,
    near_source,
    basis_in,
    coupling,
    basis_out,
    admissible,
    port_mesh,
    port_coupling,
):
    chips = lax.axis_size("chips")
    peers = 2 * chips
    core = lax.axis_index("core")
    device = 2 * lax.axis_index("chips") + core
    mesh_dev = mesh_current.shape[1]
    tiles, near_count, width, _ = near_blocks.shape
    rank = basis_in.shape[1]
    far_count = admissible.shape[1]
    own_rows = mesh_dev // 128
    vmem = pl.BlockSpec(memory_space=pltpu.VMEM)
    smem = pl.BlockSpec(memory_space=pltpu.SMEM)
    shape = jax.ShapeDtypeStruct

    port_here = port_mesh - device * mesh_dev
    owned = (port_here >= 0) & (port_here < mesh_dev)
    port_here = jnp.where(owned, port_here, -1)
    port_pair = jnp.concatenate([port_here, port_here]).reshape(1, 128)
    code = (branch_entry * 2 + branch_sign).reshape(2, tiles, width)
    coupling_lanes = jnp.transpose(coupling, (1, 2, 3, 0))
    basis_in_rows = basis_in.reshape(tiles * rank, width)
    basis_out_rows = basis_out.reshape(tiles * rank, width)
    half = jnp.arange(2 * tiles, dtype=jnp.int32) // tiles
    sources = jnp.transpose(near_source)
    sources = jnp.concatenate([sources, sources], axis=1) + half[None] * tiles
    band = peers * tiles // far_count
    spans = band // tiles + 1
    bases = device * tiles + jnp.arange(far_count, dtype=jnp.int32) * band
    shifted = (jnp.transpose(admissible) - bases[:, None]) % (peers * tiles)
    shifted = jnp.concatenate([shifted, shifted], axis=1)[:, None, :]
    shifted = shifted - jnp.arange(spans, dtype=jnp.int32)[None, :, None] * tiles
    inside = (shifted >= 0) & (shifted < tiles)
    targets = jnp.where(inside, shifted + half * tiles, -1).reshape(far_count * spans, 2 * tiles)

    core_word = core.reshape(1)
    device_word = device.reshape(1)
    pack_rows = (2 * own_rows + 3 + 7) // 8 * 8
    pack = pl.pallas_call(
        pack_kernel,
        out_shape=shape((chips, pack_rows, 128), F32),
        in_specs=[smem] + [vmem] * 3,
        out_specs=vmem,
        compiler_params=params(),
        name="pack",
    )(core_word, mesh_current, need_slots, port_pair)
    same = lax.all_to_all(pack, "chips", 0, 0, tiled=True)
    other = lax.ppermute(same, "core", [(0, 1), (1, 0)])
    own_part = pl.pallas_call(
        own_lookup_kernel,
        out_shape=shape((2, tiles, width), F32),
        in_specs=[vmem] * 2,
        out_specs=vmem,
        compiler_params=params(),
        cost_estimate=small_cost(),
        name="own_lookup",
    )(mesh_current, code)
    current, coeff = pl.pallas_call(
        functools.partial(current_kernel, first=own_rows),
        out_shape=(shape((2, tiles, width), F32), shape((peers, rank, 2 * tiles), BF16)),
        in_specs=[smem] + [vmem] * 6,
        out_specs=(vmem,) * 2,
        scratch_shapes=[pltpu.VMEM((2, peers, 128), F32)],
        compiler_params=params(),
        name="currents",
    )(core_word, own_part, same, other, need_slots, code, basis_in_rows)
    all_coeff = lax.all_to_all(coeff, ("chips", "core"), 0, 0, tiled=True)
    near = pl.pallas_call(
        near_kernel,
        out_shape=shape((2, tiles, width), F32),
        in_specs=[vmem] * 3,
        out_specs=vmem,
        scratch_shapes=[pltpu.VMEM((near_count * width, 2 * tiles), BF16)],
        compiler_params=params(),
        cost_estimate=pl.CostEstimate(
            flops=256 * near_blocks.size, bytes_accessed=2 * near_blocks.size, transcendentals=0
        ),
        name="near_field",
    )(sources, current, near_blocks)
    voltage, slots = pl.pallas_call(
        functools.partial(voltage_kernel, first=own_rows),
        out_shape=(shape((2, tiles, width), F32), shape((peers, 2, 128), F32)),
        in_specs=[smem] + [vmem] * 8,
        out_specs=(vmem,) * 2,
        scratch_shapes=[
            pltpu.VMEM((2, far_count, rank, tiles), F32),
            pltpu.VMEM((rank, 2 * tiles), F32),
            pltpu.VMEM((4 * peers, 128), F32),
        ],
        compiler_params=params(),
        name="voltages",
    )(
        device_word,
        all_coeff,
        targets,
        coupling_lanes,
        basis_out_rows,
        near,
        current,
        resistance.reshape(tiles, width),
        code,
    )
    arrived = lax.all_to_all(slots, ("chips", "core"), 0, 0, tiled=True)
    own = pl.pallas_call(
        own_sum_kernel,
        out_shape=shape((2, own_rows, 128), F32),
        in_specs=[vmem] * 2,
        out_specs=vmem,
        scratch_shapes=[pltpu.VMEM((4 * own_rows, 128), F32)],
        compiler_params=params(),
        cost_estimate=small_cost(),
        name="own_sums",
    )(code, voltage)
    return pl.pallas_call(
        finish_kernel,
        out_shape=shape((2, mesh_dev), F32),
        in_specs=[smem] + [vmem] * 6,
        out_specs=vmem,
        compiler_params=params(),
        name="finish",
    )(
        core_word,
        own,
        arrived.reshape(chips, 2, 2, 128),
        same,
        other,
        port_pair,
        port_coupling,
    )


def solution(mesh):
    groups, peers = mesh.devices.shape
    split_mesh = jax.sharding.Mesh(
        mesh.devices.reshape(groups, peers // 2, 2), ("groups", "chips", "core")
    )
    in_specs = (
        P(None, SPREAD),
        P(None, SPREAD),
        P(None, SPREAD),
        P(SPREAD, None),
        P(SPREAD),
        P(SPREAD, None, None, None),
        P(SPREAD, None),
        P(SPREAD, None, None),
        P(SPREAD, None, None, None),
        P(SPREAD, None, None),
        P(SPREAD, None),
        P("groups"),
        P(),
    )
    out_specs = P(None, SPREAD)
    return jax.shard_map(
        per_device, mesh=split_mesh, in_specs=in_specs, out_specs=out_specs, check_vma=False
    )
```

```python
import functools

import jax
import jax.numpy as jnp
from jax import lax
from jax.experimental import pallas as pl
from jax.experimental.pallas import tpu as pltpu
from jax.sharding import PartitionSpec as P

F32 = jnp.float32
BF16 = jnp.bfloat16
SPREAD = ("groups", "chips", "core")
VMEM_LIMIT = 24 * 1024 * 1024
NT = (((1,), (1,)), ((), ()))


def params():
    return pltpu.CompilerParams(vmem_limit_bytes=VMEM_LIMIT)


def small_cost():
    return pl.CostEstimate(flops=10**9, bytes_accessed=8 * 10**6, transcendentals=0)


def lane_pick(row, lanes):
    spread = jnp.broadcast_to(row, lanes.shape)
    return jnp.take_along_axis(spread, lanes, axis=1, mode="promise_in_bounds")


def dot_nt(left, right, precision=None):
    return lax.dot_general(
        left, right, NT, preferred_element_type=F32, precision=precision
    )


def fetch(copies):
    for copy in copies:
        copy.start()
    for copy in copies:
        copy.wait()


def pack_kernel(
    place_ref, mesh_hbm, need_hbm, port_hbm, out_ref, mesh_ref, need_ref, port_ref, sems
):
    rows = mesh_ref.shape[1] // 128
    ports = port_ref.shape[1]
    chips = out_ref.shape[0]
    fetch(
        [
            pltpu.make_async_copy(source, target, sems.at[i])
            for i, (source, target) in enumerate(
                [(mesh_hbm, mesh_ref), (need_hbm, need_ref), (port_hbm, port_ref)]
            )
        ]
    )
    port = port_ref[...] - place_ref[0] * (rows * 128)
    port = jnp.where((port >= 0) & (port < rows * 128), port, -1)
    port = jnp.broadcast_to(jnp.concatenate([port, port], axis=1), (8, 128))
    port_high, port_low = port >> 7, port & 127
    port_value = jnp.zeros((8, 128), F32)
    lane = lax.broadcasted_iota(jnp.int32, (8, 128), 1)
    for r in range(rows):
        real_row = mesh_ref[0:1, r * 128 : (r + 1) * 128]
        imag_row = mesh_ref[1:2, r * 128 : (r + 1) * 128]
        both = jnp.where(
            lane < ports, lane_pick(real_row, port_low), lane_pick(imag_row, port_low)
        )
        port_value = jnp.where(port_high == r, both, port_value)
        for chip in range(chips):
            out_ref[chip, r : r + 1, :] = real_row
            out_ref[chip, rows + r : rows + r + 1, :] = imag_row
    need = [need_ref[pl.ds(c, chips, 2), :].astype(F32) for c in range(2)]
    first = place_ref[1] == 0
    out_ref[:, 2 * rows, :] = jnp.where(first, need[0], need[1])
    out_ref[:, 2 * rows + 1, :] = jnp.where(first, need[1], need[0])
    out_ref[:, 2 * rows + 2, :] = jnp.broadcast_to(port_value[0:1], (chips, 128))
    for r in range(2 * rows + 3, out_ref.shape[1]):
        out_ref[:, r, :] = jnp.zeros((chips, 128), F32)


def prep_kernel(
    blocks_hbm, coupling_hbm, basis_in_hbm, basis_out_hbm, resistance_hbm, source_ref, target_ref,
    blocks_ref, coupling_ref, basis_in_ref, basis_out_ref, resistance_ref, source_out, target_out,
    raw_ref, sems,
):
    far_count, rank = coupling_hbm.shape[:2]
    tiles = blocks_hbm.shape[0]
    parts = 8
    part = tiles // parts
    coupling_copies = [
        pltpu.make_async_copy(coupling_hbm.at[k], raw_ref.at[k], sems.at[k])
        for k in range(far_count)
    ]
    other_copies = [
        pltpu.make_async_copy(
            blocks_hbm.at[pl.ds(i * part, part)],
            blocks_ref.at[pl.ds(i * part, part)],
            sems.at[far_count + i],
        )
        for i in range(parts)
    ]
    for i, (source, target) in enumerate(
        [
            (basis_in_hbm, basis_in_ref),
            (basis_out_hbm, basis_out_ref),
            (resistance_hbm, resistance_ref),
        ]
    ):
        other_copies.append(
            pltpu.make_async_copy(source, target, sems.at[far_count + parts + i])
        )
    for copy in coupling_copies + other_copies:
        copy.start()
    source_out[...] = source_ref[...]
    target_out[...] = target_ref[...]
    for k in range(far_count):
        coupling_copies[k].wait()

        def widen(g, carry):
            for i in range(4):
                block = raw_ref[k, g * 4 + i].astype(F32)
                coupling_ref[k, g * 4 + i] = jnp.concatenate([block, block], axis=1)
            return carry

        lax.fori_loop(0, rank // 4, widen, 0)
    for copy in other_copies:
        copy.wait()


def ask(need_ref, pack_ref, core, rows):
    chips = pack_ref.shape[0]
    wanted = [jnp.maximum(need_ref[pl.ds(c, chips, 2), :], 0) for c in range(2)]
    wanted = jnp.where(core == 0, wanted[0], wanted[1])
    high, low = wanted >> 7, wanted & 127
    value = [jnp.zeros((chips, 128), F32), jnp.zeros((chips, 128), F32)]
    for r in range(rows):
        here = high == r
        for c in range(2):
            row = pack_ref[:, c * rows + r, :]
            picked = jnp.take_along_axis(row, low, axis=1, mode="promise_in_bounds")
            value[c] = jnp.where(here, picked, value[c])
    return value


def lookup(code_ref, start, tables):
    total = [None, None]
    for k in range(2):
        code = code_ref[k, pl.ds(start, 8), :]
        high, low = code >> 8, (code >> 1) & 127
        value = [jnp.zeros((8, 128), F32), jnp.zeros((8, 128), F32)]
        for first, step, count, row_of in tables:
            offset = high - first
            for r in range(count):
                here = offset == r * step
                for c in range(2):
                    value[c] = jnp.where(here, lane_pick(row_of(r, c), low), value[c])
        along = (code & 1) == 1
        for c in range(2):
            signed = jnp.where(along, value[c], -value[c])
            total[c] = signed if k == 0 else total[c] + signed
    return total


def own_lookup_kernel(place_ref, mesh_ref, same_ref, need_ref, code_ref, out_ref, table_ref):
    rows = mesh_ref.shape[1] // 128
    chips = same_ref.shape[0]
    core = place_ref[1]
    value = ask(need_ref, same_ref, core, rows)
    for c in range(2):
        table_ref[c] = value[c]

    def own_row(r, c):
        return mesh_ref[c : c + 1, r * 128 : (r + 1) * 128]

    def peer_row(r, c):
        return table_ref[c, r : r + 1, :]

    def block(g, carry):
        start = pl.multiple_of(g * 8, 8)
        total = lookup(
            code_ref, start, [(0, 1, rows, own_row), (rows + core, 2, chips, peer_row)]
        )
        out_ref[0, pl.ds(start, 8), :] = total[0]
        out_ref[1, pl.ds(start, 8), :] = total[1]
        return carry

    lax.fori_loop(0, code_ref.shape[1] // 8, block, 0)


def current_kernel(
    place_ref, part_ref, other_ref, need_ref, code_ref, basis_ref, current_ref, coeff_ref,
    table_ref, *, first,
):
    chips = other_ref.shape[0]
    tiles = code_ref.shape[1]
    rank = basis_ref.shape[0] // tiles
    core = 1 - place_ref[1]
    value = ask(need_ref, other_ref, core, first)
    for c in range(2):
        table_ref[c] = value[c]

    def peer_row(r, c):
        return table_ref[c, r : r + 1, :]

    def block(g, carry):
        start = pl.multiple_of(g * 8, 8)
        total = lookup(code_ref, start, [(first + core, 2, chips, peer_row)])
        for c in range(2):
            current_ref[c, pl.ds(start, 8), :] = total[c] + part_ref[c, pl.ds(start, 8), :]
        return carry

    lax.fori_loop(0, tiles // 8, block, 0)
    inputs = jnp.concatenate([current_ref[0], current_ref[1]], axis=0)
    inputs = inputs.T.astype(BF16)
    lane_tile = lax.broadcasted_iota(jnp.int32, (rank, 2 * tiles), 1) % tiles
    full = jnp.dot(basis_ref[...], inputs, preferred_element_type=F32)
    chosen = jnp.zeros((rank, 2 * tiles), F32)
    for t in range(tiles):
        chosen = jnp.where(lane_tile == t, full[t * rank : (t + 1) * rank], chosen)
    coeff = chosen.astype(BF16)
    for p in range(coeff_ref.shape[0]):
        coeff_ref[p] = coeff


def near_kernel(source_ref, current_ref, blocks_ref, out_ref, inputs_ref):
    tiles, count, width, _ = blocks_ref.shape
    lane_tile = lax.broadcasted_iota(jnp.int32, (width, 128), 1) % tiles
    rows = jnp.concatenate([current_ref[0], current_ref[1]], axis=0)
    columns = rows.T.astype(BF16)
    row_index = lax.broadcasted_iota(jnp.int32, (128, 128), 0)
    for k in range(count):
        picks = jnp.where(row_index == source_ref[k : k + 1, :], 1.0, 0.0).astype(BF16)
        inputs_ref[k * width : (k + 1) * width, :] = jnp.dot(
            columns, picks, preferred_element_type=F32
        ).astype(BF16)
    inputs = inputs_ref[...]
    total = jnp.zeros((width, 128), F32)
    for g in range(tiles // 8):
        block = jnp.concatenate(
            [
                blocks_ref[g * 8 : g * 8 + 8, k].reshape(8 * width, width)
                for k in range(count)
            ],
            axis=1,
        )
        full = jnp.dot(block, inputs, preferred_element_type=F32)
        for i in range(8):
            total = jnp.where(
                lane_tile == g * 8 + i, full[i * width : (i + 1) * width], total
            )
    rows = total.T
    out_ref[0] = rows[:tiles]
    out_ref[1] = rows[tiles:]


def split(value):
    top = value.astype(BF16)
    return top, (value - top.astype(F32)).astype(BF16)


def counts(rows):
    return lax.broadcasted_iota(jnp.int32, (rows, 128), 0).astype(F32).astype(BF16)


def place(high, low, values, rows):
    sub_high, sub_low = counts(rows), counts(128)
    one, zero = jnp.ones((128, 128), BF16), jnp.zeros((128, 128), BF16)
    high = high.astype(F32).astype(BF16)
    low = low.astype(F32).astype(BF16)
    parts = [part for value in values for part in split(value)]
    left, right = [], []
    for i in range(high.shape[0]):
        here = jnp.broadcast_to(high[i : i + 1], (rows, 128)) == sub_high
        left.append(
            jnp.concatenate(
                [
                    jnp.where(here, jnp.broadcast_to(part[i : i + 1], (rows, 128)), zero[:rows])
                    for part in parts
                ],
                axis=0,
            )
        )
        there = jnp.broadcast_to(low[i : i + 1], (128, 128)) == sub_low
        right.append(jnp.where(there, one, zero))
    return jnp.concatenate(left, axis=1), jnp.concatenate(right, axis=1)


def scatter(code_ref, voltage_ref, total_ref, first, rows):
    total_ref[...] = jnp.zeros_like(total_ref)

    def block(g, carry):
        start = pl.multiple_of(g * 8, 8)
        for k in range(2):
            code = code_ref[k, pl.ds(start, 8), :]
            along = (code & 1) == 1
            values = []
            for c in range(2):
                voltage = voltage_ref[c, pl.ds(start, 8), :]
                values.append(jnp.where(along, voltage, -voltage))
            left, right = place((code >> 8) - first, (code >> 1) & 127, values, rows)
            total_ref[...] += dot_nt(left, right)
        return carry

    lax.fori_loop(0, code_ref.shape[1] // 8, block, 0)
    return [
        total_ref[2 * c * rows : (2 * c + 1) * rows, :]
        + total_ref[(2 * c + 1) * rows : (2 * c + 2) * rows, :]
        for c in range(2)
    ]


def voltage_kernel(*refs, first):
    (
        place_ref, coeff_ref, target_ref, coupling_ref, basis_ref, near_ref, current_ref, resistance_ref,
        code_ref, voltage_ref, slot_ref, picked_ref, mixed_ref, total_ref,
    ) = refs
    peers, rank, lanes = coeff_ref.shape
    device = place_ref[0]
    far_count = coupling_ref.shape[0]
    tiles = lanes // 2
    spans = target_ref.shape[0] // far_count
    stride = peers // far_count
    row_index = lax.broadcasted_iota(jnp.int32, (lanes, lanes), 0)
    for k in range(far_count):
        piece = None
        for i in range(spans):
            row = k * spans + i
            picks = jnp.where(row_index == target_ref[row : row + 1, :], 1.0, 0.0).astype(BF16)
            term = jnp.dot(
                coeff_ref[(device + k * stride + i) % peers], picks, preferred_element_type=F32
            )
            piece = term if piece is None else piece + term
        picked_ref[k] = piece

    def mix(g, carry):
        total = [None] * 4
        for k in range(far_count):
            picked = picked_ref[k]
            for i in range(4):
                product = coupling_ref[k, g * 4 + i] * picked
                part = product[0:8]
                for q in range(8, rank, 8):
                    part = part + product[q : q + 8]
                total[i] = part if k == 0 else total[i] + part
        for i in range(4):
            mixed_ref[pl.ds(g * 4 + i, 1), :] = jnp.sum(total[i], axis=0, keepdims=True)
        return carry

    lax.fori_loop(0, rank // 4, mix, 0)
    mixed = mixed_ref[...].T.astype(BF16)
    wide = 8 * rank
    spread = jnp.where(
        lax.broadcasted_iota(jnp.int32, (rank, wide), 0)
        == lax.broadcasted_iota(jnp.int32, (rank, wide), 1) % rank,
        1.0,
        0.0,
    ).astype(BF16)
    repeated = jnp.dot(mixed, spread, preferred_element_type=F32)
    own_block = (
        lax.broadcasted_iota(jnp.int32, (16, wide), 0) % 8
        == lax.broadcasted_iota(jnp.int32, (16, wide), 1) // rank
    )
    for g in range(tiles // 8):
        rows8 = slice(g * 8, g * 8 + 8)
        both = jnp.concatenate(
            [repeated[rows8], repeated[tiles + g * 8 : tiles + g * 8 + 8]], axis=0
        )
        both = jnp.where(own_block, both, 0.0).astype(BF16)
        far = jnp.dot(
            both, basis_ref[g * wide : (g + 1) * wide, :], preferred_element_type=F32
        )
        resistance = resistance_ref[rows8, :]
        voltage_ref[0, rows8, :] = resistance * current_ref[0, rows8, :] - (
            near_ref[1, rows8, :] + far[8:16]
        )
        voltage_ref[1, rows8, :] = resistance * current_ref[1, rows8, :] + (
            near_ref[0, rows8, :] + far[0:8]
        )
    sums = scatter(code_ref, voltage_ref, total_ref, first, slot_ref.shape[0])
    for c in range(2):
        slot_ref[:, c, :] = sums[c]


def own_sum_kernel(code_ref, voltage_ref, own_ref, total_ref):
    sums = scatter(code_ref, voltage_ref, total_ref, 0, own_ref.shape[1])
    for c in range(2):
        own_ref[c] = sums[c]


def finish_kernel(
    place_ref, own_ref, arrived_ref, same_ref, other_ref, port_ref, impedance_ref, out_ref
):
    rows = own_ref.shape[1]
    ports = impedance_ref.shape[1]
    chips = same_ref.shape[0]
    same = same_ref[:, 2 * rows, :].astype(jnp.int32)
    other = other_ref[:, 2 * rows + 1, :].astype(jnp.int32)
    first_core = place_ref[1] == 0
    total = None
    for core in range(2):
        asked = jnp.where(first_core, same, other) if core == 0 else jnp.where(first_core, other, same)
        values = [arrived_ref[:, core, c, :] for c in range(2)]
        left, right = place(asked >> 7, asked & 127, values, rows)
        term = dot_nt(left, right)
        total = term if total is None else total + term
    port_current = jnp.sum(
        same_ref[:, 2 * rows + 2, :] + other_ref[:, 2 * rows + 2, :], axis=0, keepdims=True
    )
    real = port_current[:, :ports]
    imag = port_current[:, ports:]
    both = jnp.concatenate([real, imag, jnp.zeros((6, ports), F32)], axis=0)
    by_real = dot_nt(both, impedance_ref[0], lax.Precision.HIGHEST)
    by_imag = dot_nt(both, impedance_ref[1], lax.Precision.HIGHEST)
    pad = jnp.zeros((1, 128 - ports), F32)
    terms = [
        jnp.concatenate([by_real[0:1] - by_imag[1:2], pad], axis=1),
        jnp.concatenate([by_real[1:2] + by_imag[0:1], pad], axis=1),
    ]
    port = port_ref[...] - place_ref[0] * (rows * 128)
    port = jnp.where((port >= 0) & (port < rows * 128), port, -1)
    port = jnp.concatenate([port, jnp.full((1, 128 - ports), -1, jnp.int32)], axis=1)
    left, right = place(port >> 7, port & 127, terms, rows)
    total = total + dot_nt(left, right)
    for c in range(2):
        summed = own_ref[c] + (
            total[2 * c * rows : (2 * c + 1) * rows] + total[(2 * c + 1) * rows : (2 * c + 2) * rows]
        )
        for r in range(rows):
            out_ref[c : c + 1, r * 128 : (r + 1) * 128] = summed[r : r + 1]


def per_device(
    mesh_current,
    branch_entry,
    branch_sign,
    need_slots,
    resistance,
    near_blocks,
    near_source,
    basis_in,
    coupling,
    basis_out,
    admissible,
    port_mesh,
    port_coupling,
):
    chips = lax.axis_size("chips")
    peers = 2 * chips
    core = lax.axis_index("core")
    device = 2 * lax.axis_index("chips") + core
    mesh_dev = mesh_current.shape[1]
    tiles, near_count, width, _ = near_blocks.shape
    rank = basis_in.shape[1]
    far_count = admissible.shape[1]
    own_rows = mesh_dev // 128
    vmem = pl.BlockSpec(memory_space=pltpu.VMEM)
    smem = pl.BlockSpec(memory_space=pltpu.SMEM)
    shape = jax.ShapeDtypeStruct

    code = (branch_entry * 2 + branch_sign).reshape(2, tiles, width)
    coupling_lanes = jnp.transpose(coupling, (1, 2, 3, 0))
    basis_in_rows = basis_in.reshape(tiles * rank, width)
    basis_out_rows = basis_out.reshape(tiles * rank, width)
    half = jnp.arange(2 * tiles, dtype=jnp.int32) // tiles
    sources = jnp.transpose(near_source)
    sources = jnp.concatenate([sources, sources], axis=1) + half[None] * tiles
    band = peers * tiles // far_count
    spans = band // tiles + 1
    bases = device * tiles + jnp.arange(far_count, dtype=jnp.int32) * band
    shifted = (jnp.transpose(admissible) - bases[:, None]) % (peers * tiles)
    shifted = jnp.concatenate([shifted, shifted], axis=1)[:, None, :]
    shifted = shifted - jnp.arange(spans, dtype=jnp.int32)[None, :, None] * tiles
    inside = (shifted >= 0) & (shifted < tiles)
    targets = jnp.where(inside, shifted + half * tiles, -1).reshape(far_count * spans, 2 * tiles)

    place_word = jnp.stack([device, core])
    hbm = pl.BlockSpec(memory_space=pl.ANY)
    port_row = port_mesh.reshape(1, -1)
    pack_rows = (2 * own_rows + 3 + 7) // 8 * 8
    pack, mesh_near, need_near, port_near = pl.pallas_call(
        pack_kernel,
        out_shape=(
            shape((chips, pack_rows, 128), F32),
            pltpu.VMEM(mesh_current.shape, F32),
            pltpu.VMEM(need_slots.shape, jnp.int32),
            pltpu.VMEM(port_row.shape, jnp.int32),
        ),
        in_specs=[smem] + [hbm] * 3,
        out_specs=(vmem,) * 4,
        scratch_shapes=[pltpu.SemaphoreType.DMA((3,))],
        compiler_params=params(),
        name="pack",
    )(place_word, mesh_current, need_slots, port_row)
    same = lax.all_to_all(pack, "chips", 0, 0, tiled=True)
    blocks, wide_coupling, basis_in_rows, basis_out_rows, resistance_rows, sources, targets = (
        pl.pallas_call(
            prep_kernel,
            out_shape=(
                pltpu.VMEM(near_blocks.shape, BF16),
                pltpu.VMEM((far_count, rank, rank, 2 * tiles), F32),
                pltpu.VMEM(basis_in_rows.shape, BF16),
                pltpu.VMEM(basis_out_rows.shape, BF16),
                pltpu.VMEM((tiles, width), F32),
                pltpu.VMEM(sources.shape, jnp.int32),
                pltpu.VMEM(targets.shape, jnp.int32),
            ),
            in_specs=[hbm] * 5 + [vmem] * 2,
            out_specs=(vmem,) * 7,
            scratch_shapes=[
                pltpu.VMEM((far_count, rank, rank, tiles), BF16),
                pltpu.SemaphoreType.DMA((far_count + 11,)),
            ],
            compiler_params=params(),
            cost_estimate=pl.CostEstimate(
                flops=10**9, bytes_accessed=13 * 10**6, transcendentals=0
            ),
            name="prep",
        )(
            near_blocks,
            coupling_lanes,
            basis_in_rows,
            basis_out_rows,
            resistance.reshape(tiles, width),
            sources,
            targets,
        )
    )
    other = lax.ppermute(same, "core", [(0, 1), (1, 0)])
    part = pl.pallas_call(
        own_lookup_kernel,
        out_shape=shape((2, tiles, width), F32),
        in_specs=[smem] + [vmem] * 4,
        out_specs=vmem,
        scratch_shapes=[pltpu.VMEM((2, chips, 128), F32)],
        compiler_params=params(),
        cost_estimate=small_cost(),
        name="own_lookup",
    )(place_word, mesh_near, same, need_near, code)
    current, coeff = pl.pallas_call(
        functools.partial(current_kernel, first=own_rows),
        out_shape=(shape((2, tiles, width), F32), shape((peers, rank, 2 * tiles), BF16)),
        in_specs=[smem] + [vmem] * 5,
        out_specs=(vmem,) * 2,
        scratch_shapes=[pltpu.VMEM((2, chips, 128), F32)],
        compiler_params=params(),
        name="currents",
    )(place_word, part, other, need_near, code, basis_in_rows)
    all_coeff = lax.all_to_all(coeff, ("chips", "core"), 0, 0, tiled=True)
    near = pl.pallas_call(
        near_kernel,
        out_shape=shape((2, tiles, width), F32),
        in_specs=[vmem] * 3,
        out_specs=vmem,
        scratch_shapes=[pltpu.VMEM((near_count * width, 2 * tiles), BF16)],
        compiler_params=params(),
        cost_estimate=pl.CostEstimate(
            flops=256 * near_blocks.size, bytes_accessed=2 * near_blocks.size, transcendentals=0
        ),
        name="near_field",
    )(sources, current, blocks)
    voltage, slots = pl.pallas_call(
        functools.partial(voltage_kernel, first=own_rows),
        out_shape=(shape((2, tiles, width), F32), shape((peers, 2, 128), F32)),
        in_specs=[smem] + [vmem] * 8,
        out_specs=(vmem,) * 2,
        scratch_shapes=[
            pltpu.VMEM((far_count, rank, 2 * tiles), F32),
            pltpu.VMEM((rank, 2 * tiles), F32),
            pltpu.VMEM((4 * peers, 128), F32),
        ],
        compiler_params=params(),
        name="voltages",
    )(
        place_word,
        all_coeff,
        targets,
        wide_coupling,
        basis_out_rows,
        near,
        current,
        resistance_rows,
        code,
    )
    arrived = lax.all_to_all(slots, ("chips", "core"), 0, 0, tiled=True)
    own = pl.pallas_call(
        own_sum_kernel,
        out_shape=shape((2, own_rows, 128), F32),
        in_specs=[vmem] * 2,
        out_specs=vmem,
        scratch_shapes=[pltpu.VMEM((4 * own_rows, 128), F32)],
        compiler_params=params(),
        cost_estimate=small_cost(),
        name="own_sums",
    )(code, voltage)
    return pl.pallas_call(
        finish_kernel,
        out_shape=shape((2, mesh_dev), F32),
        in_specs=[smem] + [vmem] * 6,
        out_specs=vmem,
        compiler_params=params(),
        name="finish",
    )(
        place_word,
        own,
        arrived.reshape(chips, 2, 2, 128),
        same,
        other,
        port_near,
        port_coupling,
    )


def solution(mesh):
    groups, peers = mesh.devices.shape
    split_mesh = jax.sharding.Mesh(
        mesh.devices.reshape(groups, peers // 2, 2), ("groups", "chips", "core")
    )
    in_specs = (
        P(None, SPREAD),
        P(None, SPREAD),
        P(None, SPREAD),
        P(SPREAD, None),
        P(SPREAD),
        P(SPREAD, None, None, None),
        P(SPREAD, None),
        P(SPREAD, None, None),
        P(SPREAD, None, None, None),
        P(SPREAD, None, None),
        P(SPREAD, None),
        P("groups"),
        P(),
    )
    out_specs = P(None, SPREAD)
    return jax.shard_map(
        per_device, mesh=split_mesh, in_specs=in_specs, out_specs=out_specs, check_vma=False
    )
```

```python
import functools

import jax
import jax.numpy as jnp
from jax import lax
from jax.experimental import pallas as pl
from jax.experimental.pallas import tpu as pltpu
from jax.sharding import PartitionSpec as P

F32 = jnp.float32
BF16 = jnp.bfloat16
SPREAD = ("groups", "chips", "core")
VMEM_LIMIT = 24 * 1024 * 1024
NT = (((1,), (1,)), ((), ()))


def params():
    return pltpu.CompilerParams(vmem_limit_bytes=VMEM_LIMIT)


def small_cost():
    return pl.CostEstimate(flops=10**9, bytes_accessed=8 * 10**6, transcendentals=0)


def lane_pick(row, lanes):
    spread = jnp.broadcast_to(row, lanes.shape)
    return jnp.take_along_axis(spread, lanes, axis=1, mode="promise_in_bounds")


def dot_nt(left, right, precision=None):
    return lax.dot_general(
        left, right, NT, preferred_element_type=F32, precision=precision
    )


def fetch(copies):
    for copy in copies:
        copy.start()
    for copy in copies:
        copy.wait()


def pack_kernel(
    place_ref, mesh_hbm, need_hbm, port_hbm, out_ref, mesh_ref, need_ref, port_ref, sems
):
    rows = mesh_ref.shape[1] // 128
    ports = port_ref.shape[1]
    chips = out_ref.shape[0]
    fetch(
        [
            pltpu.make_async_copy(source, target, sems.at[i])
            for i, (source, target) in enumerate(
                [(mesh_hbm, mesh_ref), (need_hbm, need_ref), (port_hbm, port_ref)]
            )
        ]
    )
    port = port_ref[...] - place_ref[0] * (rows * 128)
    port = jnp.where((port >= 0) & (port < rows * 128), port, -1)
    port = jnp.broadcast_to(jnp.concatenate([port, port], axis=1), (8, 128))
    port_high, port_low = port >> 7, port & 127
    port_value = jnp.zeros((8, 128), F32)
    lane = lax.broadcasted_iota(jnp.int32, (8, 128), 1)
    for r in range(rows):
        real_row = mesh_ref[0:1, r * 128 : (r + 1) * 128]
        imag_row = mesh_ref[1:2, r * 128 : (r + 1) * 128]
        both = jnp.where(
            lane < ports, lane_pick(real_row, port_low), lane_pick(imag_row, port_low)
        )
        port_value = jnp.where(port_high == r, both, port_value)
        for chip in range(chips):
            out_ref[chip, r : r + 1, :] = real_row
            out_ref[chip, rows + r : rows + r + 1, :] = imag_row
    need = [need_ref[pl.ds(c, chips, 2), :].astype(F32) for c in range(2)]
    first = place_ref[1] == 0
    out_ref[:, 2 * rows, :] = jnp.where(first, need[0], need[1])
    out_ref[:, 2 * rows + 1, :] = jnp.where(first, need[1], need[0])
    out_ref[:, 2 * rows + 2, :] = jnp.broadcast_to(port_value[0:1], (chips, 128))
    for r in range(2 * rows + 3, out_ref.shape[1]):
        out_ref[:, r, :] = jnp.zeros((chips, 128), F32)


def ask(need_ref, pack_ref, core, rows):
    chips = pack_ref.shape[0]
    wanted = [jnp.maximum(need_ref[pl.ds(c, chips, 2), :], 0) for c in range(2)]
    wanted = jnp.where(core == 0, wanted[0], wanted[1])
    high, low = wanted >> 7, wanted & 127
    value = [jnp.zeros((chips, 128), F32), jnp.zeros((chips, 128), F32)]
    for r in range(rows):
        here = high == r
        for c in range(2):
            row = pack_ref[:, c * rows + r, :]
            picked = jnp.take_along_axis(row, low, axis=1, mode="promise_in_bounds")
            value[c] = jnp.where(here, picked, value[c])
    return value


def lookup(code_ref, start, tables):
    total = [None, None]
    for k in range(2):
        code = code_ref[k, pl.ds(start, 8), :]
        high, low = code >> 8, (code >> 1) & 127
        value = [jnp.zeros((8, 128), F32), jnp.zeros((8, 128), F32)]
        for first, step, count, row_of in tables:
            offset = high - first
            for r in range(count):
                here = offset == r * step
                for c in range(2):
                    value[c] = jnp.where(here, lane_pick(row_of(r, c), low), value[c])
        along = (code & 1) == 1
        for c in range(2):
            signed = jnp.where(along, value[c], -value[c])
            total[c] = signed if k == 0 else total[c] + signed
    return total


def own_lookup_kernel(mesh_ref, code_ref, out_ref):
    rows = mesh_ref.shape[1] // 128

    def own_row(r, c):
        return mesh_ref[c : c + 1, r * 128 : (r + 1) * 128]

    def block(g, carry):
        start = pl.multiple_of(g * 8, 8)
        total = lookup(code_ref, start, [(0, 1, rows, own_row)])
        out_ref[0, pl.ds(start, 8), :] = total[0]
        out_ref[1, pl.ds(start, 8), :] = total[1]
        return carry

    lax.fori_loop(0, code_ref.shape[1] // 8, block, 0)


def add_peers(part_ref, pack_ref, need_ref, code_ref, table_ref, out_ref, core, first):
    chips = pack_ref.shape[0]
    value = ask(need_ref, pack_ref, core, first)
    for c in range(2):
        table_ref[c] = value[c]

    def peer_row(r, c):
        return table_ref[c, r : r + 1, :]

    def block(g, carry):
        start = pl.multiple_of(g * 8, 8)
        total = lookup(code_ref, start, [(first + core, 2, chips, peer_row)])
        for c in range(2):
            out_ref[c, pl.ds(start, 8), :] = total[c] + part_ref[c, pl.ds(start, 8), :]
        return carry

    lax.fori_loop(0, code_ref.shape[1] // 8, block, 0)


def same_core_kernel(
    place_ref, part_ref, same_ref, need_ref, code_ref, out_ref, table_ref, *, first
):
    add_peers(
        part_ref, same_ref, need_ref, code_ref, table_ref, out_ref, place_ref[1], first
    )


def current_kernel(
    place_ref, part_ref, other_ref, need_ref, code_ref, basis_hbm, current_ref, coeff_ref,
    table_ref, basis_ref, sem, *, first,
):
    tiles = code_ref.shape[1]
    rank = basis_ref.shape[0] // tiles
    copy = pltpu.make_async_copy(basis_hbm, basis_ref, sem.at[0])
    copy.start()
    add_peers(
        part_ref, other_ref, need_ref, code_ref, table_ref, current_ref, 1 - place_ref[1], first
    )
    copy.wait()
    inputs = jnp.concatenate([current_ref[0], current_ref[1]], axis=0)
    inputs = inputs.T.astype(BF16)
    lane_tile = lax.broadcasted_iota(jnp.int32, (rank, 2 * tiles), 1) % tiles
    full = jnp.dot(basis_ref[...], inputs, preferred_element_type=F32)
    chosen = jnp.zeros((rank, 2 * tiles), F32)
    for t in range(tiles):
        chosen = jnp.where(lane_tile == t, full[t * rank : (t + 1) * rank], chosen)
    coeff = chosen.astype(BF16)
    for p in range(coeff_ref.shape[0]):
        coeff_ref[p] = coeff


def near_kernel(source_ref, current_ref, blocks_hbm, out_ref, inputs_ref, blocks_ref, sems):
    tiles, count, width, _ = blocks_ref.shape
    copies = [
        pltpu.make_async_copy(
            blocks_hbm.at[pl.ds(g * 8, 8)], blocks_ref.at[pl.ds(g * 8, 8)], sems.at[g]
        )
        for g in range(tiles // 8)
    ]
    for copy in copies:
        copy.start()
    lane_tile = lax.broadcasted_iota(jnp.int32, (width, 128), 1) % tiles
    rows = jnp.concatenate([current_ref[0], current_ref[1]], axis=0)
    columns = rows.T.astype(BF16)
    row_index = lax.broadcasted_iota(jnp.int32, (128, 128), 0)
    for k in range(count):
        picks = jnp.where(row_index == source_ref[k : k + 1, :], 1.0, 0.0).astype(BF16)
        inputs_ref[k * width : (k + 1) * width, :] = jnp.dot(
            columns, picks, preferred_element_type=F32
        ).astype(BF16)
    inputs = inputs_ref[...]
    total = jnp.zeros((width, 128), F32)
    for g in range(tiles // 8):
        copies[g].wait()
        block = jnp.concatenate(
            [
                blocks_ref[g * 8 : g * 8 + 8, k].reshape(8 * width, width)
                for k in range(count)
            ],
            axis=1,
        )
        full = jnp.dot(block, inputs, preferred_element_type=F32)
        for i in range(8):
            total = jnp.where(
                lane_tile == g * 8 + i, full[i * width : (i + 1) * width], total
            )
    rows = total.T
    out_ref[0] = rows[:tiles]
    out_ref[1] = rows[tiles:]


def split(value):
    top = value.astype(BF16)
    return top, (value - top.astype(F32)).astype(BF16)


def counts(rows):
    return lax.broadcasted_iota(jnp.int32, (rows, 128), 0).astype(F32)


def place(high, low, values, rows, spread_ref):
    sub_high, sub_low = counts(rows).astype(BF16), counts(128).astype(BF16)
    one, zero = jnp.ones((128, 128), BF16), jnp.zeros((128, 128), BF16)
    spread_ref[0] = high.astype(F32)
    spread_ref[1] = low.astype(F32)
    for c, value in enumerate(values):
        top, rest = split(value)
        spread_ref[2 + 2 * c] = top.astype(F32)
        spread_ref[3 + 2 * c] = rest.astype(F32)

    def spread(j, i, count):
        return jnp.broadcast_to(spread_ref[j, i : i + 1, :], (count, 128)).astype(BF16)

    left, right = [], []
    for i in range(8):
        here = spread(0, i, rows) == sub_high
        left.append(
            jnp.concatenate(
                [jnp.where(here, spread(j, i, rows), zero[:rows]) for j in range(2, 6)], axis=0
            )
        )
        right.append(jnp.where(spread(1, i, 128) == sub_low, one, zero))
    return jnp.concatenate(left, axis=1), jnp.concatenate(right, axis=1)


def place_few(high, low, values, rows):
    sub_high = lax.broadcasted_iota(jnp.int32, (rows, 128), 0)
    sub_low = lax.broadcasted_iota(jnp.int32, (128, 128), 0)
    left, right = [], []
    for i in range(high.shape[0]):
        here = jnp.broadcast_to(high[i : i + 1], (rows, 128)) == sub_high
        parts = []
        for value in values:
            spread = jnp.where(here, jnp.broadcast_to(value[i : i + 1], (rows, 128)), 0.0)
            parts.extend(split(spread))
        left.append(jnp.concatenate(parts, axis=0))
        there = jnp.broadcast_to(low[i : i + 1], (128, 128)) == sub_low
        right.append(jnp.where(there, 1.0, 0.0).astype(BF16))
    return jnp.concatenate(left, axis=1), jnp.concatenate(right, axis=1)


def scatter(code_ref, voltage_ref, total_ref, spread_ref, first, rows):
    total_ref[...] = jnp.zeros_like(total_ref)

    def block(g, carry):
        start = pl.multiple_of(g * 8, 8)
        for k in range(2):
            code = code_ref[k, pl.ds(start, 8), :]
            along = (code & 1) == 1
            values = []
            for c in range(2):
                voltage = voltage_ref[c, pl.ds(start, 8), :]
                values.append(jnp.where(along, voltage, -voltage))
            left, right = place((code >> 8) - first, (code >> 1) & 127, values, rows, spread_ref)
            total_ref[...] += dot_nt(left, right)
        return carry

    lax.fori_loop(0, code_ref.shape[1] // 8, block, 0)
    return [
        total_ref[2 * c * rows : (2 * c + 1) * rows, :]
        + total_ref[(2 * c + 1) * rows : (2 * c + 2) * rows, :]
        for c in range(2)
    ]


def voltage_kernel(
    place_ref, coeff_ref, target_ref, coupling_hbm, basis_hbm, near_ref, current_ref,
    resistance_hbm, code_ref, voltage_ref, slot_ref, picked_ref, mixed_ref, total_ref,
    spread_ref, coupling_ref, basis_ref, resistance_ref, sems, *, first,
):
    peers, rank, lanes = coeff_ref.shape
    far_count = coupling_ref.shape[0]
    tiles = lanes // 2
    half = rank // 2
    groups = half // 4
    device = place_ref[0]

    def coupling_copy(g):
        rows = pl.ds(g * 4, 4)
        return pltpu.make_async_copy(
            coupling_hbm.at[:, rows], coupling_ref.at[:, rows], sems.at[g]
        )

    for g in range(groups):
        coupling_copy(g).start()
        coupling_copy(groups + g).start()
    late_copies = [
        pltpu.make_async_copy(basis_hbm, basis_ref, sems.at[2 * groups]),
        pltpu.make_async_copy(resistance_hbm, resistance_ref, sems.at[2 * groups + 1]),
    ]
    for copy in late_copies:
        copy.start()
    spans = target_ref.shape[0] // far_count
    stride = peers // far_count
    for k in range(far_count):
        picked = [jnp.zeros((rank, lanes), F32), jnp.zeros((rank, lanes), F32)]
        for i in range(spans):
            row = k * spans + i
            block = coeff_ref[(device + k * stride + i) % peers].astype(F32)
            target = jnp.broadcast_to(target_ref[row : row + 1, :], (rank, lanes))
            inside = target >= 0
            source = jnp.maximum(target, 0)
            for c in range(2):
                value = jnp.take_along_axis(
                    block, source + c * tiles, axis=1, mode="promise_in_bounds"
                )
                picked[c] = jnp.where(inside, value, picked[c])
        for c in range(2):
            picked_ref[c, k] = picked[c]

    def mix(g, carry):
        coupling_copy(g).wait()
        coupling_copy(groups + g).wait()
        total = [[None, None] for _ in range(4)]
        for k in range(far_count):
            picked = [picked_ref[c, k] for c in range(2)]
            for i in range(4):
                block = jnp.concatenate(
                    [coupling_ref[k, g * 4 + i], coupling_ref[k, half + g * 4 + i]], axis=1
                ).astype(F32)
                for c in range(2):
                    product = block * picked[c]
                    part = product[0:8]
                    for q in range(8, rank, 8):
                        part = part + product[q : q + 8]
                    total[i][c] = part if k == 0 else total[i][c] + part
        for i in range(4):
            for c in range(2):
                row = jnp.sum(total[i][c], axis=0, keepdims=True)
                mixed_ref[pl.ds(c * half + g * 4 + i, 1), :] = row
        return carry

    lax.fori_loop(0, groups, mix, 0)
    mixed = mixed_ref[...].T
    mixed = jnp.concatenate([mixed[:tiles], mixed[tiles:]], axis=1).astype(BF16)
    wide = 8 * rank
    from_row = lax.broadcasted_iota(jnp.int32, (2 * rank, wide), 0)
    to_rank = lax.broadcasted_iota(jnp.int32, (2 * rank, wide), 1) % rank
    repeated = []
    for c in range(2):
        wanted = (to_rank // half) * rank + c * half + to_rank % half
        picks = jnp.where(from_row == wanted, 1.0, 0.0).astype(BF16)
        repeated.append(jnp.dot(mixed, picks, preferred_element_type=F32))
    for copy in late_copies:
        copy.wait()
    own_block = (
        lax.broadcasted_iota(jnp.int32, (16, wide), 0) % 8
        == lax.broadcasted_iota(jnp.int32, (16, wide), 1) // rank
    )
    for g in range(tiles // 8):
        rows8 = slice(g * 8, g * 8 + 8)
        both = jnp.concatenate([repeated[0][rows8], repeated[1][rows8]], axis=0)
        both = jnp.where(own_block, both, 0.0).astype(BF16)
        far = jnp.dot(
            both, basis_ref[g * wide : (g + 1) * wide, :], preferred_element_type=F32
        )
        resistance = resistance_ref[rows8, :]
        voltage_ref[0, rows8, :] = resistance * current_ref[0, rows8, :] - (
            near_ref[1, rows8, :] + far[8:16]
        )
        voltage_ref[1, rows8, :] = resistance * current_ref[1, rows8, :] + (
            near_ref[0, rows8, :] + far[0:8]
        )
    sums = scatter(code_ref, voltage_ref, total_ref, spread_ref, first, slot_ref.shape[0])
    for c in range(2):
        slot_ref[:, c, :] = sums[c]


def own_sum_kernel(code_ref, voltage_ref, own_ref, total_ref, spread_ref):
    sums = scatter(code_ref, voltage_ref, total_ref, spread_ref, 0, own_ref.shape[1])
    for c in range(2):
        own_ref[c] = sums[c]


def finish_kernel(
    place_ref, own_ref, arrived_ref, same_ref, other_ref, port_ref, impedance_ref, out_ref
):
    rows = own_ref.shape[1]
    ports = impedance_ref.shape[1]
    chips = same_ref.shape[0]
    same = same_ref[:, 2 * rows, :].astype(jnp.int32)
    other = other_ref[:, 2 * rows + 1, :].astype(jnp.int32)
    first_core = place_ref[1] == 0
    total = None
    for core in range(2):
        asked = jnp.where(first_core, same, other) if core == 0 else jnp.where(first_core, other, same)
        values = [arrived_ref[:, core, c, :] for c in range(2)]
        left, right = place_few(asked >> 7, asked & 127, values, rows)
        term = dot_nt(left, right)
        total = term if total is None else total + term
    port_current = jnp.sum(
        same_ref[:, 2 * rows + 2, :] + other_ref[:, 2 * rows + 2, :], axis=0, keepdims=True
    )
    real = port_current[:, :ports]
    imag = port_current[:, ports:]
    both = jnp.concatenate([real, imag, jnp.zeros((6, ports), F32)], axis=0)
    by_real = dot_nt(both, impedance_ref[0], lax.Precision.HIGHEST)
    by_imag = dot_nt(both, impedance_ref[1], lax.Precision.HIGHEST)
    pad = jnp.zeros((1, 128 - ports), F32)
    terms = [
        jnp.concatenate([by_real[0:1] - by_imag[1:2], pad], axis=1),
        jnp.concatenate([by_real[1:2] + by_imag[0:1], pad], axis=1),
    ]
    port = port_ref[...] - place_ref[0] * (rows * 128)
    port = jnp.where((port >= 0) & (port < rows * 128), port, -1)
    port = jnp.concatenate([port, jnp.full((1, 128 - ports), -1, jnp.int32)], axis=1)
    left, right = place_few(port >> 7, port & 127, terms, rows)
    total = total + dot_nt(left, right)
    for c in range(2):
        summed = own_ref[c] + (
            total[2 * c * rows : (2 * c + 1) * rows] + total[(2 * c + 1) * rows : (2 * c + 2) * rows]
        )
        for r in range(rows):
            out_ref[c : c + 1, r * 128 : (r + 1) * 128] = summed[r : r + 1]


def per_device(
    mesh_current,
    branch_entry,
    branch_sign,
    need_slots,
    resistance,
    near_blocks,
    near_source,
    basis_in,
    coupling,
    basis_out,
    admissible,
    port_mesh,
    port_coupling,
):
    chips = lax.axis_size("chips")
    peers = 2 * chips
    core = lax.axis_index("core")
    device = 2 * lax.axis_index("chips") + core
    mesh_dev = mesh_current.shape[1]
    tiles, near_count, width, _ = near_blocks.shape
    rank = basis_in.shape[1]
    far_count = admissible.shape[1]
    own_rows = mesh_dev // 128
    vmem = pl.BlockSpec(memory_space=pltpu.VMEM)
    smem = pl.BlockSpec(memory_space=pltpu.SMEM)
    shape = jax.ShapeDtypeStruct

    code = (branch_entry * 2 + branch_sign).reshape(2, tiles, width)
    coupling_lanes = jnp.transpose(coupling, (1, 2, 3, 0))
    basis_in_rows = basis_in.reshape(tiles * rank, width)
    basis_out_rows = basis_out.reshape(tiles * rank, width)
    half = jnp.arange(2 * tiles, dtype=jnp.int32) // tiles
    sources = jnp.transpose(near_source)
    sources = jnp.concatenate([sources, sources], axis=1) + half[None] * tiles
    band = peers * tiles // far_count
    spans = band // tiles + 1
    bases = device * tiles + jnp.arange(far_count, dtype=jnp.int32) * band
    shifted = (jnp.transpose(admissible) - bases[:, None]) % (peers * tiles)
    shifted = jnp.concatenate([shifted, shifted], axis=1)[:, None, :]
    shifted = shifted - jnp.arange(spans, dtype=jnp.int32)[None, :, None] * tiles
    inside = (shifted >= 0) & (shifted < tiles)
    targets = jnp.where(inside, shifted, -1).reshape(far_count * spans, 2 * tiles)

    def in_hbm(x):
        return pltpu.with_memory_space_constraint(x, pltpu.HBM)

    place_word = jnp.stack([device, core])
    hbm = pl.BlockSpec(memory_space=pl.ANY)
    port_row = port_mesh.reshape(1, -1)
    pack_rows = (2 * own_rows + 3 + 7) // 8 * 8
    pack, mesh_near, need_near, port_near = pl.pallas_call(
        pack_kernel,
        out_shape=(
            shape((chips, pack_rows, 128), F32),
            pltpu.VMEM(mesh_current.shape, F32),
            pltpu.VMEM(need_slots.shape, jnp.int32),
            pltpu.VMEM(port_row.shape, jnp.int32),
        ),
        in_specs=[smem] + [hbm] * 3,
        out_specs=(vmem,) * 4,
        scratch_shapes=[pltpu.SemaphoreType.DMA((3,))],
        compiler_params=params(),
        name="pack",
    )(place_word, in_hbm(mesh_current), in_hbm(need_slots), in_hbm(port_row))
    same = lax.all_to_all(pack, "chips", 0, 0, tiled=True)
    own_part = pl.pallas_call(
        own_lookup_kernel,
        out_shape=shape((2, tiles, width), F32),
        in_specs=[vmem] * 2,
        out_specs=vmem,
        compiler_params=params(),
        cost_estimate=small_cost(),
        name="own_lookup",
    )(mesh_near, code)
    other = lax.ppermute(same, "core", [(0, 1), (1, 0)])
    part = pl.pallas_call(
        functools.partial(same_core_kernel, first=own_rows),
        out_shape=shape((2, tiles, width), F32),
        in_specs=[smem] + [vmem] * 4,
        out_specs=vmem,
        scratch_shapes=[pltpu.VMEM((2, chips, 128), F32)],
        compiler_params=params(),
        cost_estimate=small_cost(),
        name="same_core",
    )(place_word, own_part, same, need_near, code)
    current, coeff = pl.pallas_call(
        functools.partial(current_kernel, first=own_rows),
        out_shape=(shape((2, tiles, width), F32), shape((peers, rank, 2 * tiles), BF16)),
        in_specs=[smem] + [vmem] * 4 + [hbm],
        out_specs=(vmem,) * 2,
        scratch_shapes=[
            pltpu.VMEM((2, chips, 128), F32),
            pltpu.VMEM(basis_in_rows.shape, BF16),
            pltpu.SemaphoreType.DMA((1,)),
        ],
        compiler_params=params(),
        name="currents",
    )(place_word, part, other, need_near, code, in_hbm(basis_in_rows))
    all_coeff = lax.all_to_all(coeff, ("chips", "core"), 0, 0, tiled=True)
    near = pl.pallas_call(
        near_kernel,
        out_shape=shape((2, tiles, width), F32),
        in_specs=[vmem] * 2 + [hbm],
        out_specs=vmem,
        scratch_shapes=[
            pltpu.VMEM((near_count * width, 2 * tiles), BF16),
            pltpu.VMEM(near_blocks.shape, BF16),
            pltpu.SemaphoreType.DMA((tiles // 8,)),
        ],
        compiler_params=params(),
        cost_estimate=pl.CostEstimate(
            flops=256 * near_blocks.size, bytes_accessed=2 * near_blocks.size, transcendentals=0
        ),
        name="near_field",
    )(sources, current, in_hbm(near_blocks))
    voltage, slots = pl.pallas_call(
        functools.partial(voltage_kernel, first=own_rows),
        out_shape=(shape((2, tiles, width), F32), shape((peers, 2, 128), F32)),
        in_specs=[smem] + [vmem] * 2 + [hbm] * 2 + [vmem] * 2 + [hbm, vmem],
        out_specs=(vmem,) * 2,
        scratch_shapes=[
            pltpu.VMEM((2, far_count, rank, 2 * tiles), F32),
            pltpu.VMEM((rank, 2 * tiles), F32),
            pltpu.VMEM((4 * peers, 128), F32),
            pltpu.VMEM((6, 8, 128), F32),
            pltpu.VMEM(coupling_lanes.shape, BF16),
            pltpu.VMEM(basis_out_rows.shape, BF16),
            pltpu.VMEM((tiles, width), F32),
            pltpu.SemaphoreType.DMA((rank // 4 + 2,)),
        ],
        compiler_params=params(),
        name="voltages",
    )(
        place_word,
        all_coeff,
        targets,
        in_hbm(coupling_lanes),
        in_hbm(basis_out_rows),
        near,
        current,
        in_hbm(resistance.reshape(tiles, width)),
        code,
    )
    arrived = lax.all_to_all(slots, ("chips", "core"), 0, 0, tiled=True)
    own = pl.pallas_call(
        own_sum_kernel,
        out_shape=shape((2, own_rows, 128), F32),
        in_specs=[vmem] * 2,
        out_specs=vmem,
        scratch_shapes=[pltpu.VMEM((4 * own_rows, 128), F32), pltpu.VMEM((6, 8, 128), F32)],
        compiler_params=params(),
        cost_estimate=small_cost(),
        name="own_sums",
    )(code, voltage)
    return pl.pallas_call(
        finish_kernel,
        out_shape=shape((2, mesh_dev), F32),
        in_specs=[smem] + [vmem] * 6,
        out_specs=vmem,
        compiler_params=params(),
        name="finish",
    )(
        place_word,
        own,
        arrived.reshape(chips, 2, 2, 128),
        same,
        other,
        port_near,
        port_coupling,
    )


def solution(mesh):
    groups, peers = mesh.devices.shape
    split_mesh = jax.sharding.Mesh(
        mesh.devices.reshape(groups, peers // 2, 2), ("groups", "chips", "core")
    )
    in_specs = (
        P(None, SPREAD),
        P(None, SPREAD),
        P(None, SPREAD),
        P(SPREAD, None),
        P(SPREAD),
        P(SPREAD, None, None, None),
        P(SPREAD, None),
        P(SPREAD, None, None),
        P(SPREAD, None, None, None),
        P(SPREAD, None, None),
        P(SPREAD, None),
        P("groups"),
        P(),
    )
    out_specs = P(None, SPREAD)
    return jax.shard_map(
        per_device, mesh=split_mesh, in_specs=in_specs, out_specs=out_specs, check_vma=False
    )
```

```python
import functools

import jax
import jax.numpy as jnp
from jax import lax
from jax.experimental import pallas as pl
from jax.experimental.pallas import tpu as pltpu
from jax.sharding import PartitionSpec as P

F32 = jnp.float32
BF16 = jnp.bfloat16
SPREAD = ("groups", "chips", "core")
VMEM_LIMIT = 24 * 1024 * 1024
NT = (((1,), (1,)), ((), ()))


def params():
    return pltpu.CompilerParams(vmem_limit_bytes=VMEM_LIMIT)


def small_cost():
    return pl.CostEstimate(flops=10**9, bytes_accessed=8 * 10**6, transcendentals=0)


def lane_pick(row, lanes):
    spread = jnp.broadcast_to(row, lanes.shape)
    return jnp.take_along_axis(spread, lanes, axis=1, mode="promise_in_bounds")


def dot_nt(left, right, precision=None):
    return lax.dot_general(
        left, right, NT, preferred_element_type=F32, precision=precision
    )


def device_index():
    return 2 * lax.axis_index("chips") + lax.axis_index("core")


def fetch(copies):
    for copy in copies:
        copy.start()
    for copy in copies:
        copy.wait()


def pack_kernel(
    mesh_hbm, need_hbm, port_hbm, out_ref, mesh_ref, need_ref, port_ref, sems
):
    rows = mesh_ref.shape[1] // 128
    ports = port_ref.shape[1]
    chips = out_ref.shape[0]
    fetch(
        [
            pltpu.make_async_copy(source, target, sems.at[i])
            for i, (source, target) in enumerate(
                [(mesh_hbm, mesh_ref), (need_hbm, need_ref), (port_hbm, port_ref)]
            )
        ]
    )
    port = port_ref[...] - device_index() * (rows * 128)
    port = jnp.where((port >= 0) & (port < rows * 128), port, -1)
    port = jnp.broadcast_to(jnp.concatenate([port, port], axis=1), (8, 128))
    port_high, port_low = port >> 7, port & 127
    port_value = jnp.zeros((8, 128), F32)
    lane = lax.broadcasted_iota(jnp.int32, (8, 128), 1)
    for r in range(rows):
        real_row = mesh_ref[0:1, r * 128 : (r + 1) * 128]
        imag_row = mesh_ref[1:2, r * 128 : (r + 1) * 128]
        both = jnp.where(
            lane < ports, lane_pick(real_row, port_low), lane_pick(imag_row, port_low)
        )
        port_value = jnp.where(port_high == r, both, port_value)
        for chip in range(chips):
            out_ref[chip, r : r + 1, :] = real_row
            out_ref[chip, rows + r : rows + r + 1, :] = imag_row
    need = [need_ref[pl.ds(c, chips, 2), :].astype(F32) for c in range(2)]
    first = lax.axis_index("core") == 0
    out_ref[:, 2 * rows, :] = jnp.where(first, need[0], need[1])
    out_ref[:, 2 * rows + 1, :] = jnp.where(first, need[1], need[0])
    out_ref[:, 2 * rows + 2, :] = jnp.broadcast_to(port_value[0:1], (chips, 128))
    for r in range(2 * rows + 3, out_ref.shape[1]):
        out_ref[:, r, :] = jnp.zeros((chips, 128), F32)


def ask(need_ref, pack_ref, table_ref, core, rows):
    chips = pack_ref.shape[0]
    sub = lax.broadcasted_iota(jnp.int32, (rows, 128), 0)
    for chip in range(chips):
        wanted = need_ref[pl.ds(2 * chip + core, 1), :]
        wanted = jnp.broadcast_to(jnp.maximum(wanted, 0), (rows, 128))
        here = (wanted >> 7) == sub
        low = wanted & 127
        for c in range(2):
            block = pack_ref[chip, c * rows : (c + 1) * rows, :]
            picked = jnp.take_along_axis(block, low, axis=1, mode="promise_in_bounds")
            picked = jnp.where(here, picked, 0.0)
            table_ref[c, chip : chip + 1, :] = jnp.sum(picked, axis=0, keepdims=True)


def lookup(code_ref, start, tables):
    total = [None, None]
    for k in range(2):
        code = code_ref[k, pl.ds(start, 8), :]
        high, low = code >> 8, (code >> 1) & 127
        value = [jnp.zeros((8, 128), F32), jnp.zeros((8, 128), F32)]
        for first, step, count, row_of in tables:
            offset = high - first
            for r in range(count):
                here = offset == r * step
                for c in range(2):
                    value[c] = jnp.where(here, lane_pick(row_of(r, c), low), value[c])
        along = (code & 1) == 1
        for c in range(2):
            signed = jnp.where(along, value[c], -value[c])
            total[c] = signed if k == 0 else total[c] + signed
    return total


def own_lookup_kernel(mesh_ref, code_ref, out_ref):
    rows = mesh_ref.shape[1] // 128

    def own_row(r, c):
        return mesh_ref[c : c + 1, r * 128 : (r + 1) * 128]

    def block(g, carry):
        start = pl.multiple_of(g * 8, 8)
        total = lookup(code_ref, start, [(0, 1, rows, own_row)])
        out_ref[0, pl.ds(start, 8), :] = total[0]
        out_ref[1, pl.ds(start, 8), :] = total[1]
        return carry

    lax.fori_loop(0, code_ref.shape[1] // 8, block, 0)


def add_peers(part_ref, pack_ref, need_ref, code_ref, table_ref, out_ref, core, first):
    chips = pack_ref.shape[0]
    ask(need_ref, pack_ref, table_ref, core, first)

    def peer_row(r, c):
        return table_ref[c, r : r + 1, :]

    def block(g, carry):
        start = pl.multiple_of(g * 8, 8)
        total = lookup(code_ref, start, [(first + core, 2, chips, peer_row)])
        for c in range(2):
            out_ref[c, pl.ds(start, 8), :] = total[c] + part_ref[c, pl.ds(start, 8), :]
        return carry

    lax.fori_loop(0, code_ref.shape[1] // 8, block, 0)


def same_core_kernel(
    part_ref, same_ref, need_ref, code_ref, out_ref, table_ref, *, first
):
    add_peers(
        part_ref, same_ref, need_ref, code_ref, table_ref, out_ref,
        lax.axis_index("core"), first,
    )


def current_kernel(
    part_ref, other_ref, need_ref, code_ref, basis_hbm, current_ref, coeff_ref,
    table_ref, basis_ref, sem, *, first,
):
    tiles = code_ref.shape[1]
    rank = basis_ref.shape[0] // tiles
    copy = pltpu.make_async_copy(basis_hbm, basis_ref, sem.at[0])
    copy.start()
    add_peers(
        part_ref, other_ref, need_ref, code_ref, table_ref, current_ref,
        1 - lax.axis_index("core"), first,
    )
    copy.wait()
    inputs = jnp.concatenate([current_ref[0], current_ref[1]], axis=0)
    inputs = inputs.T.astype(BF16)
    lane_tile = lax.broadcasted_iota(jnp.int32, (rank, 2 * tiles), 1) % tiles
    full = jnp.dot(basis_ref[...], inputs, preferred_element_type=F32)
    chosen = jnp.zeros((rank, 2 * tiles), F32)
    for t in range(tiles):
        chosen = jnp.where(lane_tile == t, full[t * rank : (t + 1) * rank], chosen)
    coeff = chosen.astype(BF16)
    for p in range(coeff_ref.shape[0]):
        coeff_ref[p] = coeff


def pair_kernel(coupling_hbm, out_ref, raw_ref, sems):
    far_count, rank = coupling_hbm.shape[:2]
    half = rank // 2
    depth = 4
    copies = [
        pltpu.make_async_copy(coupling_hbm.at[k], raw_ref.at[k], sems.at[k])
        for k in range(far_count)
    ]
    for k in range(depth):
        copies[k].start()
    for k in range(far_count):
        copies[k].wait()
        if k + depth < far_count:
            copies[k + depth].start()
        for r in range(half):
            out_ref[k, r] = jnp.concatenate([raw_ref[k, r], raw_ref[k, half + r]], axis=1)


def near_kernel(source_ref, current_ref, blocks_hbm, out_ref, inputs_ref, blocks_ref, sems):
    tiles, count, width, _ = blocks_ref.shape
    step, depth = 4, 4
    copies = [
        pltpu.make_async_copy(
            blocks_hbm.at[pl.ds(g * step, step)], blocks_ref.at[pl.ds(g * step, step)], sems.at[g]
        )
        for g in range(tiles // step)
    ]
    for g in range(depth):
        copies[g].start()
    lane_tile = lax.broadcasted_iota(jnp.int32, (width, 128), 1) % tiles
    rows = jnp.concatenate([current_ref[0], current_ref[1]], axis=0)
    columns = rows.T.astype(BF16)
    row_index = lax.broadcasted_iota(jnp.int32, (128, 128), 0)
    for k in range(count):
        picks = jnp.where(row_index == source_ref[k : k + 1, :], 1.0, 0.0).astype(BF16)
        inputs_ref[k * width : (k + 1) * width, :] = jnp.dot(
            columns, picks, preferred_element_type=F32
        ).astype(BF16)
    inputs = inputs_ref[...]
    total = jnp.zeros((width, 128), F32)
    for g in range(tiles // step):
        copies[g].wait()
        if g + depth < tiles // step:
            copies[g + depth].start()
        block = jnp.concatenate(
            [
                blocks_ref[g * step : (g + 1) * step, k].reshape(step * width, width)
                for k in range(count)
            ],
            axis=1,
        )
        full = jnp.dot(block, inputs, preferred_element_type=F32)
        for i in range(step):
            total = jnp.where(
                lane_tile == g * step + i, full[i * width : (i + 1) * width], total
            )
    rows = total.T
    out_ref[0] = rows[:tiles]
    out_ref[1] = rows[tiles:]


def split(value):
    top = value.astype(BF16)
    return top, (value - top.astype(F32)).astype(BF16)


def counts(rows):
    return lax.broadcasted_iota(jnp.int32, (rows, 128), 0).astype(F32)


def place(high, low, values, rows, spread_ref):
    sub_high, sub_low = counts(rows).astype(BF16), counts(128).astype(BF16)
    one, zero = jnp.ones((128, 128), BF16), jnp.zeros((128, 128), BF16)
    spread_ref[0] = high.astype(F32)
    spread_ref[1] = low.astype(F32)
    for c, value in enumerate(values):
        top, rest = split(value)
        spread_ref[2 + 2 * c] = top.astype(F32)
        spread_ref[3 + 2 * c] = rest.astype(F32)

    def spread(j, i, count):
        return jnp.broadcast_to(spread_ref[j, i : i + 1, :], (count, 128)).astype(BF16)

    left, right = [], []
    for i in range(8):
        here = spread(0, i, rows) == sub_high
        left.append(
            jnp.concatenate(
                [jnp.where(here, spread(j, i, rows), zero[:rows]) for j in range(2, 6)], axis=0
            )
        )
        right.append(jnp.where(spread(1, i, 128) == sub_low, one, zero))
    return jnp.concatenate(left, axis=1), jnp.concatenate(right, axis=1)


def place_few(high, low, values, rows):
    sub_high = lax.broadcasted_iota(jnp.int32, (rows, 128), 0)
    sub_low = lax.broadcasted_iota(jnp.int32, (128, 128), 0)
    left, right = [], []
    for i in range(high.shape[0]):
        here = jnp.broadcast_to(high[i : i + 1], (rows, 128)) == sub_high
        parts = []
        for value in values:
            spread = jnp.where(here, jnp.broadcast_to(value[i : i + 1], (rows, 128)), 0.0)
            parts.extend(split(spread))
        left.append(jnp.concatenate(parts, axis=0))
        there = jnp.broadcast_to(low[i : i + 1], (128, 128)) == sub_low
        right.append(jnp.where(there, 1.0, 0.0).astype(BF16))
    return jnp.concatenate(left, axis=1), jnp.concatenate(right, axis=1)


def scatter(code_ref, voltage_ref, total_ref, spread_ref, first, rows, low_streams):
    total_ref[...] = jnp.zeros_like(total_ref)

    def block(g, carry):
        start = pl.multiple_of(g * 8, 8)
        for k in range(2):
            code = code_ref[k, pl.ds(start, 8), :]
            along = (code & 1) == 1
            values = []
            for c in range(2):
                voltage = voltage_ref[c, pl.ds(start, 8), :]
                values.append(jnp.where(along, voltage, -voltage))
            left, right = place(
                (code >> 8) - first, (code >> 1) & 127, values, rows, spread_ref.at[k]
            )
            total_ref[...] += dot_nt(right, left) if low_streams else dot_nt(left, right)
        return carry

    lax.fori_loop(0, code_ref.shape[1] // 8, block, 0)
    total = total_ref[...].T if low_streams else total_ref[...]
    return [
        total[2 * c * rows : (2 * c + 1) * rows] + total[(2 * c + 1) * rows : (2 * c + 2) * rows]
        for c in range(2)
    ]


def voltage_kernel(
    coeff_ref, target_ref, coupling_ref, basis_ref, near_ref, current_ref, resistance_ref,
    code_ref, voltage_ref, slot_ref, picked_ref, mixed_ref, total_ref, spread_ref, *, first,
):
    peers, rank, lanes = coeff_ref.shape
    far_count = coupling_ref.shape[0]
    tiles = lanes // 2
    half = rank // 2
    groups = half // 4
    device = device_index()
    spans = target_ref.shape[0] // far_count
    stride = peers // far_count
    for k in range(far_count):
        picked = [jnp.zeros((rank, lanes), F32), jnp.zeros((rank, lanes), F32)]
        for i in range(spans):
            row = k * spans + i
            block = coeff_ref[(device + k * stride + i) % peers].astype(F32)
            target = jnp.broadcast_to(target_ref[row : row + 1, :], (rank, lanes))
            inside = target >= 0
            source = jnp.maximum(target, 0)
            for c in range(2):
                value = jnp.take_along_axis(
                    block, source + c * tiles, axis=1, mode="promise_in_bounds"
                )
                picked[c] = jnp.where(inside, value, picked[c])
        for c in range(2):
            picked_ref[c, k] = picked[c]

    def mix(g, carry):
        total = [[None, None] for _ in range(4)]
        for k in range(far_count):
            picked = [picked_ref[c, k] for c in range(2)]
            for i in range(4):
                block = coupling_ref[k, g * 4 + i].astype(F32)
                for c in range(2):
                    product = block * picked[c]
                    part = product[0:8]
                    for q in range(8, rank, 8):
                        part = part + product[q : q + 8]
                    total[i][c] = part if k == 0 else total[i][c] + part
        for i in range(4):
            for c in range(2):
                row = jnp.sum(total[i][c], axis=0, keepdims=True)
                mixed_ref[pl.ds(c * half + g * 4 + i, 1), :] = row
        return carry

    lax.fori_loop(0, groups, mix, 0)
    mixed = mixed_ref[...].T
    mixed = jnp.concatenate([mixed[:tiles], mixed[tiles:]], axis=1).astype(BF16)
    wide = 8 * rank
    from_row = lax.broadcasted_iota(jnp.int32, (2 * rank, wide), 0)
    to_rank = lax.broadcasted_iota(jnp.int32, (2 * rank, wide), 1) % rank
    repeated = []
    for c in range(2):
        wanted = (to_rank // half) * rank + c * half + to_rank % half
        picks = jnp.where(from_row == wanted, 1.0, 0.0).astype(BF16)
        repeated.append(jnp.dot(mixed, picks, preferred_element_type=F32))
    own_block = (
        lax.broadcasted_iota(jnp.int32, (16, wide), 0) % 8
        == lax.broadcasted_iota(jnp.int32, (16, wide), 1) // rank
    )
    for g in range(tiles // 8):
        rows8 = slice(g * 8, g * 8 + 8)
        both = jnp.concatenate([repeated[0][rows8], repeated[1][rows8]], axis=0)
        both = jnp.where(own_block, both, 0.0).astype(BF16)
        far = jnp.dot(
            both, basis_ref[g * wide : (g + 1) * wide, :], preferred_element_type=F32
        )
        resistance = resistance_ref[rows8, :]
        voltage_ref[0, rows8, :] = resistance * current_ref[0, rows8, :] - (
            near_ref[1, rows8, :] + far[8:16]
        )
        voltage_ref[1, rows8, :] = resistance * current_ref[1, rows8, :] + (
            near_ref[0, rows8, :] + far[0:8]
        )
    sums = scatter(
        code_ref, voltage_ref, total_ref, spread_ref, first, slot_ref.shape[0], True
    )
    for c in range(2):
        slot_ref[:, c, :] = sums[c]


def own_sum_kernel(
    code_ref, voltage_ref, same_ref, other_ref, port_ref, impedance_ref, own_ref, asked_ref,
    picks_ref, total_ref, spread_ref,
):
    rows = own_ref.shape[1]
    ports = impedance_ref.shape[1]
    chips = same_ref.shape[0]
    first_core = lax.axis_index("core") == 0
    same = same_ref[:, 2 * rows, :].astype(jnp.int32)
    other = other_ref[:, 2 * rows + 1, :].astype(jnp.int32)
    asked = [jnp.where(first_core, same, other), jnp.where(first_core, other, same)]
    sub_low = lax.broadcasted_iota(jnp.int32, (128, 128), 0)
    for core in range(2):
        asked_ref[core] = asked[core] >> 7
        low = asked[core] & 127
        for chip in range(chips):
            there = jnp.broadcast_to(low[chip : chip + 1], (128, 128)) == sub_low
            place = core * chips + chip
            picks_ref[:, place * 128 : (place + 1) * 128] = jnp.where(there, 1.0, 0.0).astype(BF16)
    port_current = jnp.sum(
        same_ref[:, 2 * rows + 2, :] + other_ref[:, 2 * rows + 2, :], axis=0, keepdims=True
    )
    real = port_current[:, :ports]
    imag = port_current[:, ports:]
    both = jnp.concatenate([real, imag, jnp.zeros((6, ports), F32)], axis=0)
    by_real = dot_nt(both, impedance_ref[0], lax.Precision.HIGHEST)
    by_imag = dot_nt(both, impedance_ref[1], lax.Precision.HIGHEST)
    pad = jnp.zeros((1, 128 - ports), F32)
    terms = [
        jnp.concatenate([by_real[0:1] - by_imag[1:2], pad], axis=1),
        jnp.concatenate([by_real[1:2] + by_imag[0:1], pad], axis=1),
    ]
    port = port_ref[...] - device_index() * (rows * 128)
    port = jnp.where((port >= 0) & (port < rows * 128), port, -1)
    port = jnp.concatenate([port, jnp.full((1, 128 - ports), -1, jnp.int32)], axis=1)
    left, right = place_few(port >> 7, port & 127, terms, rows)
    total = dot_nt(left, right)
    sums = scatter(code_ref, voltage_ref, total_ref, spread_ref, 0, rows, False)
    for c in range(2):
        own_ref[c] = sums[c] + (
            total[2 * c * rows : (2 * c + 1) * rows] + total[(2 * c + 1) * rows : (2 * c + 2) * rows]
        )


def finish_kernel(own_ref, arrived_ref, asked_ref, picks_ref, out_ref):
    rows = own_ref.shape[1]
    chips = arrived_ref.shape[0]
    sub_high = lax.broadcasted_iota(jnp.int32, (rows, 128), 0)
    left = []
    for core in range(2):
        for chip in range(chips):
            here = jnp.broadcast_to(asked_ref[core, chip : chip + 1, :], (rows, 128)) == sub_high
            parts = []
            for c in range(2):
                value = jnp.broadcast_to(arrived_ref[chip, core, c : c + 1, :], (rows, 128))
                parts.extend(split(jnp.where(here, value, 0.0)))
            left.append(jnp.concatenate(parts, axis=0))
    total = dot_nt(jnp.concatenate(left, axis=1), picks_ref[...])
    for c in range(2):
        summed = own_ref[c] + (
            total[2 * c * rows : (2 * c + 1) * rows] + total[(2 * c + 1) * rows : (2 * c + 2) * rows]
        )
        for r in range(rows):
            out_ref[c : c + 1, r * 128 : (r + 1) * 128] = summed[r : r + 1]


def per_device(
    mesh_current,
    branch_entry,
    branch_sign,
    need_slots,
    resistance,
    near_blocks,
    near_source,
    basis_in,
    coupling,
    basis_out,
    admissible,
    port_mesh,
    port_coupling,
):
    chips = lax.axis_size("chips")
    peers = 2 * chips
    core = lax.axis_index("core")
    device = 2 * lax.axis_index("chips") + core
    mesh_dev = mesh_current.shape[1]
    tiles, near_count, width, _ = near_blocks.shape
    rank = basis_in.shape[1]
    far_count = admissible.shape[1]
    own_rows = mesh_dev // 128
    vmem = pl.BlockSpec(memory_space=pltpu.VMEM)
    shape = jax.ShapeDtypeStruct

    code = (branch_entry * 2 + branch_sign).reshape(2, tiles, width)
    coupling_lanes = jnp.transpose(coupling, (1, 2, 3, 0))
    basis_in_rows = basis_in.reshape(tiles * rank, width)
    basis_out_rows = basis_out.reshape(tiles * rank, width)
    half = jnp.arange(2 * tiles, dtype=jnp.int32) // tiles
    sources = jnp.transpose(near_source)
    sources = jnp.concatenate([sources, sources], axis=1) + half[None] * tiles
    band = peers * tiles // far_count
    spans = band // tiles + 1
    bases = device * tiles + jnp.arange(far_count, dtype=jnp.int32) * band
    shifted = (jnp.transpose(admissible) - bases[:, None]) % (peers * tiles)
    shifted = jnp.concatenate([shifted, shifted], axis=1)[:, None, :]
    shifted = shifted - jnp.arange(spans, dtype=jnp.int32)[None, :, None] * tiles
    inside = (shifted >= 0) & (shifted < tiles)
    targets = jnp.where(inside, shifted, -1).reshape(far_count * spans, 2 * tiles)

    def in_hbm(x):
        return pltpu.with_memory_space_constraint(x, pltpu.HBM)

    hbm = pl.BlockSpec(memory_space=pl.ANY)
    port_row = port_mesh.reshape(1, -1)
    pack_rows = (2 * own_rows + 3 + 7) // 8 * 8
    pack, mesh_near, need_near, port_near = pl.pallas_call(
        pack_kernel,
        out_shape=(
            shape((chips, pack_rows, 128), F32),
            pltpu.VMEM(mesh_current.shape, F32),
            pltpu.VMEM(need_slots.shape, jnp.int32),
            pltpu.VMEM(port_row.shape, jnp.int32),
        ),
        in_specs=[hbm] * 3,
        out_specs=(vmem,) * 4,
        scratch_shapes=[pltpu.SemaphoreType.DMA((3,))],
        compiler_params=params(),
        name="pack",
    )(in_hbm(mesh_current), in_hbm(need_slots), in_hbm(port_row))
    same = lax.all_to_all(pack, "chips", 0, 0, tiled=True)
    own_part = pl.pallas_call(
        own_lookup_kernel,
        out_shape=shape((2, tiles, width), F32),
        in_specs=[vmem] * 2,
        out_specs=vmem,
        compiler_params=params(),
        cost_estimate=small_cost(),
        name="own_lookup",
    )(mesh_near, code)
    pairs = pl.pallas_call(
        pair_kernel,
        out_shape=pltpu.VMEM((far_count, rank // 2, rank, 2 * tiles), BF16),
        in_specs=[hbm],
        out_specs=vmem,
        scratch_shapes=[
            pltpu.VMEM(coupling_lanes.shape, BF16),
            pltpu.SemaphoreType.DMA((far_count,)),
        ],
        compiler_params=params(),
        cost_estimate=small_cost(),
        name="pair_rows",
    )(in_hbm(coupling_lanes))
    other = lax.ppermute(same, "core", [(0, 1), (1, 0)])
    part = pl.pallas_call(
        functools.partial(same_core_kernel, first=own_rows),
        out_shape=shape((2, tiles, width), F32),
        in_specs=[vmem] * 4,
        out_specs=vmem,
        scratch_shapes=[pltpu.VMEM((2, chips, 128), F32)],
        compiler_params=params(),
        cost_estimate=small_cost(),
        name="same_core",
    )(own_part, same, need_near, code)
    current, coeff = pl.pallas_call(
        functools.partial(current_kernel, first=own_rows),
        out_shape=(shape((2, tiles, width), F32), shape((peers, rank, 2 * tiles), BF16)),
        in_specs=[vmem] * 4 + [hbm],
        out_specs=(vmem,) * 2,
        scratch_shapes=[
            pltpu.VMEM((2, chips, 128), F32),
            pltpu.VMEM(basis_in_rows.shape, BF16),
            pltpu.SemaphoreType.DMA((1,)),
        ],
        compiler_params=params(),
        name="currents",
    )(part, other, need_near, code, in_hbm(basis_in_rows))
    all_coeff = lax.all_to_all(coeff, ("chips", "core"), 0, 0, tiled=True)
    near = pl.pallas_call(
        near_kernel,
        out_shape=shape((2, tiles, width), F32),
        in_specs=[vmem] * 2 + [hbm],
        out_specs=vmem,
        scratch_shapes=[
            pltpu.VMEM((near_count * width, 2 * tiles), BF16),
            pltpu.VMEM(near_blocks.shape, BF16),
            pltpu.SemaphoreType.DMA((tiles // 4,)),
        ],
        compiler_params=params(),
        cost_estimate=pl.CostEstimate(
            flops=256 * near_blocks.size, bytes_accessed=2 * near_blocks.size, transcendentals=0
        ),
        name="near_field",
    )(sources, current, in_hbm(near_blocks))
    voltage, slots = pl.pallas_call(
        functools.partial(voltage_kernel, first=own_rows),
        out_shape=(shape((2, tiles, width), F32), shape((peers, 2, 128), F32)),
        in_specs=[vmem] * 8,
        out_specs=(vmem,) * 2,
        scratch_shapes=[
            pltpu.VMEM((2, far_count, rank, 2 * tiles), F32),
            pltpu.VMEM((rank, 2 * tiles), F32),
            pltpu.VMEM((128, 4 * peers), F32),
            pltpu.VMEM((2, 6, 8, 128), F32),
        ],
        compiler_params=params(),
        name="voltages",
    )(
        all_coeff,
        targets,
        pairs,
        basis_out_rows,
        near,
        current,
        resistance.reshape(tiles, width),
        code,
    )
    arrived = lax.all_to_all(slots, ("chips", "core"), 0, 0, tiled=True)
    own, asked, picks = pl.pallas_call(
        own_sum_kernel,
        out_shape=(
            shape((2, own_rows, 128), F32),
            shape((2, chips, 128), jnp.int32),
            shape((128, peers * 128), BF16),
        ),
        in_specs=[vmem] * 6,
        out_specs=(vmem,) * 3,
        scratch_shapes=[
            pltpu.VMEM((4 * own_rows, 128), F32),
            pltpu.VMEM((2, 6, 8, 128), F32),
        ],
        compiler_params=params(),
        cost_estimate=small_cost(),
        name="own_sums",
    )(code, voltage, same, other, port_near, port_coupling)
    return pl.pallas_call(
        finish_kernel,
        out_shape=shape((2, mesh_dev), F32),
        in_specs=[vmem] * 4,
        out_specs=vmem,
        compiler_params=params(),
        name="finish",
    )(own, arrived.reshape(chips, 2, 2, 128), asked, picks)


def solution(mesh):
    groups, peers = mesh.devices.shape
    split_mesh = jax.sharding.Mesh(
        mesh.devices.reshape(groups, peers // 2, 2), ("groups", "chips", "core")
    )
    in_specs = (
        P(None, SPREAD),
        P(None, SPREAD),
        P(None, SPREAD),
        P(SPREAD, None),
        P(SPREAD),
        P(SPREAD, None, None, None),
        P(SPREAD, None),
        P(SPREAD, None, None),
        P(SPREAD, None, None, None),
        P(SPREAD, None, None),
        P(SPREAD, None),
        P("groups"),
        P(),
    )
    out_specs = P(None, SPREAD)
    return jax.shard_map(
        per_device, mesh=split_mesh, in_specs=in_specs, out_specs=out_specs, check_vma=False
    )
```

```python
import functools

import jax
import jax.numpy as jnp
from jax import lax
from jax.experimental import pallas as pl
from jax.experimental.pallas import tpu as pltpu
from jax.sharding import PartitionSpec as P

F32 = jnp.float32
BF16 = jnp.bfloat16
SPREAD = ("groups", "chips", "core")
VMEM_LIMIT = 24 * 1024 * 1024
NT = (((1,), (1,)), ((), ()))


def params():
    return pltpu.CompilerParams(vmem_limit_bytes=VMEM_LIMIT)


def small_cost():
    return pl.CostEstimate(flops=10**9, bytes_accessed=8 * 10**6, transcendentals=0)


def lane_pick(row, lanes):
    spread = jnp.broadcast_to(row, lanes.shape)
    return jnp.take_along_axis(spread, lanes, axis=1, mode="promise_in_bounds")


def dot_nt(left, right, precision=None):
    return lax.dot_general(
        left, right, NT, preferred_element_type=F32, precision=precision
    )


def device_index():
    return 2 * lax.axis_index("chips") + lax.axis_index("core")


def fetch(copies):
    for copy in copies:
        copy.start()
    for copy in copies:
        copy.wait()


def pack_kernel(
    mesh_hbm, need_hbm, port_hbm, out_ref, mesh_ref, need_ref, port_ref, sems
):
    rows = mesh_ref.shape[1] // 128
    ports = port_ref.shape[1]
    chips = out_ref.shape[0]
    fetch(
        [
            pltpu.make_async_copy(source, target, sems.at[i])
            for i, (source, target) in enumerate(
                [(mesh_hbm, mesh_ref), (need_hbm, need_ref), (port_hbm, port_ref)]
            )
        ]
    )
    port = port_ref[...] - device_index() * (rows * 128)
    port = jnp.where((port >= 0) & (port < rows * 128), port, -1)
    port = jnp.broadcast_to(jnp.concatenate([port, port], axis=1), (8, 128))
    port_high, port_low = port >> 7, port & 127
    port_value = jnp.zeros((8, 128), F32)
    lane = lax.broadcasted_iota(jnp.int32, (8, 128), 1)
    for r in range(rows):
        real_row = mesh_ref[0:1, r * 128 : (r + 1) * 128]
        imag_row = mesh_ref[1:2, r * 128 : (r + 1) * 128]
        both = jnp.where(
            lane < ports, lane_pick(real_row, port_low), lane_pick(imag_row, port_low)
        )
        port_value = jnp.where(port_high == r, both, port_value)
        for chip in range(chips):
            out_ref[chip, r : r + 1, :] = real_row
            out_ref[chip, rows + r : rows + r + 1, :] = imag_row
    need = [need_ref[pl.ds(c, chips, 2), :].astype(F32) for c in range(2)]
    first = lax.axis_index("core") == 0
    out_ref[:, 2 * rows, :] = jnp.where(first, need[0], need[1])
    out_ref[:, 2 * rows + 1, :] = jnp.where(first, need[1], need[0])
    out_ref[:, 2 * rows + 2, :] = jnp.broadcast_to(port_value[0:1], (chips, 128))
    for r in range(2 * rows + 3, out_ref.shape[1]):
        out_ref[:, r, :] = jnp.zeros((chips, 128), F32)


def ask(need_ref, pack_ref, table_ref, core, rows):
    chips = pack_ref.shape[0]
    sub = lax.broadcasted_iota(jnp.int32, (rows, 128), 0)
    for chip in range(chips):
        wanted = need_ref[pl.ds(2 * chip + core, 1), :]
        wanted = jnp.broadcast_to(jnp.maximum(wanted, 0), (rows, 128))
        here = (wanted >> 7) == sub
        low = wanted & 127
        for c in range(2):
            block = pack_ref[chip, c * rows : (c + 1) * rows, :]
            picked = jnp.take_along_axis(block, low, axis=1, mode="promise_in_bounds")
            picked = jnp.where(here, picked, 0.0)
            table_ref[c, chip : chip + 1, :] = jnp.sum(picked, axis=0, keepdims=True)


def lookup(code_ref, start, tables):
    total = [None, None]
    for k in range(2):
        code = code_ref[k, pl.ds(start, 8), :]
        high, low = code >> 8, (code >> 1) & 127
        value = [jnp.zeros((8, 128), F32), jnp.zeros((8, 128), F32)]
        for first, step, count, row_of in tables:
            offset = high - first
            for r in range(count):
                here = offset == r * step
                for c in range(2):
                    value[c] = jnp.where(here, lane_pick(row_of(r, c), low), value[c])
        along = (code & 1) == 1
        for c in range(2):
            signed = jnp.where(along, value[c], -value[c])
            total[c] = signed if k == 0 else total[c] + signed
    return total


def own_lookup_kernel(mesh_ref, code_ref, coupling_hbm, out_ref, pair_ref, raw_ref, sems):
    rows = mesh_ref.shape[1] // 128
    far_count, rank = coupling_hbm.shape[:2]
    half = rank // 2
    copies = [
        pltpu.make_async_copy(coupling_hbm.at[k], raw_ref.at[k], sems.at[k])
        for k in range(far_count)
    ]
    for k, copy in enumerate(copies):
        copy.start(priority=k % 2)

    def own_row(r, c):
        return mesh_ref[c : c + 1, r * 128 : (r + 1) * 128]

    def block(g, carry):
        start = pl.multiple_of(g * 8, 8)
        total = lookup(code_ref, start, [(0, 1, rows, own_row)])
        out_ref[0, pl.ds(start, 8), :] = total[0]
        out_ref[1, pl.ds(start, 8), :] = total[1]
        return carry

    lax.fori_loop(0, code_ref.shape[1] // 8, block, 0)
    for k in range(far_count):
        copies[k].wait()
        for r in range(half):
            pair_ref[k, r] = jnp.concatenate([raw_ref[k, r], raw_ref[k, half + r]], axis=1)


def add_peers(part_ref, pack_ref, need_ref, code_ref, table_ref, out_ref, core, first):
    chips = pack_ref.shape[0]
    ask(need_ref, pack_ref, table_ref, core, first)

    def peer_row(r, c):
        return table_ref[c, r : r + 1, :]

    def block(g, carry):
        start = pl.multiple_of(g * 8, 8)
        total = lookup(code_ref, start, [(first + core, 2, chips, peer_row)])
        for c in range(2):
            out_ref[c, pl.ds(start, 8), :] = total[c] + part_ref[c, pl.ds(start, 8), :]
        return carry

    lax.fori_loop(0, code_ref.shape[1] // 8, block, 0)


def same_core_kernel(
    part_ref, same_ref, need_ref, code_ref, out_ref, rows_ref, table_ref, *, first
):
    rows_ref[0] = same_ref[:, 2 * first, :]
    rows_ref[1] = same_ref[:, 2 * first + 2, :]
    add_peers(
        part_ref, same_ref, need_ref, code_ref, table_ref, out_ref,
        lax.axis_index("core"), first,
    )


def current_kernel(
    part_ref, other_ref, need_ref, code_ref, basis_hbm, current_ref, coeff_ref, rows_ref,
    table_ref, basis_ref, sem, *, first,
):
    tiles = code_ref.shape[1]
    rank = basis_ref.shape[0] // tiles
    copy = pltpu.make_async_copy(basis_hbm, basis_ref, sem.at[0])
    copy.start()
    rows_ref[0] = other_ref[:, 2 * first + 1, :]
    rows_ref[1] = other_ref[:, 2 * first + 2, :]
    add_peers(
        part_ref, other_ref, need_ref, code_ref, table_ref, current_ref,
        1 - lax.axis_index("core"), first,
    )
    copy.wait()
    inputs = jnp.concatenate([current_ref[0], current_ref[1]], axis=0)
    inputs = inputs.T.astype(BF16)
    lane_tile = lax.broadcasted_iota(jnp.int32, (rank, 2 * tiles), 1) % tiles
    full = jnp.dot(basis_ref[...], inputs, preferred_element_type=F32)
    chosen = jnp.zeros((rank, 2 * tiles), F32)
    for t in range(tiles):
        chosen = jnp.where(lane_tile == t, full[t * rank : (t + 1) * rank], chosen)
    coeff = chosen.astype(BF16)
    for p in range(coeff_ref.shape[0]):
        coeff_ref[p] = coeff


def near_kernel(source_ref, current_ref, blocks_hbm, out_ref, inputs_ref, blocks_ref, sems):
    tiles, count, width, _ = blocks_ref.shape
    step = 8
    copies = [
        pltpu.make_async_copy(
            blocks_hbm.at[pl.ds(g * 4, 4)], blocks_ref.at[pl.ds(g * 4, 4)], sems.at[g]
        )
        for g in range(tiles // 4)
    ]
    for g, copy in enumerate(copies):
        copy.start(priority=g % 2)
    lane_tile = lax.broadcasted_iota(jnp.int32, (width, 128), 1) % tiles
    rows = jnp.concatenate([current_ref[0], current_ref[1]], axis=0)
    columns = rows.T.astype(BF16)
    row_index = lax.broadcasted_iota(jnp.int32, (128, 128), 0)
    for k in range(count):
        picks = jnp.where(row_index == source_ref[k : k + 1, :], 1.0, 0.0).astype(BF16)
        inputs_ref[k * width : (k + 1) * width, :] = jnp.dot(
            columns, picks, preferred_element_type=F32
        ).astype(BF16)
    inputs = inputs_ref[...]
    total = jnp.zeros((width, 128), F32)
    for g in range(tiles // step):
        copies[2 * g].wait()
        copies[2 * g + 1].wait()
        block = jnp.concatenate(
            [
                blocks_ref[g * step : (g + 1) * step, k].reshape(step * width, width)
                for k in range(count)
            ],
            axis=1,
        )
        full = jnp.dot(block, inputs, preferred_element_type=F32)
        for i in range(step):
            total = jnp.where(
                lane_tile == g * step + i, full[i * width : (i + 1) * width], total
            )
    rows = total.T
    out_ref[0] = rows[:tiles]
    out_ref[1] = rows[tiles:]


def split(value):
    top = value.astype(BF16)
    return top, (value - top.astype(F32)).astype(BF16)


def counts(rows):
    return lax.broadcasted_iota(jnp.int32, (rows, 128), 0).astype(F32)


def place(high, low, values, rows, spread_ref):
    sub_high, sub_low = counts(rows).astype(BF16), counts(128).astype(BF16)
    one, zero = jnp.ones((128, 128), BF16), jnp.zeros((128, 128), BF16)
    spread_ref[0] = high.astype(F32)
    spread_ref[1] = low.astype(F32)
    for c, value in enumerate(values):
        top, rest = split(value)
        spread_ref[2 + 2 * c] = top.astype(F32)
        spread_ref[3 + 2 * c] = rest.astype(F32)

    def spread(j, i, count):
        return jnp.broadcast_to(spread_ref[j, i : i + 1, :], (count, 128)).astype(BF16)

    left, right = [], []
    for i in range(8):
        here = spread(0, i, rows) == sub_high
        left.append(
            jnp.concatenate(
                [jnp.where(here, spread(j, i, rows), zero[:rows]) for j in range(2, 6)], axis=0
            )
        )
        right.append(jnp.where(spread(1, i, 128) == sub_low, one, zero))
    return jnp.concatenate(left, axis=1), jnp.concatenate(right, axis=1)


def place_few(high, low, values, rows):
    sub_high = lax.broadcasted_iota(jnp.int32, (rows, 128), 0)
    sub_low = lax.broadcasted_iota(jnp.int32, (128, 128), 0)
    left, right = [], []
    for i in range(high.shape[0]):
        here = jnp.broadcast_to(high[i : i + 1], (rows, 128)) == sub_high
        parts = []
        for value in values:
            spread = jnp.where(here, jnp.broadcast_to(value[i : i + 1], (rows, 128)), 0.0)
            parts.extend(split(spread))
        left.append(jnp.concatenate(parts, axis=0))
        there = jnp.broadcast_to(low[i : i + 1], (128, 128)) == sub_low
        right.append(jnp.where(there, 1.0, 0.0).astype(BF16))
    return jnp.concatenate(left, axis=1), jnp.concatenate(right, axis=1)


def scatter(code_ref, voltage_ref, total_ref, spread_ref, first, rows, low_streams):
    total_ref[...] = jnp.zeros_like(total_ref)

    def block(g, carry):
        start = pl.multiple_of(g * 8, 8)
        for k in range(2):
            code = code_ref[k, pl.ds(start, 8), :]
            along = (code & 1) == 1
            values = []
            for c in range(2):
                voltage = voltage_ref[c, pl.ds(start, 8), :]
                values.append(jnp.where(along, voltage, -voltage))
            left, right = place(
                (code >> 8) - first, (code >> 1) & 127, values, rows, spread_ref.at[k]
            )
            total_ref[...] += dot_nt(right, left) if low_streams else dot_nt(left, right)
        return carry

    lax.fori_loop(0, code_ref.shape[1] // 8, block, 0)
    total = total_ref[...].T if low_streams else total_ref[...]
    return [
        total[2 * c * rows : (2 * c + 1) * rows] + total[(2 * c + 1) * rows : (2 * c + 2) * rows]
        for c in range(2)
    ]


def voltage_kernel(
    coeff_ref, target_ref, coupling_ref, basis_hbm, near_ref, current_ref, resistance_hbm,
    code_ref, voltage_ref, slot_ref, picked_ref, mixed_ref, total_ref, spread_ref,
    basis_ref, resistance_ref, sems, *, first,
):
    late_copies = [
        pltpu.make_async_copy(basis_hbm, basis_ref, sems.at[0]),
        pltpu.make_async_copy(resistance_hbm, resistance_ref, sems.at[1]),
    ]
    for i, copy in enumerate(late_copies):
        copy.start(priority=i)
    peers, rank, lanes = coeff_ref.shape
    far_count = coupling_ref.shape[0]
    tiles = lanes // 2
    half = rank // 2
    groups = half // 4
    device = device_index()
    spans = target_ref.shape[0] // far_count
    stride = peers // far_count
    for k in range(far_count):
        picked = [jnp.zeros((rank, lanes), F32), jnp.zeros((rank, lanes), F32)]
        for i in range(spans):
            row = k * spans + i
            block = coeff_ref[(device + k * stride + i) % peers].astype(F32)
            target = jnp.broadcast_to(target_ref[row : row + 1, :], (rank, lanes))
            inside = target >= 0
            source = jnp.maximum(target, 0)
            for c in range(2):
                value = jnp.take_along_axis(
                    block, source + c * tiles, axis=1, mode="promise_in_bounds"
                )
                picked[c] = jnp.where(inside, value, picked[c])
        for c in range(2):
            picked_ref[c, k] = picked[c]

    def mix(g, carry):
        total = [[None, None] for _ in range(4)]
        for k in range(far_count):
            picked = [picked_ref[c, k] for c in range(2)]
            for i in range(4):
                block = coupling_ref[k, g * 4 + i].astype(F32)
                for c in range(2):
                    product = block * picked[c]
                    part = product[0:8]
                    for q in range(8, rank, 8):
                        part = part + product[q : q + 8]
                    total[i][c] = part if k == 0 else total[i][c] + part
        for i in range(4):
            for c in range(2):
                row = jnp.sum(total[i][c], axis=0, keepdims=True)
                mixed_ref[pl.ds(c * half + g * 4 + i, 1), :] = row
        return carry

    lax.fori_loop(0, groups, mix, 0)
    mixed = mixed_ref[...].T
    mixed = jnp.concatenate([mixed[:tiles], mixed[tiles:]], axis=1).astype(BF16)
    wide = 8 * rank
    from_row = lax.broadcasted_iota(jnp.int32, (2 * rank, wide), 0)
    to_rank = lax.broadcasted_iota(jnp.int32, (2 * rank, wide), 1) % rank
    repeated = []
    for c in range(2):
        wanted = (to_rank // half) * rank + c * half + to_rank % half
        picks = jnp.where(from_row == wanted, 1.0, 0.0).astype(BF16)
        repeated.append(jnp.dot(mixed, picks, preferred_element_type=F32))
    for copy in late_copies:
        copy.wait()
    own_block = (
        lax.broadcasted_iota(jnp.int32, (16, wide), 0) % 8
        == lax.broadcasted_iota(jnp.int32, (16, wide), 1) // rank
    )
    for g in range(tiles // 8):
        rows8 = slice(g * 8, g * 8 + 8)
        both = jnp.concatenate([repeated[0][rows8], repeated[1][rows8]], axis=0)
        both = jnp.where(own_block, both, 0.0).astype(BF16)
        far = jnp.dot(
            both, basis_ref[g * wide : (g + 1) * wide, :], preferred_element_type=F32
        )
        resistance = resistance_ref[rows8, :]
        voltage_ref[0, rows8, :] = resistance * current_ref[0, rows8, :] - (
            near_ref[1, rows8, :] + far[8:16]
        )
        voltage_ref[1, rows8, :] = resistance * current_ref[1, rows8, :] + (
            near_ref[0, rows8, :] + far[0:8]
        )
    sums = scatter(
        code_ref, voltage_ref, total_ref, spread_ref, first, slot_ref.shape[0], True
    )
    for c in range(2):
        slot_ref[:, c, :] = sums[c]


def own_sum_kernel(
    code_ref, voltage_ref, same_ref, other_ref, port_ref, impedance_ref, own_ref, asked_ref,
    picks_ref, total_ref, spread_ref,
):
    rows = own_ref.shape[1]
    ports = impedance_ref.shape[1]
    chips = same_ref.shape[1]
    first_core = lax.axis_index("core") == 0
    same = same_ref[0].astype(jnp.int32)
    other = other_ref[0].astype(jnp.int32)
    asked = [jnp.where(first_core, same, other), jnp.where(first_core, other, same)]
    sub_low = lax.broadcasted_iota(jnp.int32, (128, 128), 0)
    for core in range(2):
        asked_ref[core] = asked[core] >> 7
        low = asked[core] & 127
        for chip in range(chips):
            there = jnp.broadcast_to(low[chip : chip + 1], (128, 128)) == sub_low
            place = core * chips + chip
            picks_ref[:, place * 128 : (place + 1) * 128] = jnp.where(there, 1.0, 0.0).astype(BF16)
    port_current = jnp.sum(same_ref[1] + other_ref[1], axis=0, keepdims=True)
    real = port_current[:, :ports]
    imag = port_current[:, ports:]
    both = jnp.concatenate([real, imag, jnp.zeros((6, ports), F32)], axis=0)
    by_real = dot_nt(both, impedance_ref[0], lax.Precision.HIGHEST)
    by_imag = dot_nt(both, impedance_ref[1], lax.Precision.HIGHEST)
    pad = jnp.zeros((1, 128 - ports), F32)
    terms = [
        jnp.concatenate([by_real[0:1] - by_imag[1:2], pad], axis=1),
        jnp.concatenate([by_real[1:2] + by_imag[0:1], pad], axis=1),
    ]
    port = port_ref[...] - device_index() * (rows * 128)
    port = jnp.where((port >= 0) & (port < rows * 128), port, -1)
    port = jnp.concatenate([port, jnp.full((1, 128 - ports), -1, jnp.int32)], axis=1)
    left, right = place_few(port >> 7, port & 127, terms, rows)
    total = dot_nt(left, right)
    sums = scatter(code_ref, voltage_ref, total_ref, spread_ref, 0, rows, False)
    for c in range(2):
        own_ref[c] = sums[c] + (
            total[2 * c * rows : (2 * c + 1) * rows] + total[(2 * c + 1) * rows : (2 * c + 2) * rows]
        )


def finish_kernel(own_ref, arrived_ref, asked_ref, picks_ref, out_ref):
    rows = own_ref.shape[1]
    chips = arrived_ref.shape[0]
    sub_high = lax.broadcasted_iota(jnp.int32, (rows, 128), 0)
    left = []
    for core in range(2):
        for chip in range(chips):
            here = jnp.broadcast_to(asked_ref[core, chip : chip + 1, :], (rows, 128)) == sub_high
            parts = []
            for c in range(2):
                value = jnp.broadcast_to(arrived_ref[chip, core, c : c + 1, :], (rows, 128))
                parts.extend(split(jnp.where(here, value, 0.0)))
            left.append(jnp.concatenate(parts, axis=0))
    total = dot_nt(jnp.concatenate(left, axis=1), picks_ref[...])
    for c in range(2):
        summed = own_ref[c] + (
            total[2 * c * rows : (2 * c + 1) * rows] + total[(2 * c + 1) * rows : (2 * c + 2) * rows]
        )
        for r in range(rows):
            out_ref[c : c + 1, r * 128 : (r + 1) * 128] = summed[r : r + 1]


def per_device(
    mesh_current,
    branch_entry,
    branch_sign,
    need_slots,
    resistance,
    near_blocks,
    near_source,
    basis_in,
    coupling,
    basis_out,
    admissible,
    port_mesh,
    port_coupling,
):
    chips = lax.axis_size("chips")
    peers = 2 * chips
    core = lax.axis_index("core")
    device = 2 * lax.axis_index("chips") + core
    mesh_dev = mesh_current.shape[1]
    tiles, near_count, width, _ = near_blocks.shape
    rank = basis_in.shape[1]
    far_count = admissible.shape[1]
    own_rows = mesh_dev // 128
    vmem = pl.BlockSpec(memory_space=pltpu.VMEM)
    shape = jax.ShapeDtypeStruct

    code = (branch_entry * 2 + branch_sign).reshape(2, tiles, width)
    coupling_lanes = jnp.transpose(coupling, (1, 2, 3, 0))
    basis_in_rows = basis_in.reshape(tiles * rank, width)
    basis_out_rows = basis_out.reshape(tiles * rank, width)
    half = jnp.arange(2 * tiles, dtype=jnp.int32) // tiles
    sources = jnp.transpose(near_source)
    sources = jnp.concatenate([sources, sources], axis=1) + half[None] * tiles
    band = peers * tiles // far_count
    spans = band // tiles + 1
    bases = device * tiles + jnp.arange(far_count, dtype=jnp.int32) * band
    shifted = (jnp.transpose(admissible) - bases[:, None]) % (peers * tiles)
    shifted = jnp.concatenate([shifted, shifted], axis=1)[:, None, :]
    shifted = shifted - jnp.arange(spans, dtype=jnp.int32)[None, :, None] * tiles
    inside = (shifted >= 0) & (shifted < tiles)
    targets = jnp.where(inside, shifted, -1).reshape(far_count * spans, 2 * tiles)

    def in_hbm(x):
        return pltpu.with_memory_space_constraint(x, pltpu.HBM)

    hbm = pl.BlockSpec(memory_space=pl.ANY)
    port_row = port_mesh.reshape(1, -1)
    pack_rows = (2 * own_rows + 3 + 7) // 8 * 8
    pack, mesh_near, need_near, port_near = pl.pallas_call(
        pack_kernel,
        out_shape=(
            shape((chips, pack_rows, 128), F32),
            pltpu.VMEM(mesh_current.shape, F32),
            pltpu.VMEM(need_slots.shape, jnp.int32),
            pltpu.VMEM(port_row.shape, jnp.int32),
        ),
        in_specs=[hbm] * 3,
        out_specs=(vmem,) * 4,
        scratch_shapes=[pltpu.SemaphoreType.DMA((3,))],
        compiler_params=params(),
        name="pack",
    )(in_hbm(mesh_current), in_hbm(need_slots), in_hbm(port_row))
    same = lax.all_to_all(pack, "chips", 0, 0, tiled=True)
    own_part, pairs = pl.pallas_call(
        own_lookup_kernel,
        out_shape=(
            shape((2, tiles, width), F32),
            pltpu.VMEM((far_count, rank // 2, rank, 2 * tiles), BF16),
        ),
        in_specs=[vmem] * 2 + [hbm],
        out_specs=(vmem,) * 2,
        scratch_shapes=[
            pltpu.VMEM(coupling_lanes.shape, BF16),
            pltpu.SemaphoreType.DMA((far_count,)),
        ],
        compiler_params=params(),
        cost_estimate=small_cost(),
        name="own_lookup",
    )(mesh_near, code, in_hbm(coupling_lanes))
    other = lax.ppermute(same, "core", [(0, 1), (1, 0)])
    part, same_rows = pl.pallas_call(
        functools.partial(same_core_kernel, first=own_rows),
        out_shape=(shape((2, tiles, width), F32), shape((2, chips, 128), F32)),
        in_specs=[vmem] * 4,
        out_specs=(vmem,) * 2,
        scratch_shapes=[pltpu.VMEM((2, chips, 128), F32)],
        compiler_params=params(),
        cost_estimate=small_cost(),
        name="same_core",
    )(own_part, same, need_near, code)
    current, coeff, other_rows = pl.pallas_call(
        functools.partial(current_kernel, first=own_rows),
        out_shape=(
            shape((2, tiles, width), F32),
            shape((peers, rank, 2 * tiles), BF16),
            shape((2, chips, 128), F32),
        ),
        in_specs=[vmem] * 4 + [hbm],
        out_specs=(vmem,) * 3,
        scratch_shapes=[
            pltpu.VMEM((2, chips, 128), F32),
            pltpu.VMEM(basis_in_rows.shape, BF16),
            pltpu.SemaphoreType.DMA((1,)),
        ],
        compiler_params=params(),
        name="currents",
    )(part, other, need_near, code, in_hbm(basis_in_rows))
    all_coeff = lax.all_to_all(coeff, ("chips", "core"), 0, 0, tiled=True)
    near = pl.pallas_call(
        near_kernel,
        out_shape=shape((2, tiles, width), F32),
        in_specs=[vmem] * 2 + [hbm],
        out_specs=vmem,
        scratch_shapes=[
            pltpu.VMEM((near_count * width, 2 * tiles), BF16),
            pltpu.VMEM(near_blocks.shape, BF16),
            pltpu.SemaphoreType.DMA((tiles // 4,)),
        ],
        compiler_params=params(),
        cost_estimate=pl.CostEstimate(
            flops=256 * near_blocks.size, bytes_accessed=2 * near_blocks.size, transcendentals=0
        ),
        name="near_field",
    )(sources, current, in_hbm(near_blocks))
    voltage, slots = pl.pallas_call(
        functools.partial(voltage_kernel, first=own_rows),
        out_shape=(shape((2, tiles, width), F32), shape((peers, 2, 128), F32)),
        in_specs=[vmem] * 3 + [hbm] + [vmem] * 2 + [hbm, vmem],
        out_specs=(vmem,) * 2,
        scratch_shapes=[
            pltpu.VMEM((2, far_count, rank, 2 * tiles), F32),
            pltpu.VMEM((rank, 2 * tiles), F32),
            pltpu.VMEM((128, 4 * peers), F32),
            pltpu.VMEM((2, 6, 8, 128), F32),
            pltpu.VMEM(basis_out_rows.shape, BF16),
            pltpu.VMEM((tiles, width), F32),
            pltpu.SemaphoreType.DMA((2,)),
        ],
        compiler_params=params(),
        name="voltages",
    )(
        all_coeff,
        targets,
        pairs,
        in_hbm(basis_out_rows),
        near,
        current,
        in_hbm(resistance.reshape(tiles, width)),
        code,
    )
    arrived = lax.all_to_all(slots, ("chips", "core"), 0, 0, tiled=True)
    own, asked, picks = pl.pallas_call(
        own_sum_kernel,
        out_shape=(
            shape((2, own_rows, 128), F32),
            shape((2, chips, 128), jnp.int32),
            shape((128, peers * 128), BF16),
        ),
        in_specs=[vmem] * 6,
        out_specs=(vmem,) * 3,
        scratch_shapes=[
            pltpu.VMEM((4 * own_rows, 128), F32),
            pltpu.VMEM((2, 6, 8, 128), F32),
        ],
        compiler_params=params(),
        cost_estimate=small_cost(),
        name="own_sums",
    )(code, voltage, same_rows, other_rows, port_near, port_coupling)
    return pl.pallas_call(
        finish_kernel,
        out_shape=shape((2, mesh_dev), F32),
        in_specs=[vmem] * 4,
        out_specs=vmem,
        compiler_params=params(),
        name="finish",
    )(own, arrived.reshape(chips, 2, 2, 128), asked, picks)


def solution(mesh):
    groups, peers = mesh.devices.shape
    split_mesh = jax.sharding.Mesh(
        mesh.devices.reshape(groups, peers // 2, 2), ("groups", "chips", "core")
    )
    in_specs = (
        P(None, SPREAD),
        P(None, SPREAD),
        P(None, SPREAD),
        P(SPREAD, None),
        P(SPREAD),
        P(SPREAD, None, None, None),
        P(SPREAD, None),
        P(SPREAD, None, None),
        P(SPREAD, None, None, None),
        P(SPREAD, None, None),
        P(SPREAD, None),
        P("groups"),
        P(),
    )
    out_specs = P(None, SPREAD)
    return jax.shard_map(
        per_device, mesh=split_mesh, in_specs=in_specs, out_specs=out_specs, check_vma=False
    )
```

```python
import functools

import jax
import jax.numpy as jnp
from jax import lax
from jax.experimental import pallas as pl
from jax.experimental.pallas import tpu as pltpu
from jax.sharding import PartitionSpec as P

F32 = jnp.float32
BF16 = jnp.bfloat16
SPREAD = ("groups", "chips", "core")
VMEM_LIMIT = 24 * 1024 * 1024
NT = (((1,), (1,)), ((), ()))


def params():
    return pltpu.CompilerParams(vmem_limit_bytes=VMEM_LIMIT)


def small_cost():
    return pl.CostEstimate(flops=10**9, bytes_accessed=8 * 10**6, transcendentals=0)


def lane_pick(row, lanes):
    spread = jnp.broadcast_to(row, lanes.shape)
    return jnp.take_along_axis(spread, lanes, axis=1, mode="promise_in_bounds")


def dot_nt(left, right, precision=None):
    return lax.dot_general(
        left, right, NT, preferred_element_type=F32, precision=precision
    )


def device_index():
    return 2 * lax.axis_index("chips") + lax.axis_index("core")


def fetch(copies):
    for copy in copies:
        copy.start()
    for copy in copies:
        copy.wait()


def pack_kernel(
    mesh_hbm, need_hbm, port_hbm, out_ref, mesh_ref, need_ref, port_ref, sems
):
    rows = mesh_ref.shape[1] // 128
    ports = port_ref.shape[1]
    chips = out_ref.shape[0]
    fetch(
        [
            pltpu.make_async_copy(source, target, sems.at[i])
            for i, (source, target) in enumerate(
                [(mesh_hbm, mesh_ref), (need_hbm, need_ref), (port_hbm, port_ref)]
            )
        ]
    )
    port = port_ref[...] - device_index() * (rows * 128)
    port = jnp.where((port >= 0) & (port < rows * 128), port, -1)
    port = jnp.broadcast_to(jnp.concatenate([port, port], axis=1), (8, 128))
    port_high, port_low = port >> 7, port & 127
    port_value = jnp.zeros((8, 128), F32)
    lane = lax.broadcasted_iota(jnp.int32, (8, 128), 1)
    for r in range(rows):
        real_row = mesh_ref[0:1, r * 128 : (r + 1) * 128]
        imag_row = mesh_ref[1:2, r * 128 : (r + 1) * 128]
        both = jnp.where(
            lane < ports, lane_pick(real_row, port_low), lane_pick(imag_row, port_low)
        )
        port_value = jnp.where(port_high == r, both, port_value)
        for chip in range(chips):
            out_ref[chip, r : r + 1, :] = real_row
            out_ref[chip, rows + r : rows + r + 1, :] = imag_row
    need = [need_ref[pl.ds(c, chips, 2), :].astype(F32) for c in range(2)]
    first = lax.axis_index("core") == 0
    out_ref[:, 2 * rows, :] = jnp.where(first, need[0], need[1])
    out_ref[:, 2 * rows + 1, :] = jnp.where(first, need[1], need[0])
    out_ref[:, 2 * rows + 2, :] = jnp.broadcast_to(port_value[0:1], (chips, 128))
    for r in range(2 * rows + 3, out_ref.shape[1]):
        out_ref[:, r, :] = jnp.zeros((chips, 128), F32)


def ask(need_ref, pack_ref, table_ref, core, rows):
    chips = pack_ref.shape[0]
    sub = lax.broadcasted_iota(jnp.int32, (rows, 128), 0)
    for chip in range(chips):
        wanted = need_ref[pl.ds(2 * chip + core, 1), :]
        wanted = jnp.broadcast_to(jnp.maximum(wanted, 0), (rows, 128))
        here = (wanted >> 7) == sub
        low = wanted & 127
        for c in range(2):
            block = pack_ref[chip, c * rows : (c + 1) * rows, :]
            picked = jnp.take_along_axis(block, low, axis=1, mode="promise_in_bounds")
            picked = jnp.where(here, picked, 0.0)
            table_ref[c, chip : chip + 1, :] = jnp.sum(picked, axis=0, keepdims=True)


def lookup(code_ref, start, tables):
    total = [None, None]
    for k in range(2):
        code = code_ref[k, pl.ds(start, 8), :]
        high, low = code >> 8, (code >> 1) & 127
        value = [jnp.zeros((8, 128), F32), jnp.zeros((8, 128), F32)]
        for first, step, count, row_of in tables:
            offset = high - first
            for r in range(count):
                here = offset == r * step
                for c in range(2):
                    value[c] = jnp.where(here, lane_pick(row_of(r, c), low), value[c])
        along = (code & 1) == 1
        for c in range(2):
            signed = jnp.where(along, value[c], -value[c])
            total[c] = signed if k == 0 else total[c] + signed
    return total


def own_lookup_kernel(mesh_ref, code_ref, coupling_hbm, out_ref, pair_ref, raw_ref, sems):
    rows = mesh_ref.shape[1] // 128
    far_count, rank = coupling_hbm.shape[:2]
    half = rank // 2
    copies = [
        pltpu.make_async_copy(coupling_hbm.at[k], raw_ref.at[k], sems.at[k])
        for k in range(far_count)
    ]
    for k, copy in enumerate(copies):
        copy.start(priority=k % 2)

    def own_row(r, c):
        return mesh_ref[c : c + 1, r * 128 : (r + 1) * 128]

    def block(g, carry):
        start = pl.multiple_of(g * 8, 8)
        total = lookup(code_ref, start, [(0, 1, rows, own_row)])
        out_ref[0, pl.ds(start, 8), :] = total[0]
        out_ref[1, pl.ds(start, 8), :] = total[1]
        return carry

    lax.fori_loop(0, code_ref.shape[1] // 8, block, 0)
    for k in range(far_count):
        copies[k].wait()
        for r in range(half):
            pair_ref[k, r] = jnp.concatenate([raw_ref[k, r], raw_ref[k, half + r]], axis=1)


def add_peers(part_ref, pack_ref, need_ref, code_ref, table_ref, out_ref, core, first):
    chips = pack_ref.shape[0]
    ask(need_ref, pack_ref, table_ref, core, first)

    def peer_row(r, c):
        return table_ref[c, r : r + 1, :]

    def block(g, carry):
        start = pl.multiple_of(g * 8, 8)
        total = lookup(code_ref, start, [(first + core, 2, chips, peer_row)])
        for c in range(2):
            out_ref[c, pl.ds(start, 8), :] = total[c] + part_ref[c, pl.ds(start, 8), :]
        return carry

    lax.fori_loop(0, code_ref.shape[1] // 8, block, 0)


def same_core_kernel(
    part_ref, same_ref, need_ref, code_ref, out_ref, rows_ref, table_ref, *, first
):
    rows_ref[0] = same_ref[:, 2 * first, :]
    rows_ref[1] = same_ref[:, 2 * first + 2, :]
    add_peers(
        part_ref, same_ref, need_ref, code_ref, table_ref, out_ref,
        lax.axis_index("core"), first,
    )


def current_kernel(
    part_ref, other_ref, need_ref, code_ref, basis_hbm, current_ref, coeff_ref, rows_ref,
    table_ref, basis_ref, sem, *, first,
):
    tiles = code_ref.shape[1]
    rank = basis_ref.shape[0] // tiles
    copy = pltpu.make_async_copy(basis_hbm, basis_ref, sem.at[0])
    copy.start()
    rows_ref[0] = other_ref[:, 2 * first + 1, :]
    rows_ref[1] = other_ref[:, 2 * first + 2, :]
    add_peers(
        part_ref, other_ref, need_ref, code_ref, table_ref, current_ref,
        1 - lax.axis_index("core"), first,
    )
    copy.wait()
    inputs = jnp.concatenate([current_ref[0], current_ref[1]], axis=0)
    inputs = inputs.T.astype(BF16)
    lane_tile = lax.broadcasted_iota(jnp.int32, (rank, 2 * tiles), 1) % tiles
    full = jnp.dot(basis_ref[...], inputs, preferred_element_type=F32)
    chosen = jnp.zeros((rank, 2 * tiles), F32)
    for t in range(tiles):
        chosen = jnp.where(lane_tile == t, full[t * rank : (t + 1) * rank], chosen)
    coeff = chosen.astype(BF16)
    for p in range(coeff_ref.shape[0]):
        coeff_ref[p] = coeff


def near_kernel(
    source_ref, current_ref, resistance_hbm, blocks_hbm, out_ref, inputs_ref, blocks_ref,
    resistance_ref, sems,
):
    tiles = current_ref.shape[1]
    width = blocks_ref.shape[1]
    count = blocks_ref.shape[0] // (tiles * width)
    chunks = tiles // 8
    span = 8 * count * width
    copies = [
        pltpu.make_async_copy(
            blocks_hbm.at[pl.ds(g * span, span)], blocks_ref.at[pl.ds(g * span, span)], sems.at[g]
        )
        for g in range(chunks)
    ]
    copies.append(pltpu.make_async_copy(resistance_hbm, resistance_ref, sems.at[chunks]))
    for copy in copies:
        copy.start()
    lane_tile = lax.broadcasted_iota(jnp.int32, (width, 128), 1) % tiles
    rows = jnp.concatenate([current_ref[0], current_ref[1]], axis=0)
    columns = rows.T.astype(BF16)
    row_index = lax.broadcasted_iota(jnp.int32, (128, 128), 0)
    for k in range(count):
        picks = jnp.where(row_index == source_ref[k : k + 1, :], 1.0, 0.0).astype(BF16)
        inputs_ref[k * width : (k + 1) * width, :] = jnp.dot(
            columns, picks, preferred_element_type=F32
        ).astype(BF16)
    inputs = inputs_ref[...]
    total = jnp.zeros((width, 128), F32)
    for g in range(chunks):
        copies[g].wait()
        block = jnp.concatenate(
            [
                jnp.concatenate(
                    [
                        blocks_ref[(t * count + k) * width : (t * count + k + 1) * width, :]
                        for t in range(g * 8, g * 8 + 8)
                    ],
                    axis=0,
                )
                for k in range(count)
            ],
            axis=1,
        )
        full = jnp.dot(block, inputs, preferred_element_type=F32)
        for i in range(8):
            total = jnp.where(
                lane_tile == g * 8 + i, full[i * width : (i + 1) * width], total
            )
    rows = total.T
    copies[chunks].wait()
    resistance = resistance_ref[...]
    out_ref[0] = resistance * current_ref[0] - rows[tiles:]
    out_ref[1] = resistance * current_ref[1] + rows[:tiles]


def split(value):
    top = value.astype(BF16)
    return top, (value - top.astype(F32)).astype(BF16)


def counts(rows):
    return lax.broadcasted_iota(jnp.int32, (rows, 128), 0).astype(F32)


def place(high, low, values, rows, spread_ref):
    sub_high, sub_low = counts(rows).astype(BF16), counts(128).astype(BF16)
    one, zero = jnp.ones((128, 128), BF16), jnp.zeros((128, 128), BF16)
    spread_ref[0] = high.astype(F32)
    spread_ref[1] = low.astype(F32)
    for c, value in enumerate(values):
        top, rest = split(value)
        spread_ref[2 + 2 * c] = top.astype(F32)
        spread_ref[3 + 2 * c] = rest.astype(F32)

    def spread(j, i, count):
        return jnp.broadcast_to(spread_ref[j, i : i + 1, :], (count, 128)).astype(BF16)

    left, right = [], []
    for i in range(8):
        here = spread(0, i, rows) == sub_high
        left.append(
            jnp.concatenate(
                [jnp.where(here, spread(j, i, rows), zero[:rows]) for j in range(2, 6)], axis=0
            )
        )
        right.append(jnp.where(spread(1, i, 128) == sub_low, one, zero))
    return jnp.concatenate(left, axis=1), jnp.concatenate(right, axis=1)


def place_few(high, low, values, rows):
    sub_high = lax.broadcasted_iota(jnp.int32, (rows, 128), 0)
    sub_low = lax.broadcasted_iota(jnp.int32, (128, 128), 0)
    left, right = [], []
    for i in range(high.shape[0]):
        here = jnp.broadcast_to(high[i : i + 1], (rows, 128)) == sub_high
        parts = []
        for value in values:
            spread = jnp.where(here, jnp.broadcast_to(value[i : i + 1], (rows, 128)), 0.0)
            parts.extend(split(spread))
        left.append(jnp.concatenate(parts, axis=0))
        there = jnp.broadcast_to(low[i : i + 1], (128, 128)) == sub_low
        right.append(jnp.where(there, 1.0, 0.0).astype(BF16))
    return jnp.concatenate(left, axis=1), jnp.concatenate(right, axis=1)


def scatter(code_ref, voltage_ref, total_ref, spread_ref, first, rows, low_streams):
    total_ref[...] = jnp.zeros_like(total_ref)

    def block(g, carry):
        start = pl.multiple_of(g * 8, 8)
        for k in range(2):
            code = code_ref[k, pl.ds(start, 8), :]
            along = (code & 1) == 1
            values = []
            for c in range(2):
                voltage = voltage_ref[c, pl.ds(start, 8), :]
                values.append(jnp.where(along, voltage, -voltage))
            left, right = place(
                (code >> 8) - first, (code >> 1) & 127, values, rows, spread_ref.at[k]
            )
            total_ref[...] += dot_nt(right, left) if low_streams else dot_nt(left, right)
        return carry

    lax.fori_loop(0, code_ref.shape[1] // 8, block, 0)
    total = total_ref[...].T if low_streams else total_ref[...]
    return [
        total[2 * c * rows : (2 * c + 1) * rows] + total[(2 * c + 1) * rows : (2 * c + 2) * rows]
        for c in range(2)
    ]


def voltage_kernel(
    coeff_ref, target_ref, coupling_ref, basis_ref, near_ref, code_ref, voltage_ref, slot_ref,
    picked_ref, mixed_ref, total_ref, spread_ref, *, first,
):
    peers, rank, lanes = coeff_ref.shape
    far_count = coupling_ref.shape[0]
    tiles = lanes // 2
    half = rank // 2
    groups = half // 4
    device = device_index()
    spans = target_ref.shape[0] // far_count
    stride = peers // far_count
    for k in range(far_count):
        picked = [jnp.zeros((rank, lanes), F32), jnp.zeros((rank, lanes), F32)]
        for i in range(spans):
            row = k * spans + i
            block = coeff_ref[(device + k * stride + i) % peers].astype(F32)
            target = jnp.broadcast_to(target_ref[row : row + 1, :], (rank, lanes))
            inside = target >= 0
            source = jnp.maximum(target, 0)
            for c in range(2):
                value = jnp.take_along_axis(
                    block, source + c * tiles, axis=1, mode="promise_in_bounds"
                )
                picked[c] = jnp.where(inside, value, picked[c])
        for c in range(2):
            picked_ref[c, k] = picked[c]

    def mix(g, carry):
        total = [[None, None] for _ in range(4)]
        for k in range(far_count):
            picked = [picked_ref[c, k] for c in range(2)]
            for i in range(4):
                block = coupling_ref[k, g * 4 + i].astype(F32)
                for c in range(2):
                    product = block * picked[c]
                    part = product[0:8]
                    for q in range(8, rank, 8):
                        part = part + product[q : q + 8]
                    total[i][c] = part if k == 0 else total[i][c] + part
        for i in range(4):
            for c in range(2):
                row = jnp.sum(total[i][c], axis=0, keepdims=True)
                mixed_ref[pl.ds(c * half + g * 4 + i, 1), :] = row
        return carry

    lax.fori_loop(0, groups, mix, 0)
    mixed = mixed_ref[...].T
    mixed = jnp.concatenate([mixed[:tiles], mixed[tiles:]], axis=1).astype(BF16)
    wide = 8 * rank
    from_row = lax.broadcasted_iota(jnp.int32, (2 * rank, wide), 0)
    to_rank = lax.broadcasted_iota(jnp.int32, (2 * rank, wide), 1) % rank
    repeated = []
    for c in range(2):
        wanted = (to_rank // half) * rank + c * half + to_rank % half
        picks = jnp.where(from_row == wanted, 1.0, 0.0).astype(BF16)
        repeated.append(jnp.dot(mixed, picks, preferred_element_type=F32))
    own_block = (
        lax.broadcasted_iota(jnp.int32, (16, wide), 0) % 8
        == lax.broadcasted_iota(jnp.int32, (16, wide), 1) // rank
    )
    for g in range(tiles // 8):
        rows8 = slice(g * 8, g * 8 + 8)
        both = jnp.concatenate([repeated[0][rows8], repeated[1][rows8]], axis=0)
        both = jnp.where(own_block, both, 0.0).astype(BF16)
        far = jnp.dot(
            both, basis_ref[g * wide : (g + 1) * wide, :], preferred_element_type=F32
        )
        voltage_ref[0, rows8, :] = near_ref[0, rows8, :] - far[8:16]
        voltage_ref[1, rows8, :] = near_ref[1, rows8, :] + far[0:8]
    sums = scatter(
        code_ref, voltage_ref, total_ref, spread_ref, first, slot_ref.shape[0], False
    )
    for c in range(2):
        slot_ref[:, c, :] = sums[c]


def own_sum_kernel(
    code_ref, voltage_ref, same_ref, other_ref, port_ref, impedance_ref, own_ref, asked_ref,
    picks_ref, total_ref, spread_ref,
):
    rows = own_ref.shape[1]
    ports = impedance_ref.shape[1]
    chips = same_ref.shape[1]
    first_core = lax.axis_index("core") == 0
    same = same_ref[0].astype(jnp.int32)
    other = other_ref[0].astype(jnp.int32)
    asked = [jnp.where(first_core, same, other), jnp.where(first_core, other, same)]
    sub_low = lax.broadcasted_iota(jnp.int32, (128, 128), 0)
    for core in range(2):
        asked_ref[core] = asked[core] >> 7
        low = asked[core] & 127
        for chip in range(chips):
            there = jnp.broadcast_to(low[chip : chip + 1], (128, 128)) == sub_low
            place = core * chips + chip
            picks_ref[:, place * 128 : (place + 1) * 128] = jnp.where(there, 1.0, 0.0).astype(BF16)
    port_current = jnp.sum(same_ref[1] + other_ref[1], axis=0, keepdims=True)
    real = port_current[:, :ports]
    imag = port_current[:, ports:]
    both = jnp.concatenate([real, imag, jnp.zeros((6, ports), F32)], axis=0)
    by_real = dot_nt(both, impedance_ref[0], lax.Precision.HIGHEST)
    by_imag = dot_nt(both, impedance_ref[1], lax.Precision.HIGHEST)
    pad = jnp.zeros((1, 128 - ports), F32)
    terms = [
        jnp.concatenate([by_real[0:1] - by_imag[1:2], pad], axis=1),
        jnp.concatenate([by_real[1:2] + by_imag[0:1], pad], axis=1),
    ]
    port = port_ref[...] - device_index() * (rows * 128)
    port = jnp.where((port >= 0) & (port < rows * 128), port, -1)
    port = jnp.concatenate([port, jnp.full((1, 128 - ports), -1, jnp.int32)], axis=1)
    left, right = place_few(port >> 7, port & 127, terms, rows)
    total = dot_nt(left, right)
    sums = scatter(code_ref, voltage_ref, total_ref, spread_ref, 0, rows, False)
    for c in range(2):
        own_ref[c] = sums[c] + (
            total[2 * c * rows : (2 * c + 1) * rows] + total[(2 * c + 1) * rows : (2 * c + 2) * rows]
        )


def finish_kernel(own_ref, arrived_ref, asked_ref, picks_ref, out_ref):
    rows = own_ref.shape[1]
    chips = arrived_ref.shape[0]
    sub_high = lax.broadcasted_iota(jnp.int32, (rows, 128), 0)
    left = []
    for core in range(2):
        for chip in range(chips):
            here = jnp.broadcast_to(asked_ref[core, chip : chip + 1, :], (rows, 128)) == sub_high
            parts = []
            for c in range(2):
                value = jnp.broadcast_to(arrived_ref[chip, core, c : c + 1, :], (rows, 128))
                parts.extend(split(jnp.where(here, value, 0.0)))
            left.append(jnp.concatenate(parts, axis=0))
    total = dot_nt(jnp.concatenate(left, axis=1), picks_ref[...])
    for c in range(2):
        summed = own_ref[c] + (
            total[2 * c * rows : (2 * c + 1) * rows] + total[(2 * c + 1) * rows : (2 * c + 2) * rows]
        )
        for r in range(rows):
            out_ref[c : c + 1, r * 128 : (r + 1) * 128] = summed[r : r + 1]


def per_device(
    mesh_current,
    branch_entry,
    branch_sign,
    need_slots,
    resistance,
    near_blocks,
    near_source,
    basis_in,
    coupling,
    basis_out,
    admissible,
    port_mesh,
    port_coupling,
):
    chips = lax.axis_size("chips")
    peers = 2 * chips
    core = lax.axis_index("core")
    device = 2 * lax.axis_index("chips") + core
    mesh_dev = mesh_current.shape[1]
    tiles, near_count, width, _ = near_blocks.shape
    rank = basis_in.shape[1]
    far_count = admissible.shape[1]
    own_rows = mesh_dev // 128
    vmem = pl.BlockSpec(memory_space=pltpu.VMEM)
    shape = jax.ShapeDtypeStruct

    code = (branch_entry * 2 + branch_sign).reshape(2, tiles, width)
    coupling_lanes = jnp.transpose(coupling, (1, 2, 3, 0))
    basis_in_rows = basis_in.reshape(tiles * rank, width)
    basis_out_rows = basis_out.reshape(tiles * rank, width)
    half = jnp.arange(2 * tiles, dtype=jnp.int32) // tiles
    sources = jnp.transpose(near_source)
    sources = jnp.concatenate([sources, sources], axis=1) + half[None] * tiles
    band = peers * tiles // far_count
    spans = band // tiles + 1
    bases = device * tiles + jnp.arange(far_count, dtype=jnp.int32) * band
    shifted = (jnp.transpose(admissible) - bases[:, None]) % (peers * tiles)
    shifted = jnp.concatenate([shifted, shifted], axis=1)[:, None, :]
    shifted = shifted - jnp.arange(spans, dtype=jnp.int32)[None, :, None] * tiles
    inside = (shifted >= 0) & (shifted < tiles)
    targets = jnp.where(inside, shifted, -1).reshape(far_count * spans, 2 * tiles)

    def in_hbm(x):
        return pltpu.with_memory_space_constraint(x, pltpu.HBM)

    hbm = pl.BlockSpec(memory_space=pl.ANY)
    port_row = port_mesh.reshape(1, -1)
    pack_rows = (2 * own_rows + 3 + 7) // 8 * 8
    pack, mesh_near, need_near, port_near = pl.pallas_call(
        pack_kernel,
        out_shape=(
            shape((chips, pack_rows, 128), F32),
            pltpu.VMEM(mesh_current.shape, F32),
            pltpu.VMEM(need_slots.shape, jnp.int32),
            pltpu.VMEM(port_row.shape, jnp.int32),
        ),
        in_specs=[hbm] * 3,
        out_specs=(vmem,) * 4,
        scratch_shapes=[pltpu.SemaphoreType.DMA((3,))],
        compiler_params=params(),
        name="pack",
    )(in_hbm(mesh_current), in_hbm(need_slots), in_hbm(port_row))
    same = lax.all_to_all(pack, "chips", 0, 0, tiled=True)
    own_part, pairs = pl.pallas_call(
        own_lookup_kernel,
        out_shape=(
            shape((2, tiles, width), F32),
            pltpu.VMEM((far_count, rank // 2, rank, 2 * tiles), BF16),
        ),
        in_specs=[vmem] * 2 + [hbm],
        out_specs=(vmem,) * 2,
        scratch_shapes=[
            pltpu.VMEM(coupling_lanes.shape, BF16),
            pltpu.SemaphoreType.DMA((far_count,)),
        ],
        compiler_params=params(),
        cost_estimate=small_cost(),
        name="own_lookup",
    )(mesh_near, code, in_hbm(coupling_lanes))
    other = lax.ppermute(same, "core", [(0, 1), (1, 0)])
    part, same_rows = pl.pallas_call(
        functools.partial(same_core_kernel, first=own_rows),
        out_shape=(shape((2, tiles, width), F32), shape((2, chips, 128), F32)),
        in_specs=[vmem] * 4,
        out_specs=(vmem,) * 2,
        scratch_shapes=[pltpu.VMEM((2, chips, 128), F32)],
        compiler_params=params(),
        cost_estimate=small_cost(),
        name="same_core",
    )(own_part, same, need_near, code)
    current, coeff, other_rows = pl.pallas_call(
        functools.partial(current_kernel, first=own_rows),
        out_shape=(
            shape((2, tiles, width), F32),
            shape((peers, rank, 2 * tiles), BF16),
            shape((2, chips, 128), F32),
        ),
        in_specs=[vmem] * 4 + [hbm],
        out_specs=(vmem,) * 3,
        scratch_shapes=[
            pltpu.VMEM((2, chips, 128), F32),
            pltpu.VMEM(basis_in_rows.shape, BF16),
            pltpu.SemaphoreType.DMA((1,)),
        ],
        compiler_params=params(),
        name="currents",
    )(part, other, need_near, code, in_hbm(basis_in_rows))
    all_coeff = lax.all_to_all(coeff, ("chips", "core"), 0, 0, tiled=True)
    near_rows = near_blocks.reshape(tiles * near_count * width, width)
    near = pl.pallas_call(
        near_kernel,
        out_shape=shape((2, tiles, width), F32),
        in_specs=[vmem] * 2 + [hbm] * 2,
        out_specs=vmem,
        scratch_shapes=[
            pltpu.VMEM((near_count * width, 2 * tiles), BF16),
            pltpu.VMEM(near_rows.shape, BF16),
            pltpu.VMEM((tiles, width), F32),
            pltpu.SemaphoreType.DMA((tiles // 8 + 1,)),
        ],
        compiler_params=params(),
        cost_estimate=pl.CostEstimate(
            flops=256 * near_blocks.size, bytes_accessed=2 * near_blocks.size, transcendentals=0
        ),
        name="near_field",
    )(sources, current, in_hbm(resistance.reshape(tiles, width)), in_hbm(near_rows))
    voltage, slots = pl.pallas_call(
        functools.partial(voltage_kernel, first=own_rows),
        out_shape=(shape((2, tiles, width), F32), shape((peers, 2, 128), F32)),
        in_specs=[vmem] * 6,
        out_specs=(vmem,) * 2,
        scratch_shapes=[
            pltpu.VMEM((2, far_count, rank, 2 * tiles), F32),
            pltpu.VMEM((rank, 2 * tiles), F32),
            pltpu.VMEM((4 * peers, 128), F32),
            pltpu.VMEM((2, 6, 8, 128), F32),
        ],
        compiler_params=params(),
        name="voltages",
    )(
        all_coeff,
        targets,
        pairs,
        basis_out_rows,
        near,
        code,
    )
    arrived = lax.all_to_all(slots, ("chips", "core"), 0, 0, tiled=True)
    own, asked, picks = pl.pallas_call(
        own_sum_kernel,
        out_shape=(
            shape((2, own_rows, 128), F32),
            shape((2, chips, 128), jnp.int32),
            shape((128, peers * 128), BF16),
        ),
        in_specs=[vmem] * 6,
        out_specs=(vmem,) * 3,
        scratch_shapes=[
            pltpu.VMEM((4 * own_rows, 128), F32),
            pltpu.VMEM((2, 6, 8, 128), F32),
        ],
        compiler_params=params(),
        cost_estimate=small_cost(),
        name="own_sums",
    )(code, voltage, same_rows, other_rows, port_near, port_coupling)
    return pl.pallas_call(
        finish_kernel,
        out_shape=shape((2, mesh_dev), F32),
        in_specs=[vmem] * 4,
        out_specs=vmem,
        compiler_params=params(),
        name="finish",
    )(own, arrived.reshape(chips, 2, 2, 128), asked, picks)


def solution(mesh):
    groups, peers = mesh.devices.shape
    split_mesh = jax.sharding.Mesh(
        mesh.devices.reshape(groups, peers // 2, 2), ("groups", "chips", "core")
    )
    in_specs = (
        P(None, SPREAD),
        P(None, SPREAD),
        P(None, SPREAD),
        P(SPREAD, None),
        P(SPREAD),
        P(SPREAD, None, None, None),
        P(SPREAD, None),
        P(SPREAD, None, None),
        P(SPREAD, None, None, None),
        P(SPREAD, None, None),
        P(SPREAD, None),
        P("groups"),
        P(),
    )
    out_specs = P(None, SPREAD)
    return jax.shard_map(
        per_device, mesh=split_mesh, in_specs=in_specs, out_specs=out_specs, check_vma=False
    )
```

```python
import functools

import jax
import jax.numpy as jnp
from jax import lax
from jax.experimental import pallas as pl
from jax.experimental.pallas import tpu as pltpu
from jax.sharding import PartitionSpec as P

F32 = jnp.float32
BF16 = jnp.bfloat16
SPREAD = ("groups", "chips", "core")
VMEM_LIMIT = 24 * 1024 * 1024
NT = (((1,), (1,)), ((), ()))


def params():
    return pltpu.CompilerParams(vmem_limit_bytes=VMEM_LIMIT)


def small_cost():
    return pl.CostEstimate(flops=10**9, bytes_accessed=8 * 10**6, transcendentals=0)


def lane_pick(row, lanes):
    spread = jnp.broadcast_to(row, lanes.shape)
    return jnp.take_along_axis(spread, lanes, axis=1, mode="promise_in_bounds")


def dot_nt(left, right, precision=None):
    return lax.dot_general(
        left, right, NT, preferred_element_type=F32, precision=precision
    )


def device_index():
    return 2 * lax.axis_index("chips") + lax.axis_index("core")


def fetch(copies):
    for copy in copies:
        copy.start()
    for copy in copies:
        copy.wait()


def pack_kernel(
    mesh_hbm, need_hbm, port_hbm, out_ref, mesh_ref, need_ref, port_ref, sems
):
    rows = mesh_ref.shape[1] // 128
    ports = port_ref.shape[1]
    chips = out_ref.shape[0]
    fetch(
        [
            pltpu.make_async_copy(source, target, sems.at[i])
            for i, (source, target) in enumerate(
                [(mesh_hbm, mesh_ref), (need_hbm, need_ref), (port_hbm, port_ref)]
            )
        ]
    )
    port = port_ref[...] - device_index() * (rows * 128)
    port = jnp.where((port >= 0) & (port < rows * 128), port, -1)
    port = jnp.broadcast_to(jnp.concatenate([port, port], axis=1), (8, 128))
    port_high, port_low = port >> 7, port & 127
    port_value = jnp.zeros((8, 128), F32)
    lane = lax.broadcasted_iota(jnp.int32, (8, 128), 1)
    for r in range(rows):
        real_row = mesh_ref[0:1, r * 128 : (r + 1) * 128]
        imag_row = mesh_ref[1:2, r * 128 : (r + 1) * 128]
        both = jnp.where(
            lane < ports, lane_pick(real_row, port_low), lane_pick(imag_row, port_low)
        )
        port_value = jnp.where(port_high == r, both, port_value)
        for chip in range(chips):
            out_ref[chip, r : r + 1, :] = real_row
            out_ref[chip, rows + r : rows + r + 1, :] = imag_row
    need = [need_ref[pl.ds(c, chips, 2), :].astype(F32) for c in range(2)]
    first = lax.axis_index("core") == 0
    out_ref[:, 2 * rows, :] = jnp.where(first, need[0], need[1])
    out_ref[:, 2 * rows + 1, :] = jnp.where(first, need[1], need[0])
    out_ref[:, 2 * rows + 2, :] = jnp.broadcast_to(port_value[0:1], (chips, 128))
    for r in range(2 * rows + 3, out_ref.shape[1]):
        out_ref[:, r, :] = jnp.zeros((chips, 128), F32)


def ask(need_ref, pack_ref, table_ref, core, rows):
    chips = pack_ref.shape[0]
    sub = lax.broadcasted_iota(jnp.int32, (rows, 128), 0)
    for chip in range(chips):
        wanted = need_ref[pl.ds(2 * chip + core, 1), :]
        wanted = jnp.broadcast_to(jnp.maximum(wanted, 0), (rows, 128))
        here = (wanted >> 7) == sub
        low = wanted & 127
        for c in range(2):
            block = pack_ref[chip, c * rows : (c + 1) * rows, :]
            picked = jnp.take_along_axis(block, low, axis=1, mode="promise_in_bounds")
            picked = jnp.where(here, picked, 0.0)
            table_ref[c, chip : chip + 1, :] = jnp.sum(picked, axis=0, keepdims=True)


def lookup(code_ref, start, tables):
    total = [None, None]
    for k in range(2):
        code = code_ref[k, pl.ds(start, 8), :]
        high, low = code >> 8, (code >> 1) & 127
        value = [jnp.zeros((8, 128), F32), jnp.zeros((8, 128), F32)]
        for first, step, count, row_of in tables:
            offset = high - first
            for r in range(count):
                here = offset == r * step
                for c in range(2):
                    value[c] = jnp.where(here, lane_pick(row_of(r, c), low), value[c])
        along = (code & 1) == 1
        for c in range(2):
            signed = jnp.where(along, value[c], -value[c])
            total[c] = signed if k == 0 else total[c] + signed
    return total


def own_lookup_kernel(mesh_ref, code_ref, coupling_hbm, out_ref, pair_ref, raw_ref, sems):
    rows = mesh_ref.shape[1] // 128
    far_count, rank = coupling_hbm.shape[:2]
    half = rank // 2
    copies = [
        pltpu.make_async_copy(coupling_hbm.at[k], raw_ref.at[k], sems.at[k])
        for k in range(far_count)
    ]
    for k, copy in enumerate(copies):
        copy.start(priority=k % 2)

    def own_row(r, c):
        return mesh_ref[c : c + 1, r * 128 : (r + 1) * 128]

    def block(g, carry):
        start = pl.multiple_of(g * 8, 8)
        total = lookup(code_ref, start, [(0, 1, rows, own_row)])
        out_ref[0, pl.ds(start, 8), :] = total[0]
        out_ref[1, pl.ds(start, 8), :] = total[1]
        return carry

    lax.fori_loop(0, code_ref.shape[1] // 8, block, 0)
    for k in range(far_count):
        copies[k].wait()
        for r in range(half):
            pair_ref[k, r] = jnp.concatenate([raw_ref[k, r], raw_ref[k, half + r]], axis=1)


def add_peers(part_ref, pack_ref, need_ref, code_ref, table_ref, out_ref, core, first):
    chips = pack_ref.shape[0]
    ask(need_ref, pack_ref, table_ref, core, first)

    def peer_row(r, c):
        return table_ref[c, r : r + 1, :]

    def block(g, carry):
        start = pl.multiple_of(g * 8, 8)
        total = lookup(code_ref, start, [(first + core, 2, chips, peer_row)])
        for c in range(2):
            out_ref[c, pl.ds(start, 8), :] = total[c] + part_ref[c, pl.ds(start, 8), :]
        return carry

    lax.fori_loop(0, code_ref.shape[1] // 8, block, 0)


def same_core_kernel(
    part_ref, same_ref, need_ref, code_ref, out_ref, rows_ref, table_ref, *, first
):
    rows_ref[0] = same_ref[:, 2 * first, :]
    rows_ref[1] = same_ref[:, 2 * first + 2, :]
    add_peers(
        part_ref, same_ref, need_ref, code_ref, table_ref, out_ref,
        lax.axis_index("core"), first,
    )


def current_kernel(
    part_ref, other_ref, need_ref, code_ref, basis_hbm, current_ref, coeff_ref, rows_ref,
    table_ref, basis_ref, sem, *, first,
):
    tiles = code_ref.shape[1]
    rank = basis_ref.shape[0] // tiles
    copy = pltpu.make_async_copy(basis_hbm, basis_ref, sem.at[0])
    copy.start()
    rows_ref[0] = other_ref[:, 2 * first + 1, :]
    rows_ref[1] = other_ref[:, 2 * first + 2, :]
    add_peers(
        part_ref, other_ref, need_ref, code_ref, table_ref, current_ref,
        1 - lax.axis_index("core"), first,
    )
    copy.wait()
    inputs = jnp.concatenate([current_ref[0], current_ref[1]], axis=0)
    inputs = inputs.T.astype(BF16)
    lane_tile = lax.broadcasted_iota(jnp.int32, (rank, 2 * tiles), 1) % tiles
    full = jnp.dot(basis_ref[...], inputs, preferred_element_type=F32)
    chosen = jnp.zeros((rank, 2 * tiles), F32)
    for t in range(tiles):
        chosen = jnp.where(lane_tile == t, full[t * rank : (t + 1) * rank], chosen)
    coeff_ref[0] = chosen.astype(BF16)


def near_kernel(source_ref, current_ref, resistance_ref, blocks_ref, out_ref, inputs_ref):
    tiles, count, width, _ = blocks_ref.shape
    lane_tile = lax.broadcasted_iota(jnp.int32, (width, 128), 1) % tiles
    rows = jnp.concatenate([current_ref[0], current_ref[1]], axis=0)
    columns = rows.T.astype(BF16)
    row_index = lax.broadcasted_iota(jnp.int32, (128, 128), 0)
    for k in range(count):
        picks = jnp.where(row_index == source_ref[k : k + 1, :], 1.0, 0.0).astype(BF16)
        inputs_ref[k * width : (k + 1) * width, :] = jnp.dot(
            columns, picks, preferred_element_type=F32
        ).astype(BF16)
    inputs = inputs_ref[...]
    total = jnp.zeros((width, 128), F32)
    for g in range(tiles // 8):
        block = jnp.concatenate(
            [
                blocks_ref[g * 8 : g * 8 + 8, k].reshape(8 * width, width)
                for k in range(count)
            ],
            axis=1,
        )
        full = jnp.dot(block, inputs, preferred_element_type=F32)
        for i in range(8):
            total = jnp.where(
                lane_tile == g * 8 + i, full[i * width : (i + 1) * width], total
            )
    rows = total.T
    resistance = resistance_ref[...]
    out_ref[0] = resistance * current_ref[0] - rows[tiles:]
    out_ref[1] = resistance * current_ref[1] + rows[:tiles]


def split(value):
    top = value.astype(BF16)
    return top, (value - top.astype(F32)).astype(BF16)


def counts(rows):
    return lax.broadcasted_iota(jnp.int32, (rows, 128), 0).astype(F32)


def place(high, low, values, rows, spread_ref):
    sub_high, sub_low = counts(rows).astype(BF16), counts(128).astype(BF16)
    one, zero = jnp.ones((128, 128), BF16), jnp.zeros((128, 128), BF16)
    spread_ref[0] = high.astype(F32)
    spread_ref[1] = low.astype(F32)
    for c, value in enumerate(values):
        top, rest = split(value)
        spread_ref[2 + 2 * c] = top.astype(F32)
        spread_ref[3 + 2 * c] = rest.astype(F32)

    def spread(j, i, count):
        return jnp.broadcast_to(spread_ref[j, i : i + 1, :], (count, 128)).astype(BF16)

    left, right = [], []
    for i in range(8):
        here = spread(0, i, rows) == sub_high
        left.append(
            jnp.concatenate(
                [jnp.where(here, spread(j, i, rows), zero[:rows]) for j in range(2, 6)], axis=0
            )
        )
        right.append(jnp.where(spread(1, i, 128) == sub_low, one, zero))
    return jnp.concatenate(left, axis=1), jnp.concatenate(right, axis=1)


def place_few(high, low, values, rows):
    sub_high = lax.broadcasted_iota(jnp.int32, (rows, 128), 0)
    sub_low = lax.broadcasted_iota(jnp.int32, (128, 128), 0)
    left, right = [], []
    for i in range(high.shape[0]):
        here = jnp.broadcast_to(high[i : i + 1], (rows, 128)) == sub_high
        parts = []
        for value in values:
            spread = jnp.where(here, jnp.broadcast_to(value[i : i + 1], (rows, 128)), 0.0)
            parts.extend(split(spread))
        left.append(jnp.concatenate(parts, axis=0))
        there = jnp.broadcast_to(low[i : i + 1], (128, 128)) == sub_low
        right.append(jnp.where(there, 1.0, 0.0).astype(BF16))
    return jnp.concatenate(left, axis=1), jnp.concatenate(right, axis=1)


def scatter(code_ref, voltage_ref, total_ref, spread_ref, first, rows, low_streams):
    total_ref[...] = jnp.zeros_like(total_ref)

    def block(g, carry):
        start = pl.multiple_of(g * 8, 8)
        for k in range(2):
            code = code_ref[k, pl.ds(start, 8), :]
            along = (code & 1) == 1
            values = []
            for c in range(2):
                voltage = voltage_ref[c, pl.ds(start, 8), :]
                values.append(jnp.where(along, voltage, -voltage))
            left, right = place(
                (code >> 8) - first, (code >> 1) & 127, values, rows, spread_ref.at[k]
            )
            total_ref[...] += dot_nt(right, left) if low_streams else dot_nt(left, right)
        return carry

    lax.fori_loop(0, code_ref.shape[1] // 8, block, 0)
    total = total_ref[...].T if low_streams else total_ref[...]
    return [
        total[2 * c * rows : (2 * c + 1) * rows] + total[(2 * c + 1) * rows : (2 * c + 2) * rows]
        for c in range(2)
    ]


def voltage_kernel(
    coeff_ref, other_coeff_ref, target_ref, coupling_ref, basis_ref, near_ref, code_ref, voltage_ref, slot_ref,
    picked_ref, mixed_ref, total_ref, spread_ref, *, first,
):
    chips, rank, lanes = coeff_ref.shape
    peers = 2 * chips
    bits = chips.bit_length() - 1
    far_count = coupling_ref.shape[0]
    tiles = lanes // 2
    half = rank // 2
    groups = half // 4
    device = device_index()
    spans = target_ref.shape[0] // far_count
    stride = peers // far_count
    for k in range(far_count):
        picked = [jnp.zeros((rank, lanes), F32), jnp.zeros((rank, lanes), F32)]
        for i in range(spans):
            row = k * spans + i
            apart = ((device + k * stride + i) % peers) ^ device
            place = 0
            for bit in range(bits):
                place += ((apart >> (bit + 1)) & 1) << (bits - 1 - bit)
            block = jnp.where((apart & 1) == 0, coeff_ref[place], other_coeff_ref[place])
            block = block.astype(F32)
            target = jnp.broadcast_to(target_ref[row : row + 1, :], (rank, lanes))
            inside = target >= 0
            source = jnp.maximum(target, 0)
            for c in range(2):
                value = jnp.take_along_axis(
                    block, source + c * tiles, axis=1, mode="promise_in_bounds"
                )
                picked[c] = jnp.where(inside, value, picked[c])
        for c in range(2):
            picked_ref[c, k] = picked[c]

    def mix(g, carry):
        total = [[None, None] for _ in range(4)]
        for k in range(far_count):
            picked = [picked_ref[c, k] for c in range(2)]
            for i in range(4):
                block = coupling_ref[k, g * 4 + i].astype(F32)
                for c in range(2):
                    product = block * picked[c]
                    part = product[0:8]
                    for q in range(8, rank, 8):
                        part = part + product[q : q + 8]
                    total[i][c] = part if k == 0 else total[i][c] + part
        for i in range(4):
            for c in range(2):
                row = jnp.sum(total[i][c], axis=0, keepdims=True)
                mixed_ref[pl.ds(c * half + g * 4 + i, 1), :] = row
        return carry

    lax.fori_loop(0, groups, mix, 0)
    mixed = mixed_ref[...].T
    mixed = jnp.concatenate([mixed[:tiles], mixed[tiles:]], axis=1).astype(BF16)
    wide = 8 * rank
    from_row = lax.broadcasted_iota(jnp.int32, (2 * rank, wide), 0)
    to_rank = lax.broadcasted_iota(jnp.int32, (2 * rank, wide), 1) % rank
    repeated = []
    for c in range(2):
        wanted = (to_rank // half) * rank + c * half + to_rank % half
        picks = jnp.where(from_row == wanted, 1.0, 0.0).astype(BF16)
        repeated.append(jnp.dot(mixed, picks, preferred_element_type=F32))
    own_block = (
        lax.broadcasted_iota(jnp.int32, (16, wide), 0) % 8
        == lax.broadcasted_iota(jnp.int32, (16, wide), 1) // rank
    )
    for g in range(tiles // 8):
        rows8 = slice(g * 8, g * 8 + 8)
        both = jnp.concatenate([repeated[0][rows8], repeated[1][rows8]], axis=0)
        both = jnp.where(own_block, both, 0.0).astype(BF16)
        far = jnp.dot(
            both, basis_ref[g * wide : (g + 1) * wide, :], preferred_element_type=F32
        )
        voltage_ref[0, rows8, :] = near_ref[0, rows8, :] - far[8:16]
        voltage_ref[1, rows8, :] = near_ref[1, rows8, :] + far[0:8]
    sums = scatter(
        code_ref, voltage_ref, total_ref, spread_ref, first, slot_ref.shape[0], True
    )
    for c in range(2):
        slot_ref[:, c, :] = sums[c]


def own_sum_kernel(
    code_ref, voltage_ref, same_ref, other_ref, port_ref, impedance_ref, own_ref, asked_ref,
    picks_ref, total_ref, spread_ref,
):
    rows = own_ref.shape[1]
    ports = impedance_ref.shape[1]
    chips = same_ref.shape[1]
    first_core = lax.axis_index("core") == 0
    same = same_ref[0].astype(jnp.int32)
    other = other_ref[0].astype(jnp.int32)
    asked = [jnp.where(first_core, same, other), jnp.where(first_core, other, same)]
    sub_low = lax.broadcasted_iota(jnp.int32, (128, 128), 0)
    for core in range(2):
        asked_ref[core] = asked[core] >> 7
        low = asked[core] & 127
        for chip in range(chips):
            there = jnp.broadcast_to(low[chip : chip + 1], (128, 128)) == sub_low
            place = core * chips + chip
            picks_ref[:, place * 128 : (place + 1) * 128] = jnp.where(there, 1.0, 0.0).astype(BF16)
    port_current = jnp.sum(same_ref[1] + other_ref[1], axis=0, keepdims=True)
    real = port_current[:, :ports]
    imag = port_current[:, ports:]
    both = jnp.concatenate([real, imag, jnp.zeros((6, ports), F32)], axis=0)
    by_real = dot_nt(both, impedance_ref[0], lax.Precision.HIGHEST)
    by_imag = dot_nt(both, impedance_ref[1], lax.Precision.HIGHEST)
    pad = jnp.zeros((1, 128 - ports), F32)
    terms = [
        jnp.concatenate([by_real[0:1] - by_imag[1:2], pad], axis=1),
        jnp.concatenate([by_real[1:2] + by_imag[0:1], pad], axis=1),
    ]
    port = port_ref[...] - device_index() * (rows * 128)
    port = jnp.where((port >= 0) & (port < rows * 128), port, -1)
    port = jnp.concatenate([port, jnp.full((1, 128 - ports), -1, jnp.int32)], axis=1)
    left, right = place_few(port >> 7, port & 127, terms, rows)
    total = dot_nt(left, right)
    sums = scatter(code_ref, voltage_ref, total_ref, spread_ref, 0, rows, False)
    for c in range(2):
        own_ref[c] = sums[c] + (
            total[2 * c * rows : (2 * c + 1) * rows] + total[(2 * c + 1) * rows : (2 * c + 2) * rows]
        )


def finish_kernel(own_ref, arrived_ref, asked_ref, picks_ref, out_ref):
    rows = own_ref.shape[1]
    chips = arrived_ref.shape[0]
    sub_high = lax.broadcasted_iota(jnp.int32, (rows, 128), 0)
    left = []
    for core in range(2):
        for chip in range(chips):
            here = jnp.broadcast_to(asked_ref[core, chip : chip + 1, :], (rows, 128)) == sub_high
            parts = []
            for c in range(2):
                value = jnp.broadcast_to(arrived_ref[chip, core, c : c + 1, :], (rows, 128))
                parts.extend(split(jnp.where(here, value, 0.0)))
            left.append(jnp.concatenate(parts, axis=0))
    total = dot_nt(jnp.concatenate(left, axis=1), picks_ref[...])
    for c in range(2):
        summed = own_ref[c] + (
            total[2 * c * rows : (2 * c + 1) * rows] + total[(2 * c + 1) * rows : (2 * c + 2) * rows]
        )
        for r in range(rows):
            out_ref[c : c + 1, r * 128 : (r + 1) * 128] = summed[r : r + 1]


def per_device(
    mesh_current,
    branch_entry,
    branch_sign,
    need_slots,
    resistance,
    near_blocks,
    near_source,
    basis_in,
    coupling,
    basis_out,
    admissible,
    port_mesh,
    port_coupling,
):
    chips = lax.axis_size("chips")
    peers = 2 * chips
    core = lax.axis_index("core")
    device = 2 * lax.axis_index("chips") + core
    mesh_dev = mesh_current.shape[1]
    tiles, near_count, width, _ = near_blocks.shape
    rank = basis_in.shape[1]
    far_count = admissible.shape[1]
    own_rows = mesh_dev // 128
    vmem = pl.BlockSpec(memory_space=pltpu.VMEM)
    shape = jax.ShapeDtypeStruct

    code = (branch_entry * 2 + branch_sign).reshape(2, tiles, width)
    coupling_lanes = jnp.transpose(coupling, (1, 2, 3, 0))
    basis_in_rows = basis_in.reshape(tiles * rank, width)
    basis_out_rows = basis_out.reshape(tiles * rank, width)
    half = jnp.arange(2 * tiles, dtype=jnp.int32) // tiles
    sources = jnp.transpose(near_source)
    sources = jnp.concatenate([sources, sources], axis=1) + half[None] * tiles
    band = peers * tiles // far_count
    spans = band // tiles + 1
    bases = device * tiles + jnp.arange(far_count, dtype=jnp.int32) * band
    shifted = (jnp.transpose(admissible) - bases[:, None]) % (peers * tiles)
    shifted = jnp.concatenate([shifted, shifted], axis=1)[:, None, :]
    shifted = shifted - jnp.arange(spans, dtype=jnp.int32)[None, :, None] * tiles
    inside = (shifted >= 0) & (shifted < tiles)
    targets = jnp.where(inside, shifted, -1).reshape(far_count * spans, 2 * tiles)

    def in_hbm(x):
        return pltpu.with_memory_space_constraint(x, pltpu.HBM)

    hbm = pl.BlockSpec(memory_space=pl.ANY)
    port_row = port_mesh.reshape(1, -1)
    pack_rows = (2 * own_rows + 3 + 7) // 8 * 8
    pack, mesh_near, need_near, port_near = pl.pallas_call(
        pack_kernel,
        out_shape=(
            shape((chips, pack_rows, 128), F32),
            pltpu.VMEM(mesh_current.shape, F32),
            pltpu.VMEM(need_slots.shape, jnp.int32),
            pltpu.VMEM(port_row.shape, jnp.int32),
        ),
        in_specs=[hbm] * 3,
        out_specs=(vmem,) * 4,
        scratch_shapes=[pltpu.SemaphoreType.DMA((3,))],
        compiler_params=params(),
        name="pack",
    )(in_hbm(mesh_current), in_hbm(need_slots), in_hbm(port_row))
    same = lax.all_to_all(pack, "chips", 0, 0, tiled=True)
    own_part, pairs = pl.pallas_call(
        own_lookup_kernel,
        out_shape=(
            shape((2, tiles, width), F32),
            pltpu.VMEM((far_count, rank // 2, rank, 2 * tiles), BF16),
        ),
        in_specs=[vmem] * 2 + [hbm],
        out_specs=(vmem,) * 2,
        scratch_shapes=[
            pltpu.VMEM(coupling_lanes.shape, BF16),
            pltpu.SemaphoreType.DMA((far_count,)),
        ],
        compiler_params=params(),
        cost_estimate=small_cost(),
        name="own_lookup",
    )(mesh_near, code, in_hbm(coupling_lanes))
    other = lax.ppermute(same, "core", [(0, 1), (1, 0)])
    part, same_rows = pl.pallas_call(
        functools.partial(same_core_kernel, first=own_rows),
        out_shape=(shape((2, tiles, width), F32), shape((2, chips, 128), F32)),
        in_specs=[vmem] * 4,
        out_specs=(vmem,) * 2,
        scratch_shapes=[pltpu.VMEM((2, chips, 128), F32)],
        compiler_params=params(),
        cost_estimate=small_cost(),
        name="same_core",
    )(own_part, same, need_near, code)
    current, coeff, other_rows = pl.pallas_call(
        functools.partial(current_kernel, first=own_rows),
        out_shape=(
            shape((2, tiles, width), F32),
            shape((1, rank, 2 * tiles), BF16),
            shape((2, chips, 128), F32),
        ),
        in_specs=[vmem] * 4 + [hbm],
        out_specs=(vmem,) * 3,
        scratch_shapes=[
            pltpu.VMEM((2, chips, 128), F32),
            pltpu.VMEM(basis_in_rows.shape, BF16),
            pltpu.SemaphoreType.DMA((1,)),
        ],
        compiler_params=params(),
        name="currents",
    )(part, other, need_near, code, in_hbm(basis_in_rows))
    mask = chips // 2
    while mask:
        pairing = [(i, i ^ mask) for i in range(chips)]
        coeff = jnp.concatenate([coeff, lax.ppermute(coeff, "chips", pairing)], axis=0)
        mask //= 2
    other_coeff = lax.ppermute(coeff, "core", [(0, 1), (1, 0)])
    near = pl.pallas_call(
        near_kernel,
        out_shape=shape((2, tiles, width), F32),
        in_specs=[vmem] * 4,
        out_specs=vmem,
        scratch_shapes=[pltpu.VMEM((near_count * width, 2 * tiles), BF16)],
        compiler_params=params(),
        cost_estimate=pl.CostEstimate(
            flops=256 * near_blocks.size, bytes_accessed=2 * near_blocks.size, transcendentals=0
        ),
        name="near_field",
    )(sources, current, resistance.reshape(tiles, width), near_blocks)
    voltage, slots = pl.pallas_call(
        functools.partial(voltage_kernel, first=own_rows),
        out_shape=(shape((2, tiles, width), F32), shape((peers, 2, 128), F32)),
        in_specs=[vmem] * 7,
        out_specs=(vmem,) * 2,
        scratch_shapes=[
            pltpu.VMEM((2, far_count, rank, 2 * tiles), F32),
            pltpu.VMEM((rank, 2 * tiles), F32),
            pltpu.VMEM((128, 4 * peers), F32),
            pltpu.VMEM((2, 6, 8, 128), F32),
        ],
        compiler_params=params(),
        name="voltages",
    )(
        coeff,
        other_coeff,
        targets,
        pairs,
        basis_out_rows,
        near,
        code,
    )
    arrived = lax.all_to_all(slots, ("chips", "core"), 0, 0, tiled=True)
    own, asked, picks = pl.pallas_call(
        own_sum_kernel,
        out_shape=(
            shape((2, own_rows, 128), F32),
            shape((2, chips, 128), jnp.int32),
            shape((128, peers * 128), BF16),
        ),
        in_specs=[vmem] * 6,
        out_specs=(vmem,) * 3,
        scratch_shapes=[
            pltpu.VMEM((4 * own_rows, 128), F32),
            pltpu.VMEM((2, 6, 8, 128), F32),
        ],
        compiler_params=params(),
        cost_estimate=small_cost(),
        name="own_sums",
    )(code, voltage, same_rows, other_rows, port_near, port_coupling)
    return pl.pallas_call(
        finish_kernel,
        out_shape=shape((2, mesh_dev), F32),
        in_specs=[vmem] * 4,
        out_specs=vmem,
        compiler_params=params(),
        name="finish",
    )(own, arrived.reshape(chips, 2, 2, 128), asked, picks)


def solution(mesh):
    groups, peers = mesh.devices.shape
    split_mesh = jax.sharding.Mesh(
        mesh.devices.reshape(groups, peers // 2, 2), ("groups", "chips", "core")
    )
    in_specs = (
        P(None, SPREAD),
        P(None, SPREAD),
        P(None, SPREAD),
        P(SPREAD, None),
        P(SPREAD),
        P(SPREAD, None, None, None),
        P(SPREAD, None),
        P(SPREAD, None, None),
        P(SPREAD, None, None, None),
        P(SPREAD, None, None),
        P(SPREAD, None),
        P("groups"),
        P(),
    )
    out_specs = P(None, SPREAD)
    return jax.shard_map(
        per_device, mesh=split_mesh, in_specs=in_specs, out_specs=out_specs, check_vma=False
    )
```

```python
import functools

import jax
import jax.numpy as jnp
from jax import lax
from jax.experimental import pallas as pl
from jax.experimental.pallas import tpu as pltpu
from jax.sharding import PartitionSpec as P

F32 = jnp.float32
BF16 = jnp.bfloat16
SPREAD = ("groups", "chips", "core")
VMEM_LIMIT = 24 * 1024 * 1024
NT = (((1,), (1,)), ((), ()))


def params():
    return pltpu.CompilerParams(vmem_limit_bytes=VMEM_LIMIT)


def small_cost():
    return pl.CostEstimate(flops=10**9, bytes_accessed=8 * 10**6, transcendentals=0)


def lane_pick(row, lanes):
    spread = jnp.broadcast_to(row, lanes.shape)
    return jnp.take_along_axis(spread, lanes, axis=1, mode="promise_in_bounds")


def dot_nt(left, right, precision=None):
    return lax.dot_general(
        left, right, NT, preferred_element_type=F32, precision=precision
    )


def device_index():
    return 2 * lax.axis_index("chips") + lax.axis_index("core")


def fetch(copies):
    for copy in copies:
        copy.start()
    for copy in copies:
        copy.wait()


def pack_kernel(
    mesh_hbm, need_hbm, port_hbm, out_ref, mesh_ref, need_ref, port_ref, sems
):
    rows = mesh_ref.shape[1] // 128
    ports = port_ref.shape[1]
    chips = out_ref.shape[0]
    fetch(
        [
            pltpu.make_async_copy(source, target, sems.at[i])
            for i, (source, target) in enumerate(
                [(mesh_hbm, mesh_ref), (need_hbm, need_ref), (port_hbm, port_ref)]
            )
        ]
    )
    port = port_ref[...] - device_index() * (rows * 128)
    port = jnp.where((port >= 0) & (port < rows * 128), port, -1)
    port = jnp.broadcast_to(jnp.concatenate([port, port], axis=1), (8, 128))
    port_high, port_low = port >> 7, port & 127
    port_value = jnp.zeros((8, 128), F32)
    lane = lax.broadcasted_iota(jnp.int32, (8, 128), 1)
    for r in range(rows):
        real_row = mesh_ref[0:1, r * 128 : (r + 1) * 128]
        imag_row = mesh_ref[1:2, r * 128 : (r + 1) * 128]
        both = jnp.where(
            lane < ports, lane_pick(real_row, port_low), lane_pick(imag_row, port_low)
        )
        port_value = jnp.where(port_high == r, both, port_value)
        for chip in range(chips):
            out_ref[chip, r : r + 1, :] = real_row
            out_ref[chip, rows + r : rows + r + 1, :] = imag_row
    need = [need_ref[pl.ds(c, chips, 2), :].astype(F32) for c in range(2)]
    first = lax.axis_index("core") == 0
    out_ref[:, 2 * rows, :] = jnp.where(first, need[0], need[1])
    out_ref[:, 2 * rows + 1, :] = jnp.where(first, need[1], need[0])
    out_ref[:, 2 * rows + 2, :] = jnp.broadcast_to(port_value[0:1], (chips, 128))
    for r in range(2 * rows + 3, out_ref.shape[1]):
        out_ref[:, r, :] = jnp.zeros((chips, 128), F32)


def ask(need_ref, pack_ref, table_ref, core, rows):
    chips = pack_ref.shape[0]
    sub = lax.broadcasted_iota(jnp.int32, (rows, 128), 0)
    for chip in range(chips):
        wanted = need_ref[pl.ds(2 * chip + core, 1), :]
        wanted = jnp.broadcast_to(jnp.maximum(wanted, 0), (rows, 128))
        here = (wanted >> 7) == sub
        low = wanted & 127
        for c in range(2):
            block = pack_ref[chip, c * rows : (c + 1) * rows, :]
            picked = jnp.take_along_axis(block, low, axis=1, mode="promise_in_bounds")
            picked = jnp.where(here, picked, 0.0)
            table_ref[c, chip : chip + 1, :] = jnp.sum(picked, axis=0, keepdims=True)


def lookup(code_ref, start, tables):
    total = [None, None]
    for k in range(2):
        code = code_ref[k, pl.ds(start, 8), :]
        high, low = code >> 8, (code >> 1) & 127
        value = [jnp.zeros((8, 128), F32), jnp.zeros((8, 128), F32)]
        for first, step, count, row_of in tables:
            offset = high - first
            for r in range(count):
                here = offset == r * step
                for c in range(2):
                    value[c] = jnp.where(here, lane_pick(row_of(r, c), low), value[c])
        along = (code & 1) == 1
        for c in range(2):
            signed = jnp.where(along, value[c], -value[c])
            total[c] = signed if k == 0 else total[c] + signed
    return total


def own_lookup_kernel(mesh_ref, code_ref, coupling_hbm, out_ref, pair_ref, raw_ref, sems):
    rows = mesh_ref.shape[1] // 128
    far_count, rank = coupling_hbm.shape[:2]
    half = rank // 2
    copies = [
        pltpu.make_async_copy(coupling_hbm.at[k], raw_ref.at[k], sems.at[k])
        for k in range(far_count)
    ]
    for k, copy in enumerate(copies):
        copy.start(priority=k % 2)

    def own_row(r, c):
        return mesh_ref[c : c + 1, r * 128 : (r + 1) * 128]

    def block(g, carry):
        start = pl.multiple_of(g * 8, 8)
        total = lookup(code_ref, start, [(0, 1, rows, own_row)])
        out_ref[0, pl.ds(start, 8), :] = total[0]
        out_ref[1, pl.ds(start, 8), :] = total[1]
        return carry

    lax.fori_loop(0, code_ref.shape[1] // 8, block, 0)
    for k in range(far_count):
        copies[k].wait()
        for r in range(half):
            pair_ref[k, r] = jnp.concatenate([raw_ref[k, r], raw_ref[k, half + r]], axis=1)


def add_peers(part_ref, pack_ref, need_ref, code_ref, table_ref, out_ref, core, first):
    chips = pack_ref.shape[0]
    ask(need_ref, pack_ref, table_ref, core, first)

    def peer_row(r, c):
        return table_ref[c, r : r + 1, :]

    def block(g, carry):
        start = pl.multiple_of(g * 8, 8)
        total = lookup(code_ref, start, [(first + core, 2, chips, peer_row)])
        for c in range(2):
            out_ref[c, pl.ds(start, 8), :] = total[c] + part_ref[c, pl.ds(start, 8), :]
        return carry

    lax.fori_loop(0, code_ref.shape[1] // 8, block, 0)


def same_core_kernel(
    part_ref, same_ref, need_ref, code_ref, out_ref, rows_ref, table_ref, *, first
):
    rows_ref[0] = same_ref[:, 2 * first, :]
    rows_ref[1] = same_ref[:, 2 * first + 2, :]
    add_peers(
        part_ref, same_ref, need_ref, code_ref, table_ref, out_ref,
        lax.axis_index("core"), first,
    )


def current_kernel(
    part_ref, other_ref, need_ref, code_ref, basis_hbm, current_ref, coeff_ref, rows_ref,
    table_ref, basis_ref, sem, *, first,
):
    tiles = code_ref.shape[1]
    rank = basis_ref.shape[0] // tiles
    copy = pltpu.make_async_copy(basis_hbm, basis_ref, sem.at[0])
    copy.start()
    rows_ref[0] = other_ref[:, 2 * first + 1, :]
    rows_ref[1] = other_ref[:, 2 * first + 2, :]
    add_peers(
        part_ref, other_ref, need_ref, code_ref, table_ref, current_ref,
        1 - lax.axis_index("core"), first,
    )
    copy.wait()
    inputs = jnp.concatenate([current_ref[0], current_ref[1]], axis=0)
    inputs = inputs.T.astype(BF16)
    lane_tile = lax.broadcasted_iota(jnp.int32, (rank, 2 * tiles), 1) % tiles
    full = jnp.dot(basis_ref[...], inputs, preferred_element_type=F32)
    chosen = jnp.zeros((rank, 2 * tiles), F32)
    for t in range(tiles):
        chosen = jnp.where(lane_tile == t, full[t * rank : (t + 1) * rank], chosen)
    coeff = chosen.astype(BF16)
    for p in range(coeff_ref.shape[0]):
        coeff_ref[p] = coeff


def near_kernel(
    source_ref, current_ref, resistance_hbm, blocks_hbm, out_ref, inputs_ref, blocks_ref,
    resistance_ref, sems,
):
    tiles = current_ref.shape[1]
    width = blocks_ref.shape[1]
    count = blocks_ref.shape[0] // (tiles * width)
    chunks = tiles // 8
    span = 8 * count * width
    copies = [
        pltpu.make_async_copy(
            blocks_hbm.at[pl.ds(g * span, span)], blocks_ref.at[pl.ds(g * span, span)], sems.at[g]
        )
        for g in range(chunks)
    ]
    late_copy = pltpu.make_async_copy(resistance_hbm, resistance_ref, sems.at[chunks])
    depth = 4
    for copy in copies[:depth]:
        copy.start()
    late_copy.start()
    lane_tile = lax.broadcasted_iota(jnp.int32, (width, 128), 1) % tiles
    rows = jnp.concatenate([current_ref[0], current_ref[1]], axis=0)
    columns = rows.T.astype(BF16)
    row_index = lax.broadcasted_iota(jnp.int32, (128, 128), 0)
    for k in range(count):
        picks = jnp.where(row_index == source_ref[k : k + 1, :], 1.0, 0.0).astype(BF16)
        inputs_ref[k * width : (k + 1) * width, :] = jnp.dot(
            columns, picks, preferred_element_type=F32
        ).astype(BF16)
    inputs = inputs_ref[...]
    total = jnp.zeros((width, 128), F32)
    for g in range(chunks):
        copies[g].wait()
        if g + depth < chunks:
            copies[g + depth].start()
        block = jnp.concatenate(
            [
                jnp.concatenate(
                    [
                        blocks_ref[(t * count + k) * width : (t * count + k + 1) * width, :]
                        for t in range(g * 8, g * 8 + 8)
                    ],
                    axis=0,
                )
                for k in range(count)
            ],
            axis=1,
        )
        full = jnp.dot(block, inputs, preferred_element_type=F32)
        for i in range(8):
            total = jnp.where(
                lane_tile == g * 8 + i, full[i * width : (i + 1) * width], total
            )
    rows = total.T
    late_copy.wait()
    resistance = resistance_ref[...]
    out_ref[0] = resistance * current_ref[0] - rows[tiles:]
    out_ref[1] = resistance * current_ref[1] + rows[:tiles]


def split(value):
    top = value.astype(BF16)
    return top, (value - top.astype(F32)).astype(BF16)


def counts(rows):
    return lax.broadcasted_iota(jnp.int32, (rows, 128), 0).astype(F32)


def place(high, low, values, rows, spread_ref):
    sub_high, sub_low = counts(rows).astype(BF16), counts(128).astype(BF16)
    one, zero = jnp.ones((128, 128), BF16), jnp.zeros((128, 128), BF16)
    spread_ref[0] = high.astype(F32)
    spread_ref[1] = low.astype(F32)
    for c, value in enumerate(values):
        top, rest = split(value)
        spread_ref[2 + 2 * c] = top.astype(F32)
        spread_ref[3 + 2 * c] = rest.astype(F32)

    def spread(j, i, count):
        return jnp.broadcast_to(spread_ref[j, i : i + 1, :], (count, 128)).astype(BF16)

    left, right = [], []
    for i in range(8):
        here = spread(0, i, rows) == sub_high
        left.append(
            jnp.concatenate(
                [jnp.where(here, spread(j, i, rows), zero[:rows]) for j in range(2, 6)], axis=0
            )
        )
        right.append(jnp.where(spread(1, i, 128) == sub_low, one, zero))
    return jnp.concatenate(left, axis=1), jnp.concatenate(right, axis=1)


def place_few(high, low, values, rows):
    sub_high = lax.broadcasted_iota(jnp.int32, (rows, 128), 0)
    sub_low = lax.broadcasted_iota(jnp.int32, (128, 128), 0)
    left, right = [], []
    for i in range(high.shape[0]):
        here = jnp.broadcast_to(high[i : i + 1], (rows, 128)) == sub_high
        parts = []
        for value in values:
            spread = jnp.where(here, jnp.broadcast_to(value[i : i + 1], (rows, 128)), 0.0)
            parts.extend(split(spread))
        left.append(jnp.concatenate(parts, axis=0))
        there = jnp.broadcast_to(low[i : i + 1], (128, 128)) == sub_low
        right.append(jnp.where(there, 1.0, 0.0).astype(BF16))
    return jnp.concatenate(left, axis=1), jnp.concatenate(right, axis=1)


def scatter(code_ref, voltage_ref, total_ref, spread_ref, first, rows, low_streams):
    total_ref[...] = jnp.zeros_like(total_ref)

    def block(g, carry):
        start = pl.multiple_of(g * 8, 8)
        for k in range(2):
            code = code_ref[k, pl.ds(start, 8), :]
            along = (code & 1) == 1
            values = []
            for c in range(2):
                voltage = voltage_ref[c, pl.ds(start, 8), :]
                values.append(jnp.where(along, voltage, -voltage))
            left, right = place(
                (code >> 8) - first, (code >> 1) & 127, values, rows, spread_ref.at[k]
            )
            total_ref[...] += dot_nt(right, left) if low_streams else dot_nt(left, right)
        return carry

    lax.fori_loop(0, code_ref.shape[1] // 8, block, 0)
    total = total_ref[...].T if low_streams else total_ref[...]
    return [
        total[2 * c * rows : (2 * c + 1) * rows] + total[(2 * c + 1) * rows : (2 * c + 2) * rows]
        for c in range(2)
    ]


def voltage_kernel(
    coeff_ref, target_ref, coupling_ref, basis_ref, near_ref, code_ref, voltage_ref, slot_ref,
    picked_ref, mixed_ref, total_ref, spread_ref, *, first,
):
    peers, rank, lanes = coeff_ref.shape
    far_count = coupling_ref.shape[0]
    tiles = lanes // 2
    half = rank // 2
    groups = half // 4
    device = device_index()
    spans = target_ref.shape[0] // far_count
    stride = peers // far_count
    component = lax.broadcasted_iota(jnp.int32, (rank, lanes), 1) // tiles
    for k in range(far_count):
        picked = jnp.zeros((rank, lanes), F32)
        for i in range(spans):
            row = k * spans + i
            block = coeff_ref[(device + k * stride + i) % peers].astype(F32)
            target = jnp.broadcast_to(target_ref[row : row + 1, :], (rank, lanes))
            source = jnp.maximum(target, 0) + component * tiles
            value = jnp.take_along_axis(block, source, axis=1, mode="promise_in_bounds")
            picked = jnp.where(target >= 0, value, picked)
        turned = pltpu.roll(picked, tiles, 1)
        picked_ref[0, k] = jnp.where(component == 0, picked, turned)
        picked_ref[1, k] = jnp.where(component == 0, turned, picked)

    def mix(g, carry):
        total = [[None, None] for _ in range(4)]
        for k in range(far_count):
            picked = [picked_ref[c, k] for c in range(2)]
            for i in range(4):
                block = coupling_ref[k, g * 4 + i].astype(F32)
                for c in range(2):
                    product = block * picked[c]
                    part = product[0:8]
                    for q in range(8, rank, 8):
                        part = part + product[q : q + 8]
                    total[i][c] = part if k == 0 else total[i][c] + part
        for i in range(4):
            for c in range(2):
                row = jnp.sum(total[i][c], axis=0, keepdims=True)
                mixed_ref[pl.ds(c * half + g * 4 + i, 1), :] = row
        return carry

    lax.fori_loop(0, groups, mix, 0)
    mixed = mixed_ref[...].T
    mixed = jnp.concatenate([mixed[:tiles], mixed[tiles:]], axis=1).astype(BF16)
    wide = 8 * rank
    from_row = lax.broadcasted_iota(jnp.int32, (2 * rank, wide), 0)
    to_rank = lax.broadcasted_iota(jnp.int32, (2 * rank, wide), 1) % rank
    repeated = []
    for c in range(2):
        wanted = (to_rank // half) * rank + c * half + to_rank % half
        picks = jnp.where(from_row == wanted, 1.0, 0.0).astype(BF16)
        repeated.append(jnp.dot(mixed, picks, preferred_element_type=F32))
    own_block = (
        lax.broadcasted_iota(jnp.int32, (16, wide), 0) % 8
        == lax.broadcasted_iota(jnp.int32, (16, wide), 1) // rank
    )
    for g in range(tiles // 8):
        rows8 = slice(g * 8, g * 8 + 8)
        both = jnp.concatenate([repeated[0][rows8], repeated[1][rows8]], axis=0)
        both = jnp.where(own_block, both, 0.0).astype(BF16)
        far = jnp.dot(
            both, basis_ref[g * wide : (g + 1) * wide, :], preferred_element_type=F32
        )
        voltage_ref[0, rows8, :] = near_ref[0, rows8, :] - far[8:16]
        voltage_ref[1, rows8, :] = near_ref[1, rows8, :] + far[0:8]
    sums = scatter(
        code_ref, voltage_ref, total_ref, spread_ref, first, slot_ref.shape[0], True
    )
    for c in range(2):
        slot_ref[:, c, :] = sums[c]


def own_sum_kernel(
    code_ref, voltage_ref, same_ref, other_ref, port_ref, impedance_ref, own_ref, asked_ref,
    picks_ref, total_ref, spread_ref,
):
    rows = own_ref.shape[1]
    ports = impedance_ref.shape[1]
    chips = same_ref.shape[1]
    first_core = lax.axis_index("core") == 0
    same = same_ref[0].astype(jnp.int32)
    other = other_ref[0].astype(jnp.int32)
    asked = [jnp.where(first_core, same, other), jnp.where(first_core, other, same)]
    sub_low = lax.broadcasted_iota(jnp.int32, (128, 128), 0)
    for core in range(2):
        asked_ref[core] = asked[core] >> 7
        low = asked[core] & 127
        for chip in range(chips):
            there = jnp.broadcast_to(low[chip : chip + 1], (128, 128)) == sub_low
            place = core * chips + chip
            picks_ref[:, place * 128 : (place + 1) * 128] = jnp.where(there, 1.0, 0.0).astype(BF16)
    port_current = jnp.sum(same_ref[1] + other_ref[1], axis=0, keepdims=True)
    real = port_current[:, :ports]
    imag = port_current[:, ports:]
    both = jnp.concatenate([real, imag, jnp.zeros((6, ports), F32)], axis=0)
    by_real = dot_nt(both, impedance_ref[0], lax.Precision.HIGHEST)
    by_imag = dot_nt(both, impedance_ref[1], lax.Precision.HIGHEST)
    pad = jnp.zeros((1, 128 - ports), F32)
    terms = [
        jnp.concatenate([by_real[0:1] - by_imag[1:2], pad], axis=1),
        jnp.concatenate([by_real[1:2] + by_imag[0:1], pad], axis=1),
    ]
    port = port_ref[...] - device_index() * (rows * 128)
    port = jnp.where((port >= 0) & (port < rows * 128), port, -1)
    port = jnp.concatenate([port, jnp.full((1, 128 - ports), -1, jnp.int32)], axis=1)
    left, right = place_few(port >> 7, port & 127, terms, rows)
    total = dot_nt(left, right)
    sums = scatter(code_ref, voltage_ref, total_ref, spread_ref, 0, rows, False)
    for c in range(2):
        own_ref[c] = sums[c] + (
            total[2 * c * rows : (2 * c + 1) * rows] + total[(2 * c + 1) * rows : (2 * c + 2) * rows]
        )


def finish_kernel(own_ref, arrived_ref, asked_ref, picks_ref, out_ref):
    rows = own_ref.shape[1]
    chips = arrived_ref.shape[0]
    sub_high = lax.broadcasted_iota(jnp.int32, (rows, 128), 0)
    left = []
    for core in range(2):
        for chip in range(chips):
            here = jnp.broadcast_to(asked_ref[core, chip : chip + 1, :], (rows, 128)) == sub_high
            parts = []
            for c in range(2):
                value = jnp.broadcast_to(arrived_ref[chip, core, c : c + 1, :], (rows, 128))
                parts.extend(split(jnp.where(here, value, 0.0)))
            left.append(jnp.concatenate(parts, axis=0))
    total = dot_nt(jnp.concatenate(left, axis=1), picks_ref[...])
    for c in range(2):
        summed = own_ref[c] + (
            total[2 * c * rows : (2 * c + 1) * rows] + total[(2 * c + 1) * rows : (2 * c + 2) * rows]
        )
        for r in range(rows):
            out_ref[c : c + 1, r * 128 : (r + 1) * 128] = summed[r : r + 1]


def per_device(
    mesh_current,
    branch_entry,
    branch_sign,
    need_slots,
    resistance,
    near_blocks,
    near_source,
    basis_in,
    coupling,
    basis_out,
    admissible,
    port_mesh,
    port_coupling,
):
    chips = lax.axis_size("chips")
    peers = 2 * chips
    core = lax.axis_index("core")
    device = 2 * lax.axis_index("chips") + core
    mesh_dev = mesh_current.shape[1]
    tiles, near_count, width, _ = near_blocks.shape
    rank = basis_in.shape[1]
    far_count = admissible.shape[1]
    own_rows = mesh_dev // 128
    vmem = pl.BlockSpec(memory_space=pltpu.VMEM)
    shape = jax.ShapeDtypeStruct

    code = (branch_entry * 2 + branch_sign).reshape(2, tiles, width)
    coupling_lanes = jnp.transpose(coupling, (1, 2, 3, 0))
    basis_in_rows = basis_in.reshape(tiles * rank, width)
    basis_out_rows = basis_out.reshape(tiles * rank, width)
    half = jnp.arange(2 * tiles, dtype=jnp.int32) // tiles
    sources = jnp.transpose(near_source)
    sources = jnp.concatenate([sources, sources], axis=1) + half[None] * tiles
    band = peers * tiles // far_count
    spans = band // tiles + 1
    bases = device * tiles + jnp.arange(far_count, dtype=jnp.int32) * band
    shifted = (jnp.transpose(admissible) - bases[:, None]) % (peers * tiles)
    shifted = jnp.concatenate([shifted, shifted], axis=1)[:, None, :]
    shifted = shifted - jnp.arange(spans, dtype=jnp.int32)[None, :, None] * tiles
    inside = (shifted >= 0) & (shifted < tiles)
    targets = jnp.where(inside, shifted, -1).reshape(far_count * spans, 2 * tiles)

    def in_hbm(x):
        return pltpu.with_memory_space_constraint(x, pltpu.HBM)

    hbm = pl.BlockSpec(memory_space=pl.ANY)
    port_row = port_mesh.reshape(1, -1)
    pack_rows = (2 * own_rows + 3 + 7) // 8 * 8
    pack, mesh_near, need_near, port_near = pl.pallas_call(
        pack_kernel,
        out_shape=(
            shape((chips, pack_rows, 128), F32),
            pltpu.VMEM(mesh_current.shape, F32),
            pltpu.VMEM(need_slots.shape, jnp.int32),
            pltpu.VMEM(port_row.shape, jnp.int32),
        ),
        in_specs=[hbm] * 3,
        out_specs=(vmem,) * 4,
        scratch_shapes=[pltpu.SemaphoreType.DMA((3,))],
        compiler_params=params(),
        name="pack",
    )(in_hbm(mesh_current), in_hbm(need_slots), in_hbm(port_row))
    same = lax.all_to_all(pack, "chips", 0, 0, tiled=True)
    own_part, pairs = pl.pallas_call(
        own_lookup_kernel,
        out_shape=(
            shape((2, tiles, width), F32),
            pltpu.VMEM((far_count, rank // 2, rank, 2 * tiles), BF16),
        ),
        in_specs=[vmem] * 2 + [hbm],
        out_specs=(vmem,) * 2,
        scratch_shapes=[
            pltpu.VMEM(coupling_lanes.shape, BF16),
            pltpu.SemaphoreType.DMA((far_count,)),
        ],
        compiler_params=params(),
        cost_estimate=small_cost(),
        name="own_lookup",
    )(mesh_near, code, in_hbm(coupling_lanes))
    other = lax.ppermute(same, "core", [(0, 1), (1, 0)])
    part, same_rows = pl.pallas_call(
        functools.partial(same_core_kernel, first=own_rows),
        out_shape=(shape((2, tiles, width), F32), shape((2, chips, 128), F32)),
        in_specs=[vmem] * 4,
        out_specs=(vmem,) * 2,
        scratch_shapes=[pltpu.VMEM((2, chips, 128), F32)],
        compiler_params=params(),
        cost_estimate=small_cost(),
        name="same_core",
    )(own_part, same, need_near, code)
    current, coeff, other_rows = pl.pallas_call(
        functools.partial(current_kernel, first=own_rows),
        out_shape=(
            shape((2, tiles, width), F32),
            shape((peers, rank, 2 * tiles), BF16),
            shape((2, chips, 128), F32),
        ),
        in_specs=[vmem] * 4 + [hbm],
        out_specs=(vmem,) * 3,
        scratch_shapes=[
            pltpu.VMEM((2, chips, 128), F32),
            pltpu.VMEM(basis_in_rows.shape, BF16),
            pltpu.SemaphoreType.DMA((1,)),
        ],
        compiler_params=params(),
        name="currents",
    )(part, other, need_near, code, in_hbm(basis_in_rows))
    all_coeff = lax.all_to_all(coeff, ("chips", "core"), 0, 0, tiled=True)
    near_rows = near_blocks.reshape(tiles * near_count * width, width)
    near = pl.pallas_call(
        near_kernel,
        out_shape=shape((2, tiles, width), F32),
        in_specs=[vmem] * 2 + [hbm] * 2,
        out_specs=vmem,
        scratch_shapes=[
            pltpu.VMEM((near_count * width, 2 * tiles), BF16),
            pltpu.VMEM(near_rows.shape, BF16),
            pltpu.VMEM((tiles, width), F32),
            pltpu.SemaphoreType.DMA((tiles // 8 + 1,)),
        ],
        compiler_params=params(),
        cost_estimate=pl.CostEstimate(
            flops=256 * near_blocks.size, bytes_accessed=2 * near_blocks.size, transcendentals=0
        ),
        name="near_field",
    )(sources, current, in_hbm(resistance.reshape(tiles, width)), in_hbm(near_rows))
    voltage, slots = pl.pallas_call(
        functools.partial(voltage_kernel, first=own_rows),
        out_shape=(shape((2, tiles, width), F32), shape((peers, 2, 128), F32)),
        in_specs=[vmem] * 6,
        out_specs=(vmem,) * 2,
        scratch_shapes=[
            pltpu.VMEM((2, far_count, rank, 2 * tiles), F32),
            pltpu.VMEM((rank, 2 * tiles), F32),
            pltpu.VMEM((128, 4 * peers), F32),
            pltpu.VMEM((2, 6, 8, 128), F32),
        ],
        compiler_params=params(),
        name="voltages",
    )(
        all_coeff,
        targets,
        pairs,
        basis_out_rows,
        near,
        code,
    )
    arrived = lax.all_to_all(slots, ("chips", "core"), 0, 0, tiled=True)
    own, asked, picks = pl.pallas_call(
        own_sum_kernel,
        out_shape=(
            shape((2, own_rows, 128), F32),
            shape((2, chips, 128), jnp.int32),
            shape((128, peers * 128), BF16),
        ),
        in_specs=[vmem] * 6,
        out_specs=(vmem,) * 3,
        scratch_shapes=[
            pltpu.VMEM((4 * own_rows, 128), F32),
            pltpu.VMEM((2, 6, 8, 128), F32),
        ],
        compiler_params=params(),
        cost_estimate=small_cost(),
        name="own_sums",
    )(code, voltage, same_rows, other_rows, port_near, port_coupling)
    return pl.pallas_call(
        finish_kernel,
        out_shape=shape((2, mesh_dev), F32),
        in_specs=[vmem] * 4,
        out_specs=vmem,
        compiler_params=params(),
        name="finish",
    )(own, arrived.reshape(chips, 2, 2, 128), asked, picks)


def solution(mesh):
    groups, peers = mesh.devices.shape
    split_mesh = jax.sharding.Mesh(
        mesh.devices.reshape(groups, peers // 2, 2), ("groups", "chips", "core")
    )
    in_specs = (
        P(None, SPREAD),
        P(None, SPREAD),
        P(None, SPREAD),
        P(SPREAD, None),
        P(SPREAD),
        P(SPREAD, None, None, None),
        P(SPREAD, None),
        P(SPREAD, None, None),
        P(SPREAD, None, None, None),
        P(SPREAD, None, None),
        P(SPREAD, None),
        P("groups"),
        P(),
    )
    out_specs = P(None, SPREAD)
    return jax.shard_map(
        per_device, mesh=split_mesh, in_specs=in_specs, out_specs=out_specs, check_vma=False
    )
```

```python
import functools

import jax
import jax.numpy as jnp
from jax import lax
from jax.experimental import pallas as pl
from jax.experimental.pallas import tpu as pltpu
from jax.sharding import PartitionSpec as P

F32 = jnp.float32
BF16 = jnp.bfloat16
SPREAD = ("groups", "chips", "core")
VMEM_LIMIT = 24 * 1024 * 1024
NT = (((1,), (1,)), ((), ()))


def params():
    return pltpu.CompilerParams(vmem_limit_bytes=VMEM_LIMIT)


def small_cost():
    return pl.CostEstimate(flops=10**9, bytes_accessed=8 * 10**6, transcendentals=0)


def lane_pick(row, lanes):
    spread = jnp.broadcast_to(row, lanes.shape)
    return jnp.take_along_axis(spread, lanes, axis=1, mode="promise_in_bounds")


def dot_nt(left, right, precision=None):
    return lax.dot_general(
        left, right, NT, preferred_element_type=F32, precision=precision
    )


def device_index():
    return 2 * lax.axis_index("chips") + lax.axis_index("core")


def fetch(copies):
    for copy in copies:
        copy.start()
    for copy in copies:
        copy.wait()


def pack_kernel(
    mesh_hbm, need_hbm, port_hbm, out_ref, mesh_ref, need_ref, port_ref, sems
):
    rows = mesh_ref.shape[1] // 128
    ports = port_ref.shape[1]
    chips = out_ref.shape[0]
    fetch(
        [
            pltpu.make_async_copy(source, target, sems.at[i])
            for i, (source, target) in enumerate(
                [(mesh_hbm, mesh_ref), (need_hbm, need_ref), (port_hbm, port_ref)]
            )
        ]
    )
    port = port_ref[...] - device_index() * (rows * 128)
    port = jnp.where((port >= 0) & (port < rows * 128), port, -1)
    port = jnp.broadcast_to(jnp.concatenate([port, port], axis=1), (8, 128))
    port_high, port_low = port >> 7, port & 127
    port_value = jnp.zeros((8, 128), F32)
    lane = lax.broadcasted_iota(jnp.int32, (8, 128), 1)
    for r in range(rows):
        real_row = mesh_ref[0:1, r * 128 : (r + 1) * 128]
        imag_row = mesh_ref[1:2, r * 128 : (r + 1) * 128]
        both = jnp.where(
            lane < ports, lane_pick(real_row, port_low), lane_pick(imag_row, port_low)
        )
        port_value = jnp.where(port_high == r, both, port_value)
        for chip in range(chips):
            out_ref[chip, r : r + 1, :] = real_row
            out_ref[chip, rows + r : rows + r + 1, :] = imag_row
    need = [need_ref[pl.ds(c, chips, 2), :].astype(F32) for c in range(2)]
    first = lax.axis_index("core") == 0
    out_ref[:, 2 * rows, :] = jnp.where(first, need[0], need[1])
    out_ref[:, 2 * rows + 1, :] = jnp.where(first, need[1], need[0])
    out_ref[:, 2 * rows + 2, :] = jnp.broadcast_to(port_value[0:1], (chips, 128))
    for r in range(2 * rows + 3, out_ref.shape[1]):
        out_ref[:, r, :] = jnp.zeros((chips, 128), F32)


def ask(need_ref, pack_ref, table_ref, core, rows):
    chips = pack_ref.shape[0]
    sub = lax.broadcasted_iota(jnp.int32, (rows, 128), 0)
    for chip in range(chips):
        wanted = need_ref[pl.ds(2 * chip + core, 1), :]
        wanted = jnp.broadcast_to(jnp.maximum(wanted, 0), (rows, 128))
        here = (wanted >> 7) == sub
        low = wanted & 127
        for c in range(2):
            block = pack_ref[chip, c * rows : (c + 1) * rows, :]
            picked = jnp.take_along_axis(block, low, axis=1, mode="promise_in_bounds")
            picked = jnp.where(here, picked, 0.0)
            table_ref[c, chip : chip + 1, :] = jnp.sum(picked, axis=0, keepdims=True)


def lookup(code_ref, start, tables):
    total = [None, None]
    for k in range(2):
        code = code_ref[k, pl.ds(start, 8), :]
        high, low = code >> 8, (code >> 1) & 127
        value = [jnp.zeros((8, 128), F32), jnp.zeros((8, 128), F32)]
        for first, step, count, row_of in tables:
            offset = high - first
            for r in range(count):
                here = offset == r * step
                for c in range(2):
                    value[c] = jnp.where(here, lane_pick(row_of(r, c), low), value[c])
        along = (code & 1) == 1
        for c in range(2):
            signed = jnp.where(along, value[c], -value[c])
            total[c] = signed if k == 0 else total[c] + signed
    return total


def own_lookup_kernel(mesh_ref, code_ref, coupling_hbm, out_ref, pair_ref, raw_ref, sems):
    rows = mesh_ref.shape[1] // 128
    far_count, rank = coupling_hbm.shape[:2]
    half = rank // 2
    copies = [
        pltpu.make_async_copy(coupling_hbm.at[k], raw_ref.at[k], sems.at[k])
        for k in range(far_count)
    ]
    for k, copy in enumerate(copies):
        copy.start(priority=k % 2)

    def own_row(r, c):
        return mesh_ref[c : c + 1, r * 128 : (r + 1) * 128]

    def block(g, carry):
        start = pl.multiple_of(g * 8, 8)
        total = lookup(code_ref, start, [(0, 1, rows, own_row)])
        out_ref[0, pl.ds(start, 8), :] = total[0]
        out_ref[1, pl.ds(start, 8), :] = total[1]
        return carry

    lax.fori_loop(0, code_ref.shape[1] // 8, block, 0)
    for k in range(far_count):
        copies[k].wait()
        for r in range(half):
            pair_ref[k, r] = jnp.concatenate([raw_ref[k, r], raw_ref[k, half + r]], axis=1)


def add_peers(part_ref, pack_ref, need_ref, code_ref, table_ref, out_ref, core, first):
    chips = pack_ref.shape[0]
    ask(need_ref, pack_ref, table_ref, core, first)

    def peer_row(r, c):
        return table_ref[c, r : r + 1, :]

    def block(g, carry):
        start = pl.multiple_of(g * 8, 8)
        total = lookup(code_ref, start, [(first + core, 2, chips, peer_row)])
        for c in range(2):
            out_ref[c, pl.ds(start, 8), :] = total[c] + part_ref[c, pl.ds(start, 8), :]
        return carry

    lax.fori_loop(0, code_ref.shape[1] // 8, block, 0)


def same_core_kernel(
    part_ref, same_ref, need_ref, code_ref, out_ref, rows_ref, table_ref, *, first
):
    rows_ref[0] = same_ref[:, 2 * first, :]
    rows_ref[1] = same_ref[:, 2 * first + 2, :]
    add_peers(
        part_ref, same_ref, need_ref, code_ref, table_ref, out_ref,
        lax.axis_index("core"), first,
    )


def current_kernel(
    part_ref, other_ref, need_ref, code_ref, basis_hbm, current_ref, coeff_ref, rows_ref,
    table_ref, basis_ref, sem, *, first,
):
    tiles = code_ref.shape[1]
    rank = basis_ref.shape[0] // tiles
    copy = pltpu.make_async_copy(basis_hbm, basis_ref, sem.at[0])
    copy.start()
    rows_ref[0] = other_ref[:, 2 * first + 1, :]
    rows_ref[1] = other_ref[:, 2 * first + 2, :]
    add_peers(
        part_ref, other_ref, need_ref, code_ref, table_ref, current_ref,
        1 - lax.axis_index("core"), first,
    )
    copy.wait()
    inputs = jnp.concatenate([current_ref[0], current_ref[1]], axis=0)
    inputs = inputs.T.astype(BF16)
    lane_tile = lax.broadcasted_iota(jnp.int32, (rank, 2 * tiles), 1) % tiles
    full = jnp.dot(basis_ref[...], inputs, preferred_element_type=F32)
    chosen = jnp.zeros((rank, 2 * tiles), F32)
    for t in range(tiles):
        chosen = jnp.where(lane_tile == t, full[t * rank : (t + 1) * rank], chosen)
    coeff = chosen.astype(BF16)
    for p in range(coeff_ref.shape[0]):
        coeff_ref[p] = coeff


def near_kernel(
    source_ref, current_ref, resistance_hbm, blocks_hbm, out_ref, inputs_ref, blocks_ref,
    resistance_ref, sems,
):
    tiles = current_ref.shape[1]
    width = blocks_ref.shape[1]
    count = blocks_ref.shape[0] // (tiles * width)
    chunks = 2
    span = blocks_ref.shape[0] // chunks
    copies = [
        pltpu.make_async_copy(
            blocks_hbm.at[pl.ds(g * span, span)], blocks_ref.at[pl.ds(g * span, span)], sems.at[g]
        )
        for g in range(chunks)
    ]
    late_copy = pltpu.make_async_copy(resistance_hbm, resistance_ref, sems.at[chunks])
    for copy in copies:
        copy.start()
    late_copy.start()
    lane_tile = lax.broadcasted_iota(jnp.int32, (width, 128), 1) % tiles
    rows = jnp.concatenate([current_ref[0], current_ref[1]], axis=0)
    columns = rows.T.astype(BF16)
    row_index = lax.broadcasted_iota(jnp.int32, (128, 128), 0)
    for k in range(count):
        picks = jnp.where(row_index == source_ref[k : k + 1, :], 1.0, 0.0).astype(BF16)
        inputs_ref[k * width : (k + 1) * width, :] = jnp.dot(
            columns, picks, preferred_element_type=F32
        ).astype(BF16)
    inputs = inputs_ref[...]
    total = jnp.zeros((width, 128), F32)
    for g in range(tiles // 8):
        if g % (tiles // (8 * chunks)) == 0:
            copies[g // (tiles // (8 * chunks))].wait()
        block = jnp.concatenate(
            [
                jnp.concatenate(
                    [
                        blocks_ref[(t * count + k) * width : (t * count + k + 1) * width, :]
                        for t in range(g * 8, g * 8 + 8)
                    ],
                    axis=0,
                )
                for k in range(count)
            ],
            axis=1,
        )
        full = jnp.dot(block, inputs, preferred_element_type=F32)
        for i in range(8):
            total = jnp.where(
                lane_tile == g * 8 + i, full[i * width : (i + 1) * width], total
            )
    rows = total.T
    late_copy.wait()
    resistance = resistance_ref[...]
    out_ref[0] = resistance * current_ref[0] - rows[tiles:]
    out_ref[1] = resistance * current_ref[1] + rows[:tiles]


def split(value):
    top = value.astype(BF16)
    return top, (value - top.astype(F32)).astype(BF16)


def counts(rows):
    return lax.broadcasted_iota(jnp.int32, (rows, 128), 0).astype(F32)


def place(high, low, values, rows, spread_ref):
    sub_high, sub_low = counts(rows).astype(BF16), counts(128).astype(BF16)
    one, zero = jnp.ones((128, 128), BF16), jnp.zeros((128, 128), BF16)
    spread_ref[0] = high.astype(F32)
    spread_ref[1] = low.astype(F32)
    for c, value in enumerate(values):
        top, rest = split(value)
        spread_ref[2 + 2 * c] = top.astype(F32)
        spread_ref[3 + 2 * c] = rest.astype(F32)

    def spread(j, i, count):
        return jnp.broadcast_to(spread_ref[j, i : i + 1, :], (count, 128)).astype(BF16)

    left, right = [], []
    for i in range(8):
        here = spread(0, i, rows) == sub_high
        left.append(
            jnp.concatenate(
                [jnp.where(here, spread(j, i, rows), zero[:rows]) for j in range(2, 6)], axis=0
            )
        )
        right.append(jnp.where(spread(1, i, 128) == sub_low, one, zero))
    return jnp.concatenate(left, axis=1), jnp.concatenate(right, axis=1)


def place_few(high, low, values, rows):
    sub_high = lax.broadcasted_iota(jnp.int32, (rows, 128), 0)
    sub_low = lax.broadcasted_iota(jnp.int32, (128, 128), 0)
    left, right = [], []
    for i in range(high.shape[0]):
        here = jnp.broadcast_to(high[i : i + 1], (rows, 128)) == sub_high
        parts = []
        for value in values:
            spread = jnp.where(here, jnp.broadcast_to(value[i : i + 1], (rows, 128)), 0.0)
            parts.extend(split(spread))
        left.append(jnp.concatenate(parts, axis=0))
        there = jnp.broadcast_to(low[i : i + 1], (128, 128)) == sub_low
        right.append(jnp.where(there, 1.0, 0.0).astype(BF16))
    return jnp.concatenate(left, axis=1), jnp.concatenate(right, axis=1)


def scatter(code_ref, voltage_ref, total_ref, spread_ref, first, rows, low_streams):
    total_ref[...] = jnp.zeros_like(total_ref)

    def block(g, carry):
        start = pl.multiple_of(g * 8, 8)
        for k in range(2):
            code = code_ref[k, pl.ds(start, 8), :]
            along = (code & 1) == 1
            values = []
            for c in range(2):
                voltage = voltage_ref[c, pl.ds(start, 8), :]
                values.append(jnp.where(along, voltage, -voltage))
            left, right = place(
                (code >> 8) - first, (code >> 1) & 127, values, rows, spread_ref.at[k]
            )
            total_ref[...] += dot_nt(right, left) if low_streams else dot_nt(left, right)
        return carry

    lax.fori_loop(0, code_ref.shape[1] // 8, block, 0)
    total = total_ref[...].T if low_streams else total_ref[...]
    return [
        total[2 * c * rows : (2 * c + 1) * rows] + total[(2 * c + 1) * rows : (2 * c + 2) * rows]
        for c in range(2)
    ]


def voltage_kernel(
    coeff_ref, target_ref, coupling_ref, basis_ref, near_ref, code_ref, voltage_ref, slot_ref,
    picked_ref, mixed_ref, total_ref, spread_ref, *, first,
):
    peers, rank, lanes = coeff_ref.shape
    far_count = coupling_ref.shape[0]
    tiles = lanes // 2
    half = rank // 2
    groups = half // 4
    device = device_index()
    spans = target_ref.shape[0] // far_count
    stride = peers // far_count
    component = lax.broadcasted_iota(jnp.int32, (rank, lanes), 1) // tiles
    for k in range(far_count):
        picked = jnp.zeros((rank, lanes), F32)
        for i in range(spans):
            row = k * spans + i
            block = coeff_ref[(device + k * stride + i) % peers].astype(F32)
            target = jnp.broadcast_to(target_ref[row : row + 1, :], (rank, lanes))
            source = jnp.maximum(target, 0) + component * tiles
            value = jnp.take_along_axis(block, source, axis=1, mode="promise_in_bounds")
            picked = jnp.where(target >= 0, value, picked)
        turned = pltpu.roll(picked, tiles, 1)
        picked_ref[0, k] = jnp.where(component == 0, picked, turned)
        picked_ref[1, k] = jnp.where(component == 0, turned, picked)

    def mix(g, carry):
        total = [[None, None] for _ in range(4)]
        for k in range(far_count):
            picked = [picked_ref[c, k] for c in range(2)]
            for i in range(4):
                block = coupling_ref[k, g * 4 + i].astype(F32)
                for c in range(2):
                    product = block * picked[c]
                    part = product[0:8]
                    for q in range(8, rank, 8):
                        part = part + product[q : q + 8]
                    total[i][c] = part if k == 0 else total[i][c] + part
        for i in range(4):
            for c in range(2):
                row = jnp.sum(total[i][c], axis=0, keepdims=True)
                mixed_ref[pl.ds(c * half + g * 4 + i, 1), :] = row
        return carry

    lax.fori_loop(0, groups, mix, 0)
    mixed = mixed_ref[...].T
    mixed = jnp.concatenate([mixed[:tiles], mixed[tiles:]], axis=1).astype(BF16)
    wide = 8 * rank
    from_row = lax.broadcasted_iota(jnp.int32, (2 * rank, wide), 0)
    to_rank = lax.broadcasted_iota(jnp.int32, (2 * rank, wide), 1) % rank
    repeated = []
    for c in range(2):
        wanted = (to_rank // half) * rank + c * half + to_rank % half
        picks = jnp.where(from_row == wanted, 1.0, 0.0).astype(BF16)
        repeated.append(jnp.dot(mixed, picks, preferred_element_type=F32))
    own_block = (
        lax.broadcasted_iota(jnp.int32, (16, wide), 0) % 8
        == lax.broadcasted_iota(jnp.int32, (16, wide), 1) // rank
    )
    for g in range(tiles // 8):
        rows8 = slice(g * 8, g * 8 + 8)
        both = jnp.concatenate([repeated[0][rows8], repeated[1][rows8]], axis=0)
        both = jnp.where(own_block, both, 0.0).astype(BF16)
        far = jnp.dot(
            both, basis_ref[g * wide : (g + 1) * wide, :], preferred_element_type=F32
        )
        voltage_ref[0, rows8, :] = near_ref[0, rows8, :] - far[8:16]
        voltage_ref[1, rows8, :] = near_ref[1, rows8, :] + far[0:8]
    sums = scatter(
        code_ref, voltage_ref, total_ref, spread_ref, first, slot_ref.shape[0], True
    )
    for c in range(2):
        slot_ref[:, c, :] = sums[c]


def own_sum_kernel(
    code_ref, voltage_ref, same_ref, other_ref, port_ref, impedance_ref, own_ref, asked_ref,
    picks_ref, total_ref, spread_ref,
):
    rows = own_ref.shape[1]
    ports = impedance_ref.shape[1]
    chips = same_ref.shape[1]
    first_core = lax.axis_index("core") == 0
    same = same_ref[0].astype(jnp.int32)
    other = other_ref[0].astype(jnp.int32)
    asked = [jnp.where(first_core, same, other), jnp.where(first_core, other, same)]
    sub_low = lax.broadcasted_iota(jnp.int32, (128, 128), 0)
    for core in range(2):
        asked_ref[core] = asked[core] >> 7
        low = asked[core] & 127
        for chip in range(chips):
            there = jnp.broadcast_to(low[chip : chip + 1], (128, 128)) == sub_low
            place = core * chips + chip
            picks_ref[:, place * 128 : (place + 1) * 128] = jnp.where(there, 1.0, 0.0).astype(BF16)
    port_current = jnp.sum(same_ref[1] + other_ref[1], axis=0, keepdims=True)
    real = port_current[:, :ports]
    imag = port_current[:, ports:]
    both = jnp.concatenate([real, imag, jnp.zeros((6, ports), F32)], axis=0)
    by_real = dot_nt(both, impedance_ref[0], lax.Precision.HIGHEST)
    by_imag = dot_nt(both, impedance_ref[1], lax.Precision.HIGHEST)
    pad = jnp.zeros((1, 128 - ports), F32)
    terms = [
        jnp.concatenate([by_real[0:1] - by_imag[1:2], pad], axis=1),
        jnp.concatenate([by_real[1:2] + by_imag[0:1], pad], axis=1),
    ]
    port = port_ref[...] - device_index() * (rows * 128)
    port = jnp.where((port >= 0) & (port < rows * 128), port, -1)
    port = jnp.concatenate([port, jnp.full((1, 128 - ports), -1, jnp.int32)], axis=1)
    left, right = place_few(port >> 7, port & 127, terms, rows)
    total = dot_nt(left, right)
    sums = scatter(code_ref, voltage_ref, total_ref, spread_ref, 0, rows, False)
    for c in range(2):
        own_ref[c] = sums[c] + (
            total[2 * c * rows : (2 * c + 1) * rows] + total[(2 * c + 1) * rows : (2 * c + 2) * rows]
        )


def finish_kernel(own_ref, arrived_ref, asked_ref, picks_ref, out_ref):
    rows = own_ref.shape[1]
    chips = arrived_ref.shape[0]
    sub_high = lax.broadcasted_iota(jnp.int32, (rows, 128), 0)
    left = []
    for core in range(2):
        for chip in range(chips):
            here = jnp.broadcast_to(asked_ref[core, chip : chip + 1, :], (rows, 128)) == sub_high
            parts = []
            for c in range(2):
                value = jnp.broadcast_to(arrived_ref[chip, core, c : c + 1, :], (rows, 128))
                parts.extend(split(jnp.where(here, value, 0.0)))
            left.append(jnp.concatenate(parts, axis=0))
    total = dot_nt(jnp.concatenate(left, axis=1), picks_ref[...])
    for c in range(2):
        summed = own_ref[c] + (
            total[2 * c * rows : (2 * c + 1) * rows] + total[(2 * c + 1) * rows : (2 * c + 2) * rows]
        )
        for r in range(rows):
            out_ref[c : c + 1, r * 128 : (r + 1) * 128] = summed[r : r + 1]


def per_device(
    mesh_current,
    branch_entry,
    branch_sign,
    need_slots,
    resistance,
    near_blocks,
    near_source,
    basis_in,
    coupling,
    basis_out,
    admissible,
    port_mesh,
    port_coupling,
):
    chips = lax.axis_size("chips")
    peers = 2 * chips
    core = lax.axis_index("core")
    device = 2 * lax.axis_index("chips") + core
    mesh_dev = mesh_current.shape[1]
    tiles, near_count, width, _ = near_blocks.shape
    rank = basis_in.shape[1]
    far_count = admissible.shape[1]
    own_rows = mesh_dev // 128
    vmem = pl.BlockSpec(memory_space=pltpu.VMEM)
    shape = jax.ShapeDtypeStruct

    code = (branch_entry * 2 + branch_sign).reshape(2, tiles, width)
    coupling_lanes = jnp.transpose(coupling, (1, 2, 3, 0))
    basis_in_rows = basis_in.reshape(tiles * rank, width)
    basis_out_rows = basis_out.reshape(tiles * rank, width)
    half = jnp.arange(2 * tiles, dtype=jnp.int32) // tiles
    sources = jnp.transpose(near_source)
    sources = jnp.concatenate([sources, sources], axis=1) + half[None] * tiles
    band = peers * tiles // far_count
    spans = band // tiles + 1
    bases = device * tiles + jnp.arange(far_count, dtype=jnp.int32) * band
    shifted = (jnp.transpose(admissible) - bases[:, None]) % (peers * tiles)
    shifted = jnp.concatenate([shifted, shifted], axis=1)[:, None, :]
    shifted = shifted - jnp.arange(spans, dtype=jnp.int32)[None, :, None] * tiles
    inside = (shifted >= 0) & (shifted < tiles)
    targets = jnp.where(inside, shifted, -1).reshape(far_count * spans, 2 * tiles)

    def in_hbm(x):
        return pltpu.with_memory_space_constraint(x, pltpu.HBM)

    hbm = pl.BlockSpec(memory_space=pl.ANY)
    port_row = port_mesh.reshape(1, -1)
    pack_rows = (2 * own_rows + 3 + 7) // 8 * 8
    pack, mesh_near, need_near, port_near = pl.pallas_call(
        pack_kernel,
        out_shape=(
            shape((chips, pack_rows, 128), F32),
            pltpu.VMEM(mesh_current.shape, F32),
            pltpu.VMEM(need_slots.shape, jnp.int32),
            pltpu.VMEM(port_row.shape, jnp.int32),
        ),
        in_specs=[hbm] * 3,
        out_specs=(vmem,) * 4,
        scratch_shapes=[pltpu.SemaphoreType.DMA((3,))],
        compiler_params=params(),
        name="pack",
    )(in_hbm(mesh_current), in_hbm(need_slots), in_hbm(port_row))
    same = lax.all_to_all(pack, "chips", 0, 0, tiled=True)
    own_part, pairs = pl.pallas_call(
        own_lookup_kernel,
        out_shape=(
            shape((2, tiles, width), F32),
            pltpu.VMEM((far_count, rank // 2, rank, 2 * tiles), BF16),
        ),
        in_specs=[vmem] * 2 + [hbm],
        out_specs=(vmem,) * 2,
        scratch_shapes=[
            pltpu.VMEM(coupling_lanes.shape, BF16),
            pltpu.SemaphoreType.DMA((far_count,)),
        ],
        compiler_params=params(),
        cost_estimate=small_cost(),
        name="own_lookup",
    )(mesh_near, code, in_hbm(coupling_lanes))
    other = lax.ppermute(same, "core", [(0, 1), (1, 0)])
    part, same_rows = pl.pallas_call(
        functools.partial(same_core_kernel, first=own_rows),
        out_shape=(shape((2, tiles, width), F32), shape((2, chips, 128), F32)),
        in_specs=[vmem] * 4,
        out_specs=(vmem,) * 2,
        scratch_shapes=[pltpu.VMEM((2, chips, 128), F32)],
        compiler_params=params(),
        cost_estimate=small_cost(),
        name="same_core",
    )(own_part, same, need_near, code)
    current, coeff, other_rows = pl.pallas_call(
        functools.partial(current_kernel, first=own_rows),
        out_shape=(
            shape((2, tiles, width), F32),
            shape((peers, rank, 2 * tiles), BF16),
            shape((2, chips, 128), F32),
        ),
        in_specs=[vmem] * 4 + [hbm],
        out_specs=(vmem,) * 3,
        scratch_shapes=[
            pltpu.VMEM((2, chips, 128), F32),
            pltpu.VMEM(basis_in_rows.shape, BF16),
            pltpu.SemaphoreType.DMA((1,)),
        ],
        compiler_params=params(),
        name="currents",
    )(part, other, need_near, code, in_hbm(basis_in_rows))
    all_coeff = lax.all_to_all(coeff, ("chips", "core"), 0, 0, tiled=True)
    near_rows = near_blocks.reshape(tiles * near_count * width, width)
    near = pl.pallas_call(
        near_kernel,
        out_shape=shape((2, tiles, width), F32),
        in_specs=[vmem] * 2 + [hbm] * 2,
        out_specs=vmem,
        scratch_shapes=[
            pltpu.VMEM((near_count * width, 2 * tiles), BF16),
            pltpu.VMEM(near_rows.shape, BF16),
            pltpu.VMEM((tiles, width), F32),
            pltpu.SemaphoreType.DMA((3,)),
        ],
        compiler_params=params(),
        cost_estimate=pl.CostEstimate(
            flops=256 * near_blocks.size, bytes_accessed=2 * near_blocks.size, transcendentals=0
        ),
        name="near_field",
    )(sources, current, in_hbm(resistance.reshape(tiles, width)), in_hbm(near_rows))
    voltage, slots = pl.pallas_call(
        functools.partial(voltage_kernel, first=own_rows),
        out_shape=(shape((2, tiles, width), F32), shape((peers, 2, 128), F32)),
        in_specs=[vmem] * 6,
        out_specs=(vmem,) * 2,
        scratch_shapes=[
            pltpu.VMEM((2, far_count, rank, 2 * tiles), F32),
            pltpu.VMEM((rank, 2 * tiles), F32),
            pltpu.VMEM((128, 4 * peers), F32),
            pltpu.VMEM((2, 6, 8, 128), F32),
        ],
        compiler_params=params(),
        name="voltages",
    )(
        all_coeff,
        targets,
        pairs,
        basis_out_rows,
        near,
        code,
    )
    arrived = lax.all_to_all(slots, ("chips", "core"), 0, 0, tiled=True)
    own, asked, picks = pl.pallas_call(
        own_sum_kernel,
        out_shape=(
            shape((2, own_rows, 128), F32),
            shape((2, chips, 128), jnp.int32),
            shape((128, peers * 128), BF16),
        ),
        in_specs=[vmem] * 6,
        out_specs=(vmem,) * 3,
        scratch_shapes=[
            pltpu.VMEM((4 * own_rows, 128), F32),
            pltpu.VMEM((2, 6, 8, 128), F32),
        ],
        compiler_params=params(),
        cost_estimate=small_cost(),
        name="own_sums",
    )(code, voltage, same_rows, other_rows, port_near, port_coupling)
    return pl.pallas_call(
        finish_kernel,
        out_shape=shape((2, mesh_dev), F32),
        in_specs=[vmem] * 4,
        out_specs=vmem,
        compiler_params=params(),
        name="finish",
    )(own, arrived.reshape(chips, 2, 2, 128), asked, picks)


def solution(mesh):
    groups, peers = mesh.devices.shape
    split_mesh = jax.sharding.Mesh(
        mesh.devices.reshape(groups, peers // 2, 2), ("groups", "chips", "core")
    )
    in_specs = (
        P(None, SPREAD),
        P(None, SPREAD),
        P(None, SPREAD),
        P(SPREAD, None),
        P(SPREAD),
        P(SPREAD, None, None, None),
        P(SPREAD, None),
        P(SPREAD, None, None),
        P(SPREAD, None, None, None),
        P(SPREAD, None, None),
        P(SPREAD, None),
        P("groups"),
        P(),
    )
    out_specs = P(None, SPREAD)
    return jax.shard_map(
        per_device, mesh=split_mesh, in_specs=in_specs, out_specs=out_specs, check_vma=False
    )
```

```python
import functools

import jax
import jax.numpy as jnp
from jax import lax
from jax.experimental import pallas as pl
from jax.experimental.pallas import tpu as pltpu
from jax.sharding import PartitionSpec as P

F32 = jnp.float32
BF16 = jnp.bfloat16
SPREAD = ("groups", "chips", "core")
VMEM_LIMIT = 24 * 1024 * 1024
NT = (((1,), (1,)), ((), ()))


def params():
    return pltpu.CompilerParams(vmem_limit_bytes=VMEM_LIMIT)


def small_cost():
    return pl.CostEstimate(flops=10**9, bytes_accessed=8 * 10**6, transcendentals=0)


def lane_pick(row, lanes):
    spread = jnp.broadcast_to(row, lanes.shape)
    return jnp.take_along_axis(spread, lanes, axis=1, mode="promise_in_bounds")


def dot_nt(left, right, precision=None):
    return lax.dot_general(
        left, right, NT, preferred_element_type=F32, precision=precision
    )


def device_index():
    return 2 * lax.axis_index("chips") + lax.axis_index("core")


def fetch(copies):
    for copy in copies:
        copy.start()
    for copy in copies:
        copy.wait()


def pack_kernel(
    mesh_hbm, need_hbm, port_hbm, out_ref, mesh_ref, need_ref, port_ref, sems
):
    rows = mesh_ref.shape[1] // 128
    ports = port_ref.shape[1]
    chips = out_ref.shape[0]
    fetch(
        [
            pltpu.make_async_copy(source, target, sems.at[i])
            for i, (source, target) in enumerate(
                [(mesh_hbm, mesh_ref), (need_hbm, need_ref), (port_hbm, port_ref)]
            )
        ]
    )
    port = port_ref[...] - device_index() * (rows * 128)
    port = jnp.where((port >= 0) & (port < rows * 128), port, -1)
    port = jnp.broadcast_to(jnp.concatenate([port, port], axis=1), (8, 128))
    port_high, port_low = port >> 7, port & 127
    port_value = jnp.zeros((8, 128), F32)
    lane = lax.broadcasted_iota(jnp.int32, (8, 128), 1)
    for r in range(rows):
        real_row = mesh_ref[0:1, r * 128 : (r + 1) * 128]
        imag_row = mesh_ref[1:2, r * 128 : (r + 1) * 128]
        both = jnp.where(
            lane < ports, lane_pick(real_row, port_low), lane_pick(imag_row, port_low)
        )
        port_value = jnp.where(port_high == r, both, port_value)
        for chip in range(chips):
            out_ref[chip, r : r + 1, :] = real_row
            out_ref[chip, rows + r : rows + r + 1, :] = imag_row
    need = [need_ref[pl.ds(c, chips, 2), :].astype(F32) for c in range(2)]
    first = lax.axis_index("core") == 0
    out_ref[:, 2 * rows, :] = jnp.where(first, need[0], need[1])
    out_ref[:, 2 * rows + 1, :] = jnp.where(first, need[1], need[0])
    out_ref[:, 2 * rows + 2, :] = jnp.broadcast_to(port_value[0:1], (chips, 128))
    for r in range(2 * rows + 3, out_ref.shape[1]):
        out_ref[:, r, :] = jnp.zeros((chips, 128), F32)


def ask(need_ref, pack_ref, table_ref, core, rows):
    chips = pack_ref.shape[0]
    sub = lax.broadcasted_iota(jnp.int32, (rows, 128), 0)
    for chip in range(chips):
        wanted = need_ref[pl.ds(2 * chip + core, 1), :]
        wanted = jnp.broadcast_to(jnp.maximum(wanted, 0), (rows, 128))
        here = (wanted >> 7) == sub
        low = wanted & 127
        for c in range(2):
            block = pack_ref[chip, c * rows : (c + 1) * rows, :]
            picked = jnp.take_along_axis(block, low, axis=1, mode="promise_in_bounds")
            picked = jnp.where(here, picked, 0.0)
            table_ref[c, chip : chip + 1, :] = jnp.sum(picked, axis=0, keepdims=True)


def lookup(code_ref, start, tables):
    total = [None, None]
    for k in range(2):
        code = code_ref[k, pl.ds(start, 8), :]
        high, low = code >> 8, (code >> 1) & 127
        value = [jnp.zeros((8, 128), F32), jnp.zeros((8, 128), F32)]
        for first, step, count, row_of in tables:
            offset = high - first
            for r in range(count):
                here = offset == r * step
                for c in range(2):
                    value[c] = jnp.where(here, lane_pick(row_of(r, c), low), value[c])
        along = (code & 1) == 1
        for c in range(2):
            signed = jnp.where(along, value[c], -value[c])
            total[c] = signed if k == 0 else total[c] + signed
    return total


def own_lookup_kernel(mesh_ref, code_ref, coupling_hbm, out_ref, pair_ref, raw_ref, sems):
    rows = mesh_ref.shape[1] // 128
    far_count, rank = coupling_hbm.shape[:2]
    half = rank // 2
    part = far_count // 2
    copies = [
        pltpu.make_async_copy(
            coupling_hbm.at[pl.ds(i * part, part)], raw_ref.at[pl.ds(i * part, part)], sems.at[i]
        )
        for i in range(2)
    ]
    for copy in copies:
        copy.start()

    def own_row(r, c):
        return mesh_ref[c : c + 1, r * 128 : (r + 1) * 128]

    def block(g, carry):
        start = pl.multiple_of(g * 8, 8)
        total = lookup(code_ref, start, [(0, 1, rows, own_row)])
        out_ref[0, pl.ds(start, 8), :] = total[0]
        out_ref[1, pl.ds(start, 8), :] = total[1]
        return carry

    lax.fori_loop(0, code_ref.shape[1] // 8, block, 0, unroll=True)
    for k in range(far_count):
        if k % part == 0:
            copies[k // part].wait()
        for r in range(half):
            pair_ref[k, r] = jnp.concatenate([raw_ref[k, r], raw_ref[k, half + r]], axis=1)


def add_peers(part_ref, pack_ref, need_ref, code_ref, table_ref, out_ref, core, first):
    chips = pack_ref.shape[0]
    ask(need_ref, pack_ref, table_ref, core, first)

    def peer_row(r, c):
        return table_ref[c, r : r + 1, :]

    def block(g, carry):
        start = pl.multiple_of(g * 8, 8)
        total = lookup(code_ref, start, [(first + core, 2, chips, peer_row)])
        for c in range(2):
            out_ref[c, pl.ds(start, 8), :] = total[c] + part_ref[c, pl.ds(start, 8), :]
        return carry

    lax.fori_loop(0, code_ref.shape[1] // 8, block, 0, unroll=True)


def same_core_kernel(
    part_ref, same_ref, need_ref, code_ref, out_ref, rows_ref, table_ref, *, first
):
    rows_ref[0] = same_ref[:, 2 * first, :]
    rows_ref[1] = same_ref[:, 2 * first + 2, :]
    add_peers(
        part_ref, same_ref, need_ref, code_ref, table_ref, out_ref,
        lax.axis_index("core"), first,
    )


def current_kernel(
    part_ref, other_ref, need_ref, code_ref, basis_hbm, current_ref, coeff_ref, rows_ref,
    table_ref, basis_ref, sem, *, first,
):
    tiles = code_ref.shape[1]
    rank = basis_ref.shape[0] // tiles
    copy = pltpu.make_async_copy(basis_hbm, basis_ref, sem.at[0])
    copy.start()
    rows_ref[0] = other_ref[:, 2 * first + 1, :]
    rows_ref[1] = other_ref[:, 2 * first + 2, :]
    add_peers(
        part_ref, other_ref, need_ref, code_ref, table_ref, current_ref,
        1 - lax.axis_index("core"), first,
    )
    copy.wait()
    inputs = jnp.concatenate([current_ref[0], current_ref[1]], axis=0)
    inputs = inputs.T.astype(BF16)
    lane_tile = lax.broadcasted_iota(jnp.int32, (rank, 2 * tiles), 1) % tiles
    full = jnp.dot(basis_ref[...], inputs, preferred_element_type=F32)
    chosen = jnp.zeros((rank, 2 * tiles), F32)
    for t in range(tiles):
        chosen = jnp.where(lane_tile == t, full[t * rank : (t + 1) * rank], chosen)
    coeff = chosen.astype(BF16)
    for p in range(coeff_ref.shape[0]):
        coeff_ref[p] = coeff


def near_kernel(
    source_ref, current_ref, resistance_hbm, blocks_hbm, out_ref, inputs_ref, blocks_ref,
    resistance_ref, sems,
):
    tiles = current_ref.shape[1]
    width = blocks_ref.shape[1]
    count = blocks_ref.shape[0] // (tiles * width)
    chunks = 2
    span = blocks_ref.shape[0] // chunks
    copies = [
        pltpu.make_async_copy(
            blocks_hbm.at[pl.ds(g * span, span)], blocks_ref.at[pl.ds(g * span, span)], sems.at[g]
        )
        for g in range(chunks)
    ]
    late_copy = pltpu.make_async_copy(resistance_hbm, resistance_ref, sems.at[chunks])
    for copy in copies:
        copy.start()
    late_copy.start()
    lane_tile = lax.broadcasted_iota(jnp.int32, (width, 128), 1) % tiles
    rows = jnp.concatenate([current_ref[0], current_ref[1]], axis=0)
    columns = rows.T.astype(BF16)
    row_index = lax.broadcasted_iota(jnp.int32, (128, 128), 0)
    for k in range(count):
        picks = jnp.where(row_index == source_ref[k : k + 1, :], 1.0, 0.0).astype(BF16)
        inputs_ref[k * width : (k + 1) * width, :] = jnp.dot(
            columns, picks, preferred_element_type=F32
        ).astype(BF16)
    inputs = inputs_ref[...]
    total = jnp.zeros((width, 128), F32)
    for g in range(tiles // 8):
        if g % (tiles // (8 * chunks)) == 0:
            copies[g // (tiles // (8 * chunks))].wait()
        block = jnp.concatenate(
            [
                jnp.concatenate(
                    [
                        blocks_ref[(t * count + k) * width : (t * count + k + 1) * width, :]
                        for t in range(g * 8, g * 8 + 8)
                    ],
                    axis=0,
                )
                for k in range(count)
            ],
            axis=1,
        )
        full = jnp.dot(block, inputs, preferred_element_type=F32)
        for i in range(8):
            total = jnp.where(
                lane_tile == g * 8 + i, full[i * width : (i + 1) * width], total
            )
    rows = total.T
    late_copy.wait()
    resistance = resistance_ref[...]
    out_ref[0] = resistance * current_ref[0] - rows[tiles:]
    out_ref[1] = resistance * current_ref[1] + rows[:tiles]


def split(value):
    top = value.astype(BF16)
    return top, (value - top.astype(F32)).astype(BF16)


def counts(rows):
    return lax.broadcasted_iota(jnp.int32, (rows, 128), 0).astype(F32)


def place(high, low, values, rows, spread_ref):
    sub_high, sub_low = counts(rows).astype(BF16), counts(128).astype(BF16)
    one, zero = jnp.ones((128, 128), BF16), jnp.zeros((128, 128), BF16)
    spread_ref[0] = high.astype(F32)
    spread_ref[1] = low.astype(F32)
    for c, value in enumerate(values):
        top, rest = split(value)
        spread_ref[2 + 2 * c] = top.astype(F32)
        spread_ref[3 + 2 * c] = rest.astype(F32)

    def spread(j, i, count):
        return jnp.broadcast_to(spread_ref[j, i : i + 1, :], (count, 128)).astype(BF16)

    left, right = [], []
    for i in range(8):
        here = spread(0, i, rows) == sub_high
        left.append(
            jnp.concatenate(
                [jnp.where(here, spread(j, i, rows), zero[:rows]) for j in range(2, 6)], axis=0
            )
        )
        right.append(jnp.where(spread(1, i, 128) == sub_low, one, zero))
    return jnp.concatenate(left, axis=1), jnp.concatenate(right, axis=1)


def place_few(high, low, values, rows):
    sub_high = lax.broadcasted_iota(jnp.int32, (rows, 128), 0)
    sub_low = lax.broadcasted_iota(jnp.int32, (128, 128), 0)
    left, right = [], []
    for i in range(high.shape[0]):
        here = jnp.broadcast_to(high[i : i + 1], (rows, 128)) == sub_high
        parts = []
        for value in values:
            spread = jnp.where(here, jnp.broadcast_to(value[i : i + 1], (rows, 128)), 0.0)
            parts.extend(split(spread))
        left.append(jnp.concatenate(parts, axis=0))
        there = jnp.broadcast_to(low[i : i + 1], (128, 128)) == sub_low
        right.append(jnp.where(there, 1.0, 0.0).astype(BF16))
    return jnp.concatenate(left, axis=1), jnp.concatenate(right, axis=1)


def scatter(code_ref, voltage_ref, spread_ref, first, rows, low_streams):
    total = None
    for g in range(code_ref.shape[1] // 8):
        for k in range(2):
            code = code_ref[k, g * 8 : g * 8 + 8, :]
            along = (code & 1) == 1
            values = []
            for c in range(2):
                voltage = voltage_ref[c, g * 8 : g * 8 + 8, :]
                values.append(jnp.where(along, voltage, -voltage))
            left, right = place(
                (code >> 8) - first, (code >> 1) & 127, values, rows, spread_ref.at[g, k]
            )
            term = dot_nt(right, left) if low_streams else dot_nt(left, right)
            total = term if total is None else total + term
    total = total.T if low_streams else total
    return [
        total[2 * c * rows : (2 * c + 1) * rows] + total[(2 * c + 1) * rows : (2 * c + 2) * rows]
        for c in range(2)
    ]


def voltage_kernel(
    coeff_ref, target_ref, coupling_ref, basis_ref, near_ref, code_ref, voltage_ref, slot_ref,
    picked_ref, mixed_ref, spread_ref, *, first,
):
    peers, rank, lanes = coeff_ref.shape
    far_count = coupling_ref.shape[0]
    tiles = lanes // 2
    half = rank // 2
    groups = half // 4
    device = device_index()
    spans = target_ref.shape[0] // far_count
    stride = peers // far_count
    component = lax.broadcasted_iota(jnp.int32, (rank, lanes), 1) // tiles
    for k in range(far_count):
        picked = jnp.zeros((rank, lanes), F32)
        for i in range(spans):
            row = k * spans + i
            block = coeff_ref[(device + k * stride + i) % peers].astype(F32)
            target = jnp.broadcast_to(target_ref[row : row + 1, :], (rank, lanes))
            source = jnp.maximum(target, 0) + component * tiles
            value = jnp.take_along_axis(block, source, axis=1, mode="promise_in_bounds")
            picked = jnp.where(target >= 0, value, picked)
        turned = pltpu.roll(picked, tiles, 1)
        picked_ref[0, k] = jnp.where(component == 0, picked, turned)
        picked_ref[1, k] = jnp.where(component == 0, turned, picked)

    def mix(g, carry):
        total = [[None, None] for _ in range(4)]
        for k in range(far_count):
            picked = [picked_ref[c, k] for c in range(2)]
            for i in range(4):
                block = coupling_ref[k, g * 4 + i].astype(F32)
                for c in range(2):
                    product = block * picked[c]
                    part = product[0:8]
                    for q in range(8, rank, 8):
                        part = part + product[q : q + 8]
                    total[i][c] = part if k == 0 else total[i][c] + part
        for i in range(4):
            for c in range(2):
                row = jnp.sum(total[i][c], axis=0, keepdims=True)
                mixed_ref[pl.ds(c * half + g * 4 + i, 1), :] = row
        return carry

    lax.fori_loop(0, groups, mix, 0, unroll=True)
    mixed = mixed_ref[...].T
    mixed = jnp.concatenate([mixed[:tiles], mixed[tiles:]], axis=1).astype(BF16)
    wide = 8 * rank
    from_row = lax.broadcasted_iota(jnp.int32, (2 * rank, wide), 0)
    to_rank = lax.broadcasted_iota(jnp.int32, (2 * rank, wide), 1) % rank
    repeated = []
    for c in range(2):
        wanted = (to_rank // half) * rank + c * half + to_rank % half
        picks = jnp.where(from_row == wanted, 1.0, 0.0).astype(BF16)
        repeated.append(jnp.dot(mixed, picks, preferred_element_type=F32))
    own_block = (
        lax.broadcasted_iota(jnp.int32, (16, wide), 0) % 8
        == lax.broadcasted_iota(jnp.int32, (16, wide), 1) // rank
    )
    for g in range(tiles // 8):
        rows8 = slice(g * 8, g * 8 + 8)
        both = jnp.concatenate([repeated[0][rows8], repeated[1][rows8]], axis=0)
        both = jnp.where(own_block, both, 0.0).astype(BF16)
        far = jnp.dot(
            both, basis_ref[g * wide : (g + 1) * wide, :], preferred_element_type=F32
        )
        voltage_ref[0, rows8, :] = near_ref[0, rows8, :] - far[8:16]
        voltage_ref[1, rows8, :] = near_ref[1, rows8, :] + far[0:8]
    sums = scatter(
        code_ref, voltage_ref, spread_ref, first, slot_ref.shape[0], True
    )
    for c in range(2):
        slot_ref[:, c, :] = sums[c]


def own_sum_kernel(
    code_ref, voltage_ref, same_ref, other_ref, port_ref, impedance_ref, own_ref, asked_ref,
    picks_ref, spread_ref,
):
    rows = own_ref.shape[1]
    ports = impedance_ref.shape[1]
    chips = same_ref.shape[1]
    first_core = lax.axis_index("core") == 0
    same = same_ref[0].astype(jnp.int32)
    other = other_ref[0].astype(jnp.int32)
    asked = [jnp.where(first_core, same, other), jnp.where(first_core, other, same)]
    sub_low = lax.broadcasted_iota(jnp.int32, (128, 128), 0)
    for core in range(2):
        asked_ref[core] = asked[core] >> 7
        low = asked[core] & 127
        for chip in range(chips):
            there = jnp.broadcast_to(low[chip : chip + 1], (128, 128)) == sub_low
            place = core * chips + chip
            picks_ref[:, place * 128 : (place + 1) * 128] = jnp.where(there, 1.0, 0.0).astype(BF16)
    port_current = jnp.sum(same_ref[1] + other_ref[1], axis=0, keepdims=True)
    real = port_current[:, :ports]
    imag = port_current[:, ports:]
    both = jnp.concatenate([real, imag, jnp.zeros((6, ports), F32)], axis=0)
    by_real = dot_nt(both, impedance_ref[0], lax.Precision.HIGHEST)
    by_imag = dot_nt(both, impedance_ref[1], lax.Precision.HIGHEST)
    pad = jnp.zeros((1, 128 - ports), F32)
    terms = [
        jnp.concatenate([by_real[0:1] - by_imag[1:2], pad], axis=1),
        jnp.concatenate([by_real[1:2] + by_imag[0:1], pad], axis=1),
    ]
    port = port_ref[...] - device_index() * (rows * 128)
    port = jnp.where((port >= 0) & (port < rows * 128), port, -1)
    port = jnp.concatenate([port, jnp.full((1, 128 - ports), -1, jnp.int32)], axis=1)
    left, right = place_few(port >> 7, port & 127, terms, rows)
    total = dot_nt(left, right)
    sums = scatter(code_ref, voltage_ref, spread_ref, 0, rows, False)
    for c in range(2):
        own_ref[c] = sums[c] + (
            total[2 * c * rows : (2 * c + 1) * rows] + total[(2 * c + 1) * rows : (2 * c + 2) * rows]
        )


def finish_kernel(own_ref, arrived_ref, asked_ref, picks_ref, out_ref):
    rows = own_ref.shape[1]
    chips = arrived_ref.shape[0]
    sub_high = lax.broadcasted_iota(jnp.int32, (rows, 128), 0)
    left = []
    for core in range(2):
        for chip in range(chips):
            here = jnp.broadcast_to(asked_ref[core, chip : chip + 1, :], (rows, 128)) == sub_high
            parts = []
            for c in range(2):
                value = jnp.broadcast_to(arrived_ref[chip, core, c : c + 1, :], (rows, 128))
                parts.extend(split(jnp.where(here, value, 0.0)))
            left.append(jnp.concatenate(parts, axis=0))
    total = dot_nt(jnp.concatenate(left, axis=1), picks_ref[...])
    for c in range(2):
        summed = own_ref[c] + (
            total[2 * c * rows : (2 * c + 1) * rows] + total[(2 * c + 1) * rows : (2 * c + 2) * rows]
        )
        for r in range(rows):
            out_ref[c : c + 1, r * 128 : (r + 1) * 128] = summed[r : r + 1]


def per_device(
    mesh_current,
    branch_entry,
    branch_sign,
    need_slots,
    resistance,
    near_blocks,
    near_source,
    basis_in,
    coupling,
    basis_out,
    admissible,
    port_mesh,
    port_coupling,
):
    chips = lax.axis_size("chips")
    peers = 2 * chips
    core = lax.axis_index("core")
    device = 2 * lax.axis_index("chips") + core
    mesh_dev = mesh_current.shape[1]
    tiles, near_count, width, _ = near_blocks.shape
    rank = basis_in.shape[1]
    far_count = admissible.shape[1]
    own_rows = mesh_dev // 128
    vmem = pl.BlockSpec(memory_space=pltpu.VMEM)
    shape = jax.ShapeDtypeStruct

    code = (branch_entry * 2 + branch_sign).reshape(2, tiles, width)
    coupling_lanes = jnp.transpose(coupling, (1, 2, 3, 0))
    basis_in_rows = basis_in.reshape(tiles * rank, width)
    basis_out_rows = basis_out.reshape(tiles * rank, width)
    half = jnp.arange(2 * tiles, dtype=jnp.int32) // tiles
    sources = jnp.transpose(near_source)
    sources = jnp.concatenate([sources, sources], axis=1) + half[None] * tiles
    band = peers * tiles // far_count
    spans = band // tiles + 1
    bases = device * tiles + jnp.arange(far_count, dtype=jnp.int32) * band
    shifted = (jnp.transpose(admissible) - bases[:, None]) % (peers * tiles)
    shifted = jnp.concatenate([shifted, shifted], axis=1)[:, None, :]
    shifted = shifted - jnp.arange(spans, dtype=jnp.int32)[None, :, None] * tiles
    inside = (shifted >= 0) & (shifted < tiles)
    targets = jnp.where(inside, shifted, -1).reshape(far_count * spans, 2 * tiles)

    def in_hbm(x):
        return pltpu.with_memory_space_constraint(x, pltpu.HBM)

    hbm = pl.BlockSpec(memory_space=pl.ANY)
    port_row = port_mesh.reshape(1, -1)
    pack_rows = (2 * own_rows + 3 + 7) // 8 * 8
    pack, mesh_near, need_near, port_near = pl.pallas_call(
        pack_kernel,
        out_shape=(
            shape((chips, pack_rows, 128), F32),
            pltpu.VMEM(mesh_current.shape, F32),
            pltpu.VMEM(need_slots.shape, jnp.int32),
            pltpu.VMEM(port_row.shape, jnp.int32),
        ),
        in_specs=[hbm] * 3,
        out_specs=(vmem,) * 4,
        scratch_shapes=[pltpu.SemaphoreType.DMA((3,))],
        compiler_params=params(),
        name="pack",
    )(in_hbm(mesh_current), in_hbm(need_slots), in_hbm(port_row))
    same = lax.all_to_all(pack, "chips", 0, 0, tiled=True)
    own_part, pairs = pl.pallas_call(
        own_lookup_kernel,
        out_shape=(
            shape((2, tiles, width), F32),
            pltpu.VMEM((far_count, rank // 2, rank, 2 * tiles), BF16),
        ),
        in_specs=[vmem] * 2 + [hbm],
        out_specs=(vmem,) * 2,
        scratch_shapes=[
            pltpu.VMEM(coupling_lanes.shape, BF16),
            pltpu.SemaphoreType.DMA((2,)),
        ],
        compiler_params=params(),
        cost_estimate=small_cost(),
        name="own_lookup",
    )(mesh_near, code, in_hbm(coupling_lanes))
    other = lax.ppermute(same, "core", [(0, 1), (1, 0)])
    part, same_rows = pl.pallas_call(
        functools.partial(same_core_kernel, first=own_rows),
        out_shape=(shape((2, tiles, width), F32), shape((2, chips, 128), F32)),
        in_specs=[vmem] * 4,
        out_specs=(vmem,) * 2,
        scratch_shapes=[pltpu.VMEM((2, chips, 128), F32)],
        compiler_params=params(),
        cost_estimate=small_cost(),
        name="same_core",
    )(own_part, same, need_near, code)
    current, coeff, other_rows = pl.pallas_call(
        functools.partial(current_kernel, first=own_rows),
        out_shape=(
            shape((2, tiles, width), F32),
            shape((peers, rank, 2 * tiles), BF16),
            shape((2, chips, 128), F32),
        ),
        in_specs=[vmem] * 4 + [hbm],
        out_specs=(vmem,) * 3,
        scratch_shapes=[
            pltpu.VMEM((2, chips, 128), F32),
            pltpu.VMEM(basis_in_rows.shape, BF16),
            pltpu.SemaphoreType.DMA((1,)),
        ],
        compiler_params=params(),
        name="currents",
    )(part, other, need_near, code, in_hbm(basis_in_rows))
    all_coeff = lax.all_to_all(coeff, ("chips", "core"), 0, 0, tiled=True)
    near_rows = near_blocks.reshape(tiles * near_count * width, width)
    near = pl.pallas_call(
        near_kernel,
        out_shape=shape((2, tiles, width), F32),
        in_specs=[vmem] * 2 + [hbm] * 2,
        out_specs=vmem,
        scratch_shapes=[
            pltpu.VMEM((near_count * width, 2 * tiles), BF16),
            pltpu.VMEM(near_rows.shape, BF16),
            pltpu.VMEM((tiles, width), F32),
            pltpu.SemaphoreType.DMA((3,)),
        ],
        compiler_params=params(),
        cost_estimate=pl.CostEstimate(
            flops=256 * near_blocks.size, bytes_accessed=2 * near_blocks.size, transcendentals=0
        ),
        name="near_field",
    )(sources, current, in_hbm(resistance.reshape(tiles, width)), in_hbm(near_rows))
    voltage, slots = pl.pallas_call(
        functools.partial(voltage_kernel, first=own_rows),
        out_shape=(shape((2, tiles, width), F32), shape((peers, 2, 128), F32)),
        in_specs=[vmem] * 6,
        out_specs=(vmem,) * 2,
        scratch_shapes=[
            pltpu.VMEM((2, far_count, rank, 2 * tiles), F32),
            pltpu.VMEM((rank, 2 * tiles), F32),
            pltpu.VMEM((tiles // 8, 2, 6, 8, 128), F32),
        ],
        compiler_params=params(),
        name="voltages",
    )(
        all_coeff,
        targets,
        pairs,
        basis_out_rows,
        near,
        code,
    )
    arrived = lax.all_to_all(slots, ("chips", "core"), 0, 0, tiled=True)
    own, asked, picks = pl.pallas_call(
        own_sum_kernel,
        out_shape=(
            shape((2, own_rows, 128), F32),
            shape((2, chips, 128), jnp.int32),
            shape((128, peers * 128), BF16),
        ),
        in_specs=[vmem] * 6,
        out_specs=(vmem,) * 3,
        scratch_shapes=[
            pltpu.VMEM((tiles // 8, 2, 6, 8, 128), F32),
        ],
        compiler_params=params(),
        cost_estimate=small_cost(),
        name="own_sums",
    )(code, voltage, same_rows, other_rows, port_near, port_coupling)
    return pl.pallas_call(
        finish_kernel,
        out_shape=shape((2, mesh_dev), F32),
        in_specs=[vmem] * 4,
        out_specs=vmem,
        compiler_params=params(),
        name="finish",
    )(own, arrived.reshape(chips, 2, 2, 128), asked, picks)


def solution(mesh):
    groups, peers = mesh.devices.shape
    split_mesh = jax.sharding.Mesh(
        mesh.devices.reshape(groups, peers // 2, 2), ("groups", "chips", "core")
    )
    in_specs = (
        P(None, SPREAD),
        P(None, SPREAD),
        P(None, SPREAD),
        P(SPREAD, None),
        P(SPREAD),
        P(SPREAD, None, None, None),
        P(SPREAD, None),
        P(SPREAD, None, None),
        P(SPREAD, None, None, None),
        P(SPREAD, None, None),
        P(SPREAD, None),
        P("groups"),
        P(),
    )
    out_specs = P(None, SPREAD)
    return jax.shard_map(
        per_device, mesh=split_mesh, in_specs=in_specs, out_specs=out_specs, check_vma=False
    )
```

```python
import functools

import jax
import jax.numpy as jnp
from jax import lax
from jax.experimental import pallas as pl
from jax.experimental.pallas import tpu as pltpu
from jax.sharding import PartitionSpec as P

F32 = jnp.float32
BF16 = jnp.bfloat16
SPREAD = ("groups", "chips", "core")
VMEM_LIMIT = 24 * 1024 * 1024
NT = (((1,), (1,)), ((), ()))


def params():
    return pltpu.CompilerParams(vmem_limit_bytes=VMEM_LIMIT)


def small_cost():
    return pl.CostEstimate(flops=10**9, bytes_accessed=8 * 10**6, transcendentals=0)


def lane_pick(row, lanes):
    spread = jnp.broadcast_to(row, lanes.shape)
    return jnp.take_along_axis(spread, lanes, axis=1, mode="promise_in_bounds")


def dot_nt(left, right, precision=None):
    return lax.dot_general(
        left, right, NT, preferred_element_type=F32, precision=precision
    )


def device_index():
    return 2 * lax.axis_index("chips") + lax.axis_index("core")


def fetch(copies):
    for copy in copies:
        copy.start()
    for copy in copies:
        copy.wait()


def pack_kernel(
    mesh_hbm, need_hbm, port_hbm, out_ref, mesh_ref, need_ref, port_ref, sems
):
    rows = mesh_ref.shape[1] // 128
    ports = port_ref.shape[1]
    chips = out_ref.shape[0]
    fetch(
        [
            pltpu.make_async_copy(source, target, sems.at[i])
            for i, (source, target) in enumerate(
                [(mesh_hbm, mesh_ref), (need_hbm, need_ref), (port_hbm, port_ref)]
            )
        ]
    )
    port = port_ref[...] - device_index() * (rows * 128)
    port = jnp.where((port >= 0) & (port < rows * 128), port, -1)
    port = jnp.broadcast_to(jnp.concatenate([port, port], axis=1), (8, 128))
    port_high, port_low = port >> 7, port & 127
    port_value = jnp.zeros((8, 128), F32)
    lane = lax.broadcasted_iota(jnp.int32, (8, 128), 1)
    for r in range(rows):
        real_row = mesh_ref[0:1, r * 128 : (r + 1) * 128]
        imag_row = mesh_ref[1:2, r * 128 : (r + 1) * 128]
        both = jnp.where(
            lane < ports, lane_pick(real_row, port_low), lane_pick(imag_row, port_low)
        )
        port_value = jnp.where(port_high == r, both, port_value)
        out_ref[0, r : r + 1, :] = real_row
        out_ref[0, rows + r : rows + r + 1, :] = imag_row
    block = out_ref[0, : 2 * rows, :]
    for chip in range(1, chips):
        out_ref[chip, : 2 * rows, :] = block
    need = [need_ref[pl.ds(c, chips, 2), :].astype(F32) for c in range(2)]
    first = lax.axis_index("core") == 0
    out_ref[:, 2 * rows, :] = jnp.where(first, need[0], need[1])
    out_ref[:, 2 * rows + 1, :] = jnp.where(first, need[1], need[0])
    out_ref[:, 2 * rows + 2, :] = jnp.broadcast_to(port_value[0:1], (chips, 128))
    for r in range(2 * rows + 3, out_ref.shape[1]):
        out_ref[:, r, :] = jnp.zeros((chips, 128), F32)


def ask(need_ref, pack_ref, table_ref, core, rows):
    chips = pack_ref.shape[0]
    sub = lax.broadcasted_iota(jnp.int32, (rows, 128), 0)
    for chip in range(chips):
        wanted = need_ref[pl.ds(2 * chip + core, 1), :]
        wanted = jnp.broadcast_to(jnp.maximum(wanted, 0), (rows, 128))
        here = (wanted >> 7) == sub
        low = wanted & 127
        for c in range(2):
            block = pack_ref[chip, c * rows : (c + 1) * rows, :]
            picked = jnp.take_along_axis(block, low, axis=1, mode="promise_in_bounds")
            picked = jnp.where(here, picked, 0.0)
            table_ref[c, chip : chip + 1, :] = jnp.sum(picked, axis=0, keepdims=True)


def lookup(code_ref, start, tables):
    total = [None, None]
    for k in range(2):
        code = code_ref[k, pl.ds(start, 8), :]
        high, low = code >> 8, (code >> 1) & 127
        value = [jnp.zeros((8, 128), F32), jnp.zeros((8, 128), F32)]
        for first, step, count, row_of in tables:
            offset = high - first
            for r in range(count):
                here = offset == r * step
                for c in range(2):
                    value[c] = jnp.where(here, lane_pick(row_of(r, c), low), value[c])
        along = (code & 1) == 1
        for c in range(2):
            signed = jnp.where(along, value[c], -value[c])
            total[c] = signed if k == 0 else total[c] + signed
    return total


def own_lookup_kernel(mesh_ref, code_ref, coupling_hbm, out_ref, pair_ref, raw_ref, sems):
    rows = mesh_ref.shape[1] // 128
    far_count, rank = coupling_hbm.shape[:2]
    half = rank // 2
    part = far_count // 2
    copies = [
        pltpu.make_async_copy(
            coupling_hbm.at[pl.ds(i * part, part)], raw_ref.at[pl.ds(i * part, part)], sems.at[i]
        )
        for i in range(2)
    ]
    for copy in copies:
        copy.start()

    def own_row(r, c):
        return mesh_ref[c : c + 1, r * 128 : (r + 1) * 128]

    def block(g, carry):
        start = pl.multiple_of(g * 8, 8)
        total = lookup(code_ref, start, [(0, 1, rows, own_row)])
        out_ref[0, pl.ds(start, 8), :] = total[0]
        out_ref[1, pl.ds(start, 8), :] = total[1]
        return carry

    lax.fori_loop(0, code_ref.shape[1] // 8, block, 0, unroll=True)
    for k in range(far_count):
        if k % part == 0:
            copies[k // part].wait()
        for r in range(half):
            pair_ref[k, r] = jnp.concatenate([raw_ref[k, r], raw_ref[k, half + r]], axis=1)


def add_peers(part_ref, pack_ref, need_ref, code_ref, table_ref, out_ref, core, first):
    chips = pack_ref.shape[0]
    ask(need_ref, pack_ref, table_ref, core, first)

    def peer_row(r, c):
        return table_ref[c, r : r + 1, :]

    def block(g, carry):
        start = pl.multiple_of(g * 8, 8)
        total = lookup(code_ref, start, [(first + core, 2, chips, peer_row)])
        for c in range(2):
            out_ref[c, pl.ds(start, 8), :] = total[c] + part_ref[c, pl.ds(start, 8), :]
        return carry

    lax.fori_loop(0, code_ref.shape[1] // 8, block, 0, unroll=True)


def same_core_kernel(
    part_ref, same_ref, need_ref, code_ref, out_ref, rows_ref, table_ref, *, first
):
    rows_ref[0] = same_ref[:, 2 * first, :]
    rows_ref[1] = same_ref[:, 2 * first + 2, :]
    add_peers(
        part_ref, same_ref, need_ref, code_ref, table_ref, out_ref,
        lax.axis_index("core"), first,
    )


def current_kernel(
    part_ref, other_ref, need_ref, code_ref, basis_hbm, current_ref, coeff_ref, rows_ref,
    table_ref, basis_ref, sem, *, first,
):
    tiles = code_ref.shape[1]
    rank = basis_ref.shape[0] // tiles
    copy = pltpu.make_async_copy(basis_hbm, basis_ref, sem.at[0])
    copy.start()
    rows_ref[0] = other_ref[:, 2 * first + 1, :]
    rows_ref[1] = other_ref[:, 2 * first + 2, :]
    add_peers(
        part_ref, other_ref, need_ref, code_ref, table_ref, current_ref,
        1 - lax.axis_index("core"), first,
    )
    copy.wait()
    inputs = jnp.concatenate([current_ref[0], current_ref[1]], axis=0)
    inputs = inputs.T.astype(BF16)
    lane_tile = lax.broadcasted_iota(jnp.int32, (rank, 2 * tiles), 1) % tiles
    full = jnp.dot(basis_ref[...], inputs, preferred_element_type=F32)
    chosen = jnp.zeros((rank, 2 * tiles), F32)
    for t in range(tiles):
        chosen = jnp.where(lane_tile == t, full[t * rank : (t + 1) * rank], chosen)
    coeff = chosen.astype(BF16)
    for p in range(coeff_ref.shape[0]):
        coeff_ref[p] = coeff


def near_kernel(
    source_ref, current_ref, resistance_hbm, blocks_hbm, out_ref, inputs_ref, blocks_ref,
    resistance_ref, sems,
):
    tiles = current_ref.shape[1]
    width = blocks_ref.shape[1]
    count = blocks_ref.shape[0] // (tiles * width)
    chunks = 2
    span = blocks_ref.shape[0] // chunks
    copies = [
        pltpu.make_async_copy(
            blocks_hbm.at[pl.ds(g * span, span)], blocks_ref.at[pl.ds(g * span, span)], sems.at[g]
        )
        for g in range(chunks)
    ]
    late_copy = pltpu.make_async_copy(resistance_hbm, resistance_ref, sems.at[chunks])
    for copy in copies:
        copy.start()
    late_copy.start()
    lane_tile = lax.broadcasted_iota(jnp.int32, (width, 128), 1) % tiles
    rows = jnp.concatenate([current_ref[0], current_ref[1]], axis=0)
    columns = rows.T.astype(BF16)
    row_index = lax.broadcasted_iota(jnp.int32, (128, 128), 0)
    for k in range(count):
        picks = jnp.where(row_index == source_ref[k : k + 1, :], 1.0, 0.0).astype(BF16)
        inputs_ref[k * width : (k + 1) * width, :] = jnp.dot(
            columns, picks, preferred_element_type=F32
        ).astype(BF16)
    inputs = inputs_ref[...]
    total = jnp.zeros((width, 128), F32)
    for g in range(tiles // 8):
        if g % (tiles // (8 * chunks)) == 0:
            copies[g // (tiles // (8 * chunks))].wait()
        block = jnp.concatenate(
            [
                jnp.concatenate(
                    [
                        blocks_ref[(t * count + k) * width : (t * count + k + 1) * width, :]
                        for t in range(g * 8, g * 8 + 8)
                    ],
                    axis=0,
                )
                for k in range(count)
            ],
            axis=1,
        )
        full = jnp.dot(block, inputs, preferred_element_type=F32)
        for i in range(8):
            total = jnp.where(
                lane_tile == g * 8 + i, full[i * width : (i + 1) * width], total
            )
    rows = total.T
    late_copy.wait()
    resistance = resistance_ref[...]
    out_ref[0] = resistance * current_ref[0] - rows[tiles:]
    out_ref[1] = resistance * current_ref[1] + rows[:tiles]


def split(value):
    top = value.astype(BF16)
    return top, (value - top.astype(F32)).astype(BF16)


def counts(rows):
    return lax.broadcasted_iota(jnp.int32, (rows, 128), 0).astype(F32)


def place(high, low, values, rows, spread_ref):
    sub_high, sub_low = counts(rows).astype(BF16), counts(128).astype(BF16)
    one, zero = jnp.ones((128, 128), BF16), jnp.zeros((128, 128), BF16)
    spread_ref[0] = high.astype(F32)
    spread_ref[1] = low.astype(F32)
    for c, value in enumerate(values):
        top, rest = split(value)
        spread_ref[2 + 2 * c] = top.astype(F32)
        spread_ref[3 + 2 * c] = rest.astype(F32)

    def spread(j, i, count):
        return jnp.broadcast_to(spread_ref[j, i : i + 1, :], (count, 128)).astype(BF16)

    left, right = [], []
    for i in range(8):
        here = spread(0, i, rows) == sub_high
        left.append(
            jnp.concatenate(
                [jnp.where(here, spread(j, i, rows), zero[:rows]) for j in range(2, 6)], axis=0
            )
        )
        right.append(jnp.where(spread(1, i, 128) == sub_low, one, zero))
    return jnp.concatenate(left, axis=1), jnp.concatenate(right, axis=1)


def place_few(high, low, values, rows):
    sub_high = lax.broadcasted_iota(jnp.int32, (rows, 128), 0)
    sub_low = lax.broadcasted_iota(jnp.int32, (128, 128), 0)
    left, right = [], []
    for i in range(high.shape[0]):
        here = jnp.broadcast_to(high[i : i + 1], (rows, 128)) == sub_high
        parts = []
        for value in values:
            spread = jnp.where(here, jnp.broadcast_to(value[i : i + 1], (rows, 128)), 0.0)
            parts.extend(split(spread))
        left.append(jnp.concatenate(parts, axis=0))
        there = jnp.broadcast_to(low[i : i + 1], (128, 128)) == sub_low
        right.append(jnp.where(there, 1.0, 0.0).astype(BF16))
    return jnp.concatenate(left, axis=1), jnp.concatenate(right, axis=1)


def scatter(code_ref, voltage_ref, spread_ref, first, rows, low_streams):
    total = None
    for g in range(code_ref.shape[1] // 8):
        for k in range(2):
            code = code_ref[k, g * 8 : g * 8 + 8, :]
            along = (code & 1) == 1
            values = []
            for c in range(2):
                voltage = voltage_ref[c, g * 8 : g * 8 + 8, :]
                values.append(jnp.where(along, voltage, -voltage))
            left, right = place(
                (code >> 8) - first, (code >> 1) & 127, values, rows, spread_ref.at[g, k]
            )
            term = dot_nt(right, left) if low_streams else dot_nt(left, right)
            total = term if total is None else total + term
    total = total.T if low_streams else total
    return [
        total[2 * c * rows : (2 * c + 1) * rows] + total[(2 * c + 1) * rows : (2 * c + 2) * rows]
        for c in range(2)
    ]


def turn(peers):
    return peers // 4


def voltage_kernel(
    coeff_ref, target_ref, coupling_ref, basis_ref, near_ref, code_ref, voltage_ref, slot_ref,
    picked_ref, mixed_ref, spread_ref, *, first,
):
    peers, rank, lanes = coeff_ref.shape
    far_count = coupling_ref.shape[0]
    tiles = lanes // 2
    half = rank // 2
    groups = half // 4
    device = device_index()
    spans = target_ref.shape[0] // far_count
    stride = peers // far_count
    component = lax.broadcasted_iota(jnp.int32, (rank, lanes), 1) // tiles
    for k in range(far_count):
        picked = jnp.zeros((rank, lanes), F32)
        for i in range(spans):
            row = k * spans + i
            block = coeff_ref[(device + k * stride + i + peers - turn(peers)) % peers].astype(F32)
            target = jnp.broadcast_to(target_ref[row : row + 1, :], (rank, lanes))
            source = jnp.maximum(target, 0) + component * tiles
            value = jnp.take_along_axis(block, source, axis=1, mode="promise_in_bounds")
            picked = jnp.where(target >= 0, value, picked)
        turned = pltpu.roll(picked, tiles, 1)
        picked_ref[0, k] = jnp.where(component == 0, picked, turned)
        picked_ref[1, k] = jnp.where(component == 0, turned, picked)

    def mix(g, carry):
        total = [[None, None] for _ in range(4)]
        for k in range(far_count):
            picked = [picked_ref[c, k] for c in range(2)]
            for i in range(4):
                block = coupling_ref[k, g * 4 + i].astype(F32)
                for c in range(2):
                    product = block * picked[c]
                    part = product[0:8]
                    for q in range(8, rank, 8):
                        part = part + product[q : q + 8]
                    total[i][c] = part if k == 0 else total[i][c] + part
        for i in range(4):
            for c in range(2):
                row = jnp.sum(total[i][c], axis=0, keepdims=True)
                mixed_ref[pl.ds(c * half + g * 4 + i, 1), :] = row
        return carry

    lax.fori_loop(0, groups, mix, 0, unroll=True)
    mixed = mixed_ref[...].T
    mixed = jnp.concatenate([mixed[:tiles], mixed[tiles:]], axis=1).astype(BF16)
    wide = 8 * rank
    from_row = lax.broadcasted_iota(jnp.int32, (2 * rank, wide), 0)
    to_rank = lax.broadcasted_iota(jnp.int32, (2 * rank, wide), 1) % rank
    repeated = []
    for c in range(2):
        wanted = (to_rank // half) * rank + c * half + to_rank % half
        picks = jnp.where(from_row == wanted, 1.0, 0.0).astype(BF16)
        repeated.append(jnp.dot(mixed, picks, preferred_element_type=F32))
    own_block = (
        lax.broadcasted_iota(jnp.int32, (16, wide), 0) % 8
        == lax.broadcasted_iota(jnp.int32, (16, wide), 1) // rank
    )
    for g in range(tiles // 8):
        rows8 = slice(g * 8, g * 8 + 8)
        both = jnp.concatenate([repeated[0][rows8], repeated[1][rows8]], axis=0)
        both = jnp.where(own_block, both, 0.0).astype(BF16)
        far = jnp.dot(
            both, basis_ref[g * wide : (g + 1) * wide, :], preferred_element_type=F32
        )
        voltage_ref[0, rows8, :] = near_ref[0, rows8, :] - far[8:16]
        voltage_ref[1, rows8, :] = near_ref[1, rows8, :] + far[0:8]
    sums = scatter(
        code_ref, voltage_ref, spread_ref, first, slot_ref.shape[0], True
    )
    shift = turn(peers)
    for c in range(2):
        slot_ref[: peers - shift, c, :] = sums[c][shift:]
        slot_ref[peers - shift :, c, :] = sums[c][:shift]


def own_sum_kernel(
    code_ref, voltage_ref, same_ref, other_ref, port_ref, impedance_ref, own_ref, asked_ref,
    picks_ref, spread_ref,
):
    rows = own_ref.shape[1]
    ports = impedance_ref.shape[1]
    chips = same_ref.shape[1]
    first_core = lax.axis_index("core") == 0
    same = same_ref[0].astype(jnp.int32)
    other = other_ref[0].astype(jnp.int32)
    asked = [jnp.where(first_core, same, other), jnp.where(first_core, other, same)]
    sub_low = lax.broadcasted_iota(jnp.int32, (128, 128), 0)
    for core in range(2):
        asked_ref[core] = asked[core] >> 7
        low = asked[core] & 127
        for chip in range(chips):
            there = jnp.broadcast_to(low[chip : chip + 1], (128, 128)) == sub_low
            place = core * chips + chip
            picks_ref[:, place * 128 : (place + 1) * 128] = jnp.where(there, 1.0, 0.0).astype(BF16)
    port_current = jnp.sum(same_ref[1] + other_ref[1], axis=0, keepdims=True)
    real = port_current[:, :ports]
    imag = port_current[:, ports:]
    both = jnp.concatenate([real, imag, jnp.zeros((6, ports), F32)], axis=0)
    by_real = dot_nt(both, impedance_ref[0], lax.Precision.HIGHEST)
    by_imag = dot_nt(both, impedance_ref[1], lax.Precision.HIGHEST)
    pad = jnp.zeros((1, 128 - ports), F32)
    terms = [
        jnp.concatenate([by_real[0:1] - by_imag[1:2], pad], axis=1),
        jnp.concatenate([by_real[1:2] + by_imag[0:1], pad], axis=1),
    ]
    port = port_ref[...] - device_index() * (rows * 128)
    port = jnp.where((port >= 0) & (port < rows * 128), port, -1)
    port = jnp.concatenate([port, jnp.full((1, 128 - ports), -1, jnp.int32)], axis=1)
    left, right = place_few(port >> 7, port & 127, terms, rows)
    total = dot_nt(left, right)
    sums = scatter(code_ref, voltage_ref, spread_ref, 0, rows, False)
    for c in range(2):
        own_ref[c] = sums[c] + (
            total[2 * c * rows : (2 * c + 1) * rows] + total[(2 * c + 1) * rows : (2 * c + 2) * rows]
        )


def finish_kernel(own_ref, arrived_ref, asked_ref, picks_ref, out_ref):
    rows = own_ref.shape[1]
    peers = arrived_ref.shape[0]
    chips = peers // 2
    sub_high = lax.broadcasted_iota(jnp.int32, (rows, 128), 0)
    left = []
    for core in range(2):
        for chip in range(chips):
            here = jnp.broadcast_to(asked_ref[core, chip : chip + 1, :], (rows, 128)) == sub_high
            parts = []
            for c in range(2):
                place = (2 * chip + core + peers - turn(peers)) % peers
                value = jnp.broadcast_to(arrived_ref[place, c : c + 1, :], (rows, 128))
                parts.extend(split(jnp.where(here, value, 0.0)))
            left.append(jnp.concatenate(parts, axis=0))
    total = dot_nt(jnp.concatenate(left, axis=1), picks_ref[...])
    for c in range(2):
        summed = own_ref[c] + (
            total[2 * c * rows : (2 * c + 1) * rows] + total[(2 * c + 1) * rows : (2 * c + 2) * rows]
        )
        for r in range(rows):
            out_ref[c : c + 1, r * 128 : (r + 1) * 128] = summed[r : r + 1]


def per_device(
    mesh_current,
    branch_entry,
    branch_sign,
    need_slots,
    resistance,
    near_blocks,
    near_source,
    basis_in,
    coupling,
    basis_out,
    admissible,
    port_mesh,
    port_coupling,
):
    chips = lax.axis_size("chips")
    peers = 2 * chips
    core = lax.axis_index("core")
    device = 2 * lax.axis_index("chips") + core
    mesh_dev = mesh_current.shape[1]
    tiles, near_count, width, _ = near_blocks.shape
    rank = basis_in.shape[1]
    far_count = admissible.shape[1]
    own_rows = mesh_dev // 128
    vmem = pl.BlockSpec(memory_space=pltpu.VMEM)
    shape = jax.ShapeDtypeStruct

    code = (branch_entry * 2 + branch_sign).reshape(2, tiles, width)
    coupling_lanes = jnp.transpose(coupling, (1, 2, 3, 0))
    basis_in_rows = basis_in.reshape(tiles * rank, width)
    basis_out_rows = basis_out.reshape(tiles * rank, width)
    half = jnp.arange(2 * tiles, dtype=jnp.int32) // tiles
    sources = jnp.transpose(near_source)
    sources = jnp.concatenate([sources, sources], axis=1) + half[None] * tiles
    band = peers * tiles // far_count
    spans = band // tiles + 1
    bases = device * tiles + jnp.arange(far_count, dtype=jnp.int32) * band
    shifted = (jnp.transpose(admissible) - bases[:, None]) % (peers * tiles)
    shifted = jnp.concatenate([shifted, shifted], axis=1)[:, None, :]
    shifted = shifted - jnp.arange(spans, dtype=jnp.int32)[None, :, None] * tiles
    inside = (shifted >= 0) & (shifted < tiles)
    targets = jnp.where(inside, shifted, -1).reshape(far_count * spans, 2 * tiles)

    def in_hbm(x):
        return pltpu.with_memory_space_constraint(x, pltpu.HBM)

    hbm = pl.BlockSpec(memory_space=pl.ANY)
    port_row = port_mesh.reshape(1, -1)
    pack_rows = (2 * own_rows + 3 + 7) // 8 * 8
    pack, mesh_near, need_near, port_near = pl.pallas_call(
        pack_kernel,
        out_shape=(
            shape((chips, pack_rows, 128), F32),
            pltpu.VMEM(mesh_current.shape, F32),
            pltpu.VMEM(need_slots.shape, jnp.int32),
            pltpu.VMEM(port_row.shape, jnp.int32),
        ),
        in_specs=[hbm] * 3,
        out_specs=(vmem,) * 4,
        scratch_shapes=[pltpu.SemaphoreType.DMA((3,))],
        compiler_params=params(),
        name="pack",
    )(in_hbm(mesh_current), in_hbm(need_slots), in_hbm(port_row))
    same = lax.all_to_all(pack, "chips", 0, 0, tiled=True)
    own_part, pairs = pl.pallas_call(
        own_lookup_kernel,
        out_shape=(
            shape((2, tiles, width), F32),
            pltpu.VMEM((far_count, rank // 2, rank, 2 * tiles), BF16),
        ),
        in_specs=[vmem] * 2 + [hbm],
        out_specs=(vmem,) * 2,
        scratch_shapes=[
            pltpu.VMEM(coupling_lanes.shape, BF16),
            pltpu.SemaphoreType.DMA((2,)),
        ],
        compiler_params=params(),
        cost_estimate=small_cost(),
        name="own_lookup",
    )(mesh_near, code, in_hbm(coupling_lanes))
    other = lax.ppermute(same, "core", [(0, 1), (1, 0)])
    part, same_rows = pl.pallas_call(
        functools.partial(same_core_kernel, first=own_rows),
        out_shape=(shape((2, tiles, width), F32), shape((2, chips, 128), F32)),
        in_specs=[vmem] * 4,
        out_specs=(vmem,) * 2,
        scratch_shapes=[pltpu.VMEM((2, chips, 128), F32)],
        compiler_params=params(),
        cost_estimate=small_cost(),
        name="same_core",
    )(own_part, same, need_near, code)
    current, coeff, other_rows = pl.pallas_call(
        functools.partial(current_kernel, first=own_rows),
        out_shape=(
            shape((2, tiles, width), F32),
            shape((peers, rank, 2 * tiles), BF16),
            shape((2, chips, 128), F32),
        ),
        in_specs=[vmem] * 4 + [hbm],
        out_specs=(vmem,) * 3,
        scratch_shapes=[
            pltpu.VMEM((2, chips, 128), F32),
            pltpu.VMEM(basis_in_rows.shape, BF16),
            pltpu.SemaphoreType.DMA((1,)),
        ],
        compiler_params=params(),
        name="currents",
    )(part, other, need_near, code, in_hbm(basis_in_rows))
    members = [[(j + turn(peers)) % peers for j in range(peers)]]
    all_coeff = lax.all_to_all(
        coeff, ("chips", "core"), 0, 0, tiled=True, axis_index_groups=members
    )
    near_rows = near_blocks.reshape(tiles * near_count * width, width)
    near = pl.pallas_call(
        near_kernel,
        out_shape=shape((2, tiles, width), F32),
        in_specs=[vmem] * 2 + [hbm] * 2,
        out_specs=vmem,
        scratch_shapes=[
            pltpu.VMEM((near_count * width, 2 * tiles), BF16),
            pltpu.VMEM(near_rows.shape, BF16),
            pltpu.VMEM((tiles, width), F32),
            pltpu.SemaphoreType.DMA((3,)),
        ],
        compiler_params=params(),
        cost_estimate=pl.CostEstimate(
            flops=256 * near_blocks.size, bytes_accessed=2 * near_blocks.size, transcendentals=0
        ),
        name="near_field",
    )(sources, current, in_hbm(resistance.reshape(tiles, width)), in_hbm(near_rows))
    voltage, slots = pl.pallas_call(
        functools.partial(voltage_kernel, first=own_rows),
        out_shape=(shape((2, tiles, width), F32), shape((peers, 2, 128), F32)),
        in_specs=[vmem] * 6,
        out_specs=(vmem,) * 2,
        scratch_shapes=[
            pltpu.VMEM((2, far_count, rank, 2 * tiles), F32),
            pltpu.VMEM((rank, 2 * tiles), F32),
            pltpu.VMEM((tiles // 8, 2, 6, 8, 128), F32),
        ],
        compiler_params=params(),
        name="voltages",
    )(
        all_coeff,
        targets,
        pairs,
        basis_out_rows,
        near,
        code,
    )
    arrived = lax.all_to_all(
        slots, ("chips", "core"), 0, 0, tiled=True, axis_index_groups=members
    )
    own, asked, picks = pl.pallas_call(
        own_sum_kernel,
        out_shape=(
            shape((2, own_rows, 128), F32),
            shape((2, chips, 128), jnp.int32),
            shape((128, peers * 128), BF16),
        ),
        in_specs=[vmem] * 6,
        out_specs=(vmem,) * 3,
        scratch_shapes=[
            pltpu.VMEM((tiles // 8, 2, 6, 8, 128), F32),
        ],
        compiler_params=params(),
        cost_estimate=small_cost(),
        name="own_sums",
    )(code, voltage, same_rows, other_rows, port_near, port_coupling)
    return pl.pallas_call(
        finish_kernel,
        out_shape=shape((2, mesh_dev), F32),
        in_specs=[vmem] * 4,
        out_specs=vmem,
        compiler_params=params(),
        name="finish",
    )(own, arrived, asked, picks)


def solution(mesh):
    groups, peers = mesh.devices.shape
    split_mesh = jax.sharding.Mesh(
        mesh.devices.reshape(groups, peers // 2, 2), ("groups", "chips", "core")
    )
    in_specs = (
        P(None, SPREAD),
        P(None, SPREAD),
        P(None, SPREAD),
        P(SPREAD, None),
        P(SPREAD),
        P(SPREAD, None, None, None),
        P(SPREAD, None),
        P(SPREAD, None, None),
        P(SPREAD, None, None, None),
        P(SPREAD, None, None),
        P(SPREAD, None),
        P("groups"),
        P(),
    )
    out_specs = P(None, SPREAD)
    return jax.shard_map(
        per_device, mesh=split_mesh, in_specs=in_specs, out_specs=out_specs, check_vma=False
    )
```

```python
import functools

import jax
import jax.numpy as jnp
from jax import lax
from jax.experimental import pallas as pl
from jax.experimental.pallas import tpu as pltpu
from jax.sharding import PartitionSpec as P

F32 = jnp.float32
BF16 = jnp.bfloat16
SPREAD = ("groups", "chips", "core")
VMEM_LIMIT = 24 * 1024 * 1024
NT = (((1,), (1,)), ((), ()))


def params():
    return pltpu.CompilerParams(vmem_limit_bytes=VMEM_LIMIT)


def small_cost():
    return pl.CostEstimate(flops=10**9, bytes_accessed=8 * 10**6, transcendentals=0)


def lane_pick(row, lanes):
    spread = jnp.broadcast_to(row, lanes.shape)
    return jnp.take_along_axis(spread, lanes, axis=1, mode="promise_in_bounds")


def dot_nt(left, right, precision=None):
    return lax.dot_general(
        left, right, NT, preferred_element_type=F32, precision=precision
    )


def turn(members):
    return members // 4


def by_chip(rows):
    shift = turn(rows.shape[0])
    return jnp.concatenate([rows[rows.shape[0] - shift :], rows[: rows.shape[0] - shift]], axis=0)


def by_place(rows):
    shift = turn(rows.shape[0])
    return jnp.concatenate([rows[shift:], rows[:shift]], axis=0)


def device_index():
    return 2 * lax.axis_index("chips") + lax.axis_index("core")


def fetch(copies):
    for copy in copies:
        copy.start()
    for copy in copies:
        copy.wait()


def pack_kernel(
    mesh_hbm, need_hbm, port_hbm, out_ref, mesh_ref, need_ref, port_ref, sems
):
    rows = mesh_ref.shape[1] // 128
    ports = port_ref.shape[1]
    chips = out_ref.shape[0]
    fetch(
        [
            pltpu.make_async_copy(source, target, sems.at[i])
            for i, (source, target) in enumerate(
                [(mesh_hbm, mesh_ref), (need_hbm, need_ref), (port_hbm, port_ref)]
            )
        ]
    )
    port = port_ref[...] - device_index() * (rows * 128)
    port = jnp.where((port >= 0) & (port < rows * 128), port, -1)
    port = jnp.broadcast_to(jnp.concatenate([port, port], axis=1), (8, 128))
    port_high, port_low = port >> 7, port & 127
    port_value = jnp.zeros((8, 128), F32)
    lane = lax.broadcasted_iota(jnp.int32, (8, 128), 1)
    for r in range(rows):
        real_row = mesh_ref[0:1, r * 128 : (r + 1) * 128]
        imag_row = mesh_ref[1:2, r * 128 : (r + 1) * 128]
        both = jnp.where(
            lane < ports, lane_pick(real_row, port_low), lane_pick(imag_row, port_low)
        )
        port_value = jnp.where(port_high == r, both, port_value)
        out_ref[0, r : r + 1, :] = real_row
        out_ref[0, rows + r : rows + r + 1, :] = imag_row
    block = out_ref[0, : 2 * rows, :]
    for chip in range(1, chips):
        out_ref[chip, : 2 * rows, :] = block
    need = [by_place(need_ref[pl.ds(c, chips, 2), :].astype(F32)) for c in range(2)]
    first = lax.axis_index("core") == 0
    out_ref[:, 2 * rows, :] = jnp.where(first, need[0], need[1])
    out_ref[:, 2 * rows + 1, :] = jnp.where(first, need[1], need[0])
    out_ref[:, 2 * rows + 2, :] = jnp.broadcast_to(port_value[0:1], (chips, 128))
    for r in range(2 * rows + 3, out_ref.shape[1]):
        out_ref[:, r, :] = jnp.zeros((chips, 128), F32)


def ask(need_ref, pack_ref, table_ref, core, rows):
    chips = pack_ref.shape[0]
    sub = lax.broadcasted_iota(jnp.int32, (rows, 128), 0)
    for chip in range(chips):
        wanted = need_ref[pl.ds(2 * chip + core, 1), :]
        wanted = jnp.broadcast_to(jnp.maximum(wanted, 0), (rows, 128))
        here = (wanted >> 7) == sub
        low = wanted & 127
        for c in range(2):
            block = pack_ref[(chip + chips - turn(chips)) % chips, c * rows : (c + 1) * rows, :]
            picked = jnp.take_along_axis(block, low, axis=1, mode="promise_in_bounds")
            picked = jnp.where(here, picked, 0.0)
            table_ref[c, chip : chip + 1, :] = jnp.sum(picked, axis=0, keepdims=True)


def lookup(code_ref, start, tables):
    total = [None, None]
    for k in range(2):
        code = code_ref[k, pl.ds(start, 8), :]
        high, low = code >> 8, (code >> 1) & 127
        value = [jnp.zeros((8, 128), F32), jnp.zeros((8, 128), F32)]
        for first, step, count, row_of in tables:
            offset = high - first
            for r in range(count):
                here = offset == r * step
                for c in range(2):
                    value[c] = jnp.where(here, lane_pick(row_of(r, c), low), value[c])
        along = (code & 1) == 1
        for c in range(2):
            signed = jnp.where(along, value[c], -value[c])
            total[c] = signed if k == 0 else total[c] + signed
    return total


def own_lookup_kernel(mesh_ref, code_ref, coupling_hbm, out_ref, pair_ref, raw_ref, sems):
    rows = mesh_ref.shape[1] // 128
    far_count, rank = coupling_hbm.shape[:2]
    half = rank // 2
    part = far_count // 2
    copies = [
        pltpu.make_async_copy(
            coupling_hbm.at[pl.ds(i * part, part)], raw_ref.at[pl.ds(i * part, part)], sems.at[i]
        )
        for i in range(2)
    ]
    for copy in copies:
        copy.start()

    def own_row(r, c):
        return mesh_ref[c : c + 1, r * 128 : (r + 1) * 128]

    def block(g, carry):
        start = pl.multiple_of(g * 8, 8)
        total = lookup(code_ref, start, [(0, 1, rows, own_row)])
        out_ref[0, pl.ds(start, 8), :] = total[0]
        out_ref[1, pl.ds(start, 8), :] = total[1]
        return carry

    lax.fori_loop(0, code_ref.shape[1] // 8, block, 0, unroll=True)
    for k in range(far_count):
        if k % part == 0:
            copies[k // part].wait()
        for r in range(half):
            pair_ref[k, r] = jnp.concatenate([raw_ref[k, r], raw_ref[k, half + r]], axis=1)


def add_peers(part_ref, pack_ref, need_ref, code_ref, table_ref, out_ref, core, first):
    chips = pack_ref.shape[0]
    ask(need_ref, pack_ref, table_ref, core, first)

    def peer_row(r, c):
        return table_ref[c, r : r + 1, :]

    def block(g, carry):
        start = pl.multiple_of(g * 8, 8)
        total = lookup(code_ref, start, [(first + core, 2, chips, peer_row)])
        for c in range(2):
            out_ref[c, pl.ds(start, 8), :] = total[c] + part_ref[c, pl.ds(start, 8), :]
        return carry

    lax.fori_loop(0, code_ref.shape[1] // 8, block, 0, unroll=True)


def same_core_kernel(
    part_ref, same_ref, need_ref, code_ref, out_ref, rows_ref, table_ref, *, first
):
    rows_ref[0] = by_chip(same_ref[:, 2 * first, :])
    rows_ref[1] = same_ref[:, 2 * first + 2, :]
    add_peers(
        part_ref, same_ref, need_ref, code_ref, table_ref, out_ref,
        lax.axis_index("core"), first,
    )


def current_kernel(
    part_ref, other_ref, need_ref, code_ref, basis_hbm, current_ref, coeff_ref, rows_ref,
    table_ref, basis_ref, sem, *, first,
):
    tiles = code_ref.shape[1]
    rank = basis_ref.shape[0] // tiles
    copy = pltpu.make_async_copy(basis_hbm, basis_ref, sem.at[0])
    copy.start()
    rows_ref[0] = by_chip(other_ref[:, 2 * first + 1, :])
    rows_ref[1] = other_ref[:, 2 * first + 2, :]
    add_peers(
        part_ref, other_ref, need_ref, code_ref, table_ref, current_ref,
        1 - lax.axis_index("core"), first,
    )
    copy.wait()
    inputs = jnp.concatenate([current_ref[0], current_ref[1]], axis=0)
    inputs = inputs.T.astype(BF16)
    lane_tile = lax.broadcasted_iota(jnp.int32, (rank, 2 * tiles), 1) % tiles
    full = jnp.dot(basis_ref[...], inputs, preferred_element_type=F32)
    chosen = jnp.zeros((rank, 2 * tiles), F32)
    for t in range(tiles):
        chosen = jnp.where(lane_tile == t, full[t * rank : (t + 1) * rank], chosen)
    coeff = chosen.astype(BF16)
    for p in range(coeff_ref.shape[0]):
        coeff_ref[p] = coeff


def near_kernel(
    source_ref, current_ref, resistance_hbm, blocks_hbm, out_ref, inputs_ref, blocks_ref,
    resistance_ref, sems,
):
    tiles = current_ref.shape[1]
    width = blocks_ref.shape[1]
    count = blocks_ref.shape[0] // (tiles * width)
    span = 8 * count * width
    starts = [tiles * i // 64 for i in (0, 3, 6, 8)]
    copies = {}
    for i in range(3):
        rows = pl.ds(starts[i] * span, (starts[i + 1] - starts[i]) * span)
        copies[starts[i]] = pltpu.make_async_copy(
            blocks_hbm.at[rows], blocks_ref.at[rows], sems.at[i]
        )
    late_copy = pltpu.make_async_copy(resistance_hbm, resistance_ref, sems.at[3])
    for copy in copies.values():
        copy.start()
    late_copy.start()
    lane_tile = lax.broadcasted_iota(jnp.int32, (width, 128), 1) % tiles
    rows = jnp.concatenate([current_ref[0], current_ref[1]], axis=0)
    columns = rows.T.astype(BF16)
    row_index = lax.broadcasted_iota(jnp.int32, (128, 128), 0)
    for k in range(count):
        picks = jnp.where(row_index == source_ref[k : k + 1, :], 1.0, 0.0).astype(BF16)
        inputs_ref[k * width : (k + 1) * width, :] = jnp.dot(
            columns, picks, preferred_element_type=F32
        ).astype(BF16)
    inputs = inputs_ref[...]
    total = jnp.zeros((width, 128), F32)
    for g in range(tiles // 8):
        if g in copies:
            copies[g].wait()
        block = jnp.concatenate(
            [
                jnp.concatenate(
                    [
                        blocks_ref[(t * count + k) * width : (t * count + k + 1) * width, :]
                        for t in range(g * 8, g * 8 + 8)
                    ],
                    axis=0,
                )
                for k in range(count)
            ],
            axis=1,
        )
        full = jnp.dot(block, inputs, preferred_element_type=F32)
        for i in range(8):
            total = jnp.where(
                lane_tile == g * 8 + i, full[i * width : (i + 1) * width], total
            )
    rows = total.T
    late_copy.wait()
    resistance = resistance_ref[...]
    out_ref[0] = resistance * current_ref[0] - rows[tiles:]
    out_ref[1] = resistance * current_ref[1] + rows[:tiles]


def split(value):
    top = value.astype(BF16)
    return top, (value - top.astype(F32)).astype(BF16)


def counts(rows):
    return lax.broadcasted_iota(jnp.int32, (rows, 128), 0).astype(F32)


def place(high, low, values, rows, spread_ref):
    sub_high, sub_low = counts(rows).astype(BF16), counts(128).astype(BF16)
    one, zero = jnp.ones((128, 128), BF16), jnp.zeros((128, 128), BF16)
    spread_ref[0] = high.astype(F32)
    spread_ref[1] = low.astype(F32)
    for c, value in enumerate(values):
        top, rest = split(value)
        spread_ref[2 + 2 * c] = top.astype(F32)
        spread_ref[3 + 2 * c] = rest.astype(F32)

    def spread(j, i, count):
        return jnp.broadcast_to(spread_ref[j, i : i + 1, :], (count, 128)).astype(BF16)

    left, right = [], []
    for i in range(8):
        here = spread(0, i, rows) == sub_high
        left.append(
            jnp.concatenate(
                [jnp.where(here, spread(j, i, rows), zero[:rows]) for j in range(2, 6)], axis=0
            )
        )
        right.append(jnp.where(spread(1, i, 128) == sub_low, one, zero))
    return jnp.concatenate(left, axis=1), jnp.concatenate(right, axis=1)


def place_few(high, low, values, rows):
    sub_high = lax.broadcasted_iota(jnp.int32, (rows, 128), 0)
    sub_low = lax.broadcasted_iota(jnp.int32, (128, 128), 0)
    left, right = [], []
    for i in range(high.shape[0]):
        here = jnp.broadcast_to(high[i : i + 1], (rows, 128)) == sub_high
        parts = []
        for value in values:
            spread = jnp.where(here, jnp.broadcast_to(value[i : i + 1], (rows, 128)), 0.0)
            parts.extend(split(spread))
        left.append(jnp.concatenate(parts, axis=0))
        there = jnp.broadcast_to(low[i : i + 1], (128, 128)) == sub_low
        right.append(jnp.where(there, 1.0, 0.0).astype(BF16))
    return jnp.concatenate(left, axis=1), jnp.concatenate(right, axis=1)


def scatter(code_ref, voltage_ref, spread_ref, first, rows, low_streams):
    total = None
    for g in range(code_ref.shape[1] // 8):
        for k in range(2):
            code = code_ref[k, g * 8 : g * 8 + 8, :]
            along = (code & 1) == 1
            values = []
            for c in range(2):
                voltage = voltage_ref[c, g * 8 : g * 8 + 8, :]
                values.append(jnp.where(along, voltage, -voltage))
            left, right = place(
                (code >> 8) - first, (code >> 1) & 127, values, rows, spread_ref.at[g, k]
            )
            term = dot_nt(right, left) if low_streams else dot_nt(left, right)
            total = term if total is None else total + term
    total = total.T if low_streams else total
    return [
        total[2 * c * rows : (2 * c + 1) * rows] + total[(2 * c + 1) * rows : (2 * c + 2) * rows]
        for c in range(2)
    ]


def voltage_kernel(
    coeff_ref, target_ref, coupling_ref, basis_ref, near_ref, code_ref, voltage_ref, slot_ref,
    picked_ref, mixed_ref, spread_ref, *, first,
):
    peers, rank, lanes = coeff_ref.shape
    far_count = coupling_ref.shape[0]
    tiles = lanes // 2
    half = rank // 2
    groups = half // 4
    device = device_index()
    spans = target_ref.shape[0] // far_count
    stride = peers // far_count
    component = lax.broadcasted_iota(jnp.int32, (rank, lanes), 1) // tiles
    for k in range(far_count):
        picked = jnp.zeros((rank, lanes), F32)
        for i in range(spans):
            row = k * spans + i
            block = coeff_ref[(device + k * stride + i + peers - turn(peers)) % peers].astype(F32)
            target = jnp.broadcast_to(target_ref[row : row + 1, :], (rank, lanes))
            source = jnp.maximum(target, 0) + component * tiles
            value = jnp.take_along_axis(block, source, axis=1, mode="promise_in_bounds")
            picked = jnp.where(target >= 0, value, picked)
        turned = pltpu.roll(picked, tiles, 1)
        picked_ref[0, k] = jnp.where(component == 0, picked, turned)
        picked_ref[1, k] = jnp.where(component == 0, turned, picked)

    def mix(g, carry):
        total = [[None, None] for _ in range(4)]
        for k in range(far_count):
            picked = [picked_ref[c, k] for c in range(2)]
            for i in range(4):
                block = coupling_ref[k, g * 4 + i].astype(F32)
                for c in range(2):
                    product = block * picked[c]
                    part = product[0:8]
                    for q in range(8, rank, 8):
                        part = part + product[q : q + 8]
                    total[i][c] = part if k == 0 else total[i][c] + part
        for i in range(4):
            for c in range(2):
                row = jnp.sum(total[i][c], axis=0, keepdims=True)
                mixed_ref[pl.ds(c * half + g * 4 + i, 1), :] = row
        return carry

    lax.fori_loop(0, groups, mix, 0, unroll=True)
    mixed = mixed_ref[...].T
    mixed = jnp.concatenate([mixed[:tiles], mixed[tiles:]], axis=1).astype(BF16)
    wide = 8 * rank
    from_row = lax.broadcasted_iota(jnp.int32, (2 * rank, wide), 0)
    to_rank = lax.broadcasted_iota(jnp.int32, (2 * rank, wide), 1) % rank
    repeated = []
    for c in range(2):
        wanted = (to_rank // half) * rank + c * half + to_rank % half
        picks = jnp.where(from_row == wanted, 1.0, 0.0).astype(BF16)
        repeated.append(jnp.dot(mixed, picks, preferred_element_type=F32))
    own_block = (
        lax.broadcasted_iota(jnp.int32, (16, wide), 0) % 8
        == lax.broadcasted_iota(jnp.int32, (16, wide), 1) // rank
    )
    for g in range(tiles // 8):
        rows8 = slice(g * 8, g * 8 + 8)
        both = jnp.concatenate([repeated[0][rows8], repeated[1][rows8]], axis=0)
        both = jnp.where(own_block, both, 0.0).astype(BF16)
        far = jnp.dot(
            both, basis_ref[g * wide : (g + 1) * wide, :], preferred_element_type=F32
        )
        voltage_ref[0, rows8, :] = near_ref[0, rows8, :] - far[8:16]
        voltage_ref[1, rows8, :] = near_ref[1, rows8, :] + far[0:8]
    sums = scatter(
        code_ref, voltage_ref, spread_ref, first, slot_ref.shape[0], True
    )
    shift = turn(peers)
    for c in range(2):
        slot_ref[: peers - shift, c, :] = sums[c][shift:]
        slot_ref[peers - shift :, c, :] = sums[c][:shift]


def own_sum_kernel(
    code_ref, voltage_ref, same_ref, other_ref, port_ref, impedance_ref, own_ref, asked_ref,
    picks_ref, spread_ref,
):
    rows = own_ref.shape[1]
    ports = impedance_ref.shape[1]
    chips = same_ref.shape[1]
    first_core = lax.axis_index("core") == 0
    same = same_ref[0].astype(jnp.int32)
    other = other_ref[0].astype(jnp.int32)
    asked = [jnp.where(first_core, same, other), jnp.where(first_core, other, same)]
    sub_low = lax.broadcasted_iota(jnp.int32, (128, 128), 0)
    for core in range(2):
        asked_ref[core] = asked[core] >> 7
        low = asked[core] & 127
        for chip in range(chips):
            there = jnp.broadcast_to(low[chip : chip + 1], (128, 128)) == sub_low
            place = core * chips + chip
            picks_ref[:, place * 128 : (place + 1) * 128] = jnp.where(there, 1.0, 0.0).astype(BF16)
    port_current = jnp.sum(same_ref[1] + other_ref[1], axis=0, keepdims=True)
    real = port_current[:, :ports]
    imag = port_current[:, ports:]
    both = jnp.concatenate([real, imag, jnp.zeros((6, ports), F32)], axis=0)
    by_real = dot_nt(both, impedance_ref[0], lax.Precision.HIGHEST)
    by_imag = dot_nt(both, impedance_ref[1], lax.Precision.HIGHEST)
    pad = jnp.zeros((1, 128 - ports), F32)
    terms = [
        jnp.concatenate([by_real[0:1] - by_imag[1:2], pad], axis=1),
        jnp.concatenate([by_real[1:2] + by_imag[0:1], pad], axis=1),
    ]
    port = port_ref[...] - device_index() * (rows * 128)
    port = jnp.where((port >= 0) & (port < rows * 128), port, -1)
    port = jnp.concatenate([port, jnp.full((1, 128 - ports), -1, jnp.int32)], axis=1)
    left, right = place_few(port >> 7, port & 127, terms, rows)
    total = dot_nt(left, right)
    sums = scatter(code_ref, voltage_ref, spread_ref, 0, rows, False)
    for c in range(2):
        own_ref[c] = sums[c] + (
            total[2 * c * rows : (2 * c + 1) * rows] + total[(2 * c + 1) * rows : (2 * c + 2) * rows]
        )


def finish_kernel(own_ref, arrived_ref, asked_ref, picks_ref, out_ref):
    rows = own_ref.shape[1]
    peers = arrived_ref.shape[0]
    chips = peers // 2
    sub_high = lax.broadcasted_iota(jnp.int32, (rows, 128), 0)
    left = []
    for core in range(2):
        for chip in range(chips):
            here = jnp.broadcast_to(asked_ref[core, chip : chip + 1, :], (rows, 128)) == sub_high
            parts = []
            for c in range(2):
                place = (2 * chip + core + peers - turn(peers)) % peers
                value = jnp.broadcast_to(arrived_ref[place, c : c + 1, :], (rows, 128))
                parts.extend(split(jnp.where(here, value, 0.0)))
            left.append(jnp.concatenate(parts, axis=0))
    total = dot_nt(jnp.concatenate(left, axis=1), picks_ref[...])
    for c in range(2):
        summed = own_ref[c] + (
            total[2 * c * rows : (2 * c + 1) * rows] + total[(2 * c + 1) * rows : (2 * c + 2) * rows]
        )
        for r in range(rows):
            out_ref[c : c + 1, r * 128 : (r + 1) * 128] = summed[r : r + 1]


def per_device(
    mesh_current,
    branch_entry,
    branch_sign,
    need_slots,
    resistance,
    near_blocks,
    near_source,
    basis_in,
    coupling,
    basis_out,
    admissible,
    port_mesh,
    port_coupling,
):
    chips = lax.axis_size("chips")
    peers = 2 * chips
    core = lax.axis_index("core")
    device = 2 * lax.axis_index("chips") + core
    mesh_dev = mesh_current.shape[1]
    tiles, near_count, width, _ = near_blocks.shape
    rank = basis_in.shape[1]
    far_count = admissible.shape[1]
    own_rows = mesh_dev // 128
    vmem = pl.BlockSpec(memory_space=pltpu.VMEM)
    shape = jax.ShapeDtypeStruct

    code = (branch_entry * 2 + branch_sign).reshape(2, tiles, width)
    coupling_lanes = jnp.transpose(coupling, (1, 2, 3, 0))
    basis_in_rows = basis_in.reshape(tiles * rank, width)
    basis_out_rows = basis_out.reshape(tiles * rank, width)
    half = jnp.arange(2 * tiles, dtype=jnp.int32) // tiles
    sources = jnp.transpose(near_source)
    sources = jnp.concatenate([sources, sources], axis=1) + half[None] * tiles
    band = peers * tiles // far_count
    spans = band // tiles + 1
    bases = device * tiles + jnp.arange(far_count, dtype=jnp.int32) * band
    shifted = (jnp.transpose(admissible) - bases[:, None]) % (peers * tiles)
    shifted = jnp.concatenate([shifted, shifted], axis=1)[:, None, :]
    shifted = shifted - jnp.arange(spans, dtype=jnp.int32)[None, :, None] * tiles
    inside = (shifted >= 0) & (shifted < tiles)
    targets = jnp.where(inside, shifted, -1).reshape(far_count * spans, 2 * tiles)

    def in_hbm(x):
        return pltpu.with_memory_space_constraint(x, pltpu.HBM)

    hbm = pl.BlockSpec(memory_space=pl.ANY)
    port_row = port_mesh.reshape(1, -1)
    pack_rows = (2 * own_rows + 3 + 7) // 8 * 8
    pack, mesh_near, need_near, port_near = pl.pallas_call(
        pack_kernel,
        out_shape=(
            shape((chips, pack_rows, 128), F32),
            pltpu.VMEM(mesh_current.shape, F32),
            pltpu.VMEM(need_slots.shape, jnp.int32),
            pltpu.VMEM(port_row.shape, jnp.int32),
        ),
        in_specs=[hbm] * 3,
        out_specs=(vmem,) * 4,
        scratch_shapes=[pltpu.SemaphoreType.DMA((3,))],
        compiler_params=params(),
        name="pack",
    )(in_hbm(mesh_current), in_hbm(need_slots), in_hbm(port_row))
    chip_members = [[(j + turn(chips)) % chips for j in range(chips)]]
    same = lax.all_to_all(pack, "chips", 0, 0, tiled=True, axis_index_groups=chip_members)
    own_part, pairs = pl.pallas_call(
        own_lookup_kernel,
        out_shape=(
            shape((2, tiles, width), F32),
            pltpu.VMEM((far_count, rank // 2, rank, 2 * tiles), BF16),
        ),
        in_specs=[vmem] * 2 + [hbm],
        out_specs=(vmem,) * 2,
        scratch_shapes=[
            pltpu.VMEM(coupling_lanes.shape, BF16),
            pltpu.SemaphoreType.DMA((2,)),
        ],
        compiler_params=params(),
        cost_estimate=small_cost(),
        name="own_lookup",
    )(mesh_near, code, in_hbm(coupling_lanes))
    other = lax.ppermute(same, "core", [(0, 1), (1, 0)])
    part, same_rows = pl.pallas_call(
        functools.partial(same_core_kernel, first=own_rows),
        out_shape=(shape((2, tiles, width), F32), shape((2, chips, 128), F32)),
        in_specs=[vmem] * 4,
        out_specs=(vmem,) * 2,
        scratch_shapes=[pltpu.VMEM((2, chips, 128), F32)],
        compiler_params=params(),
        cost_estimate=small_cost(),
        name="same_core",
    )(own_part, same, need_near, code)
    current, coeff, other_rows = pl.pallas_call(
        functools.partial(current_kernel, first=own_rows),
        out_shape=(
            shape((2, tiles, width), F32),
            shape((peers, rank, 2 * tiles), BF16),
            shape((2, chips, 128), F32),
        ),
        in_specs=[vmem] * 4 + [hbm],
        out_specs=(vmem,) * 3,
        scratch_shapes=[
            pltpu.VMEM((2, chips, 128), F32),
            pltpu.VMEM(basis_in_rows.shape, BF16),
            pltpu.SemaphoreType.DMA((1,)),
        ],
        compiler_params=params(),
        name="currents",
    )(part, other, need_near, code, in_hbm(basis_in_rows))
    members = [[(j + turn(peers)) % peers for j in range(peers)]]
    all_coeff = lax.all_to_all(
        coeff, ("chips", "core"), 0, 0, tiled=True, axis_index_groups=members
    )
    near_rows = near_blocks.reshape(tiles * near_count * width, width)
    near = pl.pallas_call(
        near_kernel,
        out_shape=shape((2, tiles, width), F32),
        in_specs=[vmem] * 2 + [hbm] * 2,
        out_specs=vmem,
        scratch_shapes=[
            pltpu.VMEM((near_count * width, 2 * tiles), BF16),
            pltpu.VMEM(near_rows.shape, BF16),
            pltpu.VMEM((tiles, width), F32),
            pltpu.SemaphoreType.DMA((4,)),
        ],
        compiler_params=params(),
        cost_estimate=pl.CostEstimate(
            flops=256 * near_blocks.size, bytes_accessed=2 * near_blocks.size, transcendentals=0
        ),
        name="near_field",
    )(sources, current, in_hbm(resistance.reshape(tiles, width)), in_hbm(near_rows))
    voltage, slots = pl.pallas_call(
        functools.partial(voltage_kernel, first=own_rows),
        out_shape=(shape((2, tiles, width), F32), shape((peers, 2, 128), F32)),
        in_specs=[vmem] * 6,
        out_specs=(vmem,) * 2,
        scratch_shapes=[
            pltpu.VMEM((2, far_count, rank, 2 * tiles), F32),
            pltpu.VMEM((rank, 2 * tiles), F32),
            pltpu.VMEM((tiles // 8, 2, 6, 8, 128), F32),
        ],
        compiler_params=params(),
        name="voltages",
    )(
        all_coeff,
        targets,
        pairs,
        basis_out_rows,
        near,
        code,
    )
    arrived = lax.all_to_all(
        slots, ("chips", "core"), 0, 0, tiled=True, axis_index_groups=members
    )
    own, asked, picks = pl.pallas_call(
        own_sum_kernel,
        out_shape=(
            shape((2, own_rows, 128), F32),
            shape((2, chips, 128), jnp.int32),
            shape((128, peers * 128), BF16),
        ),
        in_specs=[vmem] * 6,
        out_specs=(vmem,) * 3,
        scratch_shapes=[
            pltpu.VMEM((tiles // 8, 2, 6, 8, 128), F32),
        ],
        compiler_params=params(),
        cost_estimate=small_cost(),
        name="own_sums",
    )(code, voltage, same_rows, other_rows, port_near, port_coupling)
    return pl.pallas_call(
        finish_kernel,
        out_shape=shape((2, mesh_dev), F32),
        in_specs=[vmem] * 4,
        out_specs=vmem,
        compiler_params=params(),
        name="finish",
    )(own, arrived, asked, picks)


def solution(mesh):
    groups, peers = mesh.devices.shape
    split_mesh = jax.sharding.Mesh(
        mesh.devices.reshape(groups, peers // 2, 2), ("groups", "chips", "core")
    )
    in_specs = (
        P(None, SPREAD),
        P(None, SPREAD),
        P(None, SPREAD),
        P(SPREAD, None),
        P(SPREAD),
        P(SPREAD, None, None, None),
        P(SPREAD, None),
        P(SPREAD, None, None),
        P(SPREAD, None, None, None),
        P(SPREAD, None, None),
        P(SPREAD, None),
        P("groups"),
        P(),
    )
    out_specs = P(None, SPREAD)
    return jax.shard_map(
        per_device, mesh=split_mesh, in_specs=in_specs, out_specs=out_specs, check_vma=False
    )
```

```python
import functools

import jax
import jax.numpy as jnp
from jax import lax
from jax.experimental import pallas as pl
from jax.experimental.pallas import tpu as pltpu
from jax.sharding import PartitionSpec as P

F32 = jnp.float32
BF16 = jnp.bfloat16
SPREAD = ("groups", "chips", "core")
VMEM_LIMIT = 24 * 1024 * 1024
NT = (((1,), (1,)), ((), ()))


def params():
    return pltpu.CompilerParams(vmem_limit_bytes=VMEM_LIMIT)


def small_cost():
    return pl.CostEstimate(flops=10**9, bytes_accessed=8 * 10**6, transcendentals=0)


def lane_pick(row, lanes):
    spread = jnp.broadcast_to(row, lanes.shape)
    return jnp.take_along_axis(spread, lanes, axis=1, mode="promise_in_bounds")


def dot_nt(left, right, precision=None):
    return lax.dot_general(
        left, right, NT, preferred_element_type=F32, precision=precision
    )


def turn(members):
    return members // 4


def by_chip(rows):
    shift = turn(rows.shape[0])
    return jnp.concatenate([rows[rows.shape[0] - shift :], rows[: rows.shape[0] - shift]], axis=0)


def by_place(rows):
    shift = turn(rows.shape[0])
    return jnp.concatenate([rows[shift:], rows[:shift]], axis=0)


def device_index():
    return 2 * lax.axis_index("chips") + lax.axis_index("core")


def fetch(copies):
    for copy in copies:
        copy.start()
    for copy in copies:
        copy.wait()


def pack_kernel(
    mesh_hbm, need_hbm, port_hbm, out_ref, mesh_ref, need_ref, port_ref, sems
):
    rows = mesh_ref.shape[1] // 128
    ports = port_ref.shape[1]
    chips = out_ref.shape[0]
    fetch(
        [
            pltpu.make_async_copy(source, target, sems.at[i])
            for i, (source, target) in enumerate(
                [(mesh_hbm, mesh_ref), (need_hbm, need_ref), (port_hbm, port_ref)]
            )
        ]
    )
    port = port_ref[...] - device_index() * (rows * 128)
    port = jnp.where((port >= 0) & (port < rows * 128), port, -1)
    port = jnp.broadcast_to(jnp.concatenate([port, port], axis=1), (8, 128))
    port_high, port_low = port >> 7, port & 127
    port_value = jnp.zeros((8, 128), F32)
    lane = lax.broadcasted_iota(jnp.int32, (8, 128), 1)
    for r in range(rows):
        real_row = mesh_ref[0:1, r * 128 : (r + 1) * 128]
        imag_row = mesh_ref[1:2, r * 128 : (r + 1) * 128]
        both = jnp.where(
            lane < ports, lane_pick(real_row, port_low), lane_pick(imag_row, port_low)
        )
        port_value = jnp.where(port_high == r, both, port_value)
        out_ref[0, r : r + 1, :] = real_row
        out_ref[0, rows + r : rows + r + 1, :] = imag_row
    block = out_ref[0, : 2 * rows, :]
    for chip in range(1, chips):
        out_ref[chip, : 2 * rows, :] = block
    need = [by_place(need_ref[pl.ds(c, chips, 2), :].astype(F32)) for c in range(2)]
    first = lax.axis_index("core") == 0
    out_ref[:, 2 * rows, :] = jnp.where(first, need[0], need[1])
    out_ref[:, 2 * rows + 1, :] = jnp.where(first, need[1], need[0])
    out_ref[:, 2 * rows + 2, :] = jnp.broadcast_to(port_value[0:1], (chips, 128))
    for r in range(2 * rows + 3, out_ref.shape[1]):
        out_ref[:, r, :] = jnp.zeros((chips, 128), F32)


def ask(need_ref, pack_ref, table_ref, core, rows):
    chips = pack_ref.shape[0]
    sub = lax.broadcasted_iota(jnp.int32, (rows, 128), 0)
    for chip in range(chips):
        wanted = need_ref[pl.ds(2 * chip + core, 1), :]
        wanted = jnp.broadcast_to(jnp.maximum(wanted, 0), (rows, 128))
        here = (wanted >> 7) == sub
        low = wanted & 127
        for c in range(2):
            block = pack_ref[(chip + chips - turn(chips)) % chips, c * rows : (c + 1) * rows, :]
            picked = jnp.take_along_axis(block, low, axis=1, mode="promise_in_bounds")
            picked = jnp.where(here, picked, 0.0)
            table_ref[c, chip : chip + 1, :] = jnp.sum(picked, axis=0, keepdims=True)


def lookup(code_ref, start, tables):
    total = [None, None]
    for k in range(2):
        code = code_ref[k, pl.ds(start, 8), :]
        high, low = code >> 8, (code >> 1) & 127
        value = [jnp.zeros((8, 128), F32), jnp.zeros((8, 128), F32)]
        for first, step, count, row_of in tables:
            offset = high - first
            for r in range(count):
                here = offset == r * step
                for c in range(2):
                    value[c] = jnp.where(here, lane_pick(row_of(r, c), low), value[c])
        along = (code & 1) == 1
        for c in range(2):
            signed = jnp.where(along, value[c], -value[c])
            total[c] = signed if k == 0 else total[c] + signed
    return total


def own_lookup_kernel(
    mesh_ref, code_ref, coupling_hbm, blocks_hbm, out_ref, pair_hbm, early_ref, raw_ref, pair_ref,
    sems,
):
    rows = mesh_ref.shape[1] // 128
    far_count, rank = coupling_hbm.shape[:2]
    half = rank // 2
    part = far_count // 2
    copies = [
        pltpu.make_async_copy(
            coupling_hbm.at[pl.ds(i * part, part)], raw_ref.at[pl.ds(i * part, part)], sems.at[i]
        )
        for i in range(2)
    ]
    early_copy = pltpu.make_async_copy(
        blocks_hbm.at[pl.ds(0, early_ref.shape[0])], early_ref, sems.at[2]
    )
    out_copies = [
        pltpu.make_async_copy(
            pair_ref.at[pl.ds(i * part, part)], pair_hbm.at[pl.ds(i * part, part)], sems.at[3 + i]
        )
        for i in range(2)
    ]
    for copy in copies + [early_copy]:
        copy.start()

    def own_row(r, c):
        return mesh_ref[c : c + 1, r * 128 : (r + 1) * 128]

    def block(g, carry):
        start = pl.multiple_of(g * 8, 8)
        total = lookup(code_ref, start, [(0, 1, rows, own_row)])
        out_ref[0, pl.ds(start, 8), :] = total[0]
        out_ref[1, pl.ds(start, 8), :] = total[1]
        return carry

    lax.fori_loop(0, code_ref.shape[1] // 8, block, 0, unroll=True)
    for k in range(far_count):
        if k % part == 0:
            copies[k // part].wait()
        for r in range(half):
            pair_ref[k, r] = jnp.concatenate([raw_ref[k, r], raw_ref[k, half + r]], axis=1)
        if k % part == part - 1:
            out_copies[k // part].start()
    for copy in out_copies + [early_copy]:
        copy.wait()


def add_peers(part_ref, pack_ref, need_ref, code_ref, table_ref, out_ref, core, first):
    chips = pack_ref.shape[0]
    ask(need_ref, pack_ref, table_ref, core, first)

    def peer_row(r, c):
        return table_ref[c, r : r + 1, :]

    def block(g, carry):
        start = pl.multiple_of(g * 8, 8)
        total = lookup(code_ref, start, [(first + core, 2, chips, peer_row)])
        for c in range(2):
            out_ref[c, pl.ds(start, 8), :] = total[c] + part_ref[c, pl.ds(start, 8), :]
        return carry

    lax.fori_loop(0, code_ref.shape[1] // 8, block, 0, unroll=True)


def same_core_kernel(
    part_ref, same_ref, need_ref, code_ref, out_ref, rows_ref, table_ref, *, first
):
    rows_ref[0] = by_chip(same_ref[:, 2 * first, :])
    rows_ref[1] = same_ref[:, 2 * first + 2, :]
    add_peers(
        part_ref, same_ref, need_ref, code_ref, table_ref, out_ref,
        lax.axis_index("core"), first,
    )


def current_kernel(
    part_ref, other_ref, need_ref, code_ref, basis_hbm, current_ref, coeff_ref, rows_ref,
    table_ref, basis_ref, sem, *, first,
):
    tiles = code_ref.shape[1]
    rank = basis_ref.shape[0] // tiles
    copy = pltpu.make_async_copy(basis_hbm, basis_ref, sem.at[0])
    copy.start()
    rows_ref[0] = by_chip(other_ref[:, 2 * first + 1, :])
    rows_ref[1] = other_ref[:, 2 * first + 2, :]
    add_peers(
        part_ref, other_ref, need_ref, code_ref, table_ref, current_ref,
        1 - lax.axis_index("core"), first,
    )
    copy.wait()
    inputs = jnp.concatenate([current_ref[0], current_ref[1]], axis=0)
    inputs = inputs.T.astype(BF16)
    lane_tile = lax.broadcasted_iota(jnp.int32, (rank, 2 * tiles), 1) % tiles
    full = jnp.dot(basis_ref[...], inputs, preferred_element_type=F32)
    chosen = jnp.zeros((rank, 2 * tiles), F32)
    for t in range(tiles):
        chosen = jnp.where(lane_tile == t, full[t * rank : (t + 1) * rank], chosen)
    coeff = chosen.astype(BF16)
    for p in range(coeff_ref.shape[0]):
        coeff_ref[p] = coeff


def near_kernel(
    source_ref, current_ref, resistance_hbm, blocks_hbm, early_ref, pair_hbm, out_ref, pair_ref,
    inputs_ref, blocks_ref, resistance_ref, sems,
):
    tiles = current_ref.shape[1]
    width = blocks_ref.shape[1]
    ready = early_ref.shape[0]
    count = (ready + blocks_ref.shape[0]) // (tiles * width)
    span = 8 * count * width
    groups = tiles // 8
    early_groups = ready // span
    middle = (early_groups + groups) // 2
    copies = {}
    for i, (first, last) in enumerate([(early_groups, middle), (middle, groups)]):
        length = (last - first) * span
        copies[first] = pltpu.make_async_copy(
            blocks_hbm.at[pl.ds(first * span, length)],
            blocks_ref.at[pl.ds(first * span - ready, length)],
            sems.at[i],
        )
    pair_copy = pltpu.make_async_copy(pair_hbm, pair_ref, sems.at[2])
    late_copy = pltpu.make_async_copy(resistance_hbm, resistance_ref, sems.at[3])
    for copy in copies.values():
        copy.start()
    late_copy.start()
    pair_copy.start()
    lane_tile = lax.broadcasted_iota(jnp.int32, (width, 128), 1) % tiles
    rows = jnp.concatenate([current_ref[0], current_ref[1]], axis=0)
    columns = rows.T.astype(BF16)
    row_index = lax.broadcasted_iota(jnp.int32, (128, 128), 0)
    for k in range(count):
        picks = jnp.where(row_index == source_ref[k : k + 1, :], 1.0, 0.0).astype(BF16)
        inputs_ref[k * width : (k + 1) * width, :] = jnp.dot(
            columns, picks, preferred_element_type=F32
        ).astype(BF16)
    inputs = inputs_ref[...]
    total = jnp.zeros((width, 128), F32)
    for g in range(groups):
        if g in copies:
            copies[g].wait()
        held_ref, offset = (early_ref, 0) if g < early_groups else (blocks_ref, ready)
        block = jnp.concatenate(
            [
                jnp.concatenate(
                    [
                        held_ref[pl.ds((t * count + k) * width - offset, width), :]
                        for t in range(g * 8, g * 8 + 8)
                    ],
                    axis=0,
                )
                for k in range(count)
            ],
            axis=1,
        )
        full = jnp.dot(block, inputs, preferred_element_type=F32)
        for i in range(8):
            total = jnp.where(
                lane_tile == g * 8 + i, full[i * width : (i + 1) * width], total
            )
    rows = total.T
    late_copy.wait()
    pair_copy.wait()
    resistance = resistance_ref[...]
    out_ref[0] = resistance * current_ref[0] - rows[tiles:]
    out_ref[1] = resistance * current_ref[1] + rows[:tiles]


def split(value):
    top = value.astype(BF16)
    return top, (value - top.astype(F32)).astype(BF16)


def counts(rows):
    return lax.broadcasted_iota(jnp.int32, (rows, 128), 0).astype(F32)


def place(high, low, values, rows, spread_ref):
    sub_high, sub_low = counts(rows).astype(BF16), counts(128).astype(BF16)
    one, zero = jnp.ones((128, 128), BF16), jnp.zeros((128, 128), BF16)
    spread_ref[0] = high.astype(F32)
    spread_ref[1] = low.astype(F32)
    for c, value in enumerate(values):
        top, rest = split(value)
        spread_ref[2 + 2 * c] = top.astype(F32)
        spread_ref[3 + 2 * c] = rest.astype(F32)

    def spread(j, i, count):
        return jnp.broadcast_to(spread_ref[j, i : i + 1, :], (count, 128)).astype(BF16)

    left, right = [], []
    for i in range(8):
        here = spread(0, i, rows) == sub_high
        left.append(
            jnp.concatenate(
                [jnp.where(here, spread(j, i, rows), zero[:rows]) for j in range(2, 6)], axis=0
            )
        )
        right.append(jnp.where(spread(1, i, 128) == sub_low, one, zero))
    return jnp.concatenate(left, axis=1), jnp.concatenate(right, axis=1)


def place_few(high, low, values, rows):
    sub_high = lax.broadcasted_iota(jnp.int32, (rows, 128), 0)
    sub_low = lax.broadcasted_iota(jnp.int32, (128, 128), 0)
    left, right = [], []
    for i in range(high.shape[0]):
        here = jnp.broadcast_to(high[i : i + 1], (rows, 128)) == sub_high
        parts = []
        for value in values:
            spread = jnp.where(here, jnp.broadcast_to(value[i : i + 1], (rows, 128)), 0.0)
            parts.extend(split(spread))
        left.append(jnp.concatenate(parts, axis=0))
        there = jnp.broadcast_to(low[i : i + 1], (128, 128)) == sub_low
        right.append(jnp.where(there, 1.0, 0.0).astype(BF16))
    return jnp.concatenate(left, axis=1), jnp.concatenate(right, axis=1)


def scatter(code_ref, voltage_ref, spread_ref, first, rows, low_streams):
    total = None
    for g in range(code_ref.shape[1] // 8):
        for k in range(2):
            code = code_ref[k, g * 8 : g * 8 + 8, :]
            along = (code & 1) == 1
            values = []
            for c in range(2):
                voltage = voltage_ref[c, g * 8 : g * 8 + 8, :]
                values.append(jnp.where(along, voltage, -voltage))
            left, right = place(
                (code >> 8) - first, (code >> 1) & 127, values, rows, spread_ref.at[g, k]
            )
            term = dot_nt(right, left) if low_streams else dot_nt(left, right)
            total = term if total is None else total + term
    total = total.T if low_streams else total
    return [
        total[2 * c * rows : (2 * c + 1) * rows] + total[(2 * c + 1) * rows : (2 * c + 2) * rows]
        for c in range(2)
    ]


def voltage_kernel(
    coeff_ref, target_ref, coupling_ref, basis_ref, near_ref, code_ref, voltage_ref, slot_ref,
    picked_ref, mixed_ref, spread_ref, *, first,
):
    peers, rank, lanes = coeff_ref.shape
    far_count = coupling_ref.shape[0]
    tiles = lanes // 2
    half = rank // 2
    groups = half // 4
    device = device_index()
    spans = target_ref.shape[0] // far_count
    stride = peers // far_count
    component = lax.broadcasted_iota(jnp.int32, (rank, lanes), 1) // tiles
    for k in range(far_count):
        picked = jnp.zeros((rank, lanes), F32)
        for i in range(spans):
            row = k * spans + i
            block = coeff_ref[(device + k * stride + i + peers - turn(peers)) % peers].astype(F32)
            target = jnp.broadcast_to(target_ref[row : row + 1, :], (rank, lanes))
            source = jnp.maximum(target, 0) + component * tiles
            value = jnp.take_along_axis(block, source, axis=1, mode="promise_in_bounds")
            picked = jnp.where(target >= 0, value, picked)
        turned = pltpu.roll(picked, tiles, 1)
        picked_ref[0, k] = jnp.where(component == 0, picked, turned)
        picked_ref[1, k] = jnp.where(component == 0, turned, picked)

    def mix(g, carry):
        total = [[None, None] for _ in range(4)]
        for k in range(far_count):
            picked = [picked_ref[c, k] for c in range(2)]
            for i in range(4):
                block = coupling_ref[k, g * 4 + i].astype(F32)
                for c in range(2):
                    product = block * picked[c]
                    part = product[0:8]
                    for q in range(8, rank, 8):
                        part = part + product[q : q + 8]
                    total[i][c] = part if k == 0 else total[i][c] + part
        for i in range(4):
            for c in range(2):
                row = jnp.sum(total[i][c], axis=0, keepdims=True)
                mixed_ref[pl.ds(c * half + g * 4 + i, 1), :] = row
        return carry

    lax.fori_loop(0, groups, mix, 0, unroll=True)
    mixed = mixed_ref[...].T
    mixed = jnp.concatenate([mixed[:tiles], mixed[tiles:]], axis=1).astype(BF16)
    wide = 8 * rank
    from_row = lax.broadcasted_iota(jnp.int32, (2 * rank, wide), 0)
    to_rank = lax.broadcasted_iota(jnp.int32, (2 * rank, wide), 1) % rank
    repeated = []
    for c in range(2):
        wanted = (to_rank // half) * rank + c * half + to_rank % half
        picks = jnp.where(from_row == wanted, 1.0, 0.0).astype(BF16)
        repeated.append(jnp.dot(mixed, picks, preferred_element_type=F32))
    own_block = (
        lax.broadcasted_iota(jnp.int32, (16, wide), 0) % 8
        == lax.broadcasted_iota(jnp.int32, (16, wide), 1) // rank
    )
    for g in range(tiles // 8):
        rows8 = slice(g * 8, g * 8 + 8)
        both = jnp.concatenate([repeated[0][rows8], repeated[1][rows8]], axis=0)
        both = jnp.where(own_block, both, 0.0).astype(BF16)
        far = jnp.dot(
            both, basis_ref[g * wide : (g + 1) * wide, :], preferred_element_type=F32
        )
        voltage_ref[0, rows8, :] = near_ref[0, rows8, :] - far[8:16]
        voltage_ref[1, rows8, :] = near_ref[1, rows8, :] + far[0:8]
    sums = scatter(
        code_ref, voltage_ref, spread_ref, first, slot_ref.shape[0], True
    )
    shift = turn(peers)
    for c in range(2):
        slot_ref[: peers - shift, c, :] = sums[c][shift:]
        slot_ref[peers - shift :, c, :] = sums[c][:shift]


def own_sum_kernel(
    code_ref, voltage_ref, same_ref, other_ref, port_ref, impedance_ref, own_ref, asked_ref,
    picks_ref, spread_ref,
):
    rows = own_ref.shape[1]
    ports = impedance_ref.shape[1]
    chips = same_ref.shape[1]
    first_core = lax.axis_index("core") == 0
    same = same_ref[0].astype(jnp.int32)
    other = other_ref[0].astype(jnp.int32)
    asked = [jnp.where(first_core, same, other), jnp.where(first_core, other, same)]
    sub_low = lax.broadcasted_iota(jnp.int32, (128, 128), 0)
    for core in range(2):
        asked_ref[core] = asked[core] >> 7
        low = asked[core] & 127
        for chip in range(chips):
            there = jnp.broadcast_to(low[chip : chip + 1], (128, 128)) == sub_low
            place = core * chips + chip
            picks_ref[:, place * 128 : (place + 1) * 128] = jnp.where(there, 1.0, 0.0).astype(BF16)
    port_current = jnp.sum(same_ref[1] + other_ref[1], axis=0, keepdims=True)
    real = port_current[:, :ports]
    imag = port_current[:, ports:]
    both = jnp.concatenate([real, imag, jnp.zeros((6, ports), F32)], axis=0)
    by_real = dot_nt(both, impedance_ref[0], lax.Precision.HIGHEST)
    by_imag = dot_nt(both, impedance_ref[1], lax.Precision.HIGHEST)
    pad = jnp.zeros((1, 128 - ports), F32)
    terms = [
        jnp.concatenate([by_real[0:1] - by_imag[1:2], pad], axis=1),
        jnp.concatenate([by_real[1:2] + by_imag[0:1], pad], axis=1),
    ]
    port = port_ref[...] - device_index() * (rows * 128)
    port = jnp.where((port >= 0) & (port < rows * 128), port, -1)
    port = jnp.concatenate([port, jnp.full((1, 128 - ports), -1, jnp.int32)], axis=1)
    left, right = place_few(port >> 7, port & 127, terms, rows)
    total = dot_nt(left, right)
    sums = scatter(code_ref, voltage_ref, spread_ref, 0, rows, False)
    for c in range(2):
        own_ref[c] = sums[c] + (
            total[2 * c * rows : (2 * c + 1) * rows] + total[(2 * c + 1) * rows : (2 * c + 2) * rows]
        )


def finish_kernel(own_ref, arrived_ref, asked_ref, picks_ref, out_ref):
    rows = own_ref.shape[1]
    peers = arrived_ref.shape[0]
    chips = peers // 2
    sub_high = lax.broadcasted_iota(jnp.int32, (rows, 128), 0)
    left = []
    for core in range(2):
        for chip in range(chips):
            here = jnp.broadcast_to(asked_ref[core, chip : chip + 1, :], (rows, 128)) == sub_high
            parts = []
            for c in range(2):
                place = (2 * chip + core + peers - turn(peers)) % peers
                value = jnp.broadcast_to(arrived_ref[place, c : c + 1, :], (rows, 128))
                parts.extend(split(jnp.where(here, value, 0.0)))
            left.append(jnp.concatenate(parts, axis=0))
    total = dot_nt(jnp.concatenate(left, axis=1), picks_ref[...])
    for c in range(2):
        summed = own_ref[c] + (
            total[2 * c * rows : (2 * c + 1) * rows] + total[(2 * c + 1) * rows : (2 * c + 2) * rows]
        )
        for r in range(rows):
            out_ref[c : c + 1, r * 128 : (r + 1) * 128] = summed[r : r + 1]


def per_device(
    mesh_current,
    branch_entry,
    branch_sign,
    need_slots,
    resistance,
    near_blocks,
    near_source,
    basis_in,
    coupling,
    basis_out,
    admissible,
    port_mesh,
    port_coupling,
):
    chips = lax.axis_size("chips")
    peers = 2 * chips
    core = lax.axis_index("core")
    device = 2 * lax.axis_index("chips") + core
    mesh_dev = mesh_current.shape[1]
    tiles, near_count, width, _ = near_blocks.shape
    rank = basis_in.shape[1]
    far_count = admissible.shape[1]
    own_rows = mesh_dev // 128
    vmem = pl.BlockSpec(memory_space=pltpu.VMEM)
    shape = jax.ShapeDtypeStruct

    code = (branch_entry * 2 + branch_sign).reshape(2, tiles, width)
    coupling_lanes = jnp.transpose(coupling, (1, 2, 3, 0))
    basis_in_rows = basis_in.reshape(tiles * rank, width)
    basis_out_rows = basis_out.reshape(tiles * rank, width)
    half = jnp.arange(2 * tiles, dtype=jnp.int32) // tiles
    sources = jnp.transpose(near_source)
    sources = jnp.concatenate([sources, sources], axis=1) + half[None] * tiles
    band = peers * tiles // far_count
    spans = band // tiles + 1
    bases = device * tiles + jnp.arange(far_count, dtype=jnp.int32) * band
    shifted = (jnp.transpose(admissible) - bases[:, None]) % (peers * tiles)
    shifted = jnp.concatenate([shifted, shifted], axis=1)[:, None, :]
    shifted = shifted - jnp.arange(spans, dtype=jnp.int32)[None, :, None] * tiles
    inside = (shifted >= 0) & (shifted < tiles)
    targets = jnp.where(inside, shifted, -1).reshape(far_count * spans, 2 * tiles)

    def in_hbm(x):
        return pltpu.with_memory_space_constraint(x, pltpu.HBM)

    hbm = pl.BlockSpec(memory_space=pl.ANY)
    port_row = port_mesh.reshape(1, -1)
    pack_rows = (2 * own_rows + 3 + 7) // 8 * 8
    pack, mesh_near, need_near, port_near = pl.pallas_call(
        pack_kernel,
        out_shape=(
            shape((chips, pack_rows, 128), F32),
            pltpu.VMEM(mesh_current.shape, F32),
            pltpu.VMEM(need_slots.shape, jnp.int32),
            pltpu.VMEM(port_row.shape, jnp.int32),
        ),
        in_specs=[hbm] * 3,
        out_specs=(vmem,) * 4,
        scratch_shapes=[pltpu.SemaphoreType.DMA((3,))],
        compiler_params=params(),
        name="pack",
    )(in_hbm(mesh_current), in_hbm(need_slots), in_hbm(port_row))
    chip_members = [[(j + turn(chips)) % chips for j in range(chips)]]
    same = lax.all_to_all(pack, "chips", 0, 0, tiled=True, axis_index_groups=chip_members)
    near_rows = near_blocks.reshape(tiles * near_count * width, width)
    early_rows = near_rows.shape[0] // 4
    pair_shape = (far_count, rank // 2, rank, 2 * tiles)
    own_part, pairs, early = pl.pallas_call(
        own_lookup_kernel,
        out_shape=(
            shape((2, tiles, width), F32),
            pltpu.HBM(pair_shape, BF16),
            pltpu.VMEM((early_rows, width), BF16),
        ),
        in_specs=[vmem] * 2 + [hbm] * 2,
        out_specs=(vmem, hbm, vmem),
        scratch_shapes=[
            pltpu.VMEM(coupling_lanes.shape, BF16),
            pltpu.VMEM(pair_shape, BF16),
            pltpu.SemaphoreType.DMA((5,)),
        ],
        compiler_params=params(),
        cost_estimate=small_cost(),
        name="own_lookup",
    )(mesh_near, code, in_hbm(coupling_lanes), in_hbm(near_rows))
    other = lax.ppermute(same, "core", [(0, 1), (1, 0)])
    part, same_rows = pl.pallas_call(
        functools.partial(same_core_kernel, first=own_rows),
        out_shape=(shape((2, tiles, width), F32), shape((2, chips, 128), F32)),
        in_specs=[vmem] * 4,
        out_specs=(vmem,) * 2,
        scratch_shapes=[pltpu.VMEM((2, chips, 128), F32)],
        compiler_params=params(),
        cost_estimate=small_cost(),
        name="same_core",
    )(own_part, same, need_near, code)
    current, coeff, other_rows = pl.pallas_call(
        functools.partial(current_kernel, first=own_rows),
        out_shape=(
            shape((2, tiles, width), F32),
            shape((peers, rank, 2 * tiles), BF16),
            shape((2, chips, 128), F32),
        ),
        in_specs=[vmem] * 4 + [hbm],
        out_specs=(vmem,) * 3,
        scratch_shapes=[
            pltpu.VMEM((2, chips, 128), F32),
            pltpu.VMEM(basis_in_rows.shape, BF16),
            pltpu.SemaphoreType.DMA((1,)),
        ],
        compiler_params=params(),
        name="currents",
    )(part, other, need_near, code, in_hbm(basis_in_rows))
    members = [[(j + turn(peers)) % peers for j in range(peers)]]
    all_coeff = lax.all_to_all(
        coeff, ("chips", "core"), 0, 0, tiled=True, axis_index_groups=members
    )
    near, pairs = pl.pallas_call(
        near_kernel,
        out_shape=(shape((2, tiles, width), F32), pltpu.VMEM(pair_shape, BF16)),
        in_specs=[vmem] * 2 + [hbm] * 2 + [vmem, hbm],
        out_specs=(vmem,) * 2,
        scratch_shapes=[
            pltpu.VMEM((near_count * width, 2 * tiles), BF16),
            pltpu.VMEM((near_rows.shape[0] - early_rows, width), BF16),
            pltpu.VMEM((tiles, width), F32),
            pltpu.SemaphoreType.DMA((4,)),
        ],
        compiler_params=params(),
        cost_estimate=pl.CostEstimate(
            flops=256 * near_blocks.size, bytes_accessed=2 * near_blocks.size, transcendentals=0
        ),
        name="near_field",
    )(
        sources,
        current,
        in_hbm(resistance.reshape(tiles, width)),
        in_hbm(near_rows),
        early,
        in_hbm(pairs),
    )
    voltage, slots = pl.pallas_call(
        functools.partial(voltage_kernel, first=own_rows),
        out_shape=(shape((2, tiles, width), F32), shape((peers, 2, 128), F32)),
        in_specs=[vmem] * 6,
        out_specs=(vmem,) * 2,
        scratch_shapes=[
            pltpu.VMEM((2, far_count, rank, 2 * tiles), F32),
            pltpu.VMEM((rank, 2 * tiles), F32),
            pltpu.VMEM((tiles // 8, 2, 6, 8, 128), F32),
        ],
        compiler_params=params(),
        name="voltages",
    )(
        all_coeff,
        targets,
        pairs,
        basis_out_rows,
        near,
        code,
    )
    arrived = lax.all_to_all(
        slots, ("chips", "core"), 0, 0, tiled=True, axis_index_groups=members
    )
    own, asked, picks = pl.pallas_call(
        own_sum_kernel,
        out_shape=(
            shape((2, own_rows, 128), F32),
            shape((2, chips, 128), jnp.int32),
            shape((128, peers * 128), BF16),
        ),
        in_specs=[vmem] * 6,
        out_specs=(vmem,) * 3,
        scratch_shapes=[
            pltpu.VMEM((tiles // 8, 2, 6, 8, 128), F32),
        ],
        compiler_params=params(),
        cost_estimate=small_cost(),
        name="own_sums",
    )(code, voltage, same_rows, other_rows, port_near, port_coupling)
    return pl.pallas_call(
        finish_kernel,
        out_shape=shape((2, mesh_dev), F32),
        in_specs=[vmem] * 4,
        out_specs=vmem,
        compiler_params=params(),
        name="finish",
    )(own, arrived, asked, picks)


def solution(mesh):
    groups, peers = mesh.devices.shape
    split_mesh = jax.sharding.Mesh(
        mesh.devices.reshape(groups, peers // 2, 2), ("groups", "chips", "core")
    )
    in_specs = (
        P(None, SPREAD),
        P(None, SPREAD),
        P(None, SPREAD),
        P(SPREAD, None),
        P(SPREAD),
        P(SPREAD, None, None, None),
        P(SPREAD, None),
        P(SPREAD, None, None),
        P(SPREAD, None, None, None),
        P(SPREAD, None, None),
        P(SPREAD, None),
        P("groups"),
        P(),
    )
    out_specs = P(None, SPREAD)
    return jax.shard_map(
        per_device, mesh=split_mesh, in_specs=in_specs, out_specs=out_specs, check_vma=False
    )
```

```python
import functools

import jax
import jax.numpy as jnp
from jax import lax
from jax.experimental import pallas as pl
from jax.experimental.pallas import tpu as pltpu
from jax.sharding import PartitionSpec as P

F32 = jnp.float32
BF16 = jnp.bfloat16
SPREAD = ("groups", "chips", "core")
VMEM_LIMIT = 24 * 1024 * 1024
NT = (((1,), (1,)), ((), ()))


def params():
    return pltpu.CompilerParams(vmem_limit_bytes=VMEM_LIMIT)


def small_cost():
    return pl.CostEstimate(flops=10**9, bytes_accessed=8 * 10**6, transcendentals=0)


def lane_pick(row, lanes):
    spread = jnp.broadcast_to(row, lanes.shape)
    return jnp.take_along_axis(spread, lanes, axis=1, mode="promise_in_bounds")


def dot_nt(left, right, precision=None):
    return lax.dot_general(
        left, right, NT, preferred_element_type=F32, precision=precision
    )


def turn(members):
    return members // 4


def chip_turn(chips):
    return chips // 2


def by_chip(rows):
    shift = chip_turn(rows.shape[0])
    return jnp.concatenate([rows[rows.shape[0] - shift :], rows[: rows.shape[0] - shift]], axis=0)


def by_place(rows):
    shift = chip_turn(rows.shape[0])
    return jnp.concatenate([rows[shift:], rows[:shift]], axis=0)


def device_index():
    return 2 * lax.axis_index("chips") + lax.axis_index("core")


def fetch(copies):
    for copy in copies:
        copy.start()
    for copy in copies:
        copy.wait()


def pack_kernel(
    mesh_hbm, need_hbm, port_hbm, out_ref, mesh_ref, need_ref, port_ref, sems
):
    rows = mesh_ref.shape[1] // 128
    ports = port_ref.shape[1]
    chips = out_ref.shape[0]
    fetch(
        [
            pltpu.make_async_copy(source, target, sems.at[i])
            for i, (source, target) in enumerate(
                [(mesh_hbm, mesh_ref), (need_hbm, need_ref), (port_hbm, port_ref)]
            )
        ]
    )
    port = port_ref[...] - device_index() * (rows * 128)
    port = jnp.where((port >= 0) & (port < rows * 128), port, -1)
    port = jnp.broadcast_to(jnp.concatenate([port, port], axis=1), (8, 128))
    port_high, port_low = port >> 7, port & 127
    port_value = jnp.zeros((8, 128), F32)
    lane = lax.broadcasted_iota(jnp.int32, (8, 128), 1)
    for r in range(rows):
        real_row = mesh_ref[0:1, r * 128 : (r + 1) * 128]
        imag_row = mesh_ref[1:2, r * 128 : (r + 1) * 128]
        both = jnp.where(
            lane < ports, lane_pick(real_row, port_low), lane_pick(imag_row, port_low)
        )
        port_value = jnp.where(port_high == r, both, port_value)
        out_ref[0, r : r + 1, :] = real_row
        out_ref[0, rows + r : rows + r + 1, :] = imag_row
    block = out_ref[0, : 2 * rows, :]
    for chip in range(1, chips):
        out_ref[chip, : 2 * rows, :] = block
    need = [by_place(need_ref[pl.ds(c, chips, 2), :].astype(F32)) for c in range(2)]
    first = lax.axis_index("core") == 0
    out_ref[:, 2 * rows, :] = jnp.where(first, need[0], need[1])
    out_ref[:, 2 * rows + 1, :] = jnp.where(first, need[1], need[0])
    out_ref[:, 2 * rows + 2, :] = jnp.broadcast_to(port_value[0:1], (chips, 128))
    for r in range(2 * rows + 3, out_ref.shape[1]):
        out_ref[:, r, :] = jnp.zeros((chips, 128), F32)


def ask(need_ref, pack_ref, table_ref, core, rows):
    chips = pack_ref.shape[0]
    sub = lax.broadcasted_iota(jnp.int32, (rows, 128), 0)
    for chip in range(chips):
        wanted = need_ref[pl.ds(2 * chip + core, 1), :]
        wanted = jnp.broadcast_to(jnp.maximum(wanted, 0), (rows, 128))
        here = (wanted >> 7) == sub
        low = wanted & 127
        for c in range(2):
            block = pack_ref[(chip + chips - chip_turn(chips)) % chips, c * rows : (c + 1) * rows, :]
            picked = jnp.take_along_axis(block, low, axis=1, mode="promise_in_bounds")
            picked = jnp.where(here, picked, 0.0)
            table_ref[c, chip : chip + 1, :] = jnp.sum(picked, axis=0, keepdims=True)


def lookup(code_ref, start, tables):
    total = [None, None]
    for k in range(2):
        code = code_ref[k, pl.ds(start, 8), :]
        high, low = code >> 8, (code >> 1) & 127
        value = [jnp.zeros((8, 128), F32), jnp.zeros((8, 128), F32)]
        for first, step, count, row_of in tables:
            offset = high - first
            for r in range(count):
                here = offset == r * step
                for c in range(2):
                    value[c] = jnp.where(here, lane_pick(row_of(r, c), low), value[c])
        along = (code & 1) == 1
        for c in range(2):
            signed = jnp.where(along, value[c], -value[c])
            total[c] = signed if k == 0 else total[c] + signed
    return total


def own_lookup_kernel(mesh_ref, code_ref, coupling_hbm, out_ref, pair_ref, raw_ref, sems):
    rows = mesh_ref.shape[1] // 128
    far_count, rank = coupling_hbm.shape[:2]
    half = rank // 2
    part = far_count // 2
    copies = [
        pltpu.make_async_copy(
            coupling_hbm.at[pl.ds(i * part, part)], raw_ref.at[pl.ds(i * part, part)], sems.at[i]
        )
        for i in range(2)
    ]
    for copy in copies:
        copy.start()

    def own_row(r, c):
        return mesh_ref[c : c + 1, r * 128 : (r + 1) * 128]

    def block(g, carry):
        start = pl.multiple_of(g * 8, 8)
        total = lookup(code_ref, start, [(0, 1, rows, own_row)])
        out_ref[0, pl.ds(start, 8), :] = total[0]
        out_ref[1, pl.ds(start, 8), :] = total[1]
        return carry

    lax.fori_loop(0, code_ref.shape[1] // 8, block, 0, unroll=True)
    for k in range(far_count):
        if k % part == 0:
            copies[k // part].wait()
        for r in range(half):
            pair_ref[k, r] = jnp.concatenate([raw_ref[k, r], raw_ref[k, half + r]], axis=1)


def add_peers(part_ref, pack_ref, need_ref, code_ref, table_ref, out_ref, core, first):
    chips = pack_ref.shape[0]
    ask(need_ref, pack_ref, table_ref, core, first)

    def peer_row(r, c):
        return table_ref[c, r : r + 1, :]

    def block(g, carry):
        start = pl.multiple_of(g * 8, 8)
        total = lookup(code_ref, start, [(first + core, 2, chips, peer_row)])
        for c in range(2):
            out_ref[c, pl.ds(start, 8), :] = total[c] + part_ref[c, pl.ds(start, 8), :]
        return carry

    lax.fori_loop(0, code_ref.shape[1] // 8, block, 0, unroll=True)


def same_core_kernel(
    part_ref, same_ref, need_ref, code_ref, out_ref, rows_ref, table_ref, *, first
):
    rows_ref[0] = by_chip(same_ref[:, 2 * first, :])
    rows_ref[1] = same_ref[:, 2 * first + 2, :]
    add_peers(
        part_ref, same_ref, need_ref, code_ref, table_ref, out_ref,
        lax.axis_index("core"), first,
    )


def current_kernel(
    part_ref, other_ref, need_ref, code_ref, basis_hbm, current_ref, coeff_ref, rows_ref,
    table_ref, basis_ref, sem, *, first,
):
    tiles = code_ref.shape[1]
    rank = basis_ref.shape[0] // tiles
    copy = pltpu.make_async_copy(basis_hbm, basis_ref, sem.at[0])
    copy.start()
    rows_ref[0] = by_chip(other_ref[:, 2 * first + 1, :])
    rows_ref[1] = other_ref[:, 2 * first + 2, :]
    add_peers(
        part_ref, other_ref, need_ref, code_ref, table_ref, current_ref,
        1 - lax.axis_index("core"), first,
    )
    copy.wait()
    inputs = jnp.concatenate([current_ref[0], current_ref[1]], axis=0)
    inputs = inputs.T.astype(BF16)
    lane_tile = lax.broadcasted_iota(jnp.int32, (rank, 2 * tiles), 1) % tiles
    full = jnp.dot(basis_ref[...], inputs, preferred_element_type=F32)
    chosen = jnp.zeros((rank, 2 * tiles), F32)
    for t in range(tiles):
        chosen = jnp.where(lane_tile == t, full[t * rank : (t + 1) * rank], chosen)
    coeff = chosen.astype(BF16)
    for p in range(coeff_ref.shape[0]):
        coeff_ref[p] = coeff


def near_kernel(
    source_ref, current_ref, resistance_hbm, blocks_hbm, out_ref, inputs_ref, blocks_ref,
    resistance_ref, sems,
):
    tiles = current_ref.shape[1]
    width = blocks_ref.shape[1]
    count = blocks_ref.shape[0] // (tiles * width)
    span = 8 * count * width
    starts = [tiles * i // 64 for i in (0, 4, 8)]
    copies = {}
    for i in range(2):
        rows = pl.ds(starts[i] * span, (starts[i + 1] - starts[i]) * span)
        copies[starts[i]] = pltpu.make_async_copy(
            blocks_hbm.at[rows], blocks_ref.at[rows], sems.at[i]
        )
    late_copy = pltpu.make_async_copy(resistance_hbm, resistance_ref, sems.at[2])
    for copy in copies.values():
        copy.start()
    late_copy.start()
    lane_tile = lax.broadcasted_iota(jnp.int32, (width, 128), 1) % tiles
    rows = jnp.concatenate([current_ref[0], current_ref[1]], axis=0)
    columns = rows.T.astype(BF16)
    row_index = lax.broadcasted_iota(jnp.int32, (128, 128), 0)
    for k in range(count):
        picks = jnp.where(row_index == source_ref[k : k + 1, :], 1.0, 0.0).astype(BF16)
        inputs_ref[k * width : (k + 1) * width, :] = jnp.dot(
            columns, picks, preferred_element_type=F32
        ).astype(BF16)
    inputs = inputs_ref[...]
    total = jnp.zeros((width, 128), F32)
    for g in range(tiles // 8):
        if g in copies:
            copies[g].wait()
        block = jnp.concatenate(
            [
                jnp.concatenate(
                    [
                        blocks_ref[(t * count + k) * width : (t * count + k + 1) * width, :]
                        for t in range(g * 8, g * 8 + 8)
                    ],
                    axis=0,
                )
                for k in range(count)
            ],
            axis=1,
        )
        full = jnp.dot(block, inputs, preferred_element_type=F32)
        for i in range(8):
            total = jnp.where(
                lane_tile == g * 8 + i, full[i * width : (i + 1) * width], total
            )
    rows = total.T
    late_copy.wait()
    resistance = resistance_ref[...]
    out_ref[0] = resistance * current_ref[0] - rows[tiles:]
    out_ref[1] = resistance * current_ref[1] + rows[:tiles]


def split(value):
    top = value.astype(BF16)
    return top, (value - top.astype(F32)).astype(BF16)


def counts(rows):
    return lax.broadcasted_iota(jnp.int32, (rows, 128), 0).astype(F32)


def place(high, low, values, rows, spread_ref):
    sub_high, sub_low = counts(rows).astype(BF16), counts(128).astype(BF16)
    one, zero = jnp.ones((128, 128), BF16), jnp.zeros((128, 128), BF16)
    spread_ref[0] = high.astype(F32)
    spread_ref[1] = low.astype(F32)
    for c, value in enumerate(values):
        top, rest = split(value)
        spread_ref[2 + 2 * c] = top.astype(F32)
        spread_ref[3 + 2 * c] = rest.astype(F32)

    def spread(j, i, count):
        return jnp.broadcast_to(spread_ref[j, i : i + 1, :], (count, 128)).astype(BF16)

    left, right = [], []
    for i in range(8):
        here = spread(0, i, rows) == sub_high
        left.append(
            jnp.concatenate(
                [jnp.where(here, spread(j, i, rows), zero[:rows]) for j in range(2, 6)], axis=0
            )
        )
        right.append(jnp.where(spread(1, i, 128) == sub_low, one, zero))
    return jnp.concatenate(left, axis=1), jnp.concatenate(right, axis=1)


def place_few(high, low, values, rows):
    sub_high = lax.broadcasted_iota(jnp.int32, (rows, 128), 0)
    sub_low = lax.broadcasted_iota(jnp.int32, (128, 128), 0)
    left, right = [], []
    for i in range(high.shape[0]):
        here = jnp.broadcast_to(high[i : i + 1], (rows, 128)) == sub_high
        parts = []
        for value in values:
            spread = jnp.where(here, jnp.broadcast_to(value[i : i + 1], (rows, 128)), 0.0)
            parts.extend(split(spread))
        left.append(jnp.concatenate(parts, axis=0))
        there = jnp.broadcast_to(low[i : i + 1], (128, 128)) == sub_low
        right.append(jnp.where(there, 1.0, 0.0).astype(BF16))
    return jnp.concatenate(left, axis=1), jnp.concatenate(right, axis=1)


def scatter(code_ref, voltage_ref, spread_ref, first, rows, low_streams):
    total = None
    for g in range(code_ref.shape[1] // 8):
        for k in range(2):
            code = code_ref[k, g * 8 : g * 8 + 8, :]
            along = (code & 1) == 1
            values = []
            for c in range(2):
                voltage = voltage_ref[c, g * 8 : g * 8 + 8, :]
                values.append(jnp.where(along, voltage, -voltage))
            left, right = place(
                (code >> 8) - first, (code >> 1) & 127, values, rows, spread_ref.at[g, k]
            )
            term = dot_nt(right, left) if low_streams else dot_nt(left, right)
            total = term if total is None else total + term
    total = total.T if low_streams else total
    return [
        total[2 * c * rows : (2 * c + 1) * rows] + total[(2 * c + 1) * rows : (2 * c + 2) * rows]
        for c in range(2)
    ]


def voltage_kernel(
    coeff_ref, target_ref, coupling_ref, basis_ref, near_ref, code_ref, voltage_ref, slot_ref,
    picked_ref, mixed_ref, spread_ref, *, first,
):
    peers, rank, lanes = coeff_ref.shape
    far_count = coupling_ref.shape[0]
    tiles = lanes // 2
    half = rank // 2
    groups = half // 4
    device = device_index()
    spans = target_ref.shape[0] // far_count
    stride = peers // far_count
    component = lax.broadcasted_iota(jnp.int32, (rank, lanes), 1) // tiles
    for k in range(far_count):
        picked = jnp.zeros((rank, lanes), F32)
        for i in range(spans):
            row = k * spans + i
            block = coeff_ref[(device + k * stride + i + peers - turn(peers)) % peers].astype(F32)
            target = jnp.broadcast_to(target_ref[row : row + 1, :], (rank, lanes))
            source = jnp.maximum(target, 0) + component * tiles
            value = jnp.take_along_axis(block, source, axis=1, mode="promise_in_bounds")
            picked = jnp.where(target >= 0, value, picked)
        turned = pltpu.roll(picked, tiles, 1)
        picked_ref[0, k] = jnp.where(component == 0, picked, turned)
        picked_ref[1, k] = jnp.where(component == 0, turned, picked)

    def mix(g, carry):
        total = [[None, None] for _ in range(4)]
        for k in range(far_count):
            picked = [picked_ref[c, k] for c in range(2)]
            for i in range(4):
                block = coupling_ref[k, g * 4 + i].astype(F32)
                for c in range(2):
                    product = block * picked[c]
                    part = product[0:8]
                    for q in range(8, rank, 8):
                        part = part + product[q : q + 8]
                    total[i][c] = part if k == 0 else total[i][c] + part
        for i in range(4):
            for c in range(2):
                row = jnp.sum(total[i][c], axis=0, keepdims=True)
                mixed_ref[pl.ds(c * half + g * 4 + i, 1), :] = row
        return carry

    lax.fori_loop(0, groups, mix, 0, unroll=True)
    mixed = mixed_ref[...].T
    mixed = jnp.concatenate([mixed[:tiles], mixed[tiles:]], axis=1).astype(BF16)
    wide = 8 * rank
    from_row = lax.broadcasted_iota(jnp.int32, (2 * rank, wide), 0)
    to_rank = lax.broadcasted_iota(jnp.int32, (2 * rank, wide), 1) % rank
    repeated = []
    for c in range(2):
        wanted = (to_rank // half) * rank + c * half + to_rank % half
        picks = jnp.where(from_row == wanted, 1.0, 0.0).astype(BF16)
        repeated.append(jnp.dot(mixed, picks, preferred_element_type=F32))
    own_block = (
        lax.broadcasted_iota(jnp.int32, (16, wide), 0) % 8
        == lax.broadcasted_iota(jnp.int32, (16, wide), 1) // rank
    )
    for g in range(tiles // 8):
        rows8 = slice(g * 8, g * 8 + 8)
        both = jnp.concatenate([repeated[0][rows8], repeated[1][rows8]], axis=0)
        both = jnp.where(own_block, both, 0.0).astype(BF16)
        far = jnp.dot(
            both, basis_ref[g * wide : (g + 1) * wide, :], preferred_element_type=F32
        )
        voltage_ref[0, rows8, :] = near_ref[0, rows8, :] - far[8:16]
        voltage_ref[1, rows8, :] = near_ref[1, rows8, :] + far[0:8]
    sums = scatter(
        code_ref, voltage_ref, spread_ref, first, slot_ref.shape[0], True
    )
    shift = turn(peers)
    for c in range(2):
        slot_ref[: peers - shift, c, :] = sums[c][shift:]
        slot_ref[peers - shift :, c, :] = sums[c][:shift]


def own_sum_kernel(
    code_ref, voltage_ref, same_ref, other_ref, port_ref, impedance_ref, own_ref, asked_ref,
    picks_ref, spread_ref,
):
    rows = own_ref.shape[1]
    ports = impedance_ref.shape[1]
    chips = same_ref.shape[1]
    first_core = lax.axis_index("core") == 0
    same = same_ref[0].astype(jnp.int32)
    other = other_ref[0].astype(jnp.int32)
    asked = [jnp.where(first_core, same, other), jnp.where(first_core, other, same)]
    sub_low = lax.broadcasted_iota(jnp.int32, (128, 128), 0)
    for core in range(2):
        asked_ref[core] = asked[core] >> 7
        low = asked[core] & 127
        for chip in range(chips):
            there = jnp.broadcast_to(low[chip : chip + 1], (128, 128)) == sub_low
            place = core * chips + chip
            picks_ref[:, place * 128 : (place + 1) * 128] = jnp.where(there, 1.0, 0.0).astype(BF16)
    port_current = jnp.sum(same_ref[1] + other_ref[1], axis=0, keepdims=True)
    real = port_current[:, :ports]
    imag = port_current[:, ports:]
    both = jnp.concatenate([real, imag, jnp.zeros((6, ports), F32)], axis=0)
    by_real = dot_nt(both, impedance_ref[0], lax.Precision.HIGHEST)
    by_imag = dot_nt(both, impedance_ref[1], lax.Precision.HIGHEST)
    pad = jnp.zeros((1, 128 - ports), F32)
    terms = [
        jnp.concatenate([by_real[0:1] - by_imag[1:2], pad], axis=1),
        jnp.concatenate([by_real[1:2] + by_imag[0:1], pad], axis=1),
    ]
    port = port_ref[...] - device_index() * (rows * 128)
    port = jnp.where((port >= 0) & (port < rows * 128), port, -1)
    port = jnp.concatenate([port, jnp.full((1, 128 - ports), -1, jnp.int32)], axis=1)
    left, right = place_few(port >> 7, port & 127, terms, rows)
    total = dot_nt(left, right)
    sums = scatter(code_ref, voltage_ref, spread_ref, 0, rows, False)
    for c in range(2):
        own_ref[c] = sums[c] + (
            total[2 * c * rows : (2 * c + 1) * rows] + total[(2 * c + 1) * rows : (2 * c + 2) * rows]
        )


def finish_kernel(own_ref, arrived_ref, asked_ref, picks_ref, out_ref):
    rows = own_ref.shape[1]
    peers = arrived_ref.shape[0]
    chips = peers // 2
    sub_high = lax.broadcasted_iota(jnp.int32, (rows, 128), 0)
    left = []
    for core in range(2):
        for chip in range(chips):
            here = jnp.broadcast_to(asked_ref[core, chip : chip + 1, :], (rows, 128)) == sub_high
            parts = []
            for c in range(2):
                place = (2 * chip + core + peers - turn(peers)) % peers
                value = jnp.broadcast_to(arrived_ref[place, c : c + 1, :], (rows, 128))
                parts.extend(split(jnp.where(here, value, 0.0)))
            left.append(jnp.concatenate(parts, axis=0))
    total = dot_nt(jnp.concatenate(left, axis=1), picks_ref[...])
    for c in range(2):
        summed = own_ref[c] + (
            total[2 * c * rows : (2 * c + 1) * rows] + total[(2 * c + 1) * rows : (2 * c + 2) * rows]
        )
        for r in range(rows):
            out_ref[c : c + 1, r * 128 : (r + 1) * 128] = summed[r : r + 1]


def per_device(
    mesh_current,
    branch_entry,
    branch_sign,
    need_slots,
    resistance,
    near_blocks,
    near_source,
    basis_in,
    coupling,
    basis_out,
    admissible,
    port_mesh,
    port_coupling,
):
    chips = lax.axis_size("chips")
    peers = 2 * chips
    core = lax.axis_index("core")
    device = 2 * lax.axis_index("chips") + core
    mesh_dev = mesh_current.shape[1]
    tiles, near_count, width, _ = near_blocks.shape
    rank = basis_in.shape[1]
    far_count = admissible.shape[1]
    own_rows = mesh_dev // 128
    vmem = pl.BlockSpec(memory_space=pltpu.VMEM)
    shape = jax.ShapeDtypeStruct

    code = (branch_entry * 2 + branch_sign).reshape(2, tiles, width)
    coupling_lanes = jnp.transpose(coupling, (1, 2, 3, 0))
    basis_in_rows = basis_in.reshape(tiles * rank, width)
    basis_out_rows = basis_out.reshape(tiles * rank, width)
    half = jnp.arange(2 * tiles, dtype=jnp.int32) // tiles
    sources = jnp.transpose(near_source)
    sources = jnp.concatenate([sources, sources], axis=1) + half[None] * tiles
    band = peers * tiles // far_count
    spans = band // tiles + 1
    bases = device * tiles + jnp.arange(far_count, dtype=jnp.int32) * band
    shifted = (jnp.transpose(admissible) - bases[:, None]) % (peers * tiles)
    shifted = jnp.concatenate([shifted, shifted], axis=1)[:, None, :]
    shifted = shifted - jnp.arange(spans, dtype=jnp.int32)[None, :, None] * tiles
    inside = (shifted >= 0) & (shifted < tiles)
    targets = jnp.where(inside, shifted, -1).reshape(far_count * spans, 2 * tiles)

    def in_hbm(x):
        return pltpu.with_memory_space_constraint(x, pltpu.HBM)

    hbm = pl.BlockSpec(memory_space=pl.ANY)
    port_row = port_mesh.reshape(1, -1)
    pack_rows = (2 * own_rows + 3 + 7) // 8 * 8
    pack, mesh_near, need_near, port_near = pl.pallas_call(
        pack_kernel,
        out_shape=(
            shape((chips, pack_rows, 128), F32),
            pltpu.VMEM(mesh_current.shape, F32),
            pltpu.VMEM(need_slots.shape, jnp.int32),
            pltpu.VMEM(port_row.shape, jnp.int32),
        ),
        in_specs=[hbm] * 3,
        out_specs=(vmem,) * 4,
        scratch_shapes=[pltpu.SemaphoreType.DMA((3,))],
        compiler_params=params(),
        name="pack",
    )(in_hbm(mesh_current), in_hbm(need_slots), in_hbm(port_row))
    chip_members = [[(j + chip_turn(chips)) % chips for j in range(chips)]]
    same = lax.all_to_all(pack, "chips", 0, 0, tiled=True, axis_index_groups=chip_members)
    own_part, pairs = pl.pallas_call(
        own_lookup_kernel,
        out_shape=(
            shape((2, tiles, width), F32),
            pltpu.VMEM((far_count, rank // 2, rank, 2 * tiles), BF16),
        ),
        in_specs=[vmem] * 2 + [hbm],
        out_specs=(vmem,) * 2,
        scratch_shapes=[
            pltpu.VMEM(coupling_lanes.shape, BF16),
            pltpu.SemaphoreType.DMA((2,)),
        ],
        compiler_params=params(),
        cost_estimate=small_cost(),
        name="own_lookup",
    )(mesh_near, code, in_hbm(coupling_lanes))
    other = lax.ppermute(same, "core", [(0, 1), (1, 0)])
    part, same_rows = pl.pallas_call(
        functools.partial(same_core_kernel, first=own_rows),
        out_shape=(shape((2, tiles, width), F32), shape((2, chips, 128), F32)),
        in_specs=[vmem] * 4,
        out_specs=(vmem,) * 2,
        scratch_shapes=[pltpu.VMEM((2, chips, 128), F32)],
        compiler_params=params(),
        cost_estimate=small_cost(),
        name="same_core",
    )(own_part, same, need_near, code)
    current, coeff, other_rows = pl.pallas_call(
        functools.partial(current_kernel, first=own_rows),
        out_shape=(
            shape((2, tiles, width), F32),
            shape((peers, rank, 2 * tiles), BF16),
            shape((2, chips, 128), F32),
        ),
        in_specs=[vmem] * 4 + [hbm],
        out_specs=(vmem,) * 3,
        scratch_shapes=[
            pltpu.VMEM((2, chips, 128), F32),
            pltpu.VMEM(basis_in_rows.shape, BF16),
            pltpu.SemaphoreType.DMA((1,)),
        ],
        compiler_params=params(),
        name="currents",
    )(part, other, need_near, code, in_hbm(basis_in_rows))
    members = [[(j + turn(peers)) % peers for j in range(peers)]]
    all_coeff = lax.all_to_all(
        coeff, ("chips", "core"), 0, 0, tiled=True, axis_index_groups=members
    )
    near_rows = near_blocks.reshape(tiles * near_count * width, width)
    near = pl.pallas_call(
        near_kernel,
        out_shape=shape((2, tiles, width), F32),
        in_specs=[vmem] * 2 + [hbm] * 2,
        out_specs=vmem,
        scratch_shapes=[
            pltpu.VMEM((near_count * width, 2 * tiles), BF16),
            pltpu.VMEM(near_rows.shape, BF16),
            pltpu.VMEM((tiles, width), F32),
            pltpu.SemaphoreType.DMA((3,)),
        ],
        compiler_params=params(),
        cost_estimate=pl.CostEstimate(
            flops=256 * near_blocks.size, bytes_accessed=2 * near_blocks.size, transcendentals=0
        ),
        name="near_field",
    )(sources, current, in_hbm(resistance.reshape(tiles, width)), in_hbm(near_rows))
    voltage, slots = pl.pallas_call(
        functools.partial(voltage_kernel, first=own_rows),
        out_shape=(shape((2, tiles, width), F32), shape((peers, 2, 128), F32)),
        in_specs=[vmem] * 6,
        out_specs=(vmem,) * 2,
        scratch_shapes=[
            pltpu.VMEM((2, far_count, rank, 2 * tiles), F32),
            pltpu.VMEM((rank, 2 * tiles), F32),
            pltpu.VMEM((tiles // 8, 2, 6, 8, 128), F32),
        ],
        compiler_params=params(),
        name="voltages",
    )(
        all_coeff,
        targets,
        pairs,
        basis_out_rows,
        near,
        code,
    )
    arrived = lax.all_to_all(
        slots, ("chips", "core"), 0, 0, tiled=True, axis_index_groups=members
    )
    own, asked, picks = pl.pallas_call(
        own_sum_kernel,
        out_shape=(
            shape((2, own_rows, 128), F32),
            shape((2, chips, 128), jnp.int32),
            shape((128, peers * 128), BF16),
        ),
        in_specs=[vmem] * 6,
        out_specs=(vmem,) * 3,
        scratch_shapes=[
            pltpu.VMEM((tiles // 8, 2, 6, 8, 128), F32),
        ],
        compiler_params=params(),
        cost_estimate=small_cost(),
        name="own_sums",
    )(code, voltage, same_rows, other_rows, port_near, port_coupling)
    return pl.pallas_call(
        finish_kernel,
        out_shape=shape((2, mesh_dev), F32),
        in_specs=[vmem] * 4,
        out_specs=vmem,
        compiler_params=params(),
        name="finish",
    )(own, arrived, asked, picks)


def solution(mesh):
    groups, peers = mesh.devices.shape
    split_mesh = jax.sharding.Mesh(
        mesh.devices.reshape(groups, peers // 2, 2), ("groups", "chips", "core")
    )
    in_specs = (
        P(None, SPREAD),
        P(None, SPREAD),
        P(None, SPREAD),
        P(SPREAD, None),
        P(SPREAD),
        P(SPREAD, None, None, None),
        P(SPREAD, None),
        P(SPREAD, None, None),
        P(SPREAD, None, None, None),
        P(SPREAD, None, None),
        P(SPREAD, None),
        P("groups"),
        P(),
    )
    out_specs = P(None, SPREAD)
    return jax.shard_map(
        per_device, mesh=split_mesh, in_specs=in_specs, out_specs=out_specs, check_vma=False
    )
```

```python
import functools
import math

import jax
import jax.numpy as jnp
from jax import lax
from jax.experimental import pallas as pl
from jax.experimental.pallas import tpu as pltpu
from jax.sharding import PartitionSpec as P

F32 = jnp.float32
BF16 = jnp.bfloat16
SPREAD = ("groups", "chips", "core")
STEPS = 32000.0
VMEM_LIMIT = 24 * 1024 * 1024
NT = (((1,), (1,)), ((), ()))


def params():
    return pltpu.CompilerParams(vmem_limit_bytes=VMEM_LIMIT)


def small_cost():
    return pl.CostEstimate(flops=10**9, bytes_accessed=8 * 10**6, transcendentals=0)


def lane_pick(row, lanes):
    spread = jnp.broadcast_to(row, lanes.shape)
    return jnp.take_along_axis(spread, lanes, axis=1, mode="promise_in_bounds")


def dot_nt(left, right, precision=None):
    return lax.dot_general(
        left, right, NT, preferred_element_type=F32, precision=precision
    )


def turn(members):
    return members // 4


def chip_turn(chips):
    return chips // 2


def by_place(rows):
    shift = chip_turn(rows.shape[0])
    return jnp.concatenate([rows[shift:], rows[:shift]], axis=0)


def device_index():
    return 2 * lax.axis_index("chips") + lax.axis_index("core")


def fetch(copies):
    for copy in copies:
        copy.start()
    for copy in copies:
        copy.wait()


def power_of_two(exponent):
    return jnp.exp(exponent * math.log(2.0))


def fixed(value):
    return jnp.floor(value + 0.5)


def pack_kernel(
    mesh_hbm, need_hbm, port_hbm, out_ref, mesh_ref, need_ref, port_ref, stage_ref, sems
):
    rows = mesh_ref.shape[1] // 128
    ports = port_ref.shape[1]
    chips = out_ref.shape[0]
    fetch(
        [
            pltpu.make_async_copy(source, target, sems.at[i])
            for i, (source, target) in enumerate(
                [(mesh_hbm, mesh_ref), (need_hbm, need_ref), (port_hbm, port_ref)]
            )
        ]
    )
    for r in range(rows):
        stage_ref[r : r + 1, :] = mesh_ref[0:1, r * 128 : (r + 1) * 128]
        stage_ref[rows + r : rows + r + 1, :] = mesh_ref[1:2, r * 128 : (r + 1) * 128]
    block = stage_ref[...]
    largest = jnp.max(jnp.abs(block), axis=0, keepdims=True)
    largest = jnp.maximum(jnp.max(largest, axis=1, keepdims=True), 1e-30)
    largest = jnp.broadcast_to(largest, (1, 128))
    exponent = jnp.ceil(jnp.log(largest) * (1.0 / math.log(2.0)))
    unit = power_of_two(-exponent) * STEPS
    words = fixed(block * unit).astype(jnp.int32).astype(jnp.int16)
    port = port_ref[...] - device_index() * (rows * 128)
    port = jnp.where((port >= 0) & (port < rows * 128), port, -1)
    port = jnp.broadcast_to(jnp.concatenate([port, port], axis=1), (8, 128))
    port_high, port_low = port >> 7, port & 127
    port_value = jnp.zeros((8, 128), F32)
    lane = lax.broadcasted_iota(jnp.int32, (8, 128), 1)
    for r in range(rows):
        real_row = stage_ref[r : r + 1, :]
        imag_row = stage_ref[rows + r : rows + r + 1, :]
        both = jnp.where(
            lane < ports, lane_pick(real_row, port_low), lane_pick(imag_row, port_low)
        )
        port_value = jnp.where(port_high == r, both, port_value)
    port_scaled = port_value[0:1] * unit
    port_top = fixed(port_scaled)
    port_rest = fixed((port_scaled - port_top) * STEPS)
    tail = [part.astype(jnp.int32) for part in (port_top, port_rest, exponent)]
    tail.append(jnp.zeros((11, 128), jnp.int32))
    need = [by_place(need_ref[pl.ds(c, chips, 2), :]) for c in range(2)]
    first = lax.axis_index("core") == 0
    need = [jnp.where(first, need[0], need[1]), jnp.where(first, need[1], need[0])]
    for chip in range(chips):
        out_ref[chip, : 2 * rows, :] = words
        extra = [part[chip : chip + 1] for part in need] + tail
        out_ref[chip, 2 * rows :, :] = jnp.concatenate(extra, axis=0).astype(jnp.int16)


def extras(pack_ref, place, rows):
    extra = pack_ref[place, 2 * rows :, :].astype(jnp.int32)
    return extra, power_of_two(extra[4:5].astype(F32)) * (1.0 / STEPS)


def unpack_rows(pack_ref, rows_ref, request, rows):
    chips = pack_ref.shape[0]
    for chip in range(chips):
        place = (chip + chips - chip_turn(chips)) % chips
        extra, unit = extras(pack_ref, place, rows)
        extra = extra.astype(F32)
        rows_ref[0, chip : chip + 1, :] = extra[request : request + 1]
        rows_ref[1, chip : chip + 1, :] = (extra[2:3] + extra[3:4] * (1.0 / STEPS)) * unit


def ask(need_ref, pack_ref, table_ref, core, rows):
    chips = pack_ref.shape[0]
    sub = lax.broadcasted_iota(jnp.int32, (rows, 128), 0)
    for chip in range(chips):
        place = (chip + chips - chip_turn(chips)) % chips
        wanted = need_ref[pl.ds(2 * chip + core, 1), :]
        wanted = jnp.broadcast_to(jnp.maximum(wanted, 0), (rows, 128))
        here = (wanted >> 7) == sub
        low = wanted & 127
        _, unit = extras(pack_ref, place, rows)
        for c in range(2):
            block = pack_ref[place, c * rows : (c + 1) * rows, :].astype(jnp.int32).astype(F32)
            picked = jnp.take_along_axis(block, low, axis=1, mode="promise_in_bounds")
            picked = jnp.where(here, picked, 0.0)
            table_ref[c, chip : chip + 1, :] = unit * jnp.sum(picked, axis=0, keepdims=True)


def lookup(code_ref, start, tables):
    total = [None, None]
    for k in range(2):
        code = code_ref[k, pl.ds(start, 8), :]
        high, low = code >> 8, (code >> 1) & 127
        value = [jnp.zeros((8, 128), F32), jnp.zeros((8, 128), F32)]
        for first, step, count, row_of in tables:
            offset = high - first
            for r in range(count):
                here = offset == r * step
                for c in range(2):
                    value[c] = jnp.where(here, lane_pick(row_of(r, c), low), value[c])
        along = (code & 1) == 1
        for c in range(2):
            signed = jnp.where(along, value[c], -value[c])
            total[c] = signed if k == 0 else total[c] + signed
    return total


def own_lookup_kernel(mesh_ref, code_ref, coupling_hbm, out_ref, pair_ref, raw_ref, sems):
    rows = mesh_ref.shape[1] // 128
    far_count, rank = coupling_hbm.shape[:2]
    half = rank // 2
    part = far_count // 2
    copies = [
        pltpu.make_async_copy(
            coupling_hbm.at[pl.ds(i * part, part)], raw_ref.at[pl.ds(i * part, part)], sems.at[i]
        )
        for i in range(2)
    ]
    for copy in copies:
        copy.start()

    def own_row(r, c):
        return mesh_ref[c : c + 1, r * 128 : (r + 1) * 128]

    def block(g, carry):
        start = pl.multiple_of(g * 8, 8)
        total = lookup(code_ref, start, [(0, 1, rows, own_row)])
        out_ref[0, pl.ds(start, 8), :] = total[0]
        out_ref[1, pl.ds(start, 8), :] = total[1]
        return carry

    lax.fori_loop(0, code_ref.shape[1] // 8, block, 0, unroll=True)
    for k in range(far_count):
        if k % part == 0:
            copies[k // part].wait()
        for r in range(half):
            pair_ref[k, r] = jnp.concatenate([raw_ref[k, r], raw_ref[k, half + r]], axis=1)


def add_peers(part_ref, pack_ref, need_ref, code_ref, table_ref, out_ref, core, first):
    chips = pack_ref.shape[0]
    ask(need_ref, pack_ref, table_ref, core, first)

    def peer_row(r, c):
        return table_ref[c, r : r + 1, :]

    def block(g, carry):
        start = pl.multiple_of(g * 8, 8)
        total = lookup(code_ref, start, [(first + core, 2, chips, peer_row)])
        for c in range(2):
            out_ref[c, pl.ds(start, 8), :] = total[c] + part_ref[c, pl.ds(start, 8), :]
        return carry

    lax.fori_loop(0, code_ref.shape[1] // 8, block, 0, unroll=True)


def same_core_kernel(
    part_ref, same_ref, need_ref, code_ref, out_ref, rows_ref, table_ref, *, first
):
    unpack_rows(same_ref, rows_ref, 0, first)
    add_peers(
        part_ref, same_ref, need_ref, code_ref, table_ref, out_ref,
        lax.axis_index("core"), first,
    )


def current_kernel(
    part_ref, other_ref, need_ref, code_ref, basis_hbm, current_ref, coeff_ref, rows_ref,
    table_ref, basis_ref, sem, *, first,
):
    tiles = code_ref.shape[1]
    rank = basis_ref.shape[0] // tiles
    copy = pltpu.make_async_copy(basis_hbm, basis_ref, sem.at[0])
    copy.start()
    unpack_rows(other_ref, rows_ref, 1, first)
    add_peers(
        part_ref, other_ref, need_ref, code_ref, table_ref, current_ref,
        1 - lax.axis_index("core"), first,
    )
    copy.wait()
    inputs = jnp.concatenate([current_ref[0], current_ref[1]], axis=0)
    inputs = inputs.T.astype(BF16)
    lane_tile = lax.broadcasted_iota(jnp.int32, (rank, 2 * tiles), 1) % tiles
    full = jnp.dot(basis_ref[...], inputs, preferred_element_type=F32)
    chosen = jnp.zeros((rank, 2 * tiles), F32)
    for t in range(tiles):
        chosen = jnp.where(lane_tile == t, full[t * rank : (t + 1) * rank], chosen)
    coeff = chosen.astype(BF16)
    for p in range(coeff_ref.shape[0]):
        coeff_ref[p] = coeff


def near_kernel(
    source_ref, current_ref, resistance_hbm, blocks_hbm, out_ref, inputs_ref, blocks_ref,
    resistance_ref, sems,
):
    tiles = current_ref.shape[1]
    width = blocks_ref.shape[1]
    count = blocks_ref.shape[0] // (tiles * width)
    span = 8 * count * width
    starts = [tiles * i // 64 for i in (0, 4, 8)]
    copies = {}
    for i in range(2):
        rows = pl.ds(starts[i] * span, (starts[i + 1] - starts[i]) * span)
        copies[starts[i]] = pltpu.make_async_copy(
            blocks_hbm.at[rows], blocks_ref.at[rows], sems.at[i]
        )
    late_copy = pltpu.make_async_copy(resistance_hbm, resistance_ref, sems.at[2])
    for copy in copies.values():
        copy.start()
    late_copy.start()
    lane_tile = lax.broadcasted_iota(jnp.int32, (width, 128), 1) % tiles
    rows = jnp.concatenate([current_ref[0], current_ref[1]], axis=0)
    columns = rows.T.astype(BF16)
    row_index = lax.broadcasted_iota(jnp.int32, (128, 128), 0)
    for k in range(count):
        picks = jnp.where(row_index == source_ref[k : k + 1, :], 1.0, 0.0).astype(BF16)
        inputs_ref[k * width : (k + 1) * width, :] = jnp.dot(
            columns, picks, preferred_element_type=F32
        ).astype(BF16)
    inputs = inputs_ref[...]
    total = jnp.zeros((width, 128), F32)
    for g in range(tiles // 8):
        if g in copies:
            copies[g].wait()
        block = jnp.concatenate(
            [
                jnp.concatenate(
                    [
                        blocks_ref[(t * count + k) * width : (t * count + k + 1) * width, :]
                        for t in range(g * 8, g * 8 + 8)
                    ],
                    axis=0,
                )
                for k in range(count)
            ],
            axis=1,
        )
        full = jnp.dot(block, inputs, preferred_element_type=F32)
        for i in range(8):
            total = jnp.where(
                lane_tile == g * 8 + i, full[i * width : (i + 1) * width], total
            )
    rows = total.T
    late_copy.wait()
    resistance = resistance_ref[...]
    out_ref[0] = resistance * current_ref[0] - rows[tiles:]
    out_ref[1] = resistance * current_ref[1] + rows[:tiles]


def split(value):
    top = value.astype(BF16)
    return top, (value - top.astype(F32)).astype(BF16)


def counts(rows):
    return lax.broadcasted_iota(jnp.int32, (rows, 128), 0).astype(F32)


def place(high, low, values, rows, spread_ref):
    sub_high, sub_low = counts(rows).astype(BF16), counts(128).astype(BF16)
    one, zero = jnp.ones((128, 128), BF16), jnp.zeros((128, 128), BF16)
    spread_ref[0] = high.astype(F32)
    spread_ref[1] = low.astype(F32)
    for c, value in enumerate(values):
        top, rest = split(value)
        spread_ref[2 + 2 * c] = top.astype(F32)
        spread_ref[3 + 2 * c] = rest.astype(F32)

    def spread(j, i, count):
        return jnp.broadcast_to(spread_ref[j, i : i + 1, :], (count, 128)).astype(BF16)

    left, right = [], []
    for i in range(8):
        here = spread(0, i, rows) == sub_high
        left.append(
            jnp.concatenate(
                [jnp.where(here, spread(j, i, rows), zero[:rows]) for j in range(2, 6)], axis=0
            )
        )
        right.append(jnp.where(spread(1, i, 128) == sub_low, one, zero))
    return jnp.concatenate(left, axis=1), jnp.concatenate(right, axis=1)


def place_few(high, low, values, rows):
    sub_high = lax.broadcasted_iota(jnp.int32, (rows, 128), 0)
    sub_low = lax.broadcasted_iota(jnp.int32, (128, 128), 0)
    left, right = [], []
    for i in range(high.shape[0]):
        here = jnp.broadcast_to(high[i : i + 1], (rows, 128)) == sub_high
        parts = []
        for value in values:
            spread = jnp.where(here, jnp.broadcast_to(value[i : i + 1], (rows, 128)), 0.0)
            parts.extend(split(spread))
        left.append(jnp.concatenate(parts, axis=0))
        there = jnp.broadcast_to(low[i : i + 1], (128, 128)) == sub_low
        right.append(jnp.where(there, 1.0, 0.0).astype(BF16))
    return jnp.concatenate(left, axis=1), jnp.concatenate(right, axis=1)


def scatter(code_ref, voltage_ref, spread_ref, first, rows, low_streams):
    total = None
    for g in range(code_ref.shape[1] // 8):
        for k in range(2):
            code = code_ref[k, g * 8 : g * 8 + 8, :]
            along = (code & 1) == 1
            values = []
            for c in range(2):
                voltage = voltage_ref[c, g * 8 : g * 8 + 8, :]
                values.append(jnp.where(along, voltage, -voltage))
            left, right = place(
                (code >> 8) - first, (code >> 1) & 127, values, rows, spread_ref.at[g, k]
            )
            term = dot_nt(right, left) if low_streams else dot_nt(left, right)
            total = term if total is None else total + term
    total = total.T if low_streams else total
    return [
        total[2 * c * rows : (2 * c + 1) * rows] + total[(2 * c + 1) * rows : (2 * c + 2) * rows]
        for c in range(2)
    ]


def voltage_kernel(
    coeff_ref, target_ref, coupling_ref, basis_ref, near_ref, code_ref, voltage_ref, slot_ref,
    picked_ref, mixed_ref, spread_ref, *, first,
):
    peers, rank, lanes = coeff_ref.shape
    far_count = coupling_ref.shape[0]
    tiles = lanes // 2
    half = rank // 2
    groups = half // 4
    device = device_index()
    spans = target_ref.shape[0] // far_count
    stride = peers // far_count
    component = lax.broadcasted_iota(jnp.int32, (rank, lanes), 1) // tiles
    for k in range(far_count):
        picked = jnp.zeros((rank, lanes), F32)
        for i in range(spans):
            row = k * spans + i
            block = coeff_ref[(device + k * stride + i + peers - turn(peers)) % peers].astype(F32)
            target = jnp.broadcast_to(target_ref[row : row + 1, :], (rank, lanes))
            source = jnp.maximum(target, 0) + component * tiles
            value = jnp.take_along_axis(block, source, axis=1, mode="promise_in_bounds")
            picked = jnp.where(target >= 0, value, picked)
        turned = pltpu.roll(picked, tiles, 1)
        picked_ref[0, k] = jnp.where(component == 0, picked, turned)
        picked_ref[1, k] = jnp.where(component == 0, turned, picked)

    def mix(g, carry):
        total = [[None, None] for _ in range(4)]
        for k in range(far_count):
            picked = [picked_ref[c, k] for c in range(2)]
            for i in range(4):
                block = coupling_ref[k, g * 4 + i].astype(F32)
                for c in range(2):
                    product = block * picked[c]
                    part = product[0:8]
                    for q in range(8, rank, 8):
                        part = part + product[q : q + 8]
                    total[i][c] = part if k == 0 else total[i][c] + part
        for i in range(4):
            for c in range(2):
                row = jnp.sum(total[i][c], axis=0, keepdims=True)
                mixed_ref[pl.ds(c * half + g * 4 + i, 1), :] = row
        return carry

    lax.fori_loop(0, groups, mix, 0, unroll=True)
    mixed = mixed_ref[...].T
    mixed = jnp.concatenate([mixed[:tiles], mixed[tiles:]], axis=1).astype(BF16)
    wide = 8 * rank
    from_row = lax.broadcasted_iota(jnp.int32, (2 * rank, wide), 0)
    to_rank = lax.broadcasted_iota(jnp.int32, (2 * rank, wide), 1) % rank
    repeated = []
    for c in range(2):
        wanted = (to_rank // half) * rank + c * half + to_rank % half
        picks = jnp.where(from_row == wanted, 1.0, 0.0).astype(BF16)
        repeated.append(jnp.dot(mixed, picks, preferred_element_type=F32))
    own_block = (
        lax.broadcasted_iota(jnp.int32, (16, wide), 0) % 8
        == lax.broadcasted_iota(jnp.int32, (16, wide), 1) // rank
    )
    for g in range(tiles // 8):
        rows8 = slice(g * 8, g * 8 + 8)
        both = jnp.concatenate([repeated[0][rows8], repeated[1][rows8]], axis=0)
        both = jnp.where(own_block, both, 0.0).astype(BF16)
        far = jnp.dot(
            both, basis_ref[g * wide : (g + 1) * wide, :], preferred_element_type=F32
        )
        voltage_ref[0, rows8, :] = near_ref[0, rows8, :] - far[8:16]
        voltage_ref[1, rows8, :] = near_ref[1, rows8, :] + far[0:8]
    sums = scatter(
        code_ref, voltage_ref, spread_ref, first, slot_ref.shape[0], True
    )
    shift = turn(peers)
    for c in range(2):
        slot_ref[: peers - shift, c, :] = sums[c][shift:]
        slot_ref[peers - shift :, c, :] = sums[c][:shift]


def own_sum_kernel(
    code_ref, voltage_ref, same_ref, other_ref, port_ref, impedance_ref, own_ref, asked_ref,
    picks_ref, spread_ref,
):
    rows = own_ref.shape[1]
    ports = impedance_ref.shape[1]
    chips = same_ref.shape[1]
    first_core = lax.axis_index("core") == 0
    same = same_ref[0].astype(jnp.int32)
    other = other_ref[0].astype(jnp.int32)
    asked = [jnp.where(first_core, same, other), jnp.where(first_core, other, same)]
    sub_low = lax.broadcasted_iota(jnp.int32, (128, 128), 0)
    for core in range(2):
        asked_ref[core] = asked[core] >> 7
        low = asked[core] & 127
        for chip in range(chips):
            there = jnp.broadcast_to(low[chip : chip + 1], (128, 128)) == sub_low
            place = core * chips + chip
            picks_ref[:, place * 128 : (place + 1) * 128] = jnp.where(there, 1.0, 0.0).astype(BF16)
    port_current = jnp.sum(same_ref[1] + other_ref[1], axis=0, keepdims=True)
    real = port_current[:, :ports]
    imag = port_current[:, ports:]
    both = jnp.concatenate([real, imag, jnp.zeros((6, ports), F32)], axis=0)
    by_real = dot_nt(both, impedance_ref[0], lax.Precision.HIGHEST)
    by_imag = dot_nt(both, impedance_ref[1], lax.Precision.HIGHEST)
    pad = jnp.zeros((1, 128 - ports), F32)
    terms = [
        jnp.concatenate([by_real[0:1] - by_imag[1:2], pad], axis=1),
        jnp.concatenate([by_real[1:2] + by_imag[0:1], pad], axis=1),
    ]
    port = port_ref[...] - device_index() * (rows * 128)
    port = jnp.where((port >= 0) & (port < rows * 128), port, -1)
    port = jnp.concatenate([port, jnp.full((1, 128 - ports), -1, jnp.int32)], axis=1)
    left, right = place_few(port >> 7, port & 127, terms, rows)
    total = dot_nt(left, right)
    sums = scatter(code_ref, voltage_ref, spread_ref, 0, rows, False)
    for c in range(2):
        own_ref[c] = sums[c] + (
            total[2 * c * rows : (2 * c + 1) * rows] + total[(2 * c + 1) * rows : (2 * c + 2) * rows]
        )


def finish_kernel(own_ref, arrived_ref, asked_ref, picks_ref, out_ref):
    rows = own_ref.shape[1]
    peers = arrived_ref.shape[0]
    chips = peers // 2
    sub_high = lax.broadcasted_iota(jnp.int32, (rows, 128), 0)
    left = []
    for core in range(2):
        for chip in range(chips):
            here = jnp.broadcast_to(asked_ref[core, chip : chip + 1, :], (rows, 128)) == sub_high
            parts = []
            for c in range(2):
                place = (2 * chip + core + peers - turn(peers)) % peers
                value = jnp.broadcast_to(arrived_ref[place, c : c + 1, :], (rows, 128))
                parts.extend(split(jnp.where(here, value, 0.0)))
            left.append(jnp.concatenate(parts, axis=0))
    total = dot_nt(jnp.concatenate(left, axis=1), picks_ref[...])
    for c in range(2):
        summed = own_ref[c] + (
            total[2 * c * rows : (2 * c + 1) * rows] + total[(2 * c + 1) * rows : (2 * c + 2) * rows]
        )
        for r in range(rows):
            out_ref[c : c + 1, r * 128 : (r + 1) * 128] = summed[r : r + 1]


def per_device(
    mesh_current,
    branch_entry,
    branch_sign,
    need_slots,
    resistance,
    near_blocks,
    near_source,
    basis_in,
    coupling,
    basis_out,
    admissible,
    port_mesh,
    port_coupling,
):
    chips = lax.axis_size("chips")
    peers = 2 * chips
    core = lax.axis_index("core")
    device = 2 * lax.axis_index("chips") + core
    mesh_dev = mesh_current.shape[1]
    tiles, near_count, width, _ = near_blocks.shape
    rank = basis_in.shape[1]
    far_count = admissible.shape[1]
    own_rows = mesh_dev // 128
    vmem = pl.BlockSpec(memory_space=pltpu.VMEM)
    shape = jax.ShapeDtypeStruct

    code = (branch_entry * 2 + branch_sign).reshape(2, tiles, width)
    coupling_lanes = jnp.transpose(coupling, (1, 2, 3, 0))
    basis_in_rows = basis_in.reshape(tiles * rank, width)
    basis_out_rows = basis_out.reshape(tiles * rank, width)
    half = jnp.arange(2 * tiles, dtype=jnp.int32) // tiles
    sources = jnp.transpose(near_source)
    sources = jnp.concatenate([sources, sources], axis=1) + half[None] * tiles
    band = peers * tiles // far_count
    spans = band // tiles + 1
    bases = device * tiles + jnp.arange(far_count, dtype=jnp.int32) * band
    shifted = (jnp.transpose(admissible) - bases[:, None]) % (peers * tiles)
    shifted = jnp.concatenate([shifted, shifted], axis=1)[:, None, :]
    shifted = shifted - jnp.arange(spans, dtype=jnp.int32)[None, :, None] * tiles
    inside = (shifted >= 0) & (shifted < tiles)
    targets = jnp.where(inside, shifted, -1).reshape(far_count * spans, 2 * tiles)

    def in_hbm(x):
        return pltpu.with_memory_space_constraint(x, pltpu.HBM)

    hbm = pl.BlockSpec(memory_space=pl.ANY)
    port_row = port_mesh.reshape(1, -1)
    pack_rows = 2 * own_rows + 16
    pack, mesh_near, need_near, port_near = pl.pallas_call(
        pack_kernel,
        out_shape=(
            shape((chips, pack_rows, 128), jnp.int16),
            pltpu.VMEM(mesh_current.shape, F32),
            pltpu.VMEM(need_slots.shape, jnp.int32),
            pltpu.VMEM(port_row.shape, jnp.int32),
        ),
        in_specs=[hbm] * 3,
        out_specs=(vmem,) * 4,
        scratch_shapes=[
            pltpu.VMEM((2 * own_rows, 128), F32),
            pltpu.SemaphoreType.DMA((3,)),
        ],
        compiler_params=params(),
        name="pack",
    )(in_hbm(mesh_current), in_hbm(need_slots), in_hbm(port_row))
    chip_members = [[(j + chip_turn(chips)) % chips for j in range(chips)]]
    same = lax.all_to_all(pack, "chips", 0, 0, tiled=True, axis_index_groups=chip_members)
    own_part, pairs = pl.pallas_call(
        own_lookup_kernel,
        out_shape=(
            shape((2, tiles, width), F32),
            pltpu.VMEM((far_count, rank // 2, rank, 2 * tiles), BF16),
        ),
        in_specs=[vmem] * 2 + [hbm],
        out_specs=(vmem,) * 2,
        scratch_shapes=[
            pltpu.VMEM(coupling_lanes.shape, BF16),
            pltpu.SemaphoreType.DMA((2,)),
        ],
        compiler_params=params(),
        cost_estimate=small_cost(),
        name="own_lookup",
    )(mesh_near, code, in_hbm(coupling_lanes))
    other = lax.ppermute(same, "core", [(0, 1), (1, 0)])
    part, same_rows = pl.pallas_call(
        functools.partial(same_core_kernel, first=own_rows),
        out_shape=(shape((2, tiles, width), F32), shape((2, chips, 128), F32)),
        in_specs=[vmem] * 4,
        out_specs=(vmem,) * 2,
        scratch_shapes=[pltpu.VMEM((2, chips, 128), F32)],
        compiler_params=params(),
        cost_estimate=small_cost(),
        name="same_core",
    )(own_part, same, need_near, code)
    current, coeff, other_rows = pl.pallas_call(
        functools.partial(current_kernel, first=own_rows),
        out_shape=(
            shape((2, tiles, width), F32),
            shape((peers, rank, 2 * tiles), BF16),
            shape((2, chips, 128), F32),
        ),
        in_specs=[vmem] * 4 + [hbm],
        out_specs=(vmem,) * 3,
        scratch_shapes=[
            pltpu.VMEM((2, chips, 128), F32),
            pltpu.VMEM(basis_in_rows.shape, BF16),
            pltpu.SemaphoreType.DMA((1,)),
        ],
        compiler_params=params(),
        name="currents",
    )(part, other, need_near, code, in_hbm(basis_in_rows))
    members = [[(j + turn(peers)) % peers for j in range(peers)]]
    all_coeff = lax.all_to_all(
        coeff, ("chips", "core"), 0, 0, tiled=True, axis_index_groups=members
    )
    near_rows = near_blocks.reshape(tiles * near_count * width, width)
    near = pl.pallas_call(
        near_kernel,
        out_shape=shape((2, tiles, width), F32),
        in_specs=[vmem] * 2 + [hbm] * 2,
        out_specs=vmem,
        scratch_shapes=[
            pltpu.VMEM((near_count * width, 2 * tiles), BF16),
            pltpu.VMEM(near_rows.shape, BF16),
            pltpu.VMEM((tiles, width), F32),
            pltpu.SemaphoreType.DMA((3,)),
        ],
        compiler_params=params(),
        cost_estimate=pl.CostEstimate(
            flops=256 * near_blocks.size, bytes_accessed=2 * near_blocks.size, transcendentals=0
        ),
        name="near_field",
    )(sources, current, in_hbm(resistance.reshape(tiles, width)), in_hbm(near_rows))
    voltage, slots = pl.pallas_call(
        functools.partial(voltage_kernel, first=own_rows),
        out_shape=(shape((2, tiles, width), F32), shape((peers, 2, 128), F32)),
        in_specs=[vmem] * 6,
        out_specs=(vmem,) * 2,
        scratch_shapes=[
            pltpu.VMEM((2, far_count, rank, 2 * tiles), F32),
            pltpu.VMEM((rank, 2 * tiles), F32),
            pltpu.VMEM((tiles // 8, 2, 6, 8, 128), F32),
        ],
        compiler_params=params(),
        name="voltages",
    )(
        all_coeff,
        targets,
        pairs,
        basis_out_rows,
        near,
        code,
    )
    arrived = lax.all_to_all(
        slots, ("chips", "core"), 0, 0, tiled=True, axis_index_groups=members
    )
    own, asked, picks = pl.pallas_call(
        own_sum_kernel,
        out_shape=(
            shape((2, own_rows, 128), F32),
            shape((2, chips, 128), jnp.int32),
            shape((128, peers * 128), BF16),
        ),
        in_specs=[vmem] * 6,
        out_specs=(vmem,) * 3,
        scratch_shapes=[
            pltpu.VMEM((tiles // 8, 2, 6, 8, 128), F32),
        ],
        compiler_params=params(),
        cost_estimate=small_cost(),
        name="own_sums",
    )(code, voltage, same_rows, other_rows, port_near, port_coupling)
    return pl.pallas_call(
        finish_kernel,
        out_shape=shape((2, mesh_dev), F32),
        in_specs=[vmem] * 4,
        out_specs=vmem,
        compiler_params=params(),
        name="finish",
    )(own, arrived, asked, picks)


def solution(mesh):
    groups, peers = mesh.devices.shape
    split_mesh = jax.sharding.Mesh(
        mesh.devices.reshape(groups, peers // 2, 2), ("groups", "chips", "core")
    )
    in_specs = (
        P(None, SPREAD),
        P(None, SPREAD),
        P(None, SPREAD),
        P(SPREAD, None),
        P(SPREAD),
        P(SPREAD, None, None, None),
        P(SPREAD, None),
        P(SPREAD, None, None),
        P(SPREAD, None, None, None),
        P(SPREAD, None, None),
        P(SPREAD, None),
        P("groups"),
        P(),
    )
    out_specs = P(None, SPREAD)
    return jax.shard_map(
        per_device, mesh=split_mesh, in_specs=in_specs, out_specs=out_specs, check_vma=False
    )
```

```python
import functools
import math

import jax
import jax.numpy as jnp
from jax import lax
from jax.experimental import pallas as pl
from jax.experimental.pallas import tpu as pltpu
from jax.sharding import PartitionSpec as P

F32 = jnp.float32
BF16 = jnp.bfloat16
SPREAD = ("groups", "chips", "core")
STEPS = 32000.0
VMEM_LIMIT = 24 * 1024 * 1024
NT = (((1,), (1,)), ((), ()))


def params():
    return pltpu.CompilerParams(vmem_limit_bytes=VMEM_LIMIT)


def small_cost():
    return pl.CostEstimate(flops=10**9, bytes_accessed=8 * 10**6, transcendentals=0)


def lane_pick(row, lanes):
    spread = jnp.broadcast_to(row, lanes.shape)
    return jnp.take_along_axis(spread, lanes, axis=1, mode="promise_in_bounds")


def dot_nt(left, right, precision=None):
    return lax.dot_general(
        left, right, NT, preferred_element_type=F32, precision=precision
    )


def turn(members):
    return members // 4


def chip_turn(chips):
    return chips // 2


def by_place(rows):
    shift = chip_turn(rows.shape[0])
    return jnp.concatenate([rows[shift:], rows[:shift]], axis=0)


def device_index():
    return 2 * lax.axis_index("chips") + lax.axis_index("core")


def fetch(copies):
    for copy in copies:
        copy.start()
    for copy in copies:
        copy.wait()


def power_of_two(exponent):
    return jnp.exp(exponent * math.log(2.0))


def fixed(value):
    return jnp.floor(value + 0.5)


def pack_kernel(
    mesh_hbm, need_hbm, port_hbm, out_ref, mesh_ref, need_ref, port_ref, stage_ref, sems
):
    rows = mesh_ref.shape[1] // 128
    ports = port_ref.shape[1]
    chips = out_ref.shape[0]
    fetch(
        [
            pltpu.make_async_copy(source, target, sems.at[i])
            for i, (source, target) in enumerate(
                [(mesh_hbm, mesh_ref), (need_hbm, need_ref), (port_hbm, port_ref)]
            )
        ]
    )
    for r in range(rows):
        stage_ref[r : r + 1, :] = mesh_ref[0:1, r * 128 : (r + 1) * 128]
        stage_ref[rows + r : rows + r + 1, :] = mesh_ref[1:2, r * 128 : (r + 1) * 128]
    block = stage_ref[...]
    largest = jnp.maximum(jnp.max(jnp.abs(block), axis=1, keepdims=True), 1e-30)
    largest = jnp.broadcast_to(largest, block.shape)
    exponent = jnp.ceil(jnp.log(largest) * (1.0 / math.log(2.0)))
    words = fixed(block * (power_of_two(-exponent) * STEPS)).astype(jnp.int32).astype(jnp.int16)
    top_exponent = jnp.max(exponent, axis=0, keepdims=True)
    unit = power_of_two(-top_exponent) * STEPS
    row_exponent = exponent.T[0:1]
    row_exponent = jnp.concatenate(
        [row_exponent, jnp.zeros((1, 128 - 2 * rows), F32)], axis=1
    )
    port = port_ref[...] - device_index() * (rows * 128)
    port = jnp.where((port >= 0) & (port < rows * 128), port, -1)
    port = jnp.broadcast_to(jnp.concatenate([port, port], axis=1), (8, 128))
    port_high, port_low = port >> 7, port & 127
    port_value = jnp.zeros((8, 128), F32)
    lane = lax.broadcasted_iota(jnp.int32, (8, 128), 1)
    for r in range(rows):
        real_row = stage_ref[r : r + 1, :]
        imag_row = stage_ref[rows + r : rows + r + 1, :]
        both = jnp.where(
            lane < ports, lane_pick(real_row, port_low), lane_pick(imag_row, port_low)
        )
        port_value = jnp.where(port_high == r, both, port_value)
    port_scaled = port_value[0:1] * unit
    port_top = fixed(port_scaled)
    port_rest = fixed((port_scaled - port_top) * STEPS)
    tail = [
        part.astype(jnp.int32) for part in (port_top, port_rest, row_exponent, top_exponent)
    ]
    tail.append(jnp.zeros((10, 128), jnp.int32))
    need = [by_place(need_ref[pl.ds(c, chips, 2), :]) for c in range(2)]
    first = lax.axis_index("core") == 0
    need = [jnp.where(first, need[0], need[1]), jnp.where(first, need[1], need[0])]
    for chip in range(chips):
        out_ref[chip, : 2 * rows, :] = words
        extra = [part[chip : chip + 1] for part in need] + tail
        out_ref[chip, 2 * rows :, :] = jnp.concatenate(extra, axis=0).astype(jnp.int16)


def hand_on_kernel(pack_hbm, part_hbm, out_hbm):
    pass


def extras(pack_ref, place, rows):
    extra = pack_ref[place, 2 * rows :, :].astype(jnp.int32)
    return extra, power_of_two(extra[4:6].astype(F32)) * (1.0 / STEPS)


def unpack_rows(pack_ref, rows_ref, request, rows):
    chips = pack_ref.shape[0]
    for chip in range(chips):
        place = (chip + chips - chip_turn(chips)) % chips
        extra, unit = extras(pack_ref, place, rows)
        extra = extra.astype(F32)
        rows_ref[0, chip : chip + 1, :] = extra[request : request + 1]
        rows_ref[1, chip : chip + 1, :] = (extra[2:3] + extra[3:4] * (1.0 / STEPS)) * unit[1:2]


def ask(need_ref, pack_ref, table_ref, core, rows):
    chips = pack_ref.shape[0]
    sub = lax.broadcasted_iota(jnp.int32, (rows, 128), 0)
    for chip in range(chips):
        place = (chip + chips - chip_turn(chips)) % chips
        wanted = need_ref[pl.ds(2 * chip + core, 1), :]
        wanted = jnp.broadcast_to(jnp.maximum(wanted, 0), (rows, 128))
        here = (wanted >> 7) == sub
        low = wanted & 127
        _, unit = extras(pack_ref, place, rows)
        row_of = (wanted >> 7)[0:8]
        for c in range(2):
            slot_unit = lane_pick(unit[0:1], row_of + c * rows)[0:1]
            block = pack_ref[place, c * rows : (c + 1) * rows, :].astype(jnp.int32).astype(F32)
            picked = jnp.take_along_axis(block, low, axis=1, mode="promise_in_bounds")
            picked = jnp.where(here, picked, 0.0)
            table_ref[c, chip : chip + 1, :] = slot_unit * jnp.sum(picked, axis=0, keepdims=True)


def lookup(code_ref, start, tables):
    total = [None, None]
    for k in range(2):
        code = code_ref[k, pl.ds(start, 8), :]
        high, low = code >> 8, (code >> 1) & 127
        value = [jnp.zeros((8, 128), F32), jnp.zeros((8, 128), F32)]
        for first, step, count, row_of in tables:
            offset = high - first
            for r in range(count):
                here = offset == r * step
                for c in range(2):
                    value[c] = jnp.where(here, lane_pick(row_of(r, c), low), value[c])
        along = (code & 1) == 1
        for c in range(2):
            signed = jnp.where(along, value[c], -value[c])
            total[c] = signed if k == 0 else total[c] + signed
    return total


def own_lookup_kernel(mesh_ref, code_ref, coupling_hbm, out_ref, pair_ref, raw_ref, sems):
    rows = mesh_ref.shape[1] // 128
    far_count, rank = coupling_hbm.shape[:2]
    half = rank // 2
    part = far_count // 2
    copies = [
        pltpu.make_async_copy(
            coupling_hbm.at[pl.ds(i * part, part)], raw_ref.at[pl.ds(i * part, part)], sems.at[i]
        )
        for i in range(2)
    ]
    for copy in copies:
        copy.start()

    def own_row(r, c):
        return mesh_ref[c : c + 1, r * 128 : (r + 1) * 128]

    def block(g, carry):
        start = pl.multiple_of(g * 8, 8)
        total = lookup(code_ref, start, [(0, 1, rows, own_row)])
        out_ref[0, pl.ds(start, 8), :] = total[0]
        out_ref[1, pl.ds(start, 8), :] = total[1]
        return carry

    lax.fori_loop(0, code_ref.shape[1] // 8, block, 0, unroll=True)
    for k in range(far_count):
        if k % part == 0:
            copies[k // part].wait()
        for r in range(half):
            pair_ref[k, r] = jnp.concatenate([raw_ref[k, r], raw_ref[k, half + r]], axis=1)


def add_peers(part_ref, pack_ref, need_ref, code_ref, table_ref, out_ref, core, first):
    chips = pack_ref.shape[0]
    ask(need_ref, pack_ref, table_ref, core, first)

    def peer_row(r, c):
        return table_ref[c, r : r + 1, :]

    def block(g, carry):
        start = pl.multiple_of(g * 8, 8)
        total = lookup(code_ref, start, [(first + core, 2, chips, peer_row)])
        for c in range(2):
            out_ref[c, pl.ds(start, 8), :] = total[c] + part_ref[c, pl.ds(start, 8), :]
        return carry

    lax.fori_loop(0, code_ref.shape[1] // 8, block, 0, unroll=True)


def same_core_kernel(
    part_ref, same_ref, need_ref, code_ref, out_ref, rows_ref, table_ref, *, first
):
    unpack_rows(same_ref, rows_ref, 0, first)
    add_peers(
        part_ref, same_ref, need_ref, code_ref, table_ref, out_ref,
        lax.axis_index("core"), first,
    )


def current_kernel(
    part_ref, other_ref, need_ref, code_ref, basis_hbm, current_ref, coeff_ref, rows_ref,
    table_ref, basis_ref, sem, *, first,
):
    tiles = code_ref.shape[1]
    rank = basis_ref.shape[0] // tiles
    copy = pltpu.make_async_copy(basis_hbm, basis_ref, sem.at[0])
    copy.start()
    unpack_rows(other_ref, rows_ref, 1, first)
    add_peers(
        part_ref, other_ref, need_ref, code_ref, table_ref, current_ref,
        1 - lax.axis_index("core"), first,
    )
    copy.wait()
    inputs = jnp.concatenate([current_ref[0], current_ref[1]], axis=0)
    inputs = inputs.T.astype(BF16)
    lane_tile = lax.broadcasted_iota(jnp.int32, (rank, 2 * tiles), 1) % tiles
    full = jnp.dot(basis_ref[...], inputs, preferred_element_type=F32)
    chosen = jnp.zeros((rank, 2 * tiles), F32)
    for t in range(tiles):
        chosen = jnp.where(lane_tile == t, full[t * rank : (t + 1) * rank], chosen)
    coeff = chosen.astype(BF16)
    for p in range(coeff_ref.shape[0]):
        coeff_ref[p] = coeff


def near_kernel(
    source_ref, current_ref, resistance_hbm, blocks_hbm, out_ref, inputs_ref, blocks_ref,
    resistance_ref, sems,
):
    tiles = current_ref.shape[1]
    width = blocks_ref.shape[1]
    count = blocks_ref.shape[0] // (tiles * width)
    span = 8 * count * width
    starts = [tiles * i // 64 for i in (0, 4, 8)]
    copies = {}
    for i in range(2):
        rows = pl.ds(starts[i] * span, (starts[i + 1] - starts[i]) * span)
        copies[starts[i]] = pltpu.make_async_copy(
            blocks_hbm.at[rows], blocks_ref.at[rows], sems.at[i]
        )
    late_copy = pltpu.make_async_copy(resistance_hbm, resistance_ref, sems.at[2])
    for copy in copies.values():
        copy.start()
    late_copy.start()
    lane_tile = lax.broadcasted_iota(jnp.int32, (width, 128), 1) % tiles
    rows = jnp.concatenate([current_ref[0], current_ref[1]], axis=0)
    columns = rows.T.astype(BF16)
    row_index = lax.broadcasted_iota(jnp.int32, (128, 128), 0)
    for k in range(count):
        picks = jnp.where(row_index == source_ref[k : k + 1, :], 1.0, 0.0).astype(BF16)
        inputs_ref[k * width : (k + 1) * width, :] = jnp.dot(
            columns, picks, preferred_element_type=F32
        ).astype(BF16)
    inputs = inputs_ref[...]
    total = jnp.zeros((width, 128), F32)
    for g in range(tiles // 8):
        if g in copies:
            copies[g].wait()
        block = jnp.concatenate(
            [
                jnp.concatenate(
                    [
                        blocks_ref[(t * count + k) * width : (t * count + k + 1) * width, :]
                        for t in range(g * 8, g * 8 + 8)
                    ],
                    axis=0,
                )
                for k in range(count)
            ],
            axis=1,
        )
        full = jnp.dot(block, inputs, preferred_element_type=F32)
        for i in range(8):
            total = jnp.where(
                lane_tile == g * 8 + i, full[i * width : (i + 1) * width], total
            )
    rows = total.T
    late_copy.wait()
    resistance = resistance_ref[...]
    out_ref[0] = resistance * current_ref[0] - rows[tiles:]
    out_ref[1] = resistance * current_ref[1] + rows[:tiles]


def split(value):
    top = value.astype(BF16)
    return top, (value - top.astype(F32)).astype(BF16)


def counts(rows):
    return lax.broadcasted_iota(jnp.int32, (rows, 128), 0).astype(F32)


def place(high, low, values, rows, spread_ref):
    sub_high, sub_low = counts(rows).astype(BF16), counts(128).astype(BF16)
    one, zero = jnp.ones((128, 128), BF16), jnp.zeros((128, 128), BF16)
    spread_ref[0] = high.astype(F32)
    spread_ref[1] = low.astype(F32)
    for c, value in enumerate(values):
        top, rest = split(value)
        spread_ref[2 + 2 * c] = top.astype(F32)
        spread_ref[3 + 2 * c] = rest.astype(F32)

    def spread(j, i, count):
        return jnp.broadcast_to(spread_ref[j, i : i + 1, :], (count, 128)).astype(BF16)

    left, right = [], []
    for i in range(8):
        here = spread(0, i, rows) == sub_high
        left.append(
            jnp.concatenate(
                [jnp.where(here, spread(j, i, rows), zero[:rows]) for j in range(2, 6)], axis=0
            )
        )
        right.append(jnp.where(spread(1, i, 128) == sub_low, one, zero))
    return jnp.concatenate(left, axis=1), jnp.concatenate(right, axis=1)


def place_few(high, low, values, rows):
    sub_high = lax.broadcasted_iota(jnp.int32, (rows, 128), 0)
    sub_low = lax.broadcasted_iota(jnp.int32, (128, 128), 0)
    left, right = [], []
    for i in range(high.shape[0]):
        here = jnp.broadcast_to(high[i : i + 1], (rows, 128)) == sub_high
        parts = []
        for value in values:
            spread = jnp.where(here, jnp.broadcast_to(value[i : i + 1], (rows, 128)), 0.0)
            parts.extend(split(spread))
        left.append(jnp.concatenate(parts, axis=0))
        there = jnp.broadcast_to(low[i : i + 1], (128, 128)) == sub_low
        right.append(jnp.where(there, 1.0, 0.0).astype(BF16))
    return jnp.concatenate(left, axis=1), jnp.concatenate(right, axis=1)


def scatter(code_ref, voltage_ref, spread_ref, first, rows, low_streams):
    total = None
    for g in range(code_ref.shape[1] // 8):
        for k in range(2):
            code = code_ref[k, g * 8 : g * 8 + 8, :]
            along = (code & 1) == 1
            values = []
            for c in range(2):
                voltage = voltage_ref[c, g * 8 : g * 8 + 8, :]
                values.append(jnp.where(along, voltage, -voltage))
            left, right = place(
                (code >> 8) - first, (code >> 1) & 127, values, rows, spread_ref.at[g, k]
            )
            term = dot_nt(right, left) if low_streams else dot_nt(left, right)
            total = term if total is None else total + term
    total = total.T if low_streams else total
    return [
        total[2 * c * rows : (2 * c + 1) * rows] + total[(2 * c + 1) * rows : (2 * c + 2) * rows]
        for c in range(2)
    ]


def voltage_kernel(
    coeff_ref, target_ref, coupling_ref, basis_ref, near_ref, code_ref, voltage_ref, slot_ref,
    picked_ref, mixed_ref, spread_ref, *, first,
):
    peers, rank, lanes = coeff_ref.shape
    far_count = coupling_ref.shape[0]
    tiles = lanes // 2
    half = rank // 2
    groups = half // 4
    device = device_index()
    spans = target_ref.shape[0] // far_count
    stride = peers // far_count
    component = lax.broadcasted_iota(jnp.int32, (rank, lanes), 1) // tiles
    for k in range(far_count):
        picked = jnp.zeros((rank, lanes), F32)
        for i in range(spans):
            row = k * spans + i
            block = coeff_ref[(device + k * stride + i + peers - turn(peers)) % peers].astype(F32)
            target = jnp.broadcast_to(target_ref[row : row + 1, :], (rank, lanes))
            source = jnp.maximum(target, 0) + component * tiles
            value = jnp.take_along_axis(block, source, axis=1, mode="promise_in_bounds")
            picked = jnp.where(target >= 0, value, picked)
        turned = pltpu.roll(picked, tiles, 1)
        picked_ref[0, k] = jnp.where(component == 0, picked, turned)
        picked_ref[1, k] = jnp.where(component == 0, turned, picked)

    def mix(g, carry):
        total = [[None, None] for _ in range(4)]
        for k in range(far_count):
            picked = [picked_ref[c, k] for c in range(2)]
            for i in range(4):
                block = coupling_ref[k, g * 4 + i].astype(F32)
                for c in range(2):
                    product = block * picked[c]
                    part = product[0:8]
                    for q in range(8, rank, 8):
                        part = part + product[q : q + 8]
                    total[i][c] = part if k == 0 else total[i][c] + part
        for i in range(4):
            for c in range(2):
                row = jnp.sum(total[i][c], axis=0, keepdims=True)
                mixed_ref[pl.ds(c * half + g * 4 + i, 1), :] = row
        return carry

    lax.fori_loop(0, groups, mix, 0, unroll=True)
    mixed = mixed_ref[...].T
    mixed = jnp.concatenate([mixed[:tiles], mixed[tiles:]], axis=1).astype(BF16)
    wide = 8 * rank
    from_row = lax.broadcasted_iota(jnp.int32, (2 * rank, wide), 0)
    to_rank = lax.broadcasted_iota(jnp.int32, (2 * rank, wide), 1) % rank
    repeated = []
    for c in range(2):
        wanted = (to_rank // half) * rank + c * half + to_rank % half
        picks = jnp.where(from_row == wanted, 1.0, 0.0).astype(BF16)
        repeated.append(jnp.dot(mixed, picks, preferred_element_type=F32))
    own_block = (
        lax.broadcasted_iota(jnp.int32, (16, wide), 0) % 8
        == lax.broadcasted_iota(jnp.int32, (16, wide), 1) // rank
    )
    for g in range(tiles // 8):
        rows8 = slice(g * 8, g * 8 + 8)
        both = jnp.concatenate([repeated[0][rows8], repeated[1][rows8]], axis=0)
        both = jnp.where(own_block, both, 0.0).astype(BF16)
        far = jnp.dot(
            both, basis_ref[g * wide : (g + 1) * wide, :], preferred_element_type=F32
        )
        voltage_ref[0, rows8, :] = near_ref[0, rows8, :] - far[8:16]
        voltage_ref[1, rows8, :] = near_ref[1, rows8, :] + far[0:8]
    sums = scatter(
        code_ref, voltage_ref, spread_ref, first, slot_ref.shape[0], True
    )
    shift = turn(peers)
    for c in range(2):
        slot_ref[: peers - shift, c, :] = sums[c][shift:]
        slot_ref[peers - shift :, c, :] = sums[c][:shift]


def own_sum_kernel(
    code_ref, voltage_ref, same_ref, other_ref, port_ref, impedance_ref, own_ref, asked_ref,
    picks_ref, spread_ref,
):
    rows = own_ref.shape[1]
    ports = impedance_ref.shape[1]
    chips = same_ref.shape[1]
    first_core = lax.axis_index("core") == 0
    same = same_ref[0].astype(jnp.int32)
    other = other_ref[0].astype(jnp.int32)
    asked = [jnp.where(first_core, same, other), jnp.where(first_core, other, same)]
    sub_low = lax.broadcasted_iota(jnp.int32, (128, 128), 0)
    for core in range(2):
        asked_ref[core] = asked[core] >> 7
        low = asked[core] & 127
        for chip in range(chips):
            there = jnp.broadcast_to(low[chip : chip + 1], (128, 128)) == sub_low
            place = core * chips + chip
            picks_ref[:, place * 128 : (place + 1) * 128] = jnp.where(there, 1.0, 0.0).astype(BF16)
    port_current = jnp.sum(same_ref[1] + other_ref[1], axis=0, keepdims=True)
    real = port_current[:, :ports]
    imag = port_current[:, ports:]
    both = jnp.concatenate([real, imag, jnp.zeros((6, ports), F32)], axis=0)
    by_real = dot_nt(both, impedance_ref[0], lax.Precision.HIGHEST)
    by_imag = dot_nt(both, impedance_ref[1], lax.Precision.HIGHEST)
    pad = jnp.zeros((1, 128 - ports), F32)
    terms = [
        jnp.concatenate([by_real[0:1] - by_imag[1:2], pad], axis=1),
        jnp.concatenate([by_real[1:2] + by_imag[0:1], pad], axis=1),
    ]
    port = port_ref[...] - device_index() * (rows * 128)
    port = jnp.where((port >= 0) & (port < rows * 128), port, -1)
    port = jnp.concatenate([port, jnp.full((1, 128 - ports), -1, jnp.int32)], axis=1)
    left, right = place_few(port >> 7, port & 127, terms, rows)
    total = dot_nt(left, right)
    sums = scatter(code_ref, voltage_ref, spread_ref, 0, rows, False)
    for c in range(2):
        own_ref[c] = sums[c] + (
            total[2 * c * rows : (2 * c + 1) * rows] + total[(2 * c + 1) * rows : (2 * c + 2) * rows]
        )


def finish_kernel(own_ref, arrived_ref, asked_ref, picks_ref, out_ref):
    rows = own_ref.shape[1]
    peers = arrived_ref.shape[0]
    chips = peers // 2
    sub_high = lax.broadcasted_iota(jnp.int32, (rows, 128), 0)
    left = []
    for core in range(2):
        for chip in range(chips):
            here = jnp.broadcast_to(asked_ref[core, chip : chip + 1, :], (rows, 128)) == sub_high
            parts = []
            for c in range(2):
                place = (2 * chip + core + peers - turn(peers)) % peers
                value = jnp.broadcast_to(arrived_ref[place, c : c + 1, :], (rows, 128))
                parts.extend(split(jnp.where(here, value, 0.0)))
            left.append(jnp.concatenate(parts, axis=0))
    total = dot_nt(jnp.concatenate(left, axis=1), picks_ref[...])
    for c in range(2):
        summed = own_ref[c] + (
            total[2 * c * rows : (2 * c + 1) * rows] + total[(2 * c + 1) * rows : (2 * c + 2) * rows]
        )
        for r in range(rows):
            out_ref[c : c + 1, r * 128 : (r + 1) * 128] = summed[r : r + 1]


def per_device(
    mesh_current,
    branch_entry,
    branch_sign,
    need_slots,
    resistance,
    near_blocks,
    near_source,
    basis_in,
    coupling,
    basis_out,
    admissible,
    port_mesh,
    port_coupling,
):
    chips = lax.axis_size("chips")
    peers = 2 * chips
    core = lax.axis_index("core")
    device = 2 * lax.axis_index("chips") + core
    mesh_dev = mesh_current.shape[1]
    tiles, near_count, width, _ = near_blocks.shape
    rank = basis_in.shape[1]
    far_count = admissible.shape[1]
    own_rows = mesh_dev // 128
    vmem = pl.BlockSpec(memory_space=pltpu.VMEM)
    shape = jax.ShapeDtypeStruct

    code = (branch_entry * 2 + branch_sign).reshape(2, tiles, width)
    coupling_lanes = jnp.transpose(coupling, (1, 2, 3, 0))
    basis_in_rows = basis_in.reshape(tiles * rank, width)
    basis_out_rows = basis_out.reshape(tiles * rank, width)
    half = jnp.arange(2 * tiles, dtype=jnp.int32) // tiles
    sources = jnp.transpose(near_source)
    sources = jnp.concatenate([sources, sources], axis=1) + half[None] * tiles
    band = peers * tiles // far_count
    spans = band // tiles + 1
    bases = device * tiles + jnp.arange(far_count, dtype=jnp.int32) * band
    shifted = (jnp.transpose(admissible) - bases[:, None]) % (peers * tiles)
    shifted = jnp.concatenate([shifted, shifted], axis=1)[:, None, :]
    shifted = shifted - jnp.arange(spans, dtype=jnp.int32)[None, :, None] * tiles
    inside = (shifted >= 0) & (shifted < tiles)
    targets = jnp.where(inside, shifted, -1).reshape(far_count * spans, 2 * tiles)

    def in_hbm(x):
        return pltpu.with_memory_space_constraint(x, pltpu.HBM)

    hbm = pl.BlockSpec(memory_space=pl.ANY)
    port_row = port_mesh.reshape(1, -1)
    pack_rows = 2 * own_rows + 16
    pack, mesh_near, need_near, port_near = pl.pallas_call(
        pack_kernel,
        out_shape=(
            shape((chips, pack_rows, 128), jnp.int16),
            pltpu.VMEM(mesh_current.shape, F32),
            pltpu.VMEM(need_slots.shape, jnp.int32),
            pltpu.VMEM(port_row.shape, jnp.int32),
        ),
        in_specs=[hbm] * 3,
        out_specs=(vmem,) * 4,
        scratch_shapes=[
            pltpu.VMEM((2 * own_rows, 128), F32),
            pltpu.SemaphoreType.DMA((3,)),
        ],
        compiler_params=params(),
        name="pack",
    )(in_hbm(mesh_current), in_hbm(need_slots), in_hbm(port_row))
    chip_members = [[(j + chip_turn(chips)) % chips for j in range(chips)]]
    same = lax.all_to_all(pack, "chips", 0, 0, tiled=True, axis_index_groups=chip_members)
    own_part, pairs = pl.pallas_call(
        own_lookup_kernel,
        out_shape=(
            shape((2, tiles, width), F32),
            pltpu.VMEM((far_count, rank // 2, rank, 2 * tiles), BF16),
        ),
        in_specs=[vmem] * 2 + [hbm],
        out_specs=(vmem,) * 2,
        scratch_shapes=[
            pltpu.VMEM(coupling_lanes.shape, BF16),
            pltpu.SemaphoreType.DMA((2,)),
        ],
        compiler_params=params(),
        cost_estimate=small_cost(),
        name="own_lookup",
    )(mesh_near, code, in_hbm(coupling_lanes))
    same = pl.pallas_call(
        hand_on_kernel,
        out_shape=shape(same.shape, same.dtype),
        in_specs=[hbm] * 2,
        out_specs=hbm,
        input_output_aliases={0: 0},
        compiler_params=params(),
        name="hand_on",
    )(same, own_part)
    other = lax.ppermute(same, "core", [(0, 1), (1, 0)])
    part, same_rows = pl.pallas_call(
        functools.partial(same_core_kernel, first=own_rows),
        out_shape=(shape((2, tiles, width), F32), shape((2, chips, 128), F32)),
        in_specs=[vmem] * 4,
        out_specs=(vmem,) * 2,
        scratch_shapes=[pltpu.VMEM((2, chips, 128), F32)],
        compiler_params=params(),
        cost_estimate=small_cost(),
        name="same_core",
    )(own_part, same, need_near, code)
    current, coeff, other_rows = pl.pallas_call(
        functools.partial(current_kernel, first=own_rows),
        out_shape=(
            shape((2, tiles, width), F32),
            shape((peers, rank, 2 * tiles), BF16),
            shape((2, chips, 128), F32),
        ),
        in_specs=[vmem] * 4 + [hbm],
        out_specs=(vmem,) * 3,
        scratch_shapes=[
            pltpu.VMEM((2, chips, 128), F32),
            pltpu.VMEM(basis_in_rows.shape, BF16),
            pltpu.SemaphoreType.DMA((1,)),
        ],
        compiler_params=params(),
        name="currents",
    )(part, other, need_near, code, in_hbm(basis_in_rows))
    members = [[(j + turn(peers)) % peers for j in range(peers)]]
    all_coeff = lax.all_to_all(
        coeff, ("chips", "core"), 0, 0, tiled=True, axis_index_groups=members
    )
    near_rows = near_blocks.reshape(tiles * near_count * width, width)
    near = pl.pallas_call(
        near_kernel,
        out_shape=shape((2, tiles, width), F32),
        in_specs=[vmem] * 2 + [hbm] * 2,
        out_specs=vmem,
        scratch_shapes=[
            pltpu.VMEM((near_count * width, 2 * tiles), BF16),
            pltpu.VMEM(near_rows.shape, BF16),
            pltpu.VMEM((tiles, width), F32),
            pltpu.SemaphoreType.DMA((3,)),
        ],
        compiler_params=params(),
        cost_estimate=pl.CostEstimate(
            flops=256 * near_blocks.size, bytes_accessed=2 * near_blocks.size, transcendentals=0
        ),
        name="near_field",
    )(sources, current, in_hbm(resistance.reshape(tiles, width)), in_hbm(near_rows))
    voltage, slots = pl.pallas_call(
        functools.partial(voltage_kernel, first=own_rows),
        out_shape=(shape((2, tiles, width), F32), shape((peers, 2, 128), F32)),
        in_specs=[vmem] * 6,
        out_specs=(vmem,) * 2,
        scratch_shapes=[
            pltpu.VMEM((2, far_count, rank, 2 * tiles), F32),
            pltpu.VMEM((rank, 2 * tiles), F32),
            pltpu.VMEM((tiles // 8, 2, 6, 8, 128), F32),
        ],
        compiler_params=params(),
        name="voltages",
    )(
        all_coeff,
        targets,
        pairs,
        basis_out_rows,
        near,
        code,
    )
    arrived = lax.all_to_all(
        slots, ("chips", "core"), 0, 0, tiled=True, axis_index_groups=members
    )
    own, asked, picks = pl.pallas_call(
        own_sum_kernel,
        out_shape=(
            shape((2, own_rows, 128), F32),
            shape((2, chips, 128), jnp.int32),
            shape((128, peers * 128), BF16),
        ),
        in_specs=[vmem] * 6,
        out_specs=(vmem,) * 3,
        scratch_shapes=[
            pltpu.VMEM((tiles // 8, 2, 6, 8, 128), F32),
        ],
        compiler_params=params(),
        cost_estimate=small_cost(),
        name="own_sums",
    )(code, voltage, same_rows, other_rows, port_near, port_coupling)
    return pl.pallas_call(
        finish_kernel,
        out_shape=shape((2, mesh_dev), F32),
        in_specs=[vmem] * 4,
        out_specs=vmem,
        compiler_params=params(),
        name="finish",
    )(own, arrived, asked, picks)


def solution(mesh):
    groups, peers = mesh.devices.shape
    split_mesh = jax.sharding.Mesh(
        mesh.devices.reshape(groups, peers // 2, 2), ("groups", "chips", "core")
    )
    in_specs = (
        P(None, SPREAD),
        P(None, SPREAD),
        P(None, SPREAD),
        P(SPREAD, None),
        P(SPREAD),
        P(SPREAD, None, None, None),
        P(SPREAD, None),
        P(SPREAD, None, None),
        P(SPREAD, None, None, None),
        P(SPREAD, None, None),
        P(SPREAD, None),
        P("groups"),
        P(),
    )
    out_specs = P(None, SPREAD)
    return jax.shard_map(
        per_device, mesh=split_mesh, in_specs=in_specs, out_specs=out_specs, check_vma=False
    )
```

```python
import functools
import math

import jax
import jax.numpy as jnp
from jax import lax
from jax.experimental import pallas as pl
from jax.experimental.pallas import tpu as pltpu
from jax.sharding import PartitionSpec as P

F32 = jnp.float32
BF16 = jnp.bfloat16
SPREAD = ("groups", "chips", "core")
STEPS = 32000.0
VMEM_LIMIT = 24 * 1024 * 1024
NT = (((1,), (1,)), ((), ()))


def params():
    return pltpu.CompilerParams(vmem_limit_bytes=VMEM_LIMIT)


def small_cost():
    return pl.CostEstimate(flops=10**9, bytes_accessed=8 * 10**6, transcendentals=0)


def lane_pick(row, lanes):
    spread = jnp.broadcast_to(row, lanes.shape)
    return jnp.take_along_axis(spread, lanes, axis=1, mode="promise_in_bounds")


def dot_nt(left, right, precision=None):
    return lax.dot_general(
        left, right, NT, preferred_element_type=F32, precision=precision
    )


def turn(members):
    return members // 4


def chip_turn(chips):
    return chips // 2


def by_place(rows):
    shift = chip_turn(rows.shape[0])
    return jnp.concatenate([rows[shift:], rows[:shift]], axis=0)


def device_index():
    return 2 * lax.axis_index("chips") + lax.axis_index("core")


def fetch(copies, late_copies):
    for copy in copies + late_copies:
        copy.start()
    for copy in copies:
        copy.wait()


def power_of_two(exponent):
    return jnp.exp(exponent * math.log(2.0))


def fixed(value):
    return jnp.floor(value + 0.5)


def pack_kernel(
    mesh_hbm, need_hbm, port_hbm, entry_hbm, sign_hbm, out_hbm, mesh_ref, need_ref, port_ref,
    code_ref, out_ref, stage_ref, entry_ref, sign_ref, sems,
):
    late_copies = [
        pltpu.make_async_copy(entry_hbm, entry_ref, sems.at[3]),
        pltpu.make_async_copy(sign_hbm, sign_ref, sems.at[4]),
    ]
    rows = mesh_ref.shape[1] // 128
    ports = port_ref.shape[1]
    chips = out_ref.shape[0]
    fetch(
        [
            pltpu.make_async_copy(source, target, sems.at[i])
            for i, (source, target) in enumerate(
                [(mesh_hbm, mesh_ref), (need_hbm, need_ref), (port_hbm, port_ref)]
            )
        ],
        late_copies,
    )
    for r in range(rows):
        stage_ref[r : r + 1, :] = mesh_ref[0:1, r * 128 : (r + 1) * 128]
        stage_ref[rows + r : rows + r + 1, :] = mesh_ref[1:2, r * 128 : (r + 1) * 128]
    block = stage_ref[...]
    largest = jnp.maximum(jnp.max(jnp.abs(block), axis=1, keepdims=True), 1e-30)
    largest = jnp.broadcast_to(largest, block.shape)
    exponent = jnp.ceil(jnp.log(largest) * (1.0 / math.log(2.0)))
    words = fixed(block * (power_of_two(-exponent) * STEPS)).astype(jnp.int32).astype(jnp.int16)
    top_exponent = jnp.max(exponent, axis=0, keepdims=True)
    unit = power_of_two(-top_exponent) * STEPS
    row_exponent = exponent.T[0:1]
    row_exponent = jnp.concatenate(
        [row_exponent, jnp.zeros((1, 128 - 2 * rows), F32)], axis=1
    )
    port = port_ref[...] - device_index() * (rows * 128)
    port = jnp.where((port >= 0) & (port < rows * 128), port, -1)
    port = jnp.broadcast_to(jnp.concatenate([port, port], axis=1), (8, 128))
    port_high, port_low = port >> 7, port & 127
    port_value = jnp.zeros((8, 128), F32)
    lane = lax.broadcasted_iota(jnp.int32, (8, 128), 1)
    for r in range(rows):
        real_row = stage_ref[r : r + 1, :]
        imag_row = stage_ref[rows + r : rows + r + 1, :]
        both = jnp.where(
            lane < ports, lane_pick(real_row, port_low), lane_pick(imag_row, port_low)
        )
        port_value = jnp.where(port_high == r, both, port_value)
    port_scaled = port_value[0:1] * unit
    port_top = fixed(port_scaled)
    port_rest = fixed((port_scaled - port_top) * STEPS)
    tail = [
        part.astype(jnp.int32) for part in (port_top, port_rest, row_exponent, top_exponent)
    ]
    tail.append(jnp.zeros((10, 128), jnp.int32))
    need = [by_place(need_ref[pl.ds(c, chips, 2), :]) for c in range(2)]
    first = lax.axis_index("core") == 0
    need = [jnp.where(first, need[0], need[1]), jnp.where(first, need[1], need[0])]
    for chip in range(chips):
        out_ref[chip, : 2 * rows, :] = words
        extra = [part[chip : chip + 1] for part in need] + tail
        out_ref[chip, 2 * rows :, :] = jnp.concatenate(extra, axis=0).astype(jnp.int16)
    out_copy = pltpu.make_async_copy(out_ref, out_hbm, sems.at[5])
    out_copy.start()
    for copy in late_copies:
        copy.wait()
    entry_ref[...] = entry_ref[...] * 2 + sign_ref[...]
    for k in range(2):
        for t in range(code_ref.shape[1]):
            code_ref[k, t : t + 1, :] = entry_ref[k : k + 1, t * 128 : (t + 1) * 128]
    out_copy.wait()


def hand_on_kernel(pack_hbm, part_hbm, out_hbm):
    pass


def extras(pack_ref, place, rows):
    extra = pack_ref[place, 2 * rows :, :].astype(jnp.int32)
    return extra, power_of_two(extra[4:6].astype(F32)) * (1.0 / STEPS)


def unpack_rows(pack_ref, rows_ref, request, rows):
    chips = pack_ref.shape[0]
    for chip in range(chips):
        place = (chip + chips - chip_turn(chips)) % chips
        extra, unit = extras(pack_ref, place, rows)
        extra = extra.astype(F32)
        rows_ref[0, chip : chip + 1, :] = extra[request : request + 1]
        rows_ref[1, chip : chip + 1, :] = (extra[2:3] + extra[3:4] * (1.0 / STEPS)) * unit[1:2]


def ask(need_ref, pack_ref, table_ref, core, rows):
    chips = pack_ref.shape[0]
    sub = lax.broadcasted_iota(jnp.int32, (rows, 128), 0)
    for chip in range(chips):
        place = (chip + chips - chip_turn(chips)) % chips
        wanted = need_ref[pl.ds(2 * chip + core, 1), :]
        wanted = jnp.broadcast_to(jnp.maximum(wanted, 0), (rows, 128))
        here = (wanted >> 7) == sub
        low = wanted & 127
        _, unit = extras(pack_ref, place, rows)
        row_of = (wanted >> 7)[0:8]
        for c in range(2):
            slot_unit = lane_pick(unit[0:1], row_of + c * rows)[0:1]
            block = pack_ref[place, c * rows : (c + 1) * rows, :].astype(jnp.int32).astype(F32)
            picked = jnp.take_along_axis(block, low, axis=1, mode="promise_in_bounds")
            picked = jnp.where(here, picked, 0.0)
            table_ref[c, chip : chip + 1, :] = slot_unit * jnp.sum(picked, axis=0, keepdims=True)


def lookup(code_ref, start, tables):
    total = [None, None]
    for k in range(2):
        code = code_ref[k, pl.ds(start, 8), :]
        high, low = code >> 8, (code >> 1) & 127
        value = [jnp.zeros((8, 128), F32), jnp.zeros((8, 128), F32)]
        for first, step, count, row_of in tables:
            offset = high - first
            for r in range(count):
                here = offset == r * step
                for c in range(2):
                    value[c] = jnp.where(here, lane_pick(row_of(r, c), low), value[c])
        along = (code & 1) == 1
        for c in range(2):
            signed = jnp.where(along, value[c], -value[c])
            total[c] = signed if k == 0 else total[c] + signed
    return total


def own_lookup_kernel(mesh_ref, code_ref, coupling_hbm, out_ref, pair_ref, raw_ref, sems):
    rows = mesh_ref.shape[1] // 128
    far_count, rank = coupling_hbm.shape[:2]
    half = rank // 2
    part = far_count // 2
    copies = [
        pltpu.make_async_copy(
            coupling_hbm.at[pl.ds(i * part, part)], raw_ref.at[pl.ds(i * part, part)], sems.at[i]
        )
        for i in range(2)
    ]
    for copy in copies:
        copy.start()

    def own_row(r, c):
        return mesh_ref[c : c + 1, r * 128 : (r + 1) * 128]

    def block(g, carry):
        start = pl.multiple_of(g * 8, 8)
        total = lookup(code_ref, start, [(0, 1, rows, own_row)])
        out_ref[0, pl.ds(start, 8), :] = total[0]
        out_ref[1, pl.ds(start, 8), :] = total[1]
        return carry

    lax.fori_loop(0, code_ref.shape[1] // 8, block, 0, unroll=True)
    for k in range(far_count):
        if k % part == 0:
            copies[k // part].wait()
        for r in range(half):
            pair_ref[k, r] = jnp.concatenate([raw_ref[k, r], raw_ref[k, half + r]], axis=1)


def add_peers(part_ref, pack_ref, need_ref, code_ref, table_ref, out_ref, core, first):
    chips = pack_ref.shape[0]
    ask(need_ref, pack_ref, table_ref, core, first)

    def peer_row(r, c):
        return table_ref[c, r : r + 1, :]

    def block(g, carry):
        start = pl.multiple_of(g * 8, 8)
        total = lookup(code_ref, start, [(first + core, 2, chips, peer_row)])
        for c in range(2):
            out_ref[c, pl.ds(start, 8), :] = total[c] + part_ref[c, pl.ds(start, 8), :]
        return carry

    lax.fori_loop(0, code_ref.shape[1] // 8, block, 0, unroll=True)


def same_core_kernel(
    part_ref, same_ref, need_ref, code_ref, out_ref, rows_ref, table_ref, *, first
):
    unpack_rows(same_ref, rows_ref, 0, first)
    add_peers(
        part_ref, same_ref, need_ref, code_ref, table_ref, out_ref,
        lax.axis_index("core"), first,
    )


def current_kernel(
    part_ref, other_ref, need_ref, code_ref, basis_hbm, current_ref, coeff_ref, rows_ref,
    table_ref, basis_ref, sem, *, first,
):
    tiles = code_ref.shape[1]
    rank = basis_ref.shape[0] // tiles
    copy = pltpu.make_async_copy(basis_hbm, basis_ref, sem.at[0])
    copy.start()
    unpack_rows(other_ref, rows_ref, 1, first)
    add_peers(
        part_ref, other_ref, need_ref, code_ref, table_ref, current_ref,
        1 - lax.axis_index("core"), first,
    )
    copy.wait()
    inputs = jnp.concatenate([current_ref[0], current_ref[1]], axis=0)
    inputs = inputs.T.astype(BF16)
    lane_tile = lax.broadcasted_iota(jnp.int32, (rank, 2 * tiles), 1) % tiles
    full = jnp.dot(basis_ref[...], inputs, preferred_element_type=F32)
    chosen = jnp.zeros((rank, 2 * tiles), F32)
    for t in range(tiles):
        chosen = jnp.where(lane_tile == t, full[t * rank : (t + 1) * rank], chosen)
    coeff = chosen.astype(BF16)
    for p in range(coeff_ref.shape[0]):
        coeff_ref[p] = coeff


def near_kernel(
    source_ref, current_ref, resistance_hbm, blocks_hbm, out_ref, inputs_ref, blocks_ref,
    resistance_ref, sems,
):
    tiles = current_ref.shape[1]
    width = blocks_ref.shape[1]
    count = blocks_ref.shape[0] // (tiles * width)
    span = 8 * count * width
    starts = [tiles * i // 64 for i in (0, 4, 8)]
    copies = {}
    for i in range(2):
        rows = pl.ds(starts[i] * span, (starts[i + 1] - starts[i]) * span)
        copies[starts[i]] = pltpu.make_async_copy(
            blocks_hbm.at[rows], blocks_ref.at[rows], sems.at[i]
        )
    late_copy = pltpu.make_async_copy(resistance_hbm, resistance_ref, sems.at[2])
    for copy in copies.values():
        copy.start()
    late_copy.start()
    lane_tile = lax.broadcasted_iota(jnp.int32, (width, 128), 1) % tiles
    rows = jnp.concatenate([current_ref[0], current_ref[1]], axis=0)
    columns = rows.T.astype(BF16)
    row_index = lax.broadcasted_iota(jnp.int32, (128, 128), 0)
    for k in range(count):
        picks = jnp.where(row_index == source_ref[k : k + 1, :], 1.0, 0.0).astype(BF16)
        inputs_ref[k * width : (k + 1) * width, :] = jnp.dot(
            columns, picks, preferred_element_type=F32
        ).astype(BF16)
    inputs = inputs_ref[...]
    total = jnp.zeros((width, 128), F32)
    for g in range(tiles // 8):
        if g in copies:
            copies[g].wait()
        block = jnp.concatenate(
            [
                jnp.concatenate(
                    [
                        blocks_ref[(t * count + k) * width : (t * count + k + 1) * width, :]
                        for t in range(g * 8, g * 8 + 8)
                    ],
                    axis=0,
                )
                for k in range(count)
            ],
            axis=1,
        )
        full = jnp.dot(block, inputs, preferred_element_type=F32)
        for i in range(8):
            total = jnp.where(
                lane_tile == g * 8 + i, full[i * width : (i + 1) * width], total
            )
    rows = total.T
    late_copy.wait()
    resistance = resistance_ref[...]
    out_ref[0] = resistance * current_ref[0] - rows[tiles:]
    out_ref[1] = resistance * current_ref[1] + rows[:tiles]


def split(value):
    top = value.astype(BF16)
    return top, (value - top.astype(F32)).astype(BF16)


def counts(rows):
    return lax.broadcasted_iota(jnp.int32, (rows, 128), 0).astype(F32)


def place(high, low, values, rows, spread_ref):
    sub_high, sub_low = counts(rows).astype(BF16), counts(128).astype(BF16)
    one, zero = jnp.ones((128, 128), BF16), jnp.zeros((128, 128), BF16)
    spread_ref[0] = high.astype(F32)
    spread_ref[1] = low.astype(F32)
    for c, value in enumerate(values):
        top, rest = split(value)
        spread_ref[2 + 2 * c] = top.astype(F32)
        spread_ref[3 + 2 * c] = rest.astype(F32)

    def spread(j, i, count):
        return jnp.broadcast_to(spread_ref[j, i : i + 1, :], (count, 128)).astype(BF16)

    left, right = [], []
    for i in range(8):
        here = spread(0, i, rows) == sub_high
        left.append(
            jnp.concatenate(
                [jnp.where(here, spread(j, i, rows), zero[:rows]) for j in range(2, 6)], axis=0
            )
        )
        right.append(jnp.where(spread(1, i, 128) == sub_low, one, zero))
    return jnp.concatenate(left, axis=1), jnp.concatenate(right, axis=1)


def place_few(high, low, values, rows):
    sub_high = lax.broadcasted_iota(jnp.int32, (rows, 128), 0)
    sub_low = lax.broadcasted_iota(jnp.int32, (128, 128), 0)
    left, right = [], []
    for i in range(high.shape[0]):
        here = jnp.broadcast_to(high[i : i + 1], (rows, 128)) == sub_high
        parts = []
        for value in values:
            spread = jnp.where(here, jnp.broadcast_to(value[i : i + 1], (rows, 128)), 0.0)
            parts.extend(split(spread))
        left.append(jnp.concatenate(parts, axis=0))
        there = jnp.broadcast_to(low[i : i + 1], (128, 128)) == sub_low
        right.append(jnp.where(there, 1.0, 0.0).astype(BF16))
    return jnp.concatenate(left, axis=1), jnp.concatenate(right, axis=1)


def scatter(code_ref, voltage_ref, spread_ref, first, rows, low_streams):
    total = None
    for g in range(code_ref.shape[1] // 8):
        for k in range(2):
            code = code_ref[k, g * 8 : g * 8 + 8, :]
            along = (code & 1) == 1
            values = []
            for c in range(2):
                voltage = voltage_ref[c, g * 8 : g * 8 + 8, :]
                values.append(jnp.where(along, voltage, -voltage))
            left, right = place(
                (code >> 8) - first, (code >> 1) & 127, values, rows, spread_ref.at[g, k]
            )
            term = dot_nt(right, left) if low_streams else dot_nt(left, right)
            total = term if total is None else total + term
    total = total.T if low_streams else total
    return [
        total[2 * c * rows : (2 * c + 1) * rows] + total[(2 * c + 1) * rows : (2 * c + 2) * rows]
        for c in range(2)
    ]


def voltage_kernel(
    coeff_ref, admissible_ref, coupling_ref, basis_ref, near_ref, code_ref, voltage_ref, slot_ref,
    picked_ref, mixed_ref, spread_ref, *, first,
):
    peers, rank, lanes = coeff_ref.shape
    far_count = coupling_ref.shape[0]
    tiles = lanes // 2
    half = rank // 2
    groups = half // 4
    device = device_index()
    all_tiles = peers * tiles
    band = all_tiles // far_count
    spans = band // tiles + 1
    stride = peers // far_count
    admissible = jnp.concatenate([admissible_ref[...], admissible_ref[...]], axis=1)
    window = lax.broadcasted_iota(jnp.int32, (far_count, lanes), 0) * band + device * tiles
    window = jnp.where(window >= all_tiles, window - all_tiles, window)
    shifted = admissible - window
    shifted = jnp.where(shifted < 0, shifted + all_tiles, shifted)
    component = lax.broadcasted_iota(jnp.int32, (rank, lanes), 1) // tiles
    for k in range(far_count):
        picked = jnp.zeros((rank, lanes), F32)
        for i in range(spans):
            block = coeff_ref[(device + k * stride + i + peers - turn(peers)) % peers].astype(F32)
            target = jnp.broadcast_to(shifted[k : k + 1] - i * tiles, (rank, lanes))
            source = jnp.clip(target, 0, tiles - 1) + component * tiles
            value = jnp.take_along_axis(block, source, axis=1, mode="promise_in_bounds")
            picked = jnp.where((target >= 0) & (target < tiles), value, picked)
        turned = pltpu.roll(picked, tiles, 1)
        picked_ref[0, k] = jnp.where(component == 0, picked, turned)
        picked_ref[1, k] = jnp.where(component == 0, turned, picked)

    def mix(g, carry):
        total = [[None, None] for _ in range(4)]
        for k in range(far_count):
            picked = [picked_ref[c, k] for c in range(2)]
            for i in range(4):
                block = coupling_ref[k, g * 4 + i].astype(F32)
                for c in range(2):
                    product = block * picked[c]
                    part = product[0:8]
                    for q in range(8, rank, 8):
                        part = part + product[q : q + 8]
                    total[i][c] = part if k == 0 else total[i][c] + part
        for i in range(4):
            for c in range(2):
                row = jnp.sum(total[i][c], axis=0, keepdims=True)
                mixed_ref[pl.ds(c * half + g * 4 + i, 1), :] = row
        return carry

    lax.fori_loop(0, groups, mix, 0, unroll=True)
    mixed = mixed_ref[...].T
    mixed = jnp.concatenate([mixed[:tiles], mixed[tiles:]], axis=1).astype(BF16)
    wide = 8 * rank
    from_row = lax.broadcasted_iota(jnp.int32, (2 * rank, wide), 0)
    to_rank = lax.broadcasted_iota(jnp.int32, (2 * rank, wide), 1) % rank
    repeated = []
    for c in range(2):
        wanted = (to_rank // half) * rank + c * half + to_rank % half
        picks = jnp.where(from_row == wanted, 1.0, 0.0).astype(BF16)
        repeated.append(jnp.dot(mixed, picks, preferred_element_type=F32))
    own_block = (
        lax.broadcasted_iota(jnp.int32, (16, wide), 0) % 8
        == lax.broadcasted_iota(jnp.int32, (16, wide), 1) // rank
    )
    for g in range(tiles // 8):
        rows8 = slice(g * 8, g * 8 + 8)
        both = jnp.concatenate([repeated[0][rows8], repeated[1][rows8]], axis=0)
        both = jnp.where(own_block, both, 0.0).astype(BF16)
        far = jnp.dot(
            both, basis_ref[g * wide : (g + 1) * wide, :], preferred_element_type=F32
        )
        voltage_ref[0, rows8, :] = near_ref[0, rows8, :] - far[8:16]
        voltage_ref[1, rows8, :] = near_ref[1, rows8, :] + far[0:8]
    sums = scatter(
        code_ref, voltage_ref, spread_ref, first, slot_ref.shape[0], True
    )
    shift = turn(peers)
    for c in range(2):
        slot_ref[: peers - shift, c, :] = sums[c][shift:]
        slot_ref[peers - shift :, c, :] = sums[c][:shift]


def own_sum_kernel(
    code_ref, voltage_ref, same_ref, other_ref, port_ref, impedance_ref, own_ref, asked_ref,
    picks_ref, spread_ref,
):
    rows = own_ref.shape[1]
    ports = impedance_ref.shape[1]
    chips = same_ref.shape[1]
    first_core = lax.axis_index("core") == 0
    same = same_ref[0].astype(jnp.int32)
    other = other_ref[0].astype(jnp.int32)
    asked = [jnp.where(first_core, same, other), jnp.where(first_core, other, same)]
    sub_low = lax.broadcasted_iota(jnp.int32, (128, 128), 0)
    for core in range(2):
        asked_ref[core] = asked[core] >> 7
        low = asked[core] & 127
        for chip in range(chips):
            there = jnp.broadcast_to(low[chip : chip + 1], (128, 128)) == sub_low
            place = core * chips + chip
            picks_ref[:, place * 128 : (place + 1) * 128] = jnp.where(there, 1.0, 0.0).astype(BF16)
    port_current = jnp.sum(same_ref[1] + other_ref[1], axis=0, keepdims=True)
    real = port_current[:, :ports]
    imag = port_current[:, ports:]
    both = jnp.concatenate([real, imag, jnp.zeros((6, ports), F32)], axis=0)
    by_real = dot_nt(both, impedance_ref[0], lax.Precision.HIGHEST)
    by_imag = dot_nt(both, impedance_ref[1], lax.Precision.HIGHEST)
    pad = jnp.zeros((1, 128 - ports), F32)
    terms = [
        jnp.concatenate([by_real[0:1] - by_imag[1:2], pad], axis=1),
        jnp.concatenate([by_real[1:2] + by_imag[0:1], pad], axis=1),
    ]
    port = port_ref[...] - device_index() * (rows * 128)
    port = jnp.where((port >= 0) & (port < rows * 128), port, -1)
    port = jnp.concatenate([port, jnp.full((1, 128 - ports), -1, jnp.int32)], axis=1)
    left, right = place_few(port >> 7, port & 127, terms, rows)
    total = dot_nt(left, right)
    sums = scatter(code_ref, voltage_ref, spread_ref, 0, rows, False)
    for c in range(2):
        own_ref[c] = sums[c] + (
            total[2 * c * rows : (2 * c + 1) * rows] + total[(2 * c + 1) * rows : (2 * c + 2) * rows]
        )


def finish_kernel(own_ref, arrived_ref, asked_ref, picks_ref, out_ref):
    rows = own_ref.shape[1]
    peers = arrived_ref.shape[0]
    chips = peers // 2
    sub_high = lax.broadcasted_iota(jnp.int32, (rows, 128), 0)
    left = []
    for core in range(2):
        for chip in range(chips):
            here = jnp.broadcast_to(asked_ref[core, chip : chip + 1, :], (rows, 128)) == sub_high
            parts = []
            for c in range(2):
                place = (2 * chip + core + peers - turn(peers)) % peers
                value = jnp.broadcast_to(arrived_ref[place, c : c + 1, :], (rows, 128))
                parts.extend(split(jnp.where(here, value, 0.0)))
            left.append(jnp.concatenate(parts, axis=0))
    total = dot_nt(jnp.concatenate(left, axis=1), picks_ref[...])
    for c in range(2):
        summed = own_ref[c] + (
            total[2 * c * rows : (2 * c + 1) * rows] + total[(2 * c + 1) * rows : (2 * c + 2) * rows]
        )
        for r in range(rows):
            out_ref[c : c + 1, r * 128 : (r + 1) * 128] = summed[r : r + 1]


def per_device(
    mesh_current,
    branch_entry,
    branch_sign,
    need_slots,
    resistance,
    near_blocks,
    near_source,
    basis_in,
    coupling,
    basis_out,
    admissible,
    port_mesh,
    port_coupling,
):
    chips = lax.axis_size("chips")
    peers = 2 * chips
    core = lax.axis_index("core")
    device = 2 * lax.axis_index("chips") + core
    mesh_dev = mesh_current.shape[1]
    tiles, near_count, width, _ = near_blocks.shape
    rank = basis_in.shape[1]
    far_count = admissible.shape[1]
    own_rows = mesh_dev // 128
    vmem = pl.BlockSpec(memory_space=pltpu.VMEM)
    shape = jax.ShapeDtypeStruct

    coupling_lanes = jnp.transpose(coupling, (1, 2, 3, 0))
    basis_in_rows = basis_in.reshape(tiles * rank, width)
    basis_out_rows = basis_out.reshape(tiles * rank, width)
    half = jnp.arange(2 * tiles, dtype=jnp.int32) // tiles
    sources = jnp.transpose(near_source)
    sources = jnp.concatenate([sources, sources], axis=1) + half[None] * tiles
    def in_hbm(x):
        return pltpu.with_memory_space_constraint(x, pltpu.HBM)

    hbm = pl.BlockSpec(memory_space=pl.ANY)
    port_row = port_mesh.reshape(1, -1)
    pack_rows = 2 * own_rows + 16
    pack_shape = (chips, pack_rows, 128)
    pack, mesh_near, need_near, port_near, code = pl.pallas_call(
        pack_kernel,
        out_shape=(
            pltpu.HBM(pack_shape, jnp.int16),
            pltpu.VMEM(mesh_current.shape, F32),
            pltpu.VMEM(need_slots.shape, jnp.int32),
            pltpu.VMEM(port_row.shape, jnp.int32),
            pltpu.VMEM((2, tiles, width), jnp.int32),
        ),
        in_specs=[hbm] * 5,
        out_specs=(hbm,) + (vmem,) * 4,
        scratch_shapes=[
            pltpu.VMEM(pack_shape, jnp.int16),
            pltpu.VMEM((2 * own_rows, 128), F32),
            pltpu.VMEM(branch_entry.shape, jnp.int32),
            pltpu.VMEM(branch_sign.shape, jnp.int32),
            pltpu.SemaphoreType.DMA((6,)),
        ],
        compiler_params=params(),
        name="pack",
    )(
        in_hbm(mesh_current),
        in_hbm(need_slots),
        in_hbm(port_row),
        in_hbm(branch_entry),
        in_hbm(branch_sign),
    )
    chip_members = [[(j + chip_turn(chips)) % chips for j in range(chips)]]
    same = lax.all_to_all(pack, "chips", 0, 0, tiled=True, axis_index_groups=chip_members)
    own_part, pairs = pl.pallas_call(
        own_lookup_kernel,
        out_shape=(
            shape((2, tiles, width), F32),
            pltpu.VMEM((far_count, rank // 2, rank, 2 * tiles), BF16),
        ),
        in_specs=[vmem] * 2 + [hbm],
        out_specs=(vmem,) * 2,
        scratch_shapes=[
            pltpu.VMEM(coupling_lanes.shape, BF16),
            pltpu.SemaphoreType.DMA((2,)),
        ],
        compiler_params=params(),
        cost_estimate=small_cost(),
        name="own_lookup",
    )(mesh_near, code, in_hbm(coupling_lanes))
    same = pl.pallas_call(
        hand_on_kernel,
        out_shape=shape(same.shape, same.dtype),
        in_specs=[hbm] * 2,
        out_specs=hbm,
        input_output_aliases={0: 0},
        compiler_params=params(),
        name="hand_on",
    )(same, own_part)
    other = lax.ppermute(same, "core", [(0, 1), (1, 0)])
    part, same_rows = pl.pallas_call(
        functools.partial(same_core_kernel, first=own_rows),
        out_shape=(shape((2, tiles, width), F32), shape((2, chips, 128), F32)),
        in_specs=[vmem] * 4,
        out_specs=(vmem,) * 2,
        scratch_shapes=[pltpu.VMEM((2, chips, 128), F32)],
        compiler_params=params(),
        cost_estimate=small_cost(),
        name="same_core",
    )(own_part, same, need_near, code)
    current, coeff, other_rows = pl.pallas_call(
        functools.partial(current_kernel, first=own_rows),
        out_shape=(
            shape((2, tiles, width), F32),
            shape((peers, rank, 2 * tiles), BF16),
            shape((2, chips, 128), F32),
        ),
        in_specs=[vmem] * 4 + [hbm],
        out_specs=(vmem,) * 3,
        scratch_shapes=[
            pltpu.VMEM((2, chips, 128), F32),
            pltpu.VMEM(basis_in_rows.shape, BF16),
            pltpu.SemaphoreType.DMA((1,)),
        ],
        compiler_params=params(),
        name="currents",
    )(part, other, need_near, code, in_hbm(basis_in_rows))
    members = [[(j + turn(peers)) % peers for j in range(peers)]]
    all_coeff = lax.all_to_all(
        coeff, ("chips", "core"), 0, 0, tiled=True, axis_index_groups=members
    )
    near_rows = near_blocks.reshape(tiles * near_count * width, width)
    near = pl.pallas_call(
        near_kernel,
        out_shape=shape((2, tiles, width), F32),
        in_specs=[vmem] * 2 + [hbm] * 2,
        out_specs=vmem,
        scratch_shapes=[
            pltpu.VMEM((near_count * width, 2 * tiles), BF16),
            pltpu.VMEM(near_rows.shape, BF16),
            pltpu.VMEM((tiles, width), F32),
            pltpu.SemaphoreType.DMA((3,)),
        ],
        compiler_params=params(),
        cost_estimate=pl.CostEstimate(
            flops=256 * near_blocks.size, bytes_accessed=2 * near_blocks.size, transcendentals=0
        ),
        name="near_field",
    )(sources, current, in_hbm(resistance.reshape(tiles, width)), in_hbm(near_rows))
    voltage, slots = pl.pallas_call(
        functools.partial(voltage_kernel, first=own_rows),
        out_shape=(shape((2, tiles, width), F32), shape((peers, 2, 128), F32)),
        in_specs=[vmem] * 6,
        out_specs=(vmem,) * 2,
        scratch_shapes=[
            pltpu.VMEM((2, far_count, rank, 2 * tiles), F32),
            pltpu.VMEM((rank, 2 * tiles), F32),
            pltpu.VMEM((tiles // 8, 2, 6, 8, 128), F32),
        ],
        compiler_params=params(),
        name="voltages",
    )(
        all_coeff,
        jnp.transpose(admissible),
        pairs,
        basis_out_rows,
        near,
        code,
    )
    arrived = lax.all_to_all(
        slots, ("chips", "core"), 0, 0, tiled=True, axis_index_groups=members
    )
    own, asked, picks = pl.pallas_call(
        own_sum_kernel,
        out_shape=(
            shape((2, own_rows, 128), F32),
            shape((2, chips, 128), jnp.int32),
            shape((128, peers * 128), BF16),
        ),
        in_specs=[vmem] * 6,
        out_specs=(vmem,) * 3,
        scratch_shapes=[
            pltpu.VMEM((tiles // 8, 2, 6, 8, 128), F32),
        ],
        compiler_params=params(),
        cost_estimate=small_cost(),
        name="own_sums",
    )(code, voltage, same_rows, other_rows, port_near, port_coupling)
    return pl.pallas_call(
        finish_kernel,
        out_shape=shape((2, mesh_dev), F32),
        in_specs=[vmem] * 4,
        out_specs=vmem,
        compiler_params=params(),
        name="finish",
    )(own, arrived, asked, picks)


def solution(mesh):
    groups, peers = mesh.devices.shape
    split_mesh = jax.sharding.Mesh(
        mesh.devices.reshape(groups, peers // 2, 2), ("groups", "chips", "core")
    )
    in_specs = (
        P(None, SPREAD),
        P(None, SPREAD),
        P(None, SPREAD),
        P(SPREAD, None),
        P(SPREAD),
        P(SPREAD, None, None, None),
        P(SPREAD, None),
        P(SPREAD, None, None),
        P(SPREAD, None, None, None),
        P(SPREAD, None, None),
        P(SPREAD, None),
        P("groups"),
        P(),
    )
    out_specs = P(None, SPREAD)
    return jax.shard_map(
        per_device, mesh=split_mesh, in_specs=in_specs, out_specs=out_specs, check_vma=False
    )
```

```python
import functools
import math

import jax
import jax.numpy as jnp
from jax import lax
from jax.experimental import pallas as pl
from jax.experimental.pallas import tpu as pltpu
from jax.sharding import PartitionSpec as P

F32 = jnp.float32
BF16 = jnp.bfloat16
SPREAD = ("groups", "chips", "core")
STEPS = 32000.0
VMEM_LIMIT = 24 * 1024 * 1024
NT = (((1,), (1,)), ((), ()))


def params():
    return pltpu.CompilerParams(vmem_limit_bytes=VMEM_LIMIT)


def small_cost():
    return pl.CostEstimate(flops=10**9, bytes_accessed=8 * 10**6, transcendentals=0)


def lane_pick(row, lanes):
    spread = jnp.broadcast_to(row, lanes.shape)
    return jnp.take_along_axis(spread, lanes, axis=1, mode="promise_in_bounds")


def dot_nt(left, right, precision=None):
    return lax.dot_general(
        left, right, NT, preferred_element_type=F32, precision=precision
    )


def turn(members):
    return members // 2


def chip_turn(chips):
    return chips // 2


def by_place(rows):
    shift = chip_turn(rows.shape[0])
    return jnp.concatenate([rows[shift:], rows[:shift]], axis=0)


def device_index():
    return 2 * lax.axis_index("chips") + lax.axis_index("core")


def fetch(copies, late_copies):
    for copy in copies + late_copies:
        copy.start()
    for copy in copies:
        copy.wait()


def power_of_two(exponent):
    return jnp.exp(exponent * math.log(2.0))


def fixed(value):
    return jnp.floor(value + 0.5)


def pack_kernel(
    mesh_hbm, need_hbm, port_hbm, entry_hbm, sign_hbm, out_hbm, mesh_ref, need_ref, port_ref,
    code_ref, out_ref, stage_ref, entry_ref, sign_ref, sems,
):
    late_copies = [
        pltpu.make_async_copy(entry_hbm, entry_ref, sems.at[3]),
        pltpu.make_async_copy(sign_hbm, sign_ref, sems.at[4]),
    ]
    rows = mesh_ref.shape[1] // 128
    ports = port_ref.shape[1]
    chips = out_ref.shape[0]
    fetch(
        [
            pltpu.make_async_copy(source, target, sems.at[i])
            for i, (source, target) in enumerate(
                [(mesh_hbm, mesh_ref), (need_hbm, need_ref), (port_hbm, port_ref)]
            )
        ],
        late_copies,
    )
    for r in range(rows):
        stage_ref[r : r + 1, :] = mesh_ref[0:1, r * 128 : (r + 1) * 128]
        stage_ref[rows + r : rows + r + 1, :] = mesh_ref[1:2, r * 128 : (r + 1) * 128]
    block = stage_ref[...]
    largest = jnp.maximum(jnp.max(jnp.abs(block), axis=1, keepdims=True), 1e-30)
    largest = jnp.broadcast_to(largest, block.shape)
    exponent = jnp.ceil(jnp.log(largest) * (1.0 / math.log(2.0)))
    words = fixed(block * (power_of_two(-exponent) * STEPS)).astype(jnp.int32).astype(jnp.int16)
    top_exponent = jnp.max(exponent, axis=0, keepdims=True)
    unit = power_of_two(-top_exponent) * STEPS
    row_exponent = exponent.T[0:1]
    row_exponent = jnp.concatenate(
        [row_exponent, jnp.zeros((1, 128 - 2 * rows), F32)], axis=1
    )
    port = port_ref[...] - device_index() * (rows * 128)
    port = jnp.where((port >= 0) & (port < rows * 128), port, -1)
    port = jnp.broadcast_to(jnp.concatenate([port, port], axis=1), (8, 128))
    port_high, port_low = port >> 7, port & 127
    port_value = jnp.zeros((8, 128), F32)
    lane = lax.broadcasted_iota(jnp.int32, (8, 128), 1)
    for r in range(rows):
        real_row = stage_ref[r : r + 1, :]
        imag_row = stage_ref[rows + r : rows + r + 1, :]
        both = jnp.where(
            lane < ports, lane_pick(real_row, port_low), lane_pick(imag_row, port_low)
        )
        port_value = jnp.where(port_high == r, both, port_value)
    port_scaled = port_value[0:1] * unit
    port_top = fixed(port_scaled)
    port_rest = fixed((port_scaled - port_top) * STEPS)
    tail = [
        part.astype(jnp.int32) for part in (port_top, port_rest, row_exponent, top_exponent)
    ]
    tail.append(jnp.zeros((10, 128), jnp.int32))
    need = [by_place(need_ref[pl.ds(c, chips, 2), :]) for c in range(2)]
    first = lax.axis_index("core") == 0
    need = [jnp.where(first, need[0], need[1]), jnp.where(first, need[1], need[0])]
    for chip in range(chips):
        out_ref[chip, : 2 * rows, :] = words
        extra = [part[chip : chip + 1] for part in need] + tail
        out_ref[chip, 2 * rows :, :] = jnp.concatenate(extra, axis=0).astype(jnp.int16)
    out_copy = pltpu.make_async_copy(out_ref, out_hbm, sems.at[5])
    out_copy.start()
    for copy in late_copies:
        copy.wait()
    entry_ref[...] = entry_ref[...] * 2 + sign_ref[...]
    for k in range(2):
        for t in range(code_ref.shape[1]):
            code_ref[k, t : t + 1, :] = entry_ref[k : k + 1, t * 128 : (t + 1) * 128]
    out_copy.wait()


def hand_on_kernel(pack_hbm, part_hbm, out_hbm):
    pass


def extras(pack_ref, place, rows):
    extra = pack_ref[place, 2 * rows :, :].astype(jnp.int32)
    return extra, power_of_two(extra[4:6].astype(F32)) * (1.0 / STEPS)


def unpack_rows(pack_ref, rows_ref, request, rows):
    chips = pack_ref.shape[0]
    for chip in range(chips):
        place = (chip + chips - chip_turn(chips)) % chips
        extra, unit = extras(pack_ref, place, rows)
        extra = extra.astype(F32)
        rows_ref[0, chip : chip + 1, :] = extra[request : request + 1]
        rows_ref[1, chip : chip + 1, :] = (extra[2:3] + extra[3:4] * (1.0 / STEPS)) * unit[1:2]


def ask(need_ref, pack_ref, table_ref, core, rows):
    chips = pack_ref.shape[0]
    sub = lax.broadcasted_iota(jnp.int32, (rows, 128), 0)
    for chip in range(chips):
        place = (chip + chips - chip_turn(chips)) % chips
        wanted = need_ref[pl.ds(2 * chip + core, 1), :]
        wanted = jnp.broadcast_to(jnp.maximum(wanted, 0), (rows, 128))
        here = (wanted >> 7) == sub
        low = wanted & 127
        _, unit = extras(pack_ref, place, rows)
        row_of = (wanted >> 7)[0:8]
        for c in range(2):
            slot_unit = lane_pick(unit[0:1], row_of + c * rows)[0:1]
            block = pack_ref[place, c * rows : (c + 1) * rows, :].astype(jnp.int32).astype(F32)
            picked = jnp.take_along_axis(block, low, axis=1, mode="promise_in_bounds")
            picked = jnp.where(here, picked, 0.0)
            table_ref[c, chip : chip + 1, :] = slot_unit * jnp.sum(picked, axis=0, keepdims=True)


def lookup(code_ref, start, tables):
    total = [None, None]
    for k in range(2):
        code = code_ref[k, pl.ds(start, 8), :]
        high, low = code >> 8, (code >> 1) & 127
        value = [jnp.zeros((8, 128), F32), jnp.zeros((8, 128), F32)]
        for first, step, count, row_of in tables:
            offset = high - first
            for r in range(count):
                here = offset == r * step
                for c in range(2):
                    value[c] = jnp.where(here, lane_pick(row_of(r, c), low), value[c])
        along = (code & 1) == 1
        for c in range(2):
            signed = jnp.where(along, value[c], -value[c])
            total[c] = signed if k == 0 else total[c] + signed
    return total


def own_lookup_kernel(mesh_ref, code_ref, coupling_hbm, out_ref, pair_ref, raw_ref, sems):
    rows = mesh_ref.shape[1] // 128
    far_count, rank = coupling_hbm.shape[:2]
    half = rank // 2
    part = far_count // 2
    copies = [
        pltpu.make_async_copy(
            coupling_hbm.at[pl.ds(i * part, part)], raw_ref.at[pl.ds(i * part, part)], sems.at[i]
        )
        for i in range(2)
    ]
    for copy in copies:
        copy.start()

    def own_row(r, c):
        return mesh_ref[c : c + 1, r * 128 : (r + 1) * 128]

    def block(g, carry):
        start = pl.multiple_of(g * 8, 8)
        total = lookup(code_ref, start, [(0, 1, rows, own_row)])
        out_ref[0, pl.ds(start, 8), :] = total[0]
        out_ref[1, pl.ds(start, 8), :] = total[1]
        return carry

    lax.fori_loop(0, code_ref.shape[1] // 8, block, 0, unroll=True)
    for k in range(far_count):
        if k % part == 0:
            copies[k // part].wait()
        for r in range(half):
            pair_ref[k, r] = jnp.concatenate([raw_ref[k, r], raw_ref[k, half + r]], axis=1)


def add_peers(part_ref, pack_ref, need_ref, code_ref, table_ref, out_ref, core, first):
    chips = pack_ref.shape[0]
    ask(need_ref, pack_ref, table_ref, core, first)

    def peer_row(r, c):
        return table_ref[c, r : r + 1, :]

    def block(g, carry):
        start = pl.multiple_of(g * 8, 8)
        total = lookup(code_ref, start, [(first + core, 2, chips, peer_row)])
        for c in range(2):
            out_ref[c, pl.ds(start, 8), :] = total[c] + part_ref[c, pl.ds(start, 8), :]
        return carry

    lax.fori_loop(0, code_ref.shape[1] // 8, block, 0, unroll=True)


def same_core_kernel(
    part_ref, same_ref, need_ref, code_ref, out_ref, rows_ref, table_ref, *, first
):
    unpack_rows(same_ref, rows_ref, 0, first)
    add_peers(
        part_ref, same_ref, need_ref, code_ref, table_ref, out_ref,
        lax.axis_index("core"), first,
    )


def current_kernel(
    part_ref, other_ref, need_ref, code_ref, basis_hbm, current_ref, coeff_ref, rows_ref,
    table_ref, basis_ref, sem, *, first,
):
    tiles = code_ref.shape[1]
    rank = basis_ref.shape[0] // tiles
    copy = pltpu.make_async_copy(basis_hbm, basis_ref, sem.at[0])
    copy.start()
    unpack_rows(other_ref, rows_ref, 1, first)
    add_peers(
        part_ref, other_ref, need_ref, code_ref, table_ref, current_ref,
        1 - lax.axis_index("core"), first,
    )
    copy.wait()
    inputs = jnp.concatenate([current_ref[0], current_ref[1]], axis=0)
    inputs = inputs.T.astype(BF16)
    lane_tile = lax.broadcasted_iota(jnp.int32, (rank, 2 * tiles), 1) % tiles
    full = jnp.dot(basis_ref[...], inputs, preferred_element_type=F32)
    chosen = jnp.zeros((rank, 2 * tiles), F32)
    for t in range(tiles):
        chosen = jnp.where(lane_tile == t, full[t * rank : (t + 1) * rank], chosen)
    coeff = chosen.astype(BF16)
    for p in range(coeff_ref.shape[0]):
        coeff_ref[p] = coeff


def near_kernel(
    source_ref, current_ref, resistance_hbm, blocks_hbm, out_ref, inputs_ref, blocks_ref,
    resistance_ref, sems,
):
    tiles = current_ref.shape[1]
    width = blocks_ref.shape[1]
    count = blocks_ref.shape[0] // (tiles * width)
    span = 8 * count * width
    starts = [tiles * i // 64 for i in (0, 4, 8)]
    copies = {}
    for i in range(2):
        rows = pl.ds(starts[i] * span, (starts[i + 1] - starts[i]) * span)
        copies[starts[i]] = pltpu.make_async_copy(
            blocks_hbm.at[rows], blocks_ref.at[rows], sems.at[i]
        )
    late_copy = pltpu.make_async_copy(resistance_hbm, resistance_ref, sems.at[2])
    for copy in copies.values():
        copy.start()
    late_copy.start()
    lane_tile = lax.broadcasted_iota(jnp.int32, (width, 128), 1) % tiles
    rows = jnp.concatenate([current_ref[0], current_ref[1]], axis=0)
    columns = rows.T.astype(BF16)
    row_index = lax.broadcasted_iota(jnp.int32, (128, 128), 0)
    for k in range(count):
        picks = jnp.where(row_index == source_ref[k : k + 1, :], 1.0, 0.0).astype(BF16)
        inputs_ref[k * width : (k + 1) * width, :] = jnp.dot(
            columns, picks, preferred_element_type=F32
        ).astype(BF16)
    inputs = inputs_ref[...]
    total = jnp.zeros((width, 128), F32)
    for g in range(tiles // 8):
        if g in copies:
            copies[g].wait()
        block = jnp.concatenate(
            [
                jnp.concatenate(
                    [
                        blocks_ref[(t * count + k) * width : (t * count + k + 1) * width, :]
                        for t in range(g * 8, g * 8 + 8)
                    ],
                    axis=0,
                )
                for k in range(count)
            ],
            axis=1,
        )
        full = jnp.dot(block, inputs, preferred_element_type=F32)
        for i in range(8):
            total = jnp.where(
                lane_tile == g * 8 + i, full[i * width : (i + 1) * width], total
            )
    rows = total.T
    late_copy.wait()
    resistance = resistance_ref[...]
    out_ref[0] = resistance * current_ref[0] - rows[tiles:]
    out_ref[1] = resistance * current_ref[1] + rows[:tiles]


def split(value):
    top = value.astype(BF16)
    return top, (value - top.astype(F32)).astype(BF16)


def counts(rows):
    return lax.broadcasted_iota(jnp.int32, (rows, 128), 0).astype(F32)


def place(high, low, values, rows, spread_ref):
    sub_high, sub_low = counts(rows).astype(BF16), counts(128).astype(BF16)
    one, zero = jnp.ones((128, 128), BF16), jnp.zeros((128, 128), BF16)
    spread_ref[0] = high.astype(F32)
    spread_ref[1] = low.astype(F32)
    for c, value in enumerate(values):
        top, rest = split(value)
        spread_ref[2 + 2 * c] = top.astype(F32)
        spread_ref[3 + 2 * c] = rest.astype(F32)

    def spread(j, i, count):
        return jnp.broadcast_to(spread_ref[j, i : i + 1, :], (count, 128)).astype(BF16)

    left, right = [], []
    for i in range(8):
        here = spread(0, i, rows) == sub_high
        left.append(
            jnp.concatenate(
                [jnp.where(here, spread(j, i, rows), zero[:rows]) for j in range(2, 6)], axis=0
            )
        )
        right.append(jnp.where(spread(1, i, 128) == sub_low, one, zero))
    return jnp.concatenate(left, axis=1), jnp.concatenate(right, axis=1)


def place_few(high, low, values, rows):
    sub_high = lax.broadcasted_iota(jnp.int32, (rows, 128), 0)
    sub_low = lax.broadcasted_iota(jnp.int32, (128, 128), 0)
    left, right = [], []
    for i in range(high.shape[0]):
        here = jnp.broadcast_to(high[i : i + 1], (rows, 128)) == sub_high
        parts = []
        for value in values:
            spread = jnp.where(here, jnp.broadcast_to(value[i : i + 1], (rows, 128)), 0.0)
            parts.extend(split(spread))
        left.append(jnp.concatenate(parts, axis=0))
        there = jnp.broadcast_to(low[i : i + 1], (128, 128)) == sub_low
        right.append(jnp.where(there, 1.0, 0.0).astype(BF16))
    return jnp.concatenate(left, axis=1), jnp.concatenate(right, axis=1)


def scatter(code_ref, voltage_ref, spread_ref, first, rows, low_streams):
    total = None
    for g in range(code_ref.shape[1] // 8):
        for k in range(2):
            code = code_ref[k, g * 8 : g * 8 + 8, :]
            along = (code & 1) == 1
            values = []
            for c in range(2):
                voltage = voltage_ref[c, g * 8 : g * 8 + 8, :]
                values.append(jnp.where(along, voltage, -voltage))
            left, right = place(
                (code >> 8) - first, (code >> 1) & 127, values, rows, spread_ref.at[g, k]
            )
            term = dot_nt(right, left) if low_streams else dot_nt(left, right)
            total = term if total is None else total + term
    total = total.T if low_streams else total
    return [
        total[2 * c * rows : (2 * c + 1) * rows] + total[(2 * c + 1) * rows : (2 * c + 2) * rows]
        for c in range(2)
    ]


def voltage_kernel(
    coeff_ref, admissible_ref, coupling_ref, basis_ref, near_ref, code_ref, voltage_ref, slot_ref,
    picked_ref, mixed_ref, spread_ref, *, first,
):
    peers, rank, lanes = coeff_ref.shape
    far_count = coupling_ref.shape[0]
    tiles = lanes // 2
    half = rank // 2
    groups = half // 4
    device = device_index()
    all_tiles = peers * tiles
    band = all_tiles // far_count
    spans = band // tiles + 1
    stride = peers // far_count
    admissible = jnp.concatenate([admissible_ref[...], admissible_ref[...]], axis=1)
    window = lax.broadcasted_iota(jnp.int32, (far_count, lanes), 0) * band + device * tiles
    window = jnp.where(window >= all_tiles, window - all_tiles, window)
    shifted = admissible - window
    shifted = jnp.where(shifted < 0, shifted + all_tiles, shifted)
    component = lax.broadcasted_iota(jnp.int32, (rank, lanes), 1) // tiles
    for k in range(far_count):
        picked = jnp.zeros((rank, lanes), F32)
        for i in range(spans):
            block = coeff_ref[(device + k * stride + i + peers - turn(peers)) % peers].astype(F32)
            target = jnp.broadcast_to(shifted[k : k + 1] - i * tiles, (rank, lanes))
            source = jnp.clip(target, 0, tiles - 1) + component * tiles
            value = jnp.take_along_axis(block, source, axis=1, mode="promise_in_bounds")
            picked = jnp.where((target >= 0) & (target < tiles), value, picked)
        turned = pltpu.roll(picked, tiles, 1)
        picked_ref[0, k] = jnp.where(component == 0, picked, turned)
        picked_ref[1, k] = jnp.where(component == 0, turned, picked)

    def mix(g, carry):
        total = [[None, None] for _ in range(4)]
        for k in range(far_count):
            picked = [picked_ref[c, k] for c in range(2)]
            for i in range(4):
                block = coupling_ref[k, g * 4 + i].astype(F32)
                for c in range(2):
                    product = block * picked[c]
                    part = product[0:8]
                    for q in range(8, rank, 8):
                        part = part + product[q : q + 8]
                    total[i][c] = part if k == 0 else total[i][c] + part
        for i in range(4):
            for c in range(2):
                row = jnp.sum(total[i][c], axis=0, keepdims=True)
                mixed_ref[pl.ds(c * half + g * 4 + i, 1), :] = row
        return carry

    lax.fori_loop(0, groups, mix, 0, unroll=True)
    mixed = mixed_ref[...].T
    mixed = jnp.concatenate([mixed[:tiles], mixed[tiles:]], axis=1).astype(BF16)
    wide = 8 * rank
    from_row = lax.broadcasted_iota(jnp.int32, (2 * rank, wide), 0)
    to_rank = lax.broadcasted_iota(jnp.int32, (2 * rank, wide), 1) % rank
    repeated = []
    for c in range(2):
        wanted = (to_rank // half) * rank + c * half + to_rank % half
        picks = jnp.where(from_row == wanted, 1.0, 0.0).astype(BF16)
        repeated.append(jnp.dot(mixed, picks, preferred_element_type=F32))
    own_block = (
        lax.broadcasted_iota(jnp.int32, (16, wide), 0) % 8
        == lax.broadcasted_iota(jnp.int32, (16, wide), 1) // rank
    )
    for g in range(tiles // 8):
        rows8 = slice(g * 8, g * 8 + 8)
        both = jnp.concatenate([repeated[0][rows8], repeated[1][rows8]], axis=0)
        both = jnp.where(own_block, both, 0.0).astype(BF16)
        far = jnp.dot(
            both, basis_ref[g * wide : (g + 1) * wide, :], preferred_element_type=F32
        )
        voltage_ref[0, rows8, :] = near_ref[0, rows8, :] - far[8:16]
        voltage_ref[1, rows8, :] = near_ref[1, rows8, :] + far[0:8]
    sums = scatter(
        code_ref, voltage_ref, spread_ref, first, slot_ref.shape[0], True
    )
    shift = turn(peers)
    for c in range(2):
        slot_ref[: peers - shift, c, :] = sums[c][shift:]
        slot_ref[peers - shift :, c, :] = sums[c][:shift]


def own_sum_kernel(
    code_ref, voltage_ref, same_ref, other_ref, port_ref, impedance_ref, own_ref, asked_ref,
    picks_ref, spread_ref,
):
    rows = own_ref.shape[1]
    ports = impedance_ref.shape[1]
    chips = same_ref.shape[1]
    first_core = lax.axis_index("core") == 0
    same = same_ref[0].astype(jnp.int32)
    other = other_ref[0].astype(jnp.int32)
    asked = [jnp.where(first_core, same, other), jnp.where(first_core, other, same)]
    sub_low = lax.broadcasted_iota(jnp.int32, (128, 128), 0)
    for core in range(2):
        asked_ref[core] = asked[core] >> 7
        low = asked[core] & 127
        for chip in range(chips):
            there = jnp.broadcast_to(low[chip : chip + 1], (128, 128)) == sub_low
            place = core * chips + chip
            picks_ref[:, place * 128 : (place + 1) * 128] = jnp.where(there, 1.0, 0.0).astype(BF16)
    port_current = jnp.sum(same_ref[1] + other_ref[1], axis=0, keepdims=True)
    real = port_current[:, :ports]
    imag = port_current[:, ports:]
    both = jnp.concatenate([real, imag, jnp.zeros((6, ports), F32)], axis=0)
    by_real = dot_nt(both, impedance_ref[0], lax.Precision.HIGHEST)
    by_imag = dot_nt(both, impedance_ref[1], lax.Precision.HIGHEST)
    pad = jnp.zeros((1, 128 - ports), F32)
    terms = [
        jnp.concatenate([by_real[0:1] - by_imag[1:2], pad], axis=1),
        jnp.concatenate([by_real[1:2] + by_imag[0:1], pad], axis=1),
    ]
    port = port_ref[...] - device_index() * (rows * 128)
    port = jnp.where((port >= 0) & (port < rows * 128), port, -1)
    port = jnp.concatenate([port, jnp.full((1, 128 - ports), -1, jnp.int32)], axis=1)
    left, right = place_few(port >> 7, port & 127, terms, rows)
    total = dot_nt(left, right)
    sums = scatter(code_ref, voltage_ref, spread_ref, 0, rows, False)
    for c in range(2):
        own_ref[c] = sums[c] + (
            total[2 * c * rows : (2 * c + 1) * rows] + total[(2 * c + 1) * rows : (2 * c + 2) * rows]
        )


def finish_kernel(own_ref, arrived_ref, asked_ref, picks_ref, out_ref):
    rows = own_ref.shape[1]
    peers = arrived_ref.shape[0]
    chips = peers // 2
    sub_high = lax.broadcasted_iota(jnp.int32, (rows, 128), 0)
    left = []
    for core in range(2):
        for chip in range(chips):
            here = jnp.broadcast_to(asked_ref[core, chip : chip + 1, :], (rows, 128)) == sub_high
            parts = []
            for c in range(2):
                place = (2 * chip + core + peers - turn(peers)) % peers
                value = jnp.broadcast_to(arrived_ref[place, c : c + 1, :], (rows, 128))
                parts.extend(split(jnp.where(here, value, 0.0)))
            left.append(jnp.concatenate(parts, axis=0))
    total = dot_nt(jnp.concatenate(left, axis=1), picks_ref[...])
    for c in range(2):
        summed = own_ref[c] + (
            total[2 * c * rows : (2 * c + 1) * rows] + total[(2 * c + 1) * rows : (2 * c + 2) * rows]
        )
        for r in range(rows):
            out_ref[c : c + 1, r * 128 : (r + 1) * 128] = summed[r : r + 1]


def per_device(
    mesh_current,
    branch_entry,
    branch_sign,
    need_slots,
    resistance,
    near_blocks,
    near_source,
    basis_in,
    coupling,
    basis_out,
    admissible,
    port_mesh,
    port_coupling,
):
    chips = lax.axis_size("chips")
    peers = 2 * chips
    core = lax.axis_index("core")
    device = 2 * lax.axis_index("chips") + core
    mesh_dev = mesh_current.shape[1]
    tiles, near_count, width, _ = near_blocks.shape
    rank = basis_in.shape[1]
    far_count = admissible.shape[1]
    own_rows = mesh_dev // 128
    vmem = pl.BlockSpec(memory_space=pltpu.VMEM)
    shape = jax.ShapeDtypeStruct

    coupling_lanes = jnp.transpose(coupling, (1, 2, 3, 0))
    basis_in_rows = basis_in.reshape(tiles * rank, width)
    basis_out_rows = basis_out.reshape(tiles * rank, width)
    half = jnp.arange(2 * tiles, dtype=jnp.int32) // tiles
    sources = jnp.transpose(near_source)
    sources = jnp.concatenate([sources, sources], axis=1) + half[None] * tiles
    def in_hbm(x):
        return pltpu.with_memory_space_constraint(x, pltpu.HBM)

    hbm = pl.BlockSpec(memory_space=pl.ANY)
    port_row = port_mesh.reshape(1, -1)
    pack_rows = 2 * own_rows + 16
    pack_shape = (chips, pack_rows, 128)
    pack, mesh_near, need_near, port_near, code = pl.pallas_call(
        pack_kernel,
        out_shape=(
            pltpu.HBM(pack_shape, jnp.int16),
            pltpu.VMEM(mesh_current.shape, F32),
            pltpu.VMEM(need_slots.shape, jnp.int32),
            pltpu.VMEM(port_row.shape, jnp.int32),
            pltpu.VMEM((2, tiles, width), jnp.int32),
        ),
        in_specs=[hbm] * 5,
        out_specs=(hbm,) + (vmem,) * 4,
        scratch_shapes=[
            pltpu.VMEM(pack_shape, jnp.int16),
            pltpu.VMEM((2 * own_rows, 128), F32),
            pltpu.VMEM(branch_entry.shape, jnp.int32),
            pltpu.VMEM(branch_sign.shape, jnp.int32),
            pltpu.SemaphoreType.DMA((6,)),
        ],
        compiler_params=params(),
        name="pack",
    )(
        in_hbm(mesh_current),
        in_hbm(need_slots),
        in_hbm(port_row),
        in_hbm(branch_entry),
        in_hbm(branch_sign),
    )
    chip_members = [[(j + chip_turn(chips)) % chips for j in range(chips)]]
    same = lax.all_to_all(pack, "chips", 0, 0, tiled=True, axis_index_groups=chip_members)
    own_part, pairs = pl.pallas_call(
        own_lookup_kernel,
        out_shape=(
            shape((2, tiles, width), F32),
            pltpu.VMEM((far_count, rank // 2, rank, 2 * tiles), BF16),
        ),
        in_specs=[vmem] * 2 + [hbm],
        out_specs=(vmem,) * 2,
        scratch_shapes=[
            pltpu.VMEM(coupling_lanes.shape, BF16),
            pltpu.SemaphoreType.DMA((2,)),
        ],
        compiler_params=params(),
        cost_estimate=small_cost(),
        name="own_lookup",
    )(mesh_near, code, in_hbm(coupling_lanes))
    same = pl.pallas_call(
        hand_on_kernel,
        out_shape=shape(same.shape, same.dtype),
        in_specs=[hbm] * 2,
        out_specs=hbm,
        input_output_aliases={0: 0},
        compiler_params=params(),
        name="hand_on",
    )(same, own_part)
    other = lax.ppermute(same, "core", [(0, 1), (1, 0)])
    part, same_rows = pl.pallas_call(
        functools.partial(same_core_kernel, first=own_rows),
        out_shape=(shape((2, tiles, width), F32), shape((2, chips, 128), F32)),
        in_specs=[vmem] * 4,
        out_specs=(vmem,) * 2,
        scratch_shapes=[pltpu.VMEM((2, chips, 128), F32)],
        compiler_params=params(),
        cost_estimate=small_cost(),
        name="same_core",
    )(own_part, same, need_near, code)
    current, coeff, other_rows = pl.pallas_call(
        functools.partial(current_kernel, first=own_rows),
        out_shape=(
            shape((2, tiles, width), F32),
            shape((peers, rank, 2 * tiles), BF16),
            shape((2, chips, 128), F32),
        ),
        in_specs=[vmem] * 4 + [hbm],
        out_specs=(vmem,) * 3,
        scratch_shapes=[
            pltpu.VMEM((2, chips, 128), F32),
            pltpu.VMEM(basis_in_rows.shape, BF16),
            pltpu.SemaphoreType.DMA((1,)),
        ],
        compiler_params=params(),
        name="currents",
    )(part, other, need_near, code, in_hbm(basis_in_rows))
    members = [[(j + turn(peers)) % peers for j in range(peers)]]
    all_coeff = lax.all_to_all(
        coeff, ("chips", "core"), 0, 0, tiled=True, axis_index_groups=members
    )
    near_rows = near_blocks.reshape(tiles * near_count * width, width)
    near = pl.pallas_call(
        near_kernel,
        out_shape=shape((2, tiles, width), F32),
        in_specs=[vmem] * 2 + [hbm] * 2,
        out_specs=vmem,
        scratch_shapes=[
            pltpu.VMEM((near_count * width, 2 * tiles), BF16),
            pltpu.VMEM(near_rows.shape, BF16),
            pltpu.VMEM((tiles, width), F32),
            pltpu.SemaphoreType.DMA((3,)),
        ],
        compiler_params=params(),
        cost_estimate=pl.CostEstimate(
            flops=256 * near_blocks.size, bytes_accessed=2 * near_blocks.size, transcendentals=0
        ),
        name="near_field",
    )(sources, current, in_hbm(resistance.reshape(tiles, width)), in_hbm(near_rows))
    voltage, slots = pl.pallas_call(
        functools.partial(voltage_kernel, first=own_rows),
        out_shape=(shape((2, tiles, width), F32), shape((peers, 2, 128), F32)),
        in_specs=[vmem] * 6,
        out_specs=(vmem,) * 2,
        scratch_shapes=[
            pltpu.VMEM((2, far_count, rank, 2 * tiles), F32),
            pltpu.VMEM((rank, 2 * tiles), F32),
            pltpu.VMEM((tiles // 8, 2, 6, 8, 128), F32),
        ],
        compiler_params=params(),
        name="voltages",
    )(
        all_coeff,
        jnp.transpose(admissible),
        pairs,
        basis_out_rows,
        near,
        code,
    )
    arrived = lax.all_to_all(
        slots, ("chips", "core"), 0, 0, tiled=True, axis_index_groups=members
    )
    own, asked, picks = pl.pallas_call(
        own_sum_kernel,
        out_shape=(
            shape((2, own_rows, 128), F32),
            shape((2, chips, 128), jnp.int32),
            shape((128, peers * 128), BF16),
        ),
        in_specs=[vmem] * 6,
        out_specs=(vmem,) * 3,
        scratch_shapes=[
            pltpu.VMEM((tiles // 8, 2, 6, 8, 128), F32),
        ],
        compiler_params=params(),
        cost_estimate=small_cost(),
        name="own_sums",
    )(code, voltage, same_rows, other_rows, port_near, port_coupling)
    return pl.pallas_call(
        finish_kernel,
        out_shape=shape((2, mesh_dev), F32),
        in_specs=[vmem] * 4,
        out_specs=vmem,
        compiler_params=params(),
        name="finish",
    )(own, arrived, asked, picks)


def solution(mesh):
    groups, peers = mesh.devices.shape
    split_mesh = jax.sharding.Mesh(
        mesh.devices.reshape(groups, peers // 2, 2), ("groups", "chips", "core")
    )
    in_specs = (
        P(None, SPREAD),
        P(None, SPREAD),
        P(None, SPREAD),
        P(SPREAD, None),
        P(SPREAD),
        P(SPREAD, None, None, None),
        P(SPREAD, None),
        P(SPREAD, None, None),
        P(SPREAD, None, None, None),
        P(SPREAD, None, None),
        P(SPREAD, None),
        P("groups"),
        P(),
    )
    out_specs = P(None, SPREAD)
    return jax.shard_map(
        per_device, mesh=split_mesh, in_specs=in_specs, out_specs=out_specs, check_vma=False
    )
```

```python
import functools
import math

import jax
import jax.numpy as jnp
from jax import lax
from jax.experimental import pallas as pl
from jax.experimental.pallas import tpu as pltpu
from jax.sharding import PartitionSpec as P

F32 = jnp.float32
BF16 = jnp.bfloat16
SPREAD = ("groups", "chips", "core")
STEPS = 32000.0
VMEM_LIMIT = 24 * 1024 * 1024
NT = (((1,), (1,)), ((), ()))


def params():
    return pltpu.CompilerParams(vmem_limit_bytes=VMEM_LIMIT)


def small_cost():
    return pl.CostEstimate(flops=10**9, bytes_accessed=8 * 10**6, transcendentals=0)


def lane_pick(row, lanes):
    spread = jnp.broadcast_to(row, lanes.shape)
    return jnp.take_along_axis(spread, lanes, axis=1, mode="promise_in_bounds")


def dot_nt(left, right, precision=None):
    return lax.dot_general(
        left, right, NT, preferred_element_type=F32, precision=precision
    )


def turn(members):
    return members // 2


def chip_turn(chips):
    return chips // 2


def by_place(rows):
    shift = chip_turn(rows.shape[0])
    return jnp.concatenate([rows[shift:], rows[:shift]], axis=0)


def device_index():
    return 2 * lax.axis_index("chips") + lax.axis_index("core")


def fetch(copies, late_copies):
    for copy in copies + late_copies:
        copy.start()
    for copy in copies:
        copy.wait()


def power_of_two(exponent):
    return jnp.exp(exponent * math.log(2.0))


def fixed(value):
    return jnp.floor(value + 0.5)


def pack_kernel(
    mesh_hbm, need_hbm, port_hbm, entry_hbm, sign_hbm, out_hbm, mesh_ref, need_ref, port_ref,
    code_ref, out_ref, stage_ref, entry_ref, sign_ref, sems,
):
    late_copies = [
        pltpu.make_async_copy(entry_hbm, entry_ref, sems.at[3]),
        pltpu.make_async_copy(sign_hbm, sign_ref, sems.at[4]),
    ]
    rows = mesh_ref.shape[1] // 128
    ports = port_ref.shape[1]
    chips = out_ref.shape[0]
    fetch(
        [
            pltpu.make_async_copy(source, target, sems.at[i])
            for i, (source, target) in enumerate(
                [(mesh_hbm, mesh_ref), (need_hbm, need_ref), (port_hbm, port_ref)]
            )
        ],
        late_copies,
    )
    for r in range(rows):
        stage_ref[r : r + 1, :] = mesh_ref[0:1, r * 128 : (r + 1) * 128]
        stage_ref[rows + r : rows + r + 1, :] = mesh_ref[1:2, r * 128 : (r + 1) * 128]
    block = stage_ref[...]
    largest = jnp.maximum(jnp.max(jnp.abs(block), axis=1, keepdims=True), 1e-30)
    largest = jnp.broadcast_to(largest, block.shape)
    exponent = jnp.ceil(jnp.log(largest) * (1.0 / math.log(2.0)))
    words = fixed(block * (power_of_two(-exponent) * STEPS)).astype(jnp.int32).astype(jnp.int16)
    top_exponent = jnp.max(exponent, axis=0, keepdims=True)
    unit = power_of_two(-top_exponent) * STEPS
    row_exponent = exponent.T[0:1]
    row_exponent = jnp.concatenate(
        [row_exponent, jnp.zeros((1, 128 - 2 * rows), F32)], axis=1
    )
    port = port_ref[...] - device_index() * (rows * 128)
    port = jnp.where((port >= 0) & (port < rows * 128), port, -1)
    port = jnp.broadcast_to(jnp.concatenate([port, port], axis=1), (8, 128))
    port_high, port_low = port >> 7, port & 127
    port_value = jnp.zeros((8, 128), F32)
    lane = lax.broadcasted_iota(jnp.int32, (8, 128), 1)
    for r in range(rows):
        real_row = stage_ref[r : r + 1, :]
        imag_row = stage_ref[rows + r : rows + r + 1, :]
        both = jnp.where(
            lane < ports, lane_pick(real_row, port_low), lane_pick(imag_row, port_low)
        )
        port_value = jnp.where(port_high == r, both, port_value)
    port_scaled = port_value[0:1] * unit
    port_top = fixed(port_scaled)
    port_rest = fixed((port_scaled - port_top) * STEPS)
    tail = [
        part.astype(jnp.int32) for part in (port_top, port_rest, row_exponent, top_exponent)
    ]
    tail.append(jnp.zeros((10, 128), jnp.int32))
    need = [by_place(need_ref[pl.ds(c, chips, 2), :]) for c in range(2)]
    first = lax.axis_index("core") == 0
    need = [jnp.where(first, need[0], need[1]), jnp.where(first, need[1], need[0])]
    for chip in range(chips):
        out_ref[chip, : 2 * rows, :] = words
        extra = [part[chip : chip + 1] for part in need] + tail
        out_ref[chip, 2 * rows :, :] = jnp.concatenate(extra, axis=0).astype(jnp.int16)
    out_copy = pltpu.make_async_copy(out_ref, out_hbm, sems.at[5])
    out_copy.start()
    for copy in late_copies:
        copy.wait()
    entry_ref[...] = entry_ref[...] * 2 + sign_ref[...]
    for k in range(2):
        for t in range(code_ref.shape[1]):
            code_ref[k, t : t + 1, :] = entry_ref[k : k + 1, t * 128 : (t + 1) * 128]
    out_copy.wait()


def hand_on_kernel(pack_hbm, part_hbm, out_hbm):
    pass


def extras(pack_ref, place, rows):
    extra = pack_ref[place, 2 * rows :, :].astype(jnp.int32)
    return extra, power_of_two(extra[4:6].astype(F32)) * (1.0 / STEPS)


def unpack_rows(pack_ref, rows_ref, request, rows):
    chips = pack_ref.shape[0]
    for chip in range(chips):
        place = (chip + chips - chip_turn(chips)) % chips
        extra, unit = extras(pack_ref, place, rows)
        extra = extra.astype(F32)
        rows_ref[0, chip : chip + 1, :] = extra[request : request + 1]
        rows_ref[1, chip : chip + 1, :] = (extra[2:3] + extra[3:4] * (1.0 / STEPS)) * unit[1:2]


def ask(need_ref, pack_ref, table_ref, core, rows):
    chips = pack_ref.shape[0]
    sub = lax.broadcasted_iota(jnp.int32, (rows, 128), 0)
    for chip in range(chips):
        place = (chip + chips - chip_turn(chips)) % chips
        wanted = need_ref[pl.ds(2 * chip + core, 1), :]
        wanted = jnp.broadcast_to(jnp.maximum(wanted, 0), (rows, 128))
        here = (wanted >> 7) == sub
        low = wanted & 127
        _, unit = extras(pack_ref, place, rows)
        row_of = (wanted >> 7)[0:8]
        for c in range(2):
            slot_unit = lane_pick(unit[0:1], row_of + c * rows)[0:1]
            block = pack_ref[place, c * rows : (c + 1) * rows, :].astype(jnp.int32).astype(F32)
            picked = jnp.take_along_axis(block, low, axis=1, mode="promise_in_bounds")
            picked = jnp.where(here, picked, 0.0)
            table_ref[c, chip : chip + 1, :] = slot_unit * jnp.sum(picked, axis=0, keepdims=True)


def lookup(code_ref, start, tables):
    total = [None, None]
    for k in range(2):
        code = code_ref[k, pl.ds(start, 8), :]
        high, low = code >> 8, (code >> 1) & 127
        value = [jnp.zeros((8, 128), F32), jnp.zeros((8, 128), F32)]
        for first, step, count, row_of in tables:
            offset = high - first
            for r in range(count):
                here = offset == r * step
                for c in range(2):
                    value[c] = jnp.where(here, lane_pick(row_of(r, c), low), value[c])
        along = (code & 1) == 1
        for c in range(2):
            signed = jnp.where(along, value[c], -value[c])
            total[c] = signed if k == 0 else total[c] + signed
    return total


def own_lookup_kernel(mesh_ref, code_ref, coupling_hbm, out_ref, pair_ref, raw_ref, sems):
    rows = mesh_ref.shape[1] // 128
    far_count, rank = coupling_hbm.shape[:2]
    half = rank // 2
    part = far_count // 2
    copies = [
        pltpu.make_async_copy(
            coupling_hbm.at[pl.ds(i * part, part)], raw_ref.at[pl.ds(i * part, part)], sems.at[i]
        )
        for i in range(2)
    ]
    for copy in copies:
        copy.start()

    def own_row(r, c):
        return mesh_ref[c : c + 1, r * 128 : (r + 1) * 128]

    def block(g, carry):
        start = pl.multiple_of(g * 8, 8)
        total = lookup(code_ref, start, [(0, 1, rows, own_row)])
        out_ref[0, pl.ds(start, 8), :] = total[0]
        out_ref[1, pl.ds(start, 8), :] = total[1]
        return carry

    lax.fori_loop(0, code_ref.shape[1] // 8, block, 0, unroll=True)
    for k in range(far_count):
        if k % part == 0:
            copies[k // part].wait()
        for r in range(half):
            pair_ref[k, r] = jnp.concatenate([raw_ref[k, r], raw_ref[k, half + r]], axis=1)


def add_peers(part_ref, pack_ref, need_ref, code_ref, table_ref, out_ref, core, first):
    chips = pack_ref.shape[0]
    ask(need_ref, pack_ref, table_ref, core, first)

    def peer_row(r, c):
        return table_ref[c, r : r + 1, :]

    def block(g, carry):
        start = pl.multiple_of(g * 8, 8)
        total = lookup(code_ref, start, [(first + core, 2, chips, peer_row)])
        for c in range(2):
            out_ref[c, pl.ds(start, 8), :] = total[c] + part_ref[c, pl.ds(start, 8), :]
        return carry

    lax.fori_loop(0, code_ref.shape[1] // 8, block, 0, unroll=True)


def same_core_kernel(
    part_ref, same_ref, need_ref, code_ref, out_ref, rows_ref, table_ref, *, first
):
    unpack_rows(same_ref, rows_ref, 0, first)
    add_peers(
        part_ref, same_ref, need_ref, code_ref, table_ref, out_ref,
        lax.axis_index("core"), first,
    )


def current_kernel(
    part_ref, other_ref, need_ref, code_ref, basis_hbm, current_ref, coeff_ref, rows_ref,
    table_ref, basis_ref, sem, *, first,
):
    tiles = code_ref.shape[1]
    rank = basis_ref.shape[0] // tiles
    copy = pltpu.make_async_copy(basis_hbm, basis_ref, sem.at[0])
    copy.start()
    unpack_rows(other_ref, rows_ref, 1, first)
    add_peers(
        part_ref, other_ref, need_ref, code_ref, table_ref, current_ref,
        1 - lax.axis_index("core"), first,
    )
    copy.wait()
    inputs = jnp.concatenate([current_ref[0], current_ref[1]], axis=0)
    inputs = inputs.T.astype(BF16)
    lane_tile = lax.broadcasted_iota(jnp.int32, (rank, 2 * tiles), 1) % tiles
    full = jnp.dot(basis_ref[...], inputs, preferred_element_type=F32)
    chosen = jnp.zeros((rank, 2 * tiles), F32)
    for t in range(tiles):
        chosen = jnp.where(lane_tile == t, full[t * rank : (t + 1) * rank], chosen)
    coeff = chosen.astype(BF16)
    for p in range(coeff_ref.shape[0]):
        coeff_ref[p] = coeff


def near_kernel(
    source_ref, current_ref, resistance_hbm, blocks_hbm, out_ref, inputs_ref, blocks_ref,
    resistance_ref, sems,
):
    tiles = current_ref.shape[1]
    width = blocks_ref.shape[1]
    count = blocks_ref.shape[0] // (tiles * width)
    span = 16 * count * width
    starts = [0, tiles // 32, tiles // 16]
    copies = {}
    for i in range(2):
        rows = pl.ds(starts[i] * span, (starts[i + 1] - starts[i]) * span)
        copies[starts[i]] = pltpu.make_async_copy(
            blocks_hbm.at[rows], blocks_ref.at[rows], sems.at[i]
        )
    late_copy = pltpu.make_async_copy(resistance_hbm, resistance_ref, sems.at[2])
    for copy in copies.values():
        copy.start()
    late_copy.start()
    lane_tile = lax.broadcasted_iota(jnp.int32, (width, 128), 1) % tiles
    rows = jnp.concatenate([current_ref[0], current_ref[1]], axis=0)
    columns = rows.T.astype(BF16)
    row_index = lax.broadcasted_iota(jnp.int32, (128, 128), 0)
    for k in range(count):
        picks = jnp.where(row_index == source_ref[k : k + 1, :], 1.0, 0.0).astype(BF16)
        inputs_ref[k * width : (k + 1) * width, :] = jnp.dot(
            columns, picks, preferred_element_type=F32
        ).astype(BF16)
    inputs = inputs_ref[...]
    total = jnp.zeros((width, 128), F32)
    for g in range(tiles // 16):
        if g in copies:
            copies[g].wait()
        block = jnp.concatenate(
            [
                jnp.concatenate(
                    [
                        blocks_ref[(t * count + k) * width : (t * count + k + 1) * width, :]
                        for t in range(g * 16, g * 16 + 16)
                    ],
                    axis=0,
                )
                for k in range(count)
            ],
            axis=1,
        )
        full = jnp.dot(block, inputs, preferred_element_type=F32)
        for i in range(16):
            total = jnp.where(
                lane_tile == g * 16 + i, full[i * width : (i + 1) * width], total
            )
    rows = total.T
    late_copy.wait()
    resistance = resistance_ref[...]
    out_ref[0] = resistance * current_ref[0] - rows[tiles:]
    out_ref[1] = resistance * current_ref[1] + rows[:tiles]


def split(value):
    top = value.astype(BF16)
    return top, (value - top.astype(F32)).astype(BF16)


def counts(rows):
    return lax.broadcasted_iota(jnp.int32, (rows, 128), 0).astype(F32)


def place(high, low, values, rows, spread_ref):
    sub_high, sub_low = counts(rows).astype(BF16), counts(128).astype(BF16)
    one, zero = jnp.ones((128, 128), BF16), jnp.zeros((128, 128), BF16)
    spread_ref[0] = high.astype(F32)
    spread_ref[1] = low.astype(F32)
    for c, value in enumerate(values):
        top, rest = split(value)
        spread_ref[2 + 2 * c] = top.astype(F32)
        spread_ref[3 + 2 * c] = rest.astype(F32)

    def spread(j, i, count):
        return jnp.broadcast_to(spread_ref[j, i : i + 1, :], (count, 128)).astype(BF16)

    left, right = [], []
    for i in range(8):
        here = spread(0, i, rows) == sub_high
        left.append(
            jnp.concatenate(
                [jnp.where(here, spread(j, i, rows), zero[:rows]) for j in range(2, 6)], axis=0
            )
        )
        right.append(jnp.where(spread(1, i, 128) == sub_low, one, zero))
    return jnp.concatenate(left, axis=1), jnp.concatenate(right, axis=1)


def place_few(high, low, values, rows):
    sub_high = lax.broadcasted_iota(jnp.int32, (rows, 128), 0)
    sub_low = lax.broadcasted_iota(jnp.int32, (128, 128), 0)
    left, right = [], []
    for i in range(high.shape[0]):
        here = jnp.broadcast_to(high[i : i + 1], (rows, 128)) == sub_high
        parts = []
        for value in values:
            spread = jnp.where(here, jnp.broadcast_to(value[i : i + 1], (rows, 128)), 0.0)
            parts.extend(split(spread))
        left.append(jnp.concatenate(parts, axis=0))
        there = jnp.broadcast_to(low[i : i + 1], (128, 128)) == sub_low
        right.append(jnp.where(there, 1.0, 0.0).astype(BF16))
    return jnp.concatenate(left, axis=1), jnp.concatenate(right, axis=1)


def scatter(code_ref, voltage_ref, spread_ref, first, rows, low_streams):
    total = None
    for g in range(code_ref.shape[1] // 8):
        for k in range(2):
            code = code_ref[k, g * 8 : g * 8 + 8, :]
            along = (code & 1) == 1
            values = []
            for c in range(2):
                voltage = voltage_ref[c, g * 8 : g * 8 + 8, :]
                values.append(jnp.where(along, voltage, -voltage))
            left, right = place(
                (code >> 8) - first, (code >> 1) & 127, values, rows, spread_ref.at[g, k]
            )
            term = dot_nt(right, left) if low_streams else dot_nt(left, right)
            total = term if total is None else total + term
    total = total.T if low_streams else total
    return [
        total[2 * c * rows : (2 * c + 1) * rows] + total[(2 * c + 1) * rows : (2 * c + 2) * rows]
        for c in range(2)
    ]


def voltage_kernel(
    coeff_ref, admissible_ref, coupling_ref, basis_ref, near_ref, code_ref, voltage_ref, slot_ref,
    picked_ref, mixed_ref, spread_ref, *, first,
):
    peers, rank, lanes = coeff_ref.shape
    far_count = coupling_ref.shape[0]
    tiles = lanes // 2
    half = rank // 2
    groups = half // 4
    device = device_index()
    all_tiles = peers * tiles
    band = all_tiles // far_count
    spans = band // tiles + 1
    stride = peers // far_count
    admissible = jnp.concatenate([admissible_ref[...], admissible_ref[...]], axis=1)
    window = lax.broadcasted_iota(jnp.int32, (far_count, lanes), 0) * band + device * tiles
    window = jnp.where(window >= all_tiles, window - all_tiles, window)
    shifted = admissible - window
    shifted = jnp.where(shifted < 0, shifted + all_tiles, shifted)
    component = lax.broadcasted_iota(jnp.int32, (rank, lanes), 1) // tiles
    for k in range(far_count):
        picked = jnp.zeros((rank, lanes), F32)
        for i in range(spans):
            block = coeff_ref[(device + k * stride + i + peers - turn(peers)) % peers].astype(F32)
            target = jnp.broadcast_to(shifted[k : k + 1] - i * tiles, (rank, lanes))
            source = jnp.clip(target, 0, tiles - 1) + component * tiles
            value = jnp.take_along_axis(block, source, axis=1, mode="promise_in_bounds")
            picked = jnp.where((target >= 0) & (target < tiles), value, picked)
        turned = pltpu.roll(picked, tiles, 1)
        picked_ref[0, k] = jnp.where(component == 0, picked, turned)
        picked_ref[1, k] = jnp.where(component == 0, turned, picked)

    def mix(g, carry):
        total = [[None, None] for _ in range(4)]
        for k in range(far_count):
            picked = [picked_ref[c, k] for c in range(2)]
            for i in range(4):
                block = coupling_ref[k, g * 4 + i].astype(F32)
                for c in range(2):
                    product = block * picked[c]
                    part = product[0:8]
                    for q in range(8, rank, 8):
                        part = part + product[q : q + 8]
                    total[i][c] = part if k == 0 else total[i][c] + part
        for i in range(4):
            for c in range(2):
                row = jnp.sum(total[i][c], axis=0, keepdims=True)
                mixed_ref[pl.ds(c * half + g * 4 + i, 1), :] = row
        return carry

    lax.fori_loop(0, groups, mix, 0, unroll=True)
    mixed = mixed_ref[...].T
    mixed = jnp.concatenate([mixed[:tiles], mixed[tiles:]], axis=1).astype(BF16)
    wide = 8 * rank
    from_row = lax.broadcasted_iota(jnp.int32, (2 * rank, wide), 0)
    to_rank = lax.broadcasted_iota(jnp.int32, (2 * rank, wide), 1) % rank
    repeated = []
    for c in range(2):
        wanted = (to_rank // half) * rank + c * half + to_rank % half
        picks = jnp.where(from_row == wanted, 1.0, 0.0).astype(BF16)
        repeated.append(jnp.dot(mixed, picks, preferred_element_type=F32))
    own_block = (
        lax.broadcasted_iota(jnp.int32, (16, wide), 0) % 8
        == lax.broadcasted_iota(jnp.int32, (16, wide), 1) // rank
    )
    for g in range(tiles // 8):
        rows8 = slice(g * 8, g * 8 + 8)
        both = jnp.concatenate([repeated[0][rows8], repeated[1][rows8]], axis=0)
        both = jnp.where(own_block, both, 0.0).astype(BF16)
        far = jnp.dot(
            both, basis_ref[g * wide : (g + 1) * wide, :], preferred_element_type=F32
        )
        voltage_ref[0, rows8, :] = near_ref[0, rows8, :] - far[8:16]
        voltage_ref[1, rows8, :] = near_ref[1, rows8, :] + far[0:8]
    sums = scatter(
        code_ref, voltage_ref, spread_ref, first, slot_ref.shape[0], False
    )
    shift = turn(peers)
    for c in range(2):
        slot_ref[: peers - shift, c, :] = sums[c][shift:]
        slot_ref[peers - shift :, c, :] = sums[c][:shift]


def own_sum_kernel(
    code_ref, voltage_ref, same_ref, other_ref, port_ref, impedance_ref, own_ref, asked_ref,
    picks_ref, spread_ref,
):
    rows = own_ref.shape[1]
    ports = impedance_ref.shape[1]
    chips = same_ref.shape[1]
    first_core = lax.axis_index("core") == 0
    same = same_ref[0].astype(jnp.int32)
    other = other_ref[0].astype(jnp.int32)
    asked = [jnp.where(first_core, same, other), jnp.where(first_core, other, same)]
    sub_low = lax.broadcasted_iota(jnp.int32, (128, 128), 0)
    for core in range(2):
        asked_ref[core] = asked[core] >> 7
        low = asked[core] & 127
        for chip in range(chips):
            there = jnp.broadcast_to(low[chip : chip + 1], (128, 128)) == sub_low
            place = core * chips + chip
            picks_ref[:, place * 128 : (place + 1) * 128] = jnp.where(there, 1.0, 0.0).astype(BF16)
    port_current = jnp.sum(same_ref[1] + other_ref[1], axis=0, keepdims=True)
    real = port_current[:, :ports]
    imag = port_current[:, ports:]
    both = jnp.concatenate([real, imag, jnp.zeros((6, ports), F32)], axis=0)
    by_real = dot_nt(both, impedance_ref[0], lax.Precision.HIGHEST)
    by_imag = dot_nt(both, impedance_ref[1], lax.Precision.HIGHEST)
    pad = jnp.zeros((1, 128 - ports), F32)
    terms = [
        jnp.concatenate([by_real[0:1] - by_imag[1:2], pad], axis=1),
        jnp.concatenate([by_real[1:2] + by_imag[0:1], pad], axis=1),
    ]
    port = port_ref[...] - device_index() * (rows * 128)
    port = jnp.where((port >= 0) & (port < rows * 128), port, -1)
    port = jnp.concatenate([port, jnp.full((1, 128 - ports), -1, jnp.int32)], axis=1)
    left, right = place_few(port >> 7, port & 127, terms, rows)
    total = dot_nt(left, right)
    sums = scatter(code_ref, voltage_ref, spread_ref, 0, rows, False)
    for c in range(2):
        own_ref[c] = sums[c] + (
            total[2 * c * rows : (2 * c + 1) * rows] + total[(2 * c + 1) * rows : (2 * c + 2) * rows]
        )


def finish_kernel(own_ref, arrived_ref, asked_ref, picks_ref, out_ref):
    rows = own_ref.shape[1]
    peers = arrived_ref.shape[0]
    chips = peers // 2
    sub_high = lax.broadcasted_iota(jnp.int32, (rows, 128), 0)
    left = []
    for core in range(2):
        for chip in range(chips):
            here = jnp.broadcast_to(asked_ref[core, chip : chip + 1, :], (rows, 128)) == sub_high
            parts = []
            for c in range(2):
                place = (2 * chip + core + peers - turn(peers)) % peers
                value = jnp.broadcast_to(arrived_ref[place, c : c + 1, :], (rows, 128))
                parts.extend(split(jnp.where(here, value, 0.0)))
            left.append(jnp.concatenate(parts, axis=0))
    total = dot_nt(jnp.concatenate(left, axis=1), picks_ref[...])
    for c in range(2):
        summed = own_ref[c] + (
            total[2 * c * rows : (2 * c + 1) * rows] + total[(2 * c + 1) * rows : (2 * c + 2) * rows]
        )
        for r in range(rows):
            out_ref[c : c + 1, r * 128 : (r + 1) * 128] = summed[r : r + 1]


def per_device(
    mesh_current,
    branch_entry,
    branch_sign,
    need_slots,
    resistance,
    near_blocks,
    near_source,
    basis_in,
    coupling,
    basis_out,
    admissible,
    port_mesh,
    port_coupling,
):
    chips = lax.axis_size("chips")
    peers = 2 * chips
    core = lax.axis_index("core")
    device = 2 * lax.axis_index("chips") + core
    mesh_dev = mesh_current.shape[1]
    tiles, near_count, width, _ = near_blocks.shape
    rank = basis_in.shape[1]
    far_count = admissible.shape[1]
    own_rows = mesh_dev // 128
    vmem = pl.BlockSpec(memory_space=pltpu.VMEM)
    shape = jax.ShapeDtypeStruct

    coupling_lanes = jnp.transpose(coupling, (1, 2, 3, 0))
    basis_in_rows = basis_in.reshape(tiles * rank, width)
    basis_out_rows = basis_out.reshape(tiles * rank, width)
    half = jnp.arange(2 * tiles, dtype=jnp.int32) // tiles
    sources = jnp.transpose(near_source)
    sources = jnp.concatenate([sources, sources], axis=1) + half[None] * tiles
    def in_hbm(x):
        return pltpu.with_memory_space_constraint(x, pltpu.HBM)

    hbm = pl.BlockSpec(memory_space=pl.ANY)
    port_row = port_mesh.reshape(1, -1)
    pack_rows = 2 * own_rows + 16
    pack_shape = (chips, pack_rows, 128)
    pack, mesh_near, need_near, port_near, code = pl.pallas_call(
        pack_kernel,
        out_shape=(
            pltpu.HBM(pack_shape, jnp.int16),
            pltpu.VMEM(mesh_current.shape, F32),
            pltpu.VMEM(need_slots.shape, jnp.int32),
            pltpu.VMEM(port_row.shape, jnp.int32),
            pltpu.VMEM((2, tiles, width), jnp.int32),
        ),
        in_specs=[hbm] * 5,
        out_specs=(hbm,) + (vmem,) * 4,
        scratch_shapes=[
            pltpu.VMEM(pack_shape, jnp.int16),
            pltpu.VMEM((2 * own_rows, 128), F32),
            pltpu.VMEM(branch_entry.shape, jnp.int32),
            pltpu.VMEM(branch_sign.shape, jnp.int32),
            pltpu.SemaphoreType.DMA((6,)),
        ],
        compiler_params=params(),
        name="pack",
    )(
        in_hbm(mesh_current),
        in_hbm(need_slots),
        in_hbm(port_row),
        in_hbm(branch_entry),
        in_hbm(branch_sign),
    )
    chip_members = [[(j + chip_turn(chips)) % chips for j in range(chips)]]
    same = lax.all_to_all(pack, "chips", 0, 0, tiled=True, axis_index_groups=chip_members)
    own_part, pairs = pl.pallas_call(
        own_lookup_kernel,
        out_shape=(
            shape((2, tiles, width), F32),
            pltpu.VMEM((far_count, rank // 2, rank, 2 * tiles), BF16),
        ),
        in_specs=[vmem] * 2 + [hbm],
        out_specs=(vmem,) * 2,
        scratch_shapes=[
            pltpu.VMEM(coupling_lanes.shape, BF16),
            pltpu.SemaphoreType.DMA((2,)),
        ],
        compiler_params=params(),
        cost_estimate=small_cost(),
        name="own_lookup",
    )(mesh_near, code, in_hbm(coupling_lanes))
    same = pl.pallas_call(
        hand_on_kernel,
        out_shape=shape(same.shape, same.dtype),
        in_specs=[hbm] * 2,
        out_specs=hbm,
        input_output_aliases={0: 0},
        compiler_params=params(),
        name="hand_on",
    )(same, own_part)
    other = lax.ppermute(same, "core", [(0, 1), (1, 0)])
    part, same_rows = pl.pallas_call(
        functools.partial(same_core_kernel, first=own_rows),
        out_shape=(shape((2, tiles, width), F32), shape((2, chips, 128), F32)),
        in_specs=[vmem] * 4,
        out_specs=(vmem,) * 2,
        scratch_shapes=[pltpu.VMEM((2, chips, 128), F32)],
        compiler_params=params(),
        cost_estimate=small_cost(),
        name="same_core",
    )(own_part, same, need_near, code)
    current, coeff, other_rows = pl.pallas_call(
        functools.partial(current_kernel, first=own_rows),
        out_shape=(
            shape((2, tiles, width), F32),
            shape((peers, rank, 2 * tiles), BF16),
            shape((2, chips, 128), F32),
        ),
        in_specs=[vmem] * 4 + [hbm],
        out_specs=(vmem,) * 3,
        scratch_shapes=[
            pltpu.VMEM((2, chips, 128), F32),
            pltpu.VMEM(basis_in_rows.shape, BF16),
            pltpu.SemaphoreType.DMA((1,)),
        ],
        compiler_params=params(),
        name="currents",
    )(part, other, need_near, code, in_hbm(basis_in_rows))
    members = [[(j + turn(peers)) % peers for j in range(peers)]]
    all_coeff = lax.all_to_all(
        coeff, ("chips", "core"), 0, 0, tiled=True, axis_index_groups=members
    )
    near_rows = near_blocks.reshape(tiles * near_count * width, width)
    near = pl.pallas_call(
        near_kernel,
        out_shape=shape((2, tiles, width), F32),
        in_specs=[vmem] * 2 + [hbm] * 2,
        out_specs=vmem,
        scratch_shapes=[
            pltpu.VMEM((near_count * width, 2 * tiles), BF16),
            pltpu.VMEM(near_rows.shape, BF16),
            pltpu.VMEM((tiles, width), F32),
            pltpu.SemaphoreType.DMA((3,)),
        ],
        compiler_params=params(),
        cost_estimate=pl.CostEstimate(
            flops=256 * near_blocks.size, bytes_accessed=2 * near_blocks.size, transcendentals=0
        ),
        name="near_field",
    )(sources, current, in_hbm(resistance.reshape(tiles, width)), in_hbm(near_rows))
    voltage, slots = pl.pallas_call(
        functools.partial(voltage_kernel, first=own_rows),
        out_shape=(shape((2, tiles, width), F32), shape((peers, 2, 128), F32)),
        in_specs=[vmem] * 6,
        out_specs=(vmem,) * 2,
        scratch_shapes=[
            pltpu.VMEM((2, far_count, rank, 2 * tiles), F32),
            pltpu.VMEM((rank, 2 * tiles), F32),
            pltpu.VMEM((tiles // 8, 2, 6, 8, 128), F32),
        ],
        compiler_params=params(),
        name="voltages",
    )(
        all_coeff,
        jnp.transpose(admissible),
        pairs,
        basis_out_rows,
        near,
        code,
    )
    arrived = lax.all_to_all(
        slots, ("chips", "core"), 0, 0, tiled=True, axis_index_groups=members
    )
    own, asked, picks = pl.pallas_call(
        own_sum_kernel,
        out_shape=(
            shape((2, own_rows, 128), F32),
            shape((2, chips, 128), jnp.int32),
            shape((128, peers * 128), BF16),
        ),
        in_specs=[vmem] * 6,
        out_specs=(vmem,) * 3,
        scratch_shapes=[
            pltpu.VMEM((tiles // 8, 2, 6, 8, 128), F32),
        ],
        compiler_params=params(),
        cost_estimate=small_cost(),
        name="own_sums",
    )(code, voltage, same_rows, other_rows, port_near, port_coupling)
    return pl.pallas_call(
        finish_kernel,
        out_shape=shape((2, mesh_dev), F32),
        in_specs=[vmem] * 4,
        out_specs=vmem,
        compiler_params=params(),
        name="finish",
    )(own, arrived, asked, picks)


def solution(mesh):
    groups, peers = mesh.devices.shape
    split_mesh = jax.sharding.Mesh(
        mesh.devices.reshape(groups, peers // 2, 2), ("groups", "chips", "core")
    )
    in_specs = (
        P(None, SPREAD),
        P(None, SPREAD),
        P(None, SPREAD),
        P(SPREAD, None),
        P(SPREAD),
        P(SPREAD, None, None, None),
        P(SPREAD, None),
        P(SPREAD, None, None),
        P(SPREAD, None, None, None),
        P(SPREAD, None, None),
        P(SPREAD, None),
        P("groups"),
        P(),
    )
    out_specs = P(None, SPREAD)
    return jax.shard_map(
        per_device, mesh=split_mesh, in_specs=in_specs, out_specs=out_specs, check_vma=False
    )
```

```python
import functools
import math

import jax
import jax.numpy as jnp
from jax import lax
from jax.experimental import pallas as pl
from jax.experimental.pallas import tpu as pltpu
from jax.sharding import PartitionSpec as P

F32 = jnp.float32
BF16 = jnp.bfloat16
SPREAD = ("groups", "chips", "core")
STEPS = 32000.0
VMEM_LIMIT = 24 * 1024 * 1024
NT = (((1,), (1,)), ((), ()))


def params():
    return pltpu.CompilerParams(vmem_limit_bytes=VMEM_LIMIT)


def small_cost():
    return pl.CostEstimate(flops=10**9, bytes_accessed=8 * 10**6, transcendentals=0)


def lane_pick(row, lanes):
    spread = jnp.broadcast_to(row, lanes.shape)
    return jnp.take_along_axis(spread, lanes, axis=1, mode="promise_in_bounds")


def dot_nt(left, right, precision=None):
    return lax.dot_general(
        left, right, NT, preferred_element_type=F32, precision=precision
    )


def turn(members):
    return members // 2


def chip_turn(chips):
    return 3 * chips // 4


def by_place(rows):
    shift = chip_turn(rows.shape[0])
    return jnp.concatenate([rows[shift:], rows[:shift]], axis=0)


def device_index():
    return 2 * lax.axis_index("chips") + lax.axis_index("core")


def fetch(copies, late_copies):
    for copy in copies + late_copies:
        copy.start()
    for copy in copies:
        copy.wait()


def power_of_two(exponent):
    return jnp.exp(exponent * math.log(2.0))


def fixed(value):
    return jnp.floor(value + 0.5)


def pack_kernel(
    mesh_hbm, need_hbm, port_hbm, entry_hbm, sign_hbm, out_hbm, mesh_ref, need_ref, port_ref,
    code_ref, out_ref, stage_ref, entry_ref, sign_ref, sems,
):
    late_copies = [
        pltpu.make_async_copy(entry_hbm, entry_ref, sems.at[3]),
        pltpu.make_async_copy(sign_hbm, sign_ref, sems.at[4]),
    ]
    rows = mesh_ref.shape[1] // 128
    ports = port_ref.shape[1]
    chips = out_ref.shape[0]
    fetch(
        [
            pltpu.make_async_copy(source, target, sems.at[i])
            for i, (source, target) in enumerate(
                [(mesh_hbm, mesh_ref), (need_hbm, need_ref), (port_hbm, port_ref)]
            )
        ],
        late_copies,
    )
    for r in range(rows):
        stage_ref[r : r + 1, :] = mesh_ref[0:1, r * 128 : (r + 1) * 128]
        stage_ref[rows + r : rows + r + 1, :] = mesh_ref[1:2, r * 128 : (r + 1) * 128]
    block = stage_ref[...]
    largest = jnp.maximum(jnp.max(jnp.abs(block), axis=1, keepdims=True), 1e-30)
    largest = jnp.broadcast_to(largest, block.shape)
    exponent = jnp.ceil(jnp.log(largest) * (1.0 / math.log(2.0)))
    words = fixed(block * (power_of_two(-exponent) * STEPS)).astype(jnp.int32).astype(jnp.int16)
    top_exponent = jnp.max(exponent, axis=0, keepdims=True)
    unit = power_of_two(-top_exponent) * STEPS
    row_exponent = exponent.T[0:1]
    row_exponent = jnp.concatenate(
        [row_exponent, jnp.zeros((1, 128 - 2 * rows), F32)], axis=1
    )
    port = port_ref[...] - device_index() * (rows * 128)
    port = jnp.where((port >= 0) & (port < rows * 128), port, -1)
    port = jnp.broadcast_to(jnp.concatenate([port, port], axis=1), (8, 128))
    port_high, port_low = port >> 7, port & 127
    port_value = jnp.zeros((8, 128), F32)
    lane = lax.broadcasted_iota(jnp.int32, (8, 128), 1)
    for r in range(rows):
        real_row = stage_ref[r : r + 1, :]
        imag_row = stage_ref[rows + r : rows + r + 1, :]
        both = jnp.where(
            lane < ports, lane_pick(real_row, port_low), lane_pick(imag_row, port_low)
        )
        port_value = jnp.where(port_high == r, both, port_value)
    port_scaled = port_value[0:1] * unit
    port_top = fixed(port_scaled)
    port_rest = fixed((port_scaled - port_top) * STEPS)
    tail = [
        part.astype(jnp.int32) for part in (port_top, port_rest, row_exponent, top_exponent)
    ]
    tail.append(jnp.zeros((10, 128), jnp.int32))
    need = [by_place(need_ref[pl.ds(c, chips, 2), :]) for c in range(2)]
    first = lax.axis_index("core") == 0
    need = [jnp.where(first, need[0], need[1]), jnp.where(first, need[1], need[0])]
    for chip in range(chips):
        out_ref[chip, : 2 * rows, :] = words
        extra = [part[chip : chip + 1] for part in need] + tail
        out_ref[chip, 2 * rows :, :] = jnp.concatenate(extra, axis=0).astype(jnp.int16)
    out_copy = pltpu.make_async_copy(out_ref, out_hbm, sems.at[5])
    out_copy.start()
    for copy in late_copies:
        copy.wait()
    entry_ref[...] = entry_ref[...] * 2 + sign_ref[...]
    for k in range(2):
        for t in range(code_ref.shape[1]):
            code_ref[k, t : t + 1, :] = entry_ref[k : k + 1, t * 128 : (t + 1) * 128]
    out_copy.wait()


def hand_on_kernel(pack_hbm, part_hbm, out_hbm):
    pass


def extras(pack_ref, place, rows):
    extra = pack_ref[place, 2 * rows :, :].astype(jnp.int32)
    return extra, power_of_two(extra[4:6].astype(F32)) * (1.0 / STEPS)


def unpack_rows(pack_ref, rows_ref, request, rows):
    chips = pack_ref.shape[0]
    for chip in range(chips):
        place = (chip + chips - chip_turn(chips)) % chips
        extra, unit = extras(pack_ref, place, rows)
        extra = extra.astype(F32)
        rows_ref[0, chip : chip + 1, :] = extra[request : request + 1]
        rows_ref[1, chip : chip + 1, :] = (extra[2:3] + extra[3:4] * (1.0 / STEPS)) * unit[1:2]


def ask(need_ref, pack_ref, table_ref, core, rows):
    chips = pack_ref.shape[0]
    sub = lax.broadcasted_iota(jnp.int32, (rows, 128), 0)
    for chip in range(chips):
        place = (chip + chips - chip_turn(chips)) % chips
        wanted = need_ref[pl.ds(2 * chip + core, 1), :]
        wanted = jnp.broadcast_to(jnp.maximum(wanted, 0), (rows, 128))
        here = (wanted >> 7) == sub
        low = wanted & 127
        _, unit = extras(pack_ref, place, rows)
        row_of = (wanted >> 7)[0:8]
        for c in range(2):
            slot_unit = lane_pick(unit[0:1], row_of + c * rows)[0:1]
            block = pack_ref[place, c * rows : (c + 1) * rows, :].astype(jnp.int32).astype(F32)
            picked = jnp.take_along_axis(block, low, axis=1, mode="promise_in_bounds")
            picked = jnp.where(here, picked, 0.0)
            table_ref[c, chip : chip + 1, :] = slot_unit * jnp.sum(picked, axis=0, keepdims=True)


def lookup(code_ref, start, tables):
    total = [None, None]
    for k in range(2):
        code = code_ref[k, pl.ds(start, 8), :]
        high, low = code >> 8, (code >> 1) & 127
        value = [jnp.zeros((8, 128), F32), jnp.zeros((8, 128), F32)]
        for first, step, count, row_of in tables:
            offset = high - first
            for r in range(count):
                here = offset == r * step
                for c in range(2):
                    value[c] = jnp.where(here, lane_pick(row_of(r, c), low), value[c])
        along = (code & 1) == 1
        for c in range(2):
            signed = jnp.where(along, value[c], -value[c])
            total[c] = signed if k == 0 else total[c] + signed
    return total


def own_lookup_kernel(mesh_ref, code_ref, coupling_hbm, out_ref, pair_ref, raw_ref, sems):
    rows = mesh_ref.shape[1] // 128
    far_count, rank = coupling_hbm.shape[:2]
    half = rank // 2
    part = far_count // 2
    copies = [
        pltpu.make_async_copy(
            coupling_hbm.at[pl.ds(i * part, part)], raw_ref.at[pl.ds(i * part, part)], sems.at[i]
        )
        for i in range(2)
    ]
    for copy in copies:
        copy.start()

    def own_row(r, c):
        return mesh_ref[c : c + 1, r * 128 : (r + 1) * 128]

    def block(g, carry):
        start = pl.multiple_of(g * 8, 8)
        total = lookup(code_ref, start, [(0, 1, rows, own_row)])
        out_ref[0, pl.ds(start, 8), :] = total[0]
        out_ref[1, pl.ds(start, 8), :] = total[1]
        return carry

    lax.fori_loop(0, code_ref.shape[1] // 8, block, 0, unroll=True)
    for k in range(far_count):
        if k % part == 0:
            copies[k // part].wait()
        for r in range(half):
            pair_ref[k, r] = jnp.concatenate([raw_ref[k, r], raw_ref[k, half + r]], axis=1)


def add_peers(part_ref, pack_ref, need_ref, code_ref, table_ref, out_ref, core, first):
    chips = pack_ref.shape[0]
    ask(need_ref, pack_ref, table_ref, core, first)

    def peer_row(r, c):
        return table_ref[c, r : r + 1, :]

    def block(g, carry):
        start = pl.multiple_of(g * 8, 8)
        total = lookup(code_ref, start, [(first + core, 2, chips, peer_row)])
        for c in range(2):
            out_ref[c, pl.ds(start, 8), :] = total[c] + part_ref[c, pl.ds(start, 8), :]
        return carry

    lax.fori_loop(0, code_ref.shape[1] // 8, block, 0, unroll=True)


def same_core_kernel(
    part_ref, same_ref, need_ref, code_ref, out_ref, rows_ref, table_ref, *, first
):
    unpack_rows(same_ref, rows_ref, 0, first)
    add_peers(
        part_ref, same_ref, need_ref, code_ref, table_ref, out_ref,
        lax.axis_index("core"), first,
    )


def current_kernel(
    part_ref, other_ref, need_ref, code_ref, basis_hbm, current_ref, coeff_ref, rows_ref,
    table_ref, basis_ref, sem, *, first,
):
    tiles = code_ref.shape[1]
    rank = basis_ref.shape[0] // tiles
    copy = pltpu.make_async_copy(basis_hbm, basis_ref, sem.at[0])
    copy.start()
    unpack_rows(other_ref, rows_ref, 1, first)
    add_peers(
        part_ref, other_ref, need_ref, code_ref, table_ref, current_ref,
        1 - lax.axis_index("core"), first,
    )
    copy.wait()
    inputs = jnp.concatenate([current_ref[0], current_ref[1]], axis=0)
    inputs = inputs.T.astype(BF16)
    lane_tile = lax.broadcasted_iota(jnp.int32, (rank, 2 * tiles), 1) % tiles
    full = jnp.dot(basis_ref[...], inputs, preferred_element_type=F32)
    chosen = jnp.zeros((rank, 2 * tiles), F32)
    for t in range(tiles):
        chosen = jnp.where(lane_tile == t, full[t * rank : (t + 1) * rank], chosen)
    coeff = chosen.astype(BF16)
    for p in range(coeff_ref.shape[0]):
        coeff_ref[p] = coeff


def near_kernel(
    source_ref, current_ref, resistance_hbm, blocks_hbm, out_ref, inputs_ref, blocks_ref,
    resistance_ref, sems,
):
    tiles = current_ref.shape[1]
    width = blocks_ref.shape[1]
    count = blocks_ref.shape[0] // (tiles * width)
    span = 8 * count * width
    starts = [tiles * i // 64 for i in (0, 5, 8)]
    copies = {}
    for i in range(2):
        rows = pl.ds(starts[i] * span, (starts[i + 1] - starts[i]) * span)
        copies[starts[i]] = pltpu.make_async_copy(
            blocks_hbm.at[rows], blocks_ref.at[rows], sems.at[i]
        )
    late_copy = pltpu.make_async_copy(resistance_hbm, resistance_ref, sems.at[2])
    for copy in copies.values():
        copy.start()
    late_copy.start()
    lane_tile = lax.broadcasted_iota(jnp.int32, (width, 128), 1) % tiles
    rows = jnp.concatenate([current_ref[0], current_ref[1]], axis=0)
    columns = rows.T.astype(BF16)
    row_index = lax.broadcasted_iota(jnp.int32, (128, 128), 0)
    for k in range(count):
        picks = jnp.where(row_index == source_ref[k : k + 1, :], 1.0, 0.0).astype(BF16)
        inputs_ref[k * width : (k + 1) * width, :] = jnp.dot(
            columns, picks, preferred_element_type=F32
        ).astype(BF16)
    inputs = inputs_ref[...]
    total = jnp.zeros((width, 128), F32)
    for g in range(tiles // 8):
        if g in copies:
            copies[g].wait()
        block = jnp.concatenate(
            [
                jnp.concatenate(
                    [
                        blocks_ref[(t * count + k) * width : (t * count + k + 1) * width, :]
                        for t in range(g * 8, g * 8 + 8)
                    ],
                    axis=0,
                )
                for k in range(count)
            ],
            axis=1,
        )
        full = jnp.dot(block, inputs, preferred_element_type=F32)
        for i in range(8):
            total = jnp.where(
                lane_tile == g * 8 + i, full[i * width : (i + 1) * width], total
            )
    rows = total.T
    late_copy.wait()
    resistance = resistance_ref[...]
    out_ref[0] = resistance * current_ref[0] - rows[tiles:]
    out_ref[1] = resistance * current_ref[1] + rows[:tiles]


def split(value):
    top = value.astype(BF16)
    return top, (value - top.astype(F32)).astype(BF16)


def counts(rows):
    return lax.broadcasted_iota(jnp.int32, (rows, 128), 0).astype(F32)


def place(high, low, values, rows, spread_ref):
    sub_high, sub_low = counts(rows).astype(BF16), counts(128).astype(BF16)
    one, zero = jnp.ones((128, 128), BF16), jnp.zeros((128, 128), BF16)
    spread_ref[0] = high.astype(F32)
    spread_ref[1] = low.astype(F32)
    for c, value in enumerate(values):
        top, rest = split(value)
        spread_ref[2 + 2 * c] = top.astype(F32)
        spread_ref[3 + 2 * c] = rest.astype(F32)

    def spread(j, i, count):
        return jnp.broadcast_to(spread_ref[j, i : i + 1, :], (count, 128)).astype(BF16)

    left, right = [], []
    for i in range(8):
        here = spread(0, i, rows) == sub_high
        left.append(
            jnp.concatenate(
                [jnp.where(here, spread(j, i, rows), zero[:rows]) for j in range(2, 6)], axis=0
            )
        )
        right.append(jnp.where(spread(1, i, 128) == sub_low, one, zero))
    return jnp.concatenate(left, axis=1), jnp.concatenate(right, axis=1)


def place_few(high, low, values, rows):
    sub_high = lax.broadcasted_iota(jnp.int32, (rows, 128), 0)
    sub_low = lax.broadcasted_iota(jnp.int32, (128, 128), 0)
    left, right = [], []
    for i in range(high.shape[0]):
        here = jnp.broadcast_to(high[i : i + 1], (rows, 128)) == sub_high
        parts = []
        for value in values:
            spread = jnp.where(here, jnp.broadcast_to(value[i : i + 1], (rows, 128)), 0.0)
            parts.extend(split(spread))
        left.append(jnp.concatenate(parts, axis=0))
        there = jnp.broadcast_to(low[i : i + 1], (128, 128)) == sub_low
        right.append(jnp.where(there, 1.0, 0.0).astype(BF16))
    return jnp.concatenate(left, axis=1), jnp.concatenate(right, axis=1)


def scatter(code_ref, voltage_ref, spread_ref, first, rows, low_streams):
    total = None
    for g in range(code_ref.shape[1] // 8):
        for k in range(2):
            code = code_ref[k, g * 8 : g * 8 + 8, :]
            along = (code & 1) == 1
            values = []
            for c in range(2):
                voltage = voltage_ref[c, g * 8 : g * 8 + 8, :]
                values.append(jnp.where(along, voltage, -voltage))
            left, right = place(
                (code >> 8) - first, (code >> 1) & 127, values, rows, spread_ref.at[g, k]
            )
            term = dot_nt(right, left) if low_streams else dot_nt(left, right)
            total = term if total is None else total + term
    total = total.T if low_streams else total
    return [
        total[2 * c * rows : (2 * c + 1) * rows] + total[(2 * c + 1) * rows : (2 * c + 2) * rows]
        for c in range(2)
    ]


def voltage_kernel(
    coeff_ref, admissible_ref, coupling_ref, basis_ref, near_ref, code_ref, voltage_ref, slot_ref,
    picked_ref, mixed_ref, spread_ref, *, first,
):
    peers, rank, lanes = coeff_ref.shape
    far_count = coupling_ref.shape[0]
    tiles = lanes // 2
    half = rank // 2
    groups = half // 4
    device = device_index()
    all_tiles = peers * tiles
    band = all_tiles // far_count
    spans = band // tiles + 1
    stride = peers // far_count
    admissible = jnp.concatenate([admissible_ref[...], admissible_ref[...]], axis=1)
    window = lax.broadcasted_iota(jnp.int32, (far_count, lanes), 0) * band + device * tiles
    window = jnp.where(window >= all_tiles, window - all_tiles, window)
    shifted = admissible - window
    shifted = jnp.where(shifted < 0, shifted + all_tiles, shifted)
    component = lax.broadcasted_iota(jnp.int32, (rank, lanes), 1) // tiles
    for k in range(far_count):
        picked = jnp.zeros((rank, lanes), F32)
        for i in range(spans):
            block = coeff_ref[(device + k * stride + i + peers - turn(peers)) % peers].astype(F32)
            target = jnp.broadcast_to(shifted[k : k + 1] - i * tiles, (rank, lanes))
            source = jnp.clip(target, 0, tiles - 1) + component * tiles
            value = jnp.take_along_axis(block, source, axis=1, mode="promise_in_bounds")
            picked = jnp.where((target >= 0) & (target < tiles), value, picked)
        turned = pltpu.roll(picked, tiles, 1)
        picked_ref[0, k] = jnp.where(component == 0, picked, turned)
        picked_ref[1, k] = jnp.where(component == 0, turned, picked)

    def mix(g, carry):
        total = [[None, None] for _ in range(4)]
        for k in range(far_count):
            picked = [picked_ref[c, k] for c in range(2)]
            for i in range(4):
                block = coupling_ref[k, g * 4 + i].astype(F32)
                for c in range(2):
                    product = block * picked[c]
                    part = product[0:8]
                    for q in range(8, rank, 8):
                        part = part + product[q : q + 8]
                    total[i][c] = part if k == 0 else total[i][c] + part
        for i in range(4):
            for c in range(2):
                row = jnp.sum(total[i][c], axis=0, keepdims=True)
                mixed_ref[pl.ds(c * half + g * 4 + i, 1), :] = row
        return carry

    lax.fori_loop(0, groups, mix, 0, unroll=True)
    mixed = mixed_ref[...].T
    mixed = jnp.concatenate([mixed[:tiles], mixed[tiles:]], axis=1).astype(BF16)
    wide = 8 * rank
    from_row = lax.broadcasted_iota(jnp.int32, (2 * rank, wide), 0)
    to_rank = lax.broadcasted_iota(jnp.int32, (2 * rank, wide), 1) % rank
    repeated = []
    for c in range(2):
        wanted = (to_rank // half) * rank + c * half + to_rank % half
        picks = jnp.where(from_row == wanted, 1.0, 0.0).astype(BF16)
        repeated.append(jnp.dot(mixed, picks, preferred_element_type=F32))
    own_block = (
        lax.broadcasted_iota(jnp.int32, (16, wide), 0) % 8
        == lax.broadcasted_iota(jnp.int32, (16, wide), 1) // rank
    )
    for g in range(tiles // 8):
        rows8 = slice(g * 8, g * 8 + 8)
        both = jnp.concatenate([repeated[0][rows8], repeated[1][rows8]], axis=0)
        both = jnp.where(own_block, both, 0.0).astype(BF16)
        far = jnp.dot(
            both, basis_ref[g * wide : (g + 1) * wide, :], preferred_element_type=F32
        )
        voltage_ref[0, rows8, :] = near_ref[0, rows8, :] - far[8:16]
        voltage_ref[1, rows8, :] = near_ref[1, rows8, :] + far[0:8]
    sums = scatter(
        code_ref, voltage_ref, spread_ref, first, slot_ref.shape[0], True
    )
    shift = turn(peers)
    for c in range(2):
        slot_ref[: peers - shift, c, :] = sums[c][shift:]
        slot_ref[peers - shift :, c, :] = sums[c][:shift]


def own_sum_kernel(
    code_ref, voltage_ref, same_ref, other_ref, port_ref, impedance_ref, own_ref, asked_ref,
    picks_ref, spread_ref,
):
    rows = own_ref.shape[1]
    ports = impedance_ref.shape[1]
    chips = same_ref.shape[1]
    first_core = lax.axis_index("core") == 0
    same = same_ref[0].astype(jnp.int32)
    other = other_ref[0].astype(jnp.int32)
    asked = [jnp.where(first_core, same, other), jnp.where(first_core, other, same)]
    sub_low = lax.broadcasted_iota(jnp.int32, (128, 128), 0)
    for core in range(2):
        asked_ref[core] = asked[core] >> 7
        low = asked[core] & 127
        for chip in range(chips):
            there = jnp.broadcast_to(low[chip : chip + 1], (128, 128)) == sub_low
            place = core * chips + chip
            picks_ref[:, place * 128 : (place + 1) * 128] = jnp.where(there, 1.0, 0.0).astype(BF16)
    port_current = jnp.sum(same_ref[1] + other_ref[1], axis=0, keepdims=True)
    real = port_current[:, :ports]
    imag = port_current[:, ports:]
    both = jnp.concatenate([real, imag, jnp.zeros((6, ports), F32)], axis=0)
    by_real = dot_nt(both, impedance_ref[0], lax.Precision.HIGHEST)
    by_imag = dot_nt(both, impedance_ref[1], lax.Precision.HIGHEST)
    pad = jnp.zeros((1, 128 - ports), F32)
    terms = [
        jnp.concatenate([by_real[0:1] - by_imag[1:2], pad], axis=1),
        jnp.concatenate([by_real[1:2] + by_imag[0:1], pad], axis=1),
    ]
    port = port_ref[...] - device_index() * (rows * 128)
    port = jnp.where((port >= 0) & (port < rows * 128), port, -1)
    port = jnp.concatenate([port, jnp.full((1, 128 - ports), -1, jnp.int32)], axis=1)
    left, right = place_few(port >> 7, port & 127, terms, rows)
    total = dot_nt(left, right)
    sums = scatter(code_ref, voltage_ref, spread_ref, 0, rows, False)
    for c in range(2):
        own_ref[c] = sums[c] + (
            total[2 * c * rows : (2 * c + 1) * rows] + total[(2 * c + 1) * rows : (2 * c + 2) * rows]
        )


def finish_kernel(own_ref, arrived_ref, asked_ref, picks_ref, out_ref):
    rows = own_ref.shape[1]
    peers = arrived_ref.shape[0]
    chips = peers // 2
    sub_high = lax.broadcasted_iota(jnp.int32, (rows, 128), 0)
    left = []
    for core in range(2):
        for chip in range(chips):
            here = jnp.broadcast_to(asked_ref[core, chip : chip + 1, :], (rows, 128)) == sub_high
            parts = []
            for c in range(2):
                place = (2 * chip + core + peers - turn(peers)) % peers
                value = jnp.broadcast_to(arrived_ref[place, c : c + 1, :], (rows, 128))
                parts.extend(split(jnp.where(here, value, 0.0)))
            left.append(jnp.concatenate(parts, axis=0))
    total = dot_nt(jnp.concatenate(left, axis=1), picks_ref[...])
    for c in range(2):
        summed = own_ref[c] + (
            total[2 * c * rows : (2 * c + 1) * rows] + total[(2 * c + 1) * rows : (2 * c + 2) * rows]
        )
        for r in range(rows):
            out_ref[c : c + 1, r * 128 : (r + 1) * 128] = summed[r : r + 1]


def per_device(
    mesh_current,
    branch_entry,
    branch_sign,
    need_slots,
    resistance,
    near_blocks,
    near_source,
    basis_in,
    coupling,
    basis_out,
    admissible,
    port_mesh,
    port_coupling,
):
    chips = lax.axis_size("chips")
    peers = 2 * chips
    core = lax.axis_index("core")
    device = 2 * lax.axis_index("chips") + core
    mesh_dev = mesh_current.shape[1]
    tiles, near_count, width, _ = near_blocks.shape
    rank = basis_in.shape[1]
    far_count = admissible.shape[1]
    own_rows = mesh_dev // 128
    vmem = pl.BlockSpec(memory_space=pltpu.VMEM)
    shape = jax.ShapeDtypeStruct

    coupling_lanes = jnp.transpose(coupling, (1, 2, 3, 0))
    basis_in_rows = basis_in.reshape(tiles * rank, width)
    basis_out_rows = basis_out.reshape(tiles * rank, width)
    half = jnp.arange(2 * tiles, dtype=jnp.int32) // tiles
    sources = jnp.transpose(near_source)
    sources = jnp.concatenate([sources, sources], axis=1) + half[None] * tiles
    def in_hbm(x):
        return pltpu.with_memory_space_constraint(x, pltpu.HBM)

    hbm = pl.BlockSpec(memory_space=pl.ANY)
    port_row = port_mesh.reshape(1, -1)
    pack_rows = 2 * own_rows + 16
    pack_shape = (chips, pack_rows, 128)
    pack, mesh_near, need_near, port_near, code = pl.pallas_call(
        pack_kernel,
        out_shape=(
            pltpu.HBM(pack_shape, jnp.int16),
            pltpu.VMEM(mesh_current.shape, F32),
            pltpu.VMEM(need_slots.shape, jnp.int32),
            pltpu.VMEM(port_row.shape, jnp.int32),
            pltpu.VMEM((2, tiles, width), jnp.int32),
        ),
        in_specs=[hbm] * 5,
        out_specs=(hbm,) + (vmem,) * 4,
        scratch_shapes=[
            pltpu.VMEM(pack_shape, jnp.int16),
            pltpu.VMEM((2 * own_rows, 128), F32),
            pltpu.VMEM(branch_entry.shape, jnp.int32),
            pltpu.VMEM(branch_sign.shape, jnp.int32),
            pltpu.SemaphoreType.DMA((6,)),
        ],
        compiler_params=params(),
        name="pack",
    )(
        in_hbm(mesh_current),
        in_hbm(need_slots),
        in_hbm(port_row),
        in_hbm(branch_entry),
        in_hbm(branch_sign),
    )
    chip_members = [[(j + chip_turn(chips)) % chips for j in range(chips)]]
    same = lax.all_to_all(pack, "chips", 0, 0, tiled=True, axis_index_groups=chip_members)
    own_part, pairs = pl.pallas_call(
        own_lookup_kernel,
        out_shape=(
            shape((2, tiles, width), F32),
            pltpu.VMEM((far_count, rank // 2, rank, 2 * tiles), BF16),
        ),
        in_specs=[vmem] * 2 + [hbm],
        out_specs=(vmem,) * 2,
        scratch_shapes=[
            pltpu.VMEM(coupling_lanes.shape, BF16),
            pltpu.SemaphoreType.DMA((2,)),
        ],
        compiler_params=params(),
        cost_estimate=small_cost(),
        name="own_lookup",
    )(mesh_near, code, in_hbm(coupling_lanes))
    same = pl.pallas_call(
        hand_on_kernel,
        out_shape=shape(same.shape, same.dtype),
        in_specs=[hbm] * 2,
        out_specs=hbm,
        input_output_aliases={0: 0},
        compiler_params=params(),
        name="hand_on",
    )(same, own_part)
    other = lax.ppermute(same, "core", [(0, 1), (1, 0)])
    part, same_rows = pl.pallas_call(
        functools.partial(same_core_kernel, first=own_rows),
        out_shape=(shape((2, tiles, width), F32), shape((2, chips, 128), F32)),
        in_specs=[vmem] * 4,
        out_specs=(vmem,) * 2,
        scratch_shapes=[pltpu.VMEM((2, chips, 128), F32)],
        compiler_params=params(),
        cost_estimate=small_cost(),
        name="same_core",
    )(own_part, same, need_near, code)
    current, coeff, other_rows = pl.pallas_call(
        functools.partial(current_kernel, first=own_rows),
        out_shape=(
            shape((2, tiles, width), F32),
            shape((peers, rank, 2 * tiles), BF16),
            shape((2, chips, 128), F32),
        ),
        in_specs=[vmem] * 4 + [hbm],
        out_specs=(vmem,) * 3,
        scratch_shapes=[
            pltpu.VMEM((2, chips, 128), F32),
            pltpu.VMEM(basis_in_rows.shape, BF16),
            pltpu.SemaphoreType.DMA((1,)),
        ],
        compiler_params=params(),
        name="currents",
    )(part, other, need_near, code, in_hbm(basis_in_rows))
    members = [[(j + turn(peers)) % peers for j in range(peers)]]
    all_coeff = lax.all_to_all(
        coeff, ("chips", "core"), 0, 0, tiled=True, axis_index_groups=members
    )
    near_rows = near_blocks.reshape(tiles * near_count * width, width)
    near = pl.pallas_call(
        near_kernel,
        out_shape=shape((2, tiles, width), F32),
        in_specs=[vmem] * 2 + [hbm] * 2,
        out_specs=vmem,
        scratch_shapes=[
            pltpu.VMEM((near_count * width, 2 * tiles), BF16),
            pltpu.VMEM(near_rows.shape, BF16),
            pltpu.VMEM((tiles, width), F32),
            pltpu.SemaphoreType.DMA((3,)),
        ],
        compiler_params=params(),
        cost_estimate=pl.CostEstimate(
            flops=256 * near_blocks.size, bytes_accessed=2 * near_blocks.size, transcendentals=0
        ),
        name="near_field",
    )(sources, current, in_hbm(resistance.reshape(tiles, width)), in_hbm(near_rows))
    voltage, slots = pl.pallas_call(
        functools.partial(voltage_kernel, first=own_rows),
        out_shape=(shape((2, tiles, width), F32), shape((peers, 2, 128), F32)),
        in_specs=[vmem] * 6,
        out_specs=(vmem,) * 2,
        scratch_shapes=[
            pltpu.VMEM((2, far_count, rank, 2 * tiles), F32),
            pltpu.VMEM((rank, 2 * tiles), F32),
            pltpu.VMEM((tiles // 8, 2, 6, 8, 128), F32),
        ],
        compiler_params=params(),
        name="voltages",
    )(
        all_coeff,
        jnp.transpose(admissible),
        pairs,
        basis_out_rows,
        near,
        code,
    )
    arrived = lax.all_to_all(
        slots, ("chips", "core"), 0, 0, tiled=True, axis_index_groups=members
    )
    own, asked, picks = pl.pallas_call(
        own_sum_kernel,
        out_shape=(
            shape((2, own_rows, 128), F32),
            shape((2, chips, 128), jnp.int32),
            shape((128, peers * 128), BF16),
        ),
        in_specs=[vmem] * 6,
        out_specs=(vmem,) * 3,
        scratch_shapes=[
            pltpu.VMEM((tiles // 8, 2, 6, 8, 128), F32),
        ],
        compiler_params=params(),
        cost_estimate=small_cost(),
        name="own_sums",
    )(code, voltage, same_rows, other_rows, port_near, port_coupling)
    return pl.pallas_call(
        finish_kernel,
        out_shape=shape((2, mesh_dev), F32),
        in_specs=[vmem] * 4,
        out_specs=vmem,
        compiler_params=params(),
        name="finish",
    )(own, arrived, asked, picks)


def solution(mesh):
    groups, peers = mesh.devices.shape
    split_mesh = jax.sharding.Mesh(
        mesh.devices.reshape(groups, peers // 2, 2), ("groups", "chips", "core")
    )
    in_specs = (
        P(None, SPREAD),
        P(None, SPREAD),
        P(None, SPREAD),
        P(SPREAD, None),
        P(SPREAD),
        P(SPREAD, None, None, None),
        P(SPREAD, None),
        P(SPREAD, None, None),
        P(SPREAD, None, None, None),
        P(SPREAD, None, None),
        P(SPREAD, None),
        P("groups"),
        P(),
    )
    out_specs = P(None, SPREAD)
    return jax.shard_map(
        per_device, mesh=split_mesh, in_specs=in_specs, out_specs=out_specs, check_vma=False
    )
```

```python
import functools
import math

import jax
import jax.numpy as jnp
from jax import lax
from jax.experimental import pallas as pl
from jax.experimental.pallas import tpu as pltpu
from jax.sharding import PartitionSpec as P

F32 = jnp.float32
BF16 = jnp.bfloat16
SPREAD = ("groups", "chips", "core")
STEPS = 32000.0
VMEM_LIMIT = 24 * 1024 * 1024
NT = (((1,), (1,)), ((), ()))


def params():
    return pltpu.CompilerParams(vmem_limit_bytes=VMEM_LIMIT)


def small_cost():
    return pl.CostEstimate(flops=10**9, bytes_accessed=8 * 10**6, transcendentals=0)


def lane_pick(row, lanes):
    spread = jnp.broadcast_to(row, lanes.shape)
    return jnp.take_along_axis(spread, lanes, axis=1, mode="promise_in_bounds")


def dot_nt(left, right, precision=None):
    return lax.dot_general(
        left, right, NT, preferred_element_type=F32, precision=precision
    )


def turn(members):
    return members // 2


def chip_turn(chips):
    return chips // 2


def by_place(rows):
    shift = chip_turn(rows.shape[0])
    return jnp.concatenate([rows[shift:], rows[:shift]], axis=0)


def device_index():
    return 2 * lax.axis_index("chips") + lax.axis_index("core")


def fetch(copies, late_copies):
    for copy in copies + late_copies:
        copy.start()
    for copy in copies:
        copy.wait()


def power_of_two(exponent):
    return jnp.exp(exponent * math.log(2.0))


def fixed(value):
    return jnp.floor(value + 0.5)


def pack_kernel(
    mesh_hbm, need_hbm, port_hbm, entry_hbm, sign_hbm, out_hbm, mesh_ref, need_ref, port_ref,
    code_ref, out_ref, stage_ref, entry_ref, sign_ref, sems,
):
    late_copies = [
        pltpu.make_async_copy(entry_hbm, entry_ref, sems.at[3]),
        pltpu.make_async_copy(sign_hbm, sign_ref, sems.at[4]),
    ]
    rows = mesh_ref.shape[1] // 128
    ports = port_ref.shape[1]
    chips = out_ref.shape[0]
    fetch(
        [
            pltpu.make_async_copy(source, target, sems.at[i])
            for i, (source, target) in enumerate(
                [(mesh_hbm, mesh_ref), (need_hbm, need_ref), (port_hbm, port_ref)]
            )
        ],
        late_copies,
    )
    for r in range(rows):
        stage_ref[r : r + 1, :] = mesh_ref[0:1, r * 128 : (r + 1) * 128]
        stage_ref[rows + r : rows + r + 1, :] = mesh_ref[1:2, r * 128 : (r + 1) * 128]
    block = stage_ref[...]
    largest = jnp.maximum(jnp.max(jnp.abs(block), axis=1, keepdims=True), 1e-30)
    largest = jnp.broadcast_to(largest, block.shape)
    exponent = jnp.ceil(jnp.log(largest) * (1.0 / math.log(2.0)))
    words = fixed(block * (power_of_two(-exponent) * STEPS)).astype(jnp.int32).astype(jnp.int16)
    top_exponent = jnp.max(exponent, axis=0, keepdims=True)
    unit = power_of_two(-top_exponent) * STEPS
    row_exponent = exponent.T[0:1]
    row_exponent = jnp.concatenate(
        [row_exponent, jnp.zeros((1, 128 - 2 * rows), F32)], axis=1
    )
    port = port_ref[...] - device_index() * (rows * 128)
    port = jnp.where((port >= 0) & (port < rows * 128), port, -1)
    port = jnp.broadcast_to(jnp.concatenate([port, port], axis=1), (8, 128))
    port_high, port_low = port >> 7, port & 127
    port_value = jnp.zeros((8, 128), F32)
    lane = lax.broadcasted_iota(jnp.int32, (8, 128), 1)
    for r in range(rows):
        real_row = stage_ref[r : r + 1, :]
        imag_row = stage_ref[rows + r : rows + r + 1, :]
        both = jnp.where(
            lane < ports, lane_pick(real_row, port_low), lane_pick(imag_row, port_low)
        )
        port_value = jnp.where(port_high == r, both, port_value)
    port_scaled = port_value[0:1] * unit
    port_top = fixed(port_scaled)
    port_rest = fixed((port_scaled - port_top) * STEPS)
    tail = [
        part.astype(jnp.int32) for part in (port_top, port_rest, row_exponent, top_exponent)
    ]
    tail.append(jnp.zeros((10, 128), jnp.int32))
    need = [by_place(need_ref[pl.ds(c, chips, 2), :]) for c in range(2)]
    first = lax.axis_index("core") == 0
    need = [jnp.where(first, need[0], need[1]), jnp.where(first, need[1], need[0])]
    for chip in range(chips):
        out_ref[chip, : 2 * rows, :] = words
        extra = [part[chip : chip + 1] for part in need] + tail
        out_ref[chip, 2 * rows :, :] = jnp.concatenate(extra, axis=0).astype(jnp.int16)
    out_copy = pltpu.make_async_copy(out_ref, out_hbm, sems.at[5])
    out_copy.start()
    for copy in late_copies:
        copy.wait()
    entry_ref[...] = entry_ref[...] * 2 + sign_ref[...]
    for k in range(2):
        for t in range(code_ref.shape[1]):
            code_ref[k, t : t + 1, :] = entry_ref[k : k + 1, t * 128 : (t + 1) * 128]
    out_copy.wait()


def hand_on_kernel(pack_hbm, part_hbm, out_hbm):
    pass


def extras(pack_ref, place, rows):
    extra = pack_ref[place, 2 * rows :, :].astype(jnp.int32)
    return extra, power_of_two(extra[4:6].astype(F32)) * (1.0 / STEPS)


def unpack_rows(pack_ref, rows_ref, request, rows):
    chips = pack_ref.shape[0]
    for chip in range(chips):
        place = (chip + chips - chip_turn(chips)) % chips
        extra, unit = extras(pack_ref, place, rows)
        extra = extra.astype(F32)
        rows_ref[0, chip : chip + 1, :] = extra[request : request + 1]
        rows_ref[1, chip : chip + 1, :] = (extra[2:3] + extra[3:4] * (1.0 / STEPS)) * unit[1:2]


def ask(need_ref, pack_ref, table_ref, core, rows):
    chips = pack_ref.shape[0]
    sub = lax.broadcasted_iota(jnp.int32, (rows, 128), 0)
    for chip in range(chips):
        place = (chip + chips - chip_turn(chips)) % chips
        wanted = need_ref[pl.ds(2 * chip + core, 1), :]
        wanted = jnp.broadcast_to(jnp.maximum(wanted, 0), (rows, 128))
        here = (wanted >> 7) == sub
        low = wanted & 127
        _, unit = extras(pack_ref, place, rows)
        row_of = (wanted >> 7)[0:8]
        for c in range(2):
            slot_unit = lane_pick(unit[0:1], row_of + c * rows)[0:1]
            block = pack_ref[place, c * rows : (c + 1) * rows, :].astype(jnp.int32).astype(F32)
            picked = jnp.take_along_axis(block, low, axis=1, mode="promise_in_bounds")
            picked = jnp.where(here, picked, 0.0)
            table_ref[c, chip : chip + 1, :] = slot_unit * jnp.sum(picked, axis=0, keepdims=True)


def lookup(code_ref, start, tables):
    total = [None, None]
    for k in range(2):
        code = code_ref[k, pl.ds(start, 8), :]
        high, low = code >> 8, (code >> 1) & 127
        value = [jnp.zeros((8, 128), F32), jnp.zeros((8, 128), F32)]
        for first, step, count, row_of in tables:
            offset = high - first
            for r in range(count):
                here = offset == r * step
                for c in range(2):
                    value[c] = jnp.where(here, lane_pick(row_of(r, c), low), value[c])
        along = (code & 1) == 1
        for c in range(2):
            signed = jnp.where(along, value[c], -value[c])
            total[c] = signed if k == 0 else total[c] + signed
    return total


def own_lookup_kernel(mesh_ref, code_ref, coupling_hbm, out_ref, pair_ref, raw_ref, sems):
    rows = mesh_ref.shape[1] // 128
    far_count, rank = coupling_hbm.shape[:2]
    half = rank // 2
    part = far_count // 2
    copies = [
        pltpu.make_async_copy(
            coupling_hbm.at[pl.ds(i * part, part)], raw_ref.at[pl.ds(i * part, part)], sems.at[i]
        )
        for i in range(2)
    ]
    for copy in copies:
        copy.start()

    def own_row(r, c):
        return mesh_ref[c : c + 1, r * 128 : (r + 1) * 128]

    def block(g, carry):
        start = pl.multiple_of(g * 8, 8)
        total = lookup(code_ref, start, [(0, 1, rows, own_row)])
        out_ref[0, pl.ds(start, 8), :] = total[0]
        out_ref[1, pl.ds(start, 8), :] = total[1]
        return carry

    lax.fori_loop(0, code_ref.shape[1] // 8, block, 0, unroll=True)
    for k in range(far_count):
        if k % part == 0:
            copies[k // part].wait()
        for r in range(half):
            pair_ref[k, r] = jnp.concatenate([raw_ref[k, r], raw_ref[k, half + r]], axis=1)


def add_peers(part_ref, pack_ref, need_ref, code_ref, table_ref, out_ref, core, first):
    chips = pack_ref.shape[0]
    ask(need_ref, pack_ref, table_ref, core, first)

    def peer_row(r, c):
        return table_ref[c, r : r + 1, :]

    def block(g, carry):
        start = pl.multiple_of(g * 8, 8)
        total = lookup(code_ref, start, [(first + core, 2, chips, peer_row)])
        for c in range(2):
            out_ref[c, pl.ds(start, 8), :] = total[c] + part_ref[c, pl.ds(start, 8), :]
        return carry

    lax.fori_loop(0, code_ref.shape[1] // 8, block, 0, unroll=True)


def same_core_kernel(
    part_ref, same_ref, need_ref, code_ref, out_ref, rows_ref, table_ref, *, first
):
    unpack_rows(same_ref, rows_ref, 0, first)
    add_peers(
        part_ref, same_ref, need_ref, code_ref, table_ref, out_ref,
        lax.axis_index("core"), first,
    )


def current_kernel(
    part_ref, other_ref, need_ref, code_ref, basis_hbm, current_ref, coeff_ref, rows_ref,
    table_ref, basis_ref, sem, *, first,
):
    tiles = code_ref.shape[1]
    rank = basis_ref.shape[0] // tiles
    copy = pltpu.make_async_copy(basis_hbm, basis_ref, sem.at[0])
    copy.start()
    unpack_rows(other_ref, rows_ref, 1, first)
    add_peers(
        part_ref, other_ref, need_ref, code_ref, table_ref, current_ref,
        1 - lax.axis_index("core"), first,
    )
    copy.wait()
    inputs = jnp.concatenate([current_ref[0], current_ref[1]], axis=0)
    inputs = inputs.T.astype(BF16)
    lane_tile = lax.broadcasted_iota(jnp.int32, (rank, 2 * tiles), 1) % tiles
    full = jnp.dot(basis_ref[...], inputs, preferred_element_type=F32)
    chosen = jnp.zeros((rank, 2 * tiles), F32)
    for t in range(tiles):
        chosen = jnp.where(lane_tile == t, full[t * rank : (t + 1) * rank], chosen)
    coeff = chosen.astype(BF16)
    for p in range(coeff_ref.shape[0]):
        coeff_ref[p] = coeff


def near_kernel(
    source_ref, current_ref, resistance_hbm, blocks_hbm, out_ref, inputs_ref, blocks_ref,
    resistance_ref, sems,
):
    tiles = current_ref.shape[1]
    width = blocks_ref.shape[1]
    count = blocks_ref.shape[0] // (tiles * width)
    span = 8 * count * width
    starts = [tiles * i // 64 for i in (0, 4, 8)]
    copies = {}
    for i in range(2):
        rows = pl.ds(starts[i] * span, (starts[i + 1] - starts[i]) * span)
        copies[starts[i]] = pltpu.make_async_copy(
            blocks_hbm.at[rows], blocks_ref.at[rows], sems.at[i]
        )
    late_copy = pltpu.make_async_copy(resistance_hbm, resistance_ref, sems.at[2])
    copies[starts[0]].start()
    late_copy.start()
    late_copy.wait()
    copies[starts[1]].start()
    lane_tile = lax.broadcasted_iota(jnp.int32, (width, 128), 1) % tiles
    rows = jnp.concatenate([current_ref[0], current_ref[1]], axis=0)
    columns = rows.T.astype(BF16)
    row_index = lax.broadcasted_iota(jnp.int32, (128, 128), 0)
    for k in range(count):
        picks = jnp.where(row_index == source_ref[k : k + 1, :], 1.0, 0.0).astype(BF16)
        inputs_ref[k * width : (k + 1) * width, :] = jnp.dot(
            columns, picks, preferred_element_type=F32
        ).astype(BF16)
    inputs = inputs_ref[...]
    total = jnp.zeros((width, 128), F32)
    for g in range(tiles // 8):
        if g in copies:
            copies[g].wait()
        block = jnp.concatenate(
            [
                jnp.concatenate(
                    [
                        blocks_ref[(t * count + k) * width : (t * count + k + 1) * width, :]
                        for t in range(g * 8, g * 8 + 8)
                    ],
                    axis=0,
                )
                for k in range(count)
            ],
            axis=1,
        )
        full = jnp.dot(block, inputs, preferred_element_type=F32)
        for i in range(8):
            total = jnp.where(
                lane_tile == g * 8 + i, full[i * width : (i + 1) * width], total
            )
    rows = total.T
    resistance = resistance_ref[...]
    out_ref[0] = resistance * current_ref[0] - rows[tiles:]
    out_ref[1] = resistance * current_ref[1] + rows[:tiles]


def split(value):
    top = value.astype(BF16)
    return top, (value - top.astype(F32)).astype(BF16)


def counts(rows):
    return lax.broadcasted_iota(jnp.int32, (rows, 128), 0).astype(F32)


def place(high, low, values, rows, spread_ref):
    sub_high, sub_low = counts(rows).astype(BF16), counts(128).astype(BF16)
    one, zero = jnp.ones((128, 128), BF16), jnp.zeros((128, 128), BF16)
    spread_ref[0] = high.astype(F32)
    spread_ref[1] = low.astype(F32)
    for c, value in enumerate(values):
        top, rest = split(value)
        spread_ref[2 + 2 * c] = top.astype(F32)
        spread_ref[3 + 2 * c] = rest.astype(F32)

    def spread(j, i, count):
        return jnp.broadcast_to(spread_ref[j, i : i + 1, :], (count, 128)).astype(BF16)

    left, right = [], []
    for i in range(8):
        here = spread(0, i, rows) == sub_high
        left.append(
            jnp.concatenate(
                [jnp.where(here, spread(j, i, rows), zero[:rows]) for j in range(2, 6)], axis=0
            )
        )
        right.append(jnp.where(spread(1, i, 128) == sub_low, one, zero))
    return jnp.concatenate(left, axis=1), jnp.concatenate(right, axis=1)


def place_few(high, low, values, rows):
    sub_high = lax.broadcasted_iota(jnp.int32, (rows, 128), 0)
    sub_low = lax.broadcasted_iota(jnp.int32, (128, 128), 0)
    left, right = [], []
    for i in range(high.shape[0]):
        here = jnp.broadcast_to(high[i : i + 1], (rows, 128)) == sub_high
        parts = []
        for value in values:
            spread = jnp.where(here, jnp.broadcast_to(value[i : i + 1], (rows, 128)), 0.0)
            parts.extend(split(spread))
        left.append(jnp.concatenate(parts, axis=0))
        there = jnp.broadcast_to(low[i : i + 1], (128, 128)) == sub_low
        right.append(jnp.where(there, 1.0, 0.0).astype(BF16))
    return jnp.concatenate(left, axis=1), jnp.concatenate(right, axis=1)


def scatter(code_ref, voltage_ref, spread_ref, first, rows, low_streams):
    total = None
    for g in range(code_ref.shape[1] // 8):
        for k in range(2):
            code = code_ref[k, g * 8 : g * 8 + 8, :]
            along = (code & 1) == 1
            values = []
            for c in range(2):
                voltage = voltage_ref[c, g * 8 : g * 8 + 8, :]
                values.append(jnp.where(along, voltage, -voltage))
            left, right = place(
                (code >> 8) - first, (code >> 1) & 127, values, rows, spread_ref.at[g, k]
            )
            term = dot_nt(right, left) if low_streams else dot_nt(left, right)
            total = term if total is None else total + term
    total = total.T if low_streams else total
    return [
        total[2 * c * rows : (2 * c + 1) * rows] + total[(2 * c + 1) * rows : (2 * c + 2) * rows]
        for c in range(2)
    ]


def voltage_kernel(
    coeff_ref, admissible_ref, coupling_ref, basis_ref, near_ref, code_ref, voltage_ref, slot_ref,
    picked_ref, mixed_ref, spread_ref, *, first,
):
    peers, rank, lanes = coeff_ref.shape
    far_count = coupling_ref.shape[0]
    tiles = lanes // 2
    half = rank // 2
    groups = half // 4
    device = device_index()
    all_tiles = peers * tiles
    band = all_tiles // far_count
    spans = band // tiles + 1
    stride = peers // far_count
    admissible = jnp.concatenate([admissible_ref[...], admissible_ref[...]], axis=1)
    window = lax.broadcasted_iota(jnp.int32, (far_count, lanes), 0) * band + device * tiles
    window = jnp.where(window >= all_tiles, window - all_tiles, window)
    shifted = admissible - window
    shifted = jnp.where(shifted < 0, shifted + all_tiles, shifted)
    component = lax.broadcasted_iota(jnp.int32, (rank, lanes), 1) // tiles
    for k in range(far_count):
        picked = jnp.zeros((rank, lanes), F32)
        for i in range(spans):
            block = coeff_ref[(device + k * stride + i + peers - turn(peers)) % peers].astype(F32)
            target = jnp.broadcast_to(shifted[k : k + 1] - i * tiles, (rank, lanes))
            source = jnp.clip(target, 0, tiles - 1) + component * tiles
            value = jnp.take_along_axis(block, source, axis=1, mode="promise_in_bounds")
            picked = jnp.where((target >= 0) & (target < tiles), value, picked)
        turned = pltpu.roll(picked, tiles, 1)
        picked_ref[0, k] = jnp.where(component == 0, picked, turned)
        picked_ref[1, k] = jnp.where(component == 0, turned, picked)

    def mix(g, carry):
        total = [[None, None] for _ in range(4)]
        for k in range(far_count):
            picked = [picked_ref[c, k] for c in range(2)]
            for i in range(4):
                block = coupling_ref[k, g * 4 + i].astype(F32)
                for c in range(2):
                    product = block * picked[c]
                    part = product[0:8]
                    for q in range(8, rank, 8):
                        part = part + product[q : q + 8]
                    total[i][c] = part if k == 0 else total[i][c] + part
        for i in range(4):
            for c in range(2):
                row = jnp.sum(total[i][c], axis=0, keepdims=True)
                mixed_ref[pl.ds(c * half + g * 4 + i, 1), :] = row
        return carry

    lax.fori_loop(0, groups, mix, 0, unroll=True)
    mixed = mixed_ref[...].T
    mixed = jnp.concatenate([mixed[:tiles], mixed[tiles:]], axis=1).astype(BF16)
    wide = 8 * rank
    from_row = lax.broadcasted_iota(jnp.int32, (2 * rank, wide), 0)
    to_rank = lax.broadcasted_iota(jnp.int32, (2 * rank, wide), 1) % rank
    repeated = []
    for c in range(2):
        wanted = (to_rank // half) * rank + c * half + to_rank % half
        picks = jnp.where(from_row == wanted, 1.0, 0.0).astype(BF16)
        repeated.append(jnp.dot(mixed, picks, preferred_element_type=F32))
    own_block = (
        lax.broadcasted_iota(jnp.int32, (16, wide), 0) % 8
        == lax.broadcasted_iota(jnp.int32, (16, wide), 1) // rank
    )
    for g in range(tiles // 8):
        rows8 = slice(g * 8, g * 8 + 8)
        both = jnp.concatenate([repeated[0][rows8], repeated[1][rows8]], axis=0)
        both = jnp.where(own_block, both, 0.0).astype(BF16)
        far = jnp.dot(
            both, basis_ref[g * wide : (g + 1) * wide, :], preferred_element_type=F32
        )
        voltage_ref[0, rows8, :] = near_ref[0, rows8, :] - far[8:16]
        voltage_ref[1, rows8, :] = near_ref[1, rows8, :] + far[0:8]
    sums = scatter(
        code_ref, voltage_ref, spread_ref, first, slot_ref.shape[0], True
    )
    shift = turn(peers)
    for c in range(2):
        slot_ref[: peers - shift, c, :] = sums[c][shift:]
        slot_ref[peers - shift :, c, :] = sums[c][:shift]


def own_sum_kernel(
    code_ref, voltage_ref, same_ref, other_ref, port_ref, impedance_ref, own_ref, asked_ref,
    picks_ref, spread_ref,
):
    rows = own_ref.shape[1]
    ports = impedance_ref.shape[1]
    chips = same_ref.shape[1]
    first_core = lax.axis_index("core") == 0
    same = same_ref[0].astype(jnp.int32)
    other = other_ref[0].astype(jnp.int32)
    asked = [jnp.where(first_core, same, other), jnp.where(first_core, other, same)]
    sub_low = lax.broadcasted_iota(jnp.int32, (128, 128), 0)
    for core in range(2):
        asked_ref[core] = asked[core] >> 7
        low = asked[core] & 127
        for chip in range(chips):
            there = jnp.broadcast_to(low[chip : chip + 1], (128, 128)) == sub_low
            place = core * chips + chip
            picks_ref[:, place * 128 : (place + 1) * 128] = jnp.where(there, 1.0, 0.0).astype(BF16)
    port_current = jnp.sum(same_ref[1] + other_ref[1], axis=0, keepdims=True)
    real = port_current[:, :ports]
    imag = port_current[:, ports:]
    both = jnp.concatenate([real, imag, jnp.zeros((6, ports), F32)], axis=0)
    by_real = dot_nt(both, impedance_ref[0], lax.Precision.HIGHEST)
    by_imag = dot_nt(both, impedance_ref[1], lax.Precision.HIGHEST)
    pad = jnp.zeros((1, 128 - ports), F32)
    terms = [
        jnp.concatenate([by_real[0:1] - by_imag[1:2], pad], axis=1),
        jnp.concatenate([by_real[1:2] + by_imag[0:1], pad], axis=1),
    ]
    port = port_ref[...] - device_index() * (rows * 128)
    port = jnp.where((port >= 0) & (port < rows * 128), port, -1)
    port = jnp.concatenate([port, jnp.full((1, 128 - ports), -1, jnp.int32)], axis=1)
    left, right = place_few(port >> 7, port & 127, terms, rows)
    total = dot_nt(left, right)
    sums = scatter(code_ref, voltage_ref, spread_ref, 0, rows, False)
    for c in range(2):
        own_ref[c] = sums[c] + (
            total[2 * c * rows : (2 * c + 1) * rows] + total[(2 * c + 1) * rows : (2 * c + 2) * rows]
        )


def finish_kernel(own_ref, arrived_ref, asked_ref, picks_ref, out_ref):
    rows = own_ref.shape[1]
    peers = arrived_ref.shape[0]
    chips = peers // 2
    sub_high = lax.broadcasted_iota(jnp.int32, (rows, 128), 0)
    left = []
    for core in range(2):
        for chip in range(chips):
            here = jnp.broadcast_to(asked_ref[core, chip : chip + 1, :], (rows, 128)) == sub_high
            parts = []
            for c in range(2):
                place = (2 * chip + core + peers - turn(peers)) % peers
                value = jnp.broadcast_to(arrived_ref[place, c : c + 1, :], (rows, 128))
                parts.extend(split(jnp.where(here, value, 0.0)))
            left.append(jnp.concatenate(parts, axis=0))
    total = dot_nt(jnp.concatenate(left, axis=1), picks_ref[...])
    for c in range(2):
        summed = own_ref[c] + (
            total[2 * c * rows : (2 * c + 1) * rows] + total[(2 * c + 1) * rows : (2 * c + 2) * rows]
        )
        for r in range(rows):
            out_ref[c : c + 1, r * 128 : (r + 1) * 128] = summed[r : r + 1]


def per_device(
    mesh_current,
    branch_entry,
    branch_sign,
    need_slots,
    resistance,
    near_blocks,
    near_source,
    basis_in,
    coupling,
    basis_out,
    admissible,
    port_mesh,
    port_coupling,
):
    chips = lax.axis_size("chips")
    peers = 2 * chips
    core = lax.axis_index("core")
    device = 2 * lax.axis_index("chips") + core
    mesh_dev = mesh_current.shape[1]
    tiles, near_count, width, _ = near_blocks.shape
    rank = basis_in.shape[1]
    far_count = admissible.shape[1]
    own_rows = mesh_dev // 128
    vmem = pl.BlockSpec(memory_space=pltpu.VMEM)
    shape = jax.ShapeDtypeStruct

    coupling_lanes = jnp.transpose(coupling, (1, 2, 3, 0))
    basis_in_rows = basis_in.reshape(tiles * rank, width)
    basis_out_rows = basis_out.reshape(tiles * rank, width)
    half = jnp.arange(2 * tiles, dtype=jnp.int32) // tiles
    sources = jnp.transpose(near_source)
    sources = jnp.concatenate([sources, sources], axis=1) + half[None] * tiles
    def in_hbm(x):
        return pltpu.with_memory_space_constraint(x, pltpu.HBM)

    hbm = pl.BlockSpec(memory_space=pl.ANY)
    port_row = port_mesh.reshape(1, -1)
    pack_rows = 2 * own_rows + 16
    pack_shape = (chips, pack_rows, 128)
    pack, mesh_near, need_near, port_near, code = pl.pallas_call(
        pack_kernel,
        out_shape=(
            pltpu.HBM(pack_shape, jnp.int16),
            pltpu.VMEM(mesh_current.shape, F32),
            pltpu.VMEM(need_slots.shape, jnp.int32),
            pltpu.VMEM(port_row.shape, jnp.int32),
            pltpu.VMEM((2, tiles, width), jnp.int32),
        ),
        in_specs=[hbm] * 5,
        out_specs=(hbm,) + (vmem,) * 4,
        scratch_shapes=[
            pltpu.VMEM(pack_shape, jnp.int16),
            pltpu.VMEM((2 * own_rows, 128), F32),
            pltpu.VMEM(branch_entry.shape, jnp.int32),
            pltpu.VMEM(branch_sign.shape, jnp.int32),
            pltpu.SemaphoreType.DMA((6,)),
        ],
        compiler_params=params(),
        name="pack",
    )(
        in_hbm(mesh_current),
        in_hbm(need_slots),
        in_hbm(port_row),
        in_hbm(branch_entry),
        in_hbm(branch_sign),
    )
    chip_members = [[(j + chip_turn(chips)) % chips for j in range(chips)]]
    same = lax.all_to_all(pack, "chips", 0, 0, tiled=True, axis_index_groups=chip_members)
    own_part, pairs = pl.pallas_call(
        own_lookup_kernel,
        out_shape=(
            shape((2, tiles, width), F32),
            pltpu.VMEM((far_count, rank // 2, rank, 2 * tiles), BF16),
        ),
        in_specs=[vmem] * 2 + [hbm],
        out_specs=(vmem,) * 2,
        scratch_shapes=[
            pltpu.VMEM(coupling_lanes.shape, BF16),
            pltpu.SemaphoreType.DMA((2,)),
        ],
        compiler_params=params(),
        cost_estimate=small_cost(),
        name="own_lookup",
    )(mesh_near, code, in_hbm(coupling_lanes))
    same = pl.pallas_call(
        hand_on_kernel,
        out_shape=shape(same.shape, same.dtype),
        in_specs=[hbm] * 2,
        out_specs=hbm,
        input_output_aliases={0: 0},
        compiler_params=params(),
        name="hand_on",
    )(same, own_part)
    other = lax.ppermute(same, "core", [(0, 1), (1, 0)])
    part, same_rows = pl.pallas_call(
        functools.partial(same_core_kernel, first=own_rows),
        out_shape=(shape((2, tiles, width), F32), shape((2, chips, 128), F32)),
        in_specs=[vmem] * 4,
        out_specs=(vmem,) * 2,
        scratch_shapes=[pltpu.VMEM((2, chips, 128), F32)],
        compiler_params=params(),
        cost_estimate=small_cost(),
        name="same_core",
    )(own_part, same, need_near, code)
    current, coeff, other_rows = pl.pallas_call(
        functools.partial(current_kernel, first=own_rows),
        out_shape=(
            shape((2, tiles, width), F32),
            shape((peers, rank, 2 * tiles), BF16),
            shape((2, chips, 128), F32),
        ),
        in_specs=[vmem] * 4 + [hbm],
        out_specs=(vmem,) * 3,
        scratch_shapes=[
            pltpu.VMEM((2, chips, 128), F32),
            pltpu.VMEM(basis_in_rows.shape, BF16),
            pltpu.SemaphoreType.DMA((1,)),
        ],
        compiler_params=params(),
        name="currents",
    )(part, other, need_near, code, in_hbm(basis_in_rows))
    members = [[(j + turn(peers)) % peers for j in range(peers)]]
    all_coeff = lax.all_to_all(
        coeff, ("chips", "core"), 0, 0, tiled=True, axis_index_groups=members
    )
    near_rows = near_blocks.reshape(tiles * near_count * width, width)
    near = pl.pallas_call(
        near_kernel,
        out_shape=shape((2, tiles, width), F32),
        in_specs=[vmem] * 2 + [hbm] * 2,
        out_specs=vmem,
        scratch_shapes=[
            pltpu.VMEM((near_count * width, 2 * tiles), BF16),
            pltpu.VMEM(near_rows.shape, BF16),
            pltpu.VMEM((tiles, width), F32),
            pltpu.SemaphoreType.DMA((3,)),
        ],
        compiler_params=params(),
        cost_estimate=pl.CostEstimate(
            flops=256 * near_blocks.size, bytes_accessed=2 * near_blocks.size, transcendentals=0
        ),
        name="near_field",
    )(sources, current, in_hbm(resistance.reshape(tiles, width)), in_hbm(near_rows))
    voltage, slots = pl.pallas_call(
        functools.partial(voltage_kernel, first=own_rows),
        out_shape=(shape((2, tiles, width), F32), shape((peers, 2, 128), F32)),
        in_specs=[vmem] * 6,
        out_specs=(vmem,) * 2,
        scratch_shapes=[
            pltpu.VMEM((2, far_count, rank, 2 * tiles), F32),
            pltpu.VMEM((rank, 2 * tiles), F32),
            pltpu.VMEM((tiles // 8, 2, 6, 8, 128), F32),
        ],
        compiler_params=params(),
        name="voltages",
    )(
        all_coeff,
        jnp.transpose(admissible),
        pairs,
        basis_out_rows,
        near,
        code,
    )
    arrived = lax.all_to_all(
        slots, ("chips", "core"), 0, 0, tiled=True, axis_index_groups=members
    )
    own, asked, picks = pl.pallas_call(
        own_sum_kernel,
        out_shape=(
            shape((2, own_rows, 128), F32),
            shape((2, chips, 128), jnp.int32),
            shape((128, peers * 128), BF16),
        ),
        in_specs=[vmem] * 6,
        out_specs=(vmem,) * 3,
        scratch_shapes=[
            pltpu.VMEM((tiles // 8, 2, 6, 8, 128), F32),
        ],
        compiler_params=params(),
        cost_estimate=small_cost(),
        name="own_sums",
    )(code, voltage, same_rows, other_rows, port_near, port_coupling)
    return pl.pallas_call(
        finish_kernel,
        out_shape=shape((2, mesh_dev), F32),
        in_specs=[vmem] * 4,
        out_specs=vmem,
        compiler_params=params(),
        name="finish",
    )(own, arrived, asked, picks)


def solution(mesh):
    groups, peers = mesh.devices.shape
    split_mesh = jax.sharding.Mesh(
        mesh.devices.reshape(groups, peers // 2, 2), ("groups", "chips", "core")
    )
    in_specs = (
        P(None, SPREAD),
        P(None, SPREAD),
        P(None, SPREAD),
        P(SPREAD, None),
        P(SPREAD),
        P(SPREAD, None, None, None),
        P(SPREAD, None),
        P(SPREAD, None, None),
        P(SPREAD, None, None, None),
        P(SPREAD, None, None),
        P(SPREAD, None),
        P("groups"),
        P(),
    )
    out_specs = P(None, SPREAD)
    return jax.shard_map(
        per_device, mesh=split_mesh, in_specs=in_specs, out_specs=out_specs, check_vma=False
    )
```
